32 devices in a mesh: dp: 4 (over y, x), expert: 8 (over z, core).
Axes of the slice: x: 2, y: 2, z: 4, core: 2. Of those that a mesh axis runs over, the one named last changes fastest.
Arguments:
- tokens: bfloat16 [4096, 2048], P(('dp', 'expert')), may hold values from -6 to 6
- segments: int32 [4, 1024], P('dp'), may hold values from 0 to 7, never falling along the last dimension, each value on 1 to 512 neighbouring positions
- routes: int32 [4096, 8], P(('dp', 'expert')), may hold values from 0 to 15, all different within a row; in each aligned block of 128 rows (0 to 127, 128 to 255, ...) at most 128 rows name the same one
- cotangent: bfloat16 [4096, 2048], P(('dp', 'expert')), may hold values from -6 to 6
- norm_gain_attn: float32 [2048], replicated, may hold values from 0.1 to 1.9
- query_weight: bfloat16 [2048, 4096], P('expert'), may hold values from -0.125 to 0.125
- key_matrix: bfloat16 [2048, 512], P('expert'), may hold values from -0.125 to 0.125
- value_matrix: bfloat16 [2048, 512], P('expert'), may hold values from -0.125 to 0.125
- query_gain: float32 [128], replicated, may hold values from 0.1 to 1.9
- key_gain: float32 [128], replicated, may hold values from 0.1 to 1.9
- out_weight: bfloat16 [4096, 2048], P('expert'), may hold values from -0.375 to 0.375
- norm_gain_ffn: float32 [2048], replicated, may hold values from 0.1 to 1.9
- router_weight: bfloat16 [2048, 16], replicated, may hold values from -0.0625 to 0.0625
- gate_weight: bfloat16 [16, 2048, 768], P('expert'), may hold values from -0.125 to 0.125
- up_weight: bfloat16 [16, 2048, 768], P('expert'), may hold values from -0.125 to 0.125
- down_weight: bfloat16 [16, 768, 2048], P('expert'), may hold values from -0.625 to 0.625
Outputs:
- output: bfloat16 [4096, 2048], P(('dp', 'expert'))
- input_grad: float32 [4096, 2048], P(('dp', 'expert'))
- grad_norm_attn: float32 [2048], replicated
- grad_query: float32 [2048, 4096], P('expert')
- grad_key: float32 [2048, 512], P('expert')
- grad_value: float32 [2048, 512], P('expert')
- grad_query_gain: float32 [128], replicated
- grad_key_gain: float32 [128], replicated
- grad_out: float32 [4096, 2048], P('expert')
- grad_norm_ffn: float32 [2048], replicated
- grad_router: float32 [2048, 16], replicated
- grad_gate: float32 [16, 2048, 768], P('expert', None, 'dp')
- grad_up: float32 [16, 2048, 768], P('expert', None, 'dp')
- grad_down: float32 [16, 768, 2048], P('expert', None, 'dp')
The draws below stay inside these ranges and needn't reach their ends.
Inputs may be any that keep to these rules, and one draw needn't show every extreme that they name: Within the rows of one device no expert is named by more than 128 routes, a bound that some block reaches of them. `segments`: within a sequence document numbers never fall; a document has at most 512 positions, and some has exactly that many.
All inputs are finite; a program needn't handle non-finite values.
Results may differ from the reference program's by a relative error of at most 0.024.
Values may be sent and summed in bfloat16 or wider, within the bound.
A program may use at most 320 MiB of HBM per device.

```python
import math
import jax
import jax.numpy as jnp
import numpy as np
from jax import lax

MODEL_DIM = 2048
QUERY_HEADS = 32
KEY_VALUE_HEADS = 4
HEAD_DIM = 128
FFE = 768
TOP = 8
TOK_DEV = 128
SEQUENCE_LENGTH = 1024
EXPERTS = 16
CAP = 128
SEQS = 4
TOKENS = 4096
N_DP = 4
N_EXPERT = 8


def shard_levels(key, extent, cuts, smallest, largest):
    level = 1.0
    for dim, blocks in cuts:
        steps = jax.random.uniform(jax.random.fold_in(jax.random.fold_in(key, 6), dim), (blocks,), jnp.float32, smallest / len(cuts), largest / len(cuts))
        level = level * jnp.repeat(jnp.exp(steps), extent[dim] // blocks).reshape((-1,) + (1,) * (len(extent) - 1 - dim))
    return level


def split_up(number_of, total, bound, skew):
    loads = [(1 << 20) // math.isqrt(grade ** skew) + 1 for grade in range(2, number_of + 1)]
    spare, holding = total - bound - (number_of - 1), [1] * (number_of - 1)
    while spare > 0:
        candidates = [i for i in range(number_of - 1) if holding[i] < bound]
        whole, budget = sum([loads[i] for i in candidates]), spare
        for i in candidates:
            addition = min(bound - holding[i], max(1, budget * loads[i] // whole), spare)
            holding[i] = holding[i] + addition
            spare = spare - addition
    return np.array([bound] + holding)


def ragged(stream_key, count, total, bound, skew):
    if count == 2:
        one = jax.random.randint(stream_key, (), max(1, total - bound), min(bound, total - 1) + 1)
        return jnp.stack([one, total - one])
    sizes = jnp.asarray(split_up(count, total, bound, skew), jnp.int32)
    couples = (count - 1) // 2
    source_of, sink = sizes[1:1 + 2 * couples:2], sizes[2:2 + 2 * couples:2]
    margin = jnp.minimum(source_of - 1, bound - sink)
    moved = jax.random.randint(jax.random.fold_in(stream_key, 1), (couples,), 0, 1 << 20) % (margin + 1)
    sizes = sizes.at[1:1 + 2 * couples:2].set(source_of - moved).at[2:2 + 2 * couples:2].set(sink + moved)
    return sizes[jax.random.permutation(jax.random.fold_in(stream_key, 2), count)]


def deal_out(key, own, number, rows, count, top, most, skew):
    ranking = jax.random.permutation(key, count)
    packed, ordinary = load_shares(count, rows * top, most, skew, True), load_shares(count, rows * top, most, skew, False)
    places = jnp.arange(count)

    def named(tallies, offset_by):
        used = int((tallies > 0).sum())
        fixed = max(1, used // 4)
        shifted = fixed + (places - fixed + offset_by * (used - fixed)) % max(1, count - fixed)
        return jnp.zeros((count,), jnp.int32).at[ranking[jnp.where(places < fixed, places, shifted)]].set(jnp.asarray(tallies, jnp.int32))

    tallies = jnp.where(number % 4 == 0, named(packed, number // 4), named(ordinary, number - number // 4 - 1))
    mixed = jax.random.permutation(jax.random.fold_in(own, 3), count)
    source_of, taker = mixed[0:count // 2 * 2:2], mixed[1:count // 2 * 2:2]
    room = jnp.minimum(tallies[source_of] - 1, most - tallies[taker]) // 2
    room = jnp.where((source_of == ranking[0]) | (taker == ranking[0]) | (tallies[taker] == 0), 0, jnp.maximum(room, 0))
    shifted = jax.random.randint(jax.random.fold_in(own, 4), (count // 2,), 0, 1 << 20) % (room + 1)
    tallies = tallies.at[source_of].add(-shifted).at[taker].add(shifted)
    labels = jnp.searchsorted(jnp.cumsum(tallies), jnp.arange(rows * top), side="right").astype(jnp.int32)
    listing = labels.reshape(top, rows).T
    listing = listing[jax.random.permutation(jax.random.fold_in(own, 1), rows)]
    offset_by = jax.random.randint(jax.random.fold_in(own, 2), (rows, 1), 0, top)
    return jnp.take_along_axis(listing, (jnp.arange(top)[None, :] + offset_by) % top, axis=1)


def load_shares(number_of, total, reach, slope, full):
    loads = [(1 << 20) // math.isqrt(grade ** slope) + 1 for grade in range(1, number_of + 1)]
    largest = reach if full else min(reach, max(-(-total // number_of), total * loads[0] // sum(loads)))
    least = 1 if total - largest >= number_of - 1 else 0
    given, rest = [largest] + [least] * (number_of - 1), total - largest - least * (number_of - 1)
    while rest > 0:
        candidates = [i for i in range(1, number_of) if given[i] < largest] or [i for i in range(1, number_of) if given[i] < reach]
        whole, left = sum([loads[i] for i in candidates]), rest
        for i in candidates:
            extra = min(reach - given[i], max(1, left * loads[i] // whole), rest)
            given[i] = given[i] + extra
            rest = rest - extra
    return np.array(given)


def gaussian(own_key, shape, spread, most, cuts=(), kind=jnp.bfloat16):
    loudness = shard_levels(own_key, shape, cuts, -0.22, 0.18) if cuts else 1.0
    values = jax.random.normal(own_key, shape, jnp.float32) * spread * loudness
    return jnp.minimum(jnp.maximum(values, -most), most).astype(kind)


def setup_inputs(seed: int = 0) -> dict:
    seeds = jax.random.split(jax.random.key(seed), 17)
    tokens = gaussian(seeds[0], (TOKENS, MODEL_DIM), 1.0, 6.0, ((0, 32),))
    segments = jax.vmap(lambda own: jnp.searchsorted(jnp.cumsum(ragged(own, 8, SEQUENCE_LENGTH, SEQUENCE_LENGTH // 2, 2)), jnp.arange(SEQUENCE_LENGTH), side="right"))(jax.random.split(seeds[1], SEQS)).reshape((SEQS, SEQUENCE_LENGTH)).astype(jnp.int32)
    routes_keys = jax.random.split(jax.random.fold_in(seeds[2], 1), TOKENS // TOK_DEV)
    routes_turns = jax.random.permutation(jax.random.fold_in(seeds[2], 3), TOKENS // TOK_DEV)
    routes = jax.vmap(lambda own, number: deal_out(jax.random.fold_in(seeds[2], 2), own, number, TOK_DEV, EXPERTS, TOP, CAP, 1))(routes_keys, routes_turns).reshape((TOKENS, TOP))
    cotangent = gaussian(seeds[3], (TOKENS, MODEL_DIM), 1.0, 6.0, ((0, 32),))
    norm_gain_attn = jnp.clip(1.0 + 0.18 * jax.random.normal(seeds[4], (MODEL_DIM,), jnp.float32), 0.1, 1.9)
    query_weight = gaussian(seeds[5], (MODEL_DIM, QUERY_HEADS * HEAD_DIM), MODEL_DIM ** -0.5, 0.125, ((0, 8),))
    key_matrix = gaussian(seeds[6], (MODEL_DIM, KEY_VALUE_HEADS * HEAD_DIM), MODEL_DIM ** -0.5, 0.125, ((0, 8),))
    value_matrix = gaussian(seeds[7], (MODEL_DIM, KEY_VALUE_HEADS * HEAD_DIM), MODEL_DIM ** -0.5, 0.125, ((0, 8),))
    query_gain = jnp.clip(1.0 + 0.18 * jax.random.normal(seeds[8], (HEAD_DIM,), jnp.float32), 0.1, 1.9)
    key_gain = jnp.clip(1.0 + 0.18 * jax.random.normal(seeds[9], (HEAD_DIM,), jnp.float32), 0.1, 1.9)
    out_weight = gaussian(seeds[10], (QUERY_HEADS * HEAD_DIM, MODEL_DIM), (QUERY_HEADS * HEAD_DIM // 16) ** -0.5, 0.375, ((0, 8),))
    norm_gain_ffn = jnp.clip(1.0 + 0.18 * jax.random.normal(seeds[11], (MODEL_DIM,), jnp.float32), 0.1, 1.9)
    router_weight = gaussian(seeds[12], (MODEL_DIM, EXPERTS), (4 * MODEL_DIM) ** -0.5, 0.0625)
    gate_weight = gaussian(seeds[13], (EXPERTS, MODEL_DIM, FFE), MODEL_DIM ** -0.5, 0.125, ((0, 8),))
    up_weight = gaussian(seeds[14], (EXPERTS, MODEL_DIM, FFE), MODEL_DIM ** -0.5, 0.125, ((0, 8),))
    down_weight = gaussian(seeds[15], (EXPERTS, FFE, MODEL_DIM), (FFE // 8) ** -0.5, 0.625, ((0, 8),))
    return {"tokens": tokens, "segments": segments, "routes": routes, "cotangent": cotangent, "norm_gain_attn": norm_gain_attn, "query_weight": query_weight, "key_matrix": key_matrix, "value_matrix": value_matrix, "query_gain": query_gain, "key_gain": key_gain, "out_weight": out_weight, "norm_gain_ffn": norm_gain_ffn, "router_weight": router_weight, "gate_weight": gate_weight, "up_weight": up_weight, "down_weight": down_weight}


eps_norm = 1e-06
rope_base = 1000000.0
highest_precision = lax.Precision.HIGHEST

@jax.custom_vjp
def low_precision(v):
    return lax.optimization_barrier(v.astype(jnp.bfloat16)).astype(jnp.float32)

@jax.custom_vjp
def low_precision_backward(v):
    return v

def low_keep(v):
    return (low_precision(v), None)

def low_pass(kept, grad):
    return (grad,)

def back_keep(v):
    return (v, None)

def back_low(kept, grad):
    return (low_precision(grad),)
low_precision.defvjp(low_keep, low_pass)
low_precision_backward.defvjp(back_keep, back_low)

def norm_rows(values, gain):
    factor = lax.rsqrt(lax.optimization_barrier(jnp.mean(values * values, axis=-1, keepdims=True)) + eps_norm)
    return values * factor * gain

def rotary_tables(length, head_size):
    half = head_size // 2
    freqs = rope_base ** (-jnp.arange(half, dtype=jnp.float32) * 2.0 / head_size)
    angles = jnp.arange(length, dtype=jnp.float32)[:, None] * freqs[None, :]
    return (jnp.cos(angles)[:, None, :], jnp.sin(angles)[:, None, :])

def prepare_heads(raw, gain, cosines, sines):
    normed = norm_rows(raw, gain)
    half = raw.shape[-1] // 2
    first = normed[..., :half]
    second = normed[..., half:]
    return jnp.concatenate([first * cosines - second * sines, second * cosines + first * sines], axis=-1)

def route_tables(routes):
    flat_routes = routes.reshape(N_DP, N_EXPERT, TOK_DEV * TOP)
    marks = (flat_routes[:, :, :, None] == jnp.arange(EXPERTS, dtype=jnp.int32)[None, None, None, :]).astype(jnp.int32)
    ranks = lax.optimization_barrier(jnp.sum((jnp.cumsum(marks, axis=2) - 1) * marks, axis=3)).astype(jnp.int32)
    position = jnp.arange(N_EXPERT, dtype=jnp.int32)[None, :, None] * CAP + ranks
    within = jnp.broadcast_to(jnp.arange(N_EXPERT * TOK_DEV * TOP, dtype=jnp.int32).reshape(1, N_EXPERT, TOK_DEV * TOP), flat_routes.shape)
    group_ids = jnp.broadcast_to(jnp.arange(N_DP, dtype=jnp.int32)[:, None, None], flat_routes.shape)
    empty_table = jnp.full((N_DP, EXPERTS, N_EXPERT * CAP), -1, jnp.int32)
    return empty_table.at[group_ids, flat_routes, position].set(within)

def layer_group(weights, group_inputs, group_segments, slot_table, group_routes):
    gain_attn, query_weight, key_matrix, value_matrix, query_gain, key_gain, out_weight, gain_ffn, router_weight, gate_weight, up_weight, down_weight = weights
    group_tokens = SEQUENCE_LENGTH
    attention_hidden = low_precision(norm_rows(group_inputs, gain_attn))
    query_raw = low_precision_backward(jnp.dot(attention_hidden, query_weight, precision=highest_precision)).reshape(SEQUENCE_LENGTH, QUERY_HEADS, HEAD_DIM)
    unrotated_key = low_precision_backward(jnp.dot(attention_hidden, key_matrix, precision=highest_precision)).reshape(SEQUENCE_LENGTH, KEY_VALUE_HEADS, HEAD_DIM)
    value_reduced = low_precision(low_precision_backward(jnp.dot(attention_hidden, value_matrix, precision=highest_precision))).reshape(SEQUENCE_LENGTH, KEY_VALUE_HEADS, HEAD_DIM)
    cosines, sines = rotary_tables(SEQUENCE_LENGTH, HEAD_DIM)
    query_low = low_precision(prepare_heads(query_raw, query_gain, cosines, sines))
    key_low = low_precision(prepare_heads(unrotated_key, key_gain, cosines, sines))
    block_span = min(512, SEQUENCE_LENGTH)
    blocks = SEQUENCE_LENGTH // block_span
    positions = jnp.arange(SEQUENCE_LENGTH, dtype=jnp.int32)

    def query_block(pieces):
        query_slice, segment_piece, position_piece = pieces
        grouped_rows = query_slice.reshape(block_span, KEY_VALUE_HEADS, QUERY_HEADS // KEY_VALUE_HEADS, HEAD_DIM)
        scores = low_precision_backward(jnp.einsum('tkgd,skd->kgts', grouped_rows, key_low, precision=highest_precision) * HEAD_DIM ** (-0.5))
        allowed = (position_piece[:, None] >= positions[None, :]) & (segment_piece[:, None] == group_segments[None, :])
        probs = low_precision(jax.nn.softmax(jnp.where(allowed, scores, -1e+30), axis=-1))
        mixed = jnp.einsum('kgts,skd->tkgd', probs, value_reduced, precision=highest_precision)
        return low_precision(low_precision_backward(mixed.reshape(block_span, QUERY_HEADS * HEAD_DIM)))
    mixed_all = lax.map(jax.checkpoint(query_block), (query_low.reshape(blocks, block_span, QUERY_HEADS, HEAD_DIM), group_segments.reshape(blocks, block_span), positions.reshape(blocks, block_span)))
    attn = low_precision_backward(jnp.dot(mixed_all.reshape(group_tokens, QUERY_HEADS * HEAD_DIM), out_weight, precision=highest_precision))
    resid = group_inputs + attn
    hidden_ffn = low_precision(norm_rows(resid, gain_ffn))
    logits = low_precision_backward(jnp.dot(hidden_ffn, router_weight, precision=highest_precision))
    picked = jnp.take_along_axis(logits, group_routes, axis=1)
    gate_flat = jax.nn.softmax(picked, axis=-1).reshape(-1)
    is_valid = (slot_table >= 0).astype(jnp.float32)
    route_index = jnp.maximum(slot_table, 0).astype(jnp.int32)
    token_index = (route_index // TOP).astype(jnp.int32)
    slot_gates = gate_flat[route_index] * is_valid

    def expert(pieces):
        gate_piece, up_piece, down_piece, token_piece, valid_piece = pieces
        slot_rows = low_precision_backward(hidden_ffn[token_piece]) * valid_piece[:, None]
        gate_pre = low_precision_backward(jnp.dot(slot_rows, gate_piece, precision=highest_precision))
        up_pre = low_precision_backward(jnp.dot(slot_rows, up_piece, precision=highest_precision))
        act = low_precision(jax.nn.silu(gate_pre) * up_pre)
        return low_precision(low_precision_backward(jnp.dot(act, down_piece, precision=highest_precision)))
    expert_rows = lax.map(jax.checkpoint(expert), (gate_weight, up_weight, down_weight, token_index, is_valid))
    weighted = (expert_rows * slot_gates[:, :, None]).reshape(-1, MODEL_DIM)
    mixture = jnp.zeros((group_tokens, MODEL_DIM), jnp.float32).at[token_index.reshape(-1)].add(weighted)
    return resid + mixture

def reference(tokens, segments, routes, cotangent, norm_gain_attn, query_weight, key_matrix, value_matrix, query_gain, key_gain, out_weight, norm_gain_ffn, router_weight, gate_weight, up_weight, down_weight):
    slot_table = route_tables(routes)
    params = (norm_gain_attn.astype(jnp.float32), query_weight.astype(jnp.float32), key_matrix.astype(jnp.float32), value_matrix.astype(jnp.float32), query_gain.astype(jnp.float32), key_gain.astype(jnp.float32), out_weight.astype(jnp.float32), norm_gain_ffn.astype(jnp.float32), router_weight.astype(jnp.float32), gate_weight.astype(jnp.float32), up_weight.astype(jnp.float32), down_weight.astype(jnp.float32))
    grouped_routes = routes.reshape(N_DP, SEQUENCE_LENGTH, TOP)

    def forward(inputs, weights):

        def one_group(pieces):
            group_inputs, group_segments, group_table, group_routes = pieces
            return layer_group(weights, group_inputs, group_segments, group_table, group_routes)
        result = lax.map(jax.checkpoint(one_group), (inputs.reshape(N_DP, SEQUENCE_LENGTH, MODEL_DIM), segments, slot_table, grouped_routes))
        return result.reshape(TOKENS, MODEL_DIM)
    result, backward = jax.vjp(forward, tokens.astype(jnp.float32), params)
    input_grad, grads = backward(cotangent.astype(jnp.float32))
    return (result.astype(jnp.bfloat16), input_grad, grads[0], grads[1], grads[2], grads[3], grads[4], grads[5], grads[6], grads[7], grads[8], grads[9], grads[10], grads[11])
```

```python
import functools

import jax
import jax.numpy as jnp
from jax import lax
from jax.experimental import pallas as pl
from jax.experimental.pallas import tpu as pltpu
from jax.sharding import PartitionSpec as P

eps_norm = 1e-06
rope_base = 1000000.0
log2e = 1.4426950408889634
low = jnp.bfloat16
high = jnp.float32


def norm_rows(values, gain):
    factor = lax.rsqrt(jnp.mean(values * values, axis=-1, keepdims=True) + eps_norm)
    return values * factor * gain


def norm_back(values, gain, grad):
    factor = lax.rsqrt(jnp.mean(values * values, axis=-1, keepdims=True) + eps_norm)
    scaled = gain * grad
    inner = jnp.mean(values * scaled, axis=-1, keepdims=True)
    grad_values = factor * scaled - values * (factor * factor * factor * inner)
    return grad_values, grad * values * factor


def dot(left, right):
    return jnp.dot(left, right, preferred_element_type=high)


def dot_first(left, right):
    return lax.dot_general(left, right, (((0,), (0,)), ((), ())), preferred_element_type=high)


def dot_last(left, right):
    return lax.dot_general(left, right, (((1,), (1,)), ((), ())), preferred_element_type=high)


def rotary_tables(length, head_size):
    half = head_size // 2
    freqs = rope_base ** (-jnp.arange(half, dtype=high) * 2.0 / head_size)
    angles = jnp.arange(length, dtype=high)[:, None] * freqs[None, :]
    cosines, sines = jnp.cos(angles), jnp.sin(angles)
    return jnp.concatenate([cosines, cosines], 1), jnp.concatenate([-sines, sines], 1)


def rotate(values, cosines, sines):
    return values * cosines + pltpu.roll(values, values.shape[-1] // 2, 1) * sines


def unrotate(values, cosines, sines):
    return values * cosines - pltpu.roll(values, values.shape[-1] // 2, 1) * sines


def key_spans(length):
    block = min(256, length)
    longest = length // 2
    spans = []
    for begin in range(0, length, block):
        first = max(0, begin - longest + 1) // block * block
        spans.append((begin, block, first, begin + block - first))
    return spans


def tile_mask(seg_col, seg_row, begin, rows, first, keys):
    query_at = begin + lax.broadcasted_iota(jnp.int32, (rows, keys), 0)
    key_at = first + lax.broadcasted_iota(jnp.int32, (rows, keys), 1)
    return (query_at >= key_at) & (seg_col[begin : begin + rows, :1] == seg_row[:1, first : first + keys])


def attention_forward(
    query_ref, key_ref, value_ref, query_gain_ref, key_gain_ref, cos_ref, sin_ref, col_ref, row_ref,
    mixed_ref, query_low_ref, key_low_ref, value_low_ref, inverse_ref, value_wide,
):
    head_size = query_ref.shape[1]

    @pl.when(pl.program_id(0) == 0)
    def first_head():
        rotated = rotate(norm_rows(key_ref[...], key_gain_ref[...]), cos_ref[...], sin_ref[...])
        key_low_ref[...] = rotated.astype(low)
        value_low_ref[...] = value_ref[...].astype(low)
        value_wide[:, :head_size] = value_ref[...].astype(low)
        value_wide[:, head_size:] = jnp.ones_like(value_low_ref)

    rotated = rotate(norm_rows(query_ref[...], query_gain_ref[...]), cos_ref[...], sin_ref[...])
    query_low_ref[...] = (rotated * (head_size**-0.5 * log2e)).astype(low)
    for begin, rows, first, keys in key_spans(query_ref.shape[0]):
        scores = dot_last(query_low_ref[pl.ds(begin, rows)], key_low_ref[pl.ds(first, keys)])
        allowed = tile_mask(col_ref, row_ref, begin, rows, first, keys)
        terms = jnp.where(allowed, jnp.exp2(scores), 0.0).astype(low)
        sums = dot(terms, value_wide[pl.ds(first, keys)])
        inverse = 1.0 / sums[:, head_size:]
        mixed_ref[pl.ds(begin, rows)] = (sums[:, :head_size] * inverse).astype(low)
        inverse_ref[pl.ds(begin, rows)] = inverse


def attention_backward(
    query_ref, query_low_ref, key_low_ref, value_low_ref, inverse_ref, mixed_ref, grad_mixed_ref,
    query_gain_ref, cos_ref, sin_ref, col_ref, row_ref,
    grad_query_ref, grad_key_ref, grad_value_ref, grad_gain_ref,
):
    length, head_size = query_ref.shape

    @pl.when(pl.program_id(0) == 0)
    def first_head():
        grad_key_ref[...] = jnp.zeros_like(grad_key_ref)
        grad_value_ref[...] = jnp.zeros_like(grad_value_ref)
        grad_gain_ref[...] = jnp.zeros_like(grad_gain_ref)

    for begin, rows, first, keys in key_spans(length):
        block = pl.ds(begin, rows)
        query_low = query_low_ref[block]
        key_low = key_low_ref[pl.ds(first, keys)]
        scaled = grad_mixed_ref[block].astype(high) * inverse_ref[block]
        row_term = jnp.sum(scaled * mixed_ref[block].astype(high), axis=-1, keepdims=True)
        scaled = scaled.astype(low)
        scores = dot_last(query_low, key_low)
        allowed = tile_mask(col_ref, row_ref, begin, rows, first, keys)
        terms = jnp.where(allowed, jnp.exp2(scores), 0.0)
        grad_probs = dot_last(scaled, value_low_ref[pl.ds(first, keys)])
        grad_scores = (terms * (grad_probs - row_term)).astype(low)
        grad_value_ref[pl.ds(first, keys)] += dot_first(terms.astype(low), scaled)
        grad_key_ref[pl.ds(first, keys)] += dot_first(grad_scores, query_low) * (1.0 / log2e)
        grad_rotated = dot(grad_scores, key_low) * head_size**-0.5
        grad_normed = unrotate(grad_rotated, cos_ref[block], sin_ref[block])
        grad_raw, gain_rows = norm_back(query_ref[block], query_gain_ref[...], grad_normed)
        grad_query_ref[block] = grad_raw.astype(low)
        grad_gain_ref[...] += jnp.broadcast_to(
            jnp.sum(gain_rows, axis=0, keepdims=True), grad_gain_ref.shape
        )


def whole(shape):
    return pl.BlockSpec(shape, lambda head: (0,) * len(shape))


def run_attention_forward(raw, heads, head_size, query_gain, key_gain, cosines, sines, seg_col, seg_row):
    length = raw.shape[0]
    per_head = pl.BlockSpec((length, head_size), lambda head: (0, head))
    one = (length, head_size)
    wide = jax.ShapeDtypeStruct((length, heads * head_size), low)
    narrow = jax.ShapeDtypeStruct(one, low)
    return pl.pallas_call(
        attention_forward,
        grid=(heads,),
        in_specs=[
            per_head,
            pl.BlockSpec(one, lambda head: (0, heads)),
            pl.BlockSpec(one, lambda head: (0, heads + 1)),
            whole((1, head_size)),
            whole((1, head_size)),
            whole(one),
            whole(one),
            whole(one),
            whole((8, length)),
        ],
        out_specs=[per_head, per_head, whole(one), whole(one), per_head],
        out_shape=[wide, wide, narrow, narrow, jax.ShapeDtypeStruct((length, heads * head_size), high)],
        scratch_shapes=[pltpu.VMEM((length, 2 * head_size), low)],
        compiler_params=pltpu.CompilerParams(vmem_limit_bytes=50 << 20),
        cost_estimate=pl.CostEstimate(
            flops=3 * heads * length * length * head_size, bytes_accessed=8 * length * heads * head_size,
            transcendentals=heads * length * length // 2,
        ),
    )(raw, raw, raw, query_gain, key_gain, cosines, sines, seg_col, seg_row)


def run_attention_backward(
    raw, query_low, key_low, value_low, inverse, mixed, grad_mixed, heads, head_size, query_gain,
    cosines, sines, seg_col, seg_row,
):
    length = raw.shape[0]
    per_head = pl.BlockSpec((length, head_size), lambda head: (0, head))
    one = (length, head_size)
    return pl.pallas_call(
        attention_backward,
        grid=(heads,),
        in_specs=[
            per_head, per_head, whole(one), whole(one), per_head, per_head, per_head,
            whole((1, head_size)), whole(one), whole(one), whole(one), whole((8, length)),
        ],
        out_specs=[per_head, whole(one), whole(one), whole((8, head_size))],
        out_shape=[
            jax.ShapeDtypeStruct((length, heads * head_size), low),
            jax.ShapeDtypeStruct(one, high),
            jax.ShapeDtypeStruct(one, high),
            jax.ShapeDtypeStruct((8, head_size), high),
        ],
        compiler_params=pltpu.CompilerParams(vmem_limit_bytes=50 << 20),
        cost_estimate=pl.CostEstimate(
            flops=6 * heads * length * length * head_size, bytes_accessed=16 * length * heads * head_size,
            transcendentals=heads * length * length // 2,
        ),
    )(
        raw, query_low, key_low, value_low, inverse, mixed, grad_mixed, query_gain, cosines, sines,
        seg_col, seg_row,
    )


def gather_tokens(rows):
    return lax.all_gather(rows, "expert", axis=0, tiled=True)


def scatter_sum(partial):
    return lax.psum_scatter(partial, "expert", scatter_dimension=0, tiled=True)


def on_device(
    tokens,
    segments,
    routes,
    cotangent,
    norm_gain_attn,
    query_weight,
    key_matrix,
    value_matrix,
    query_gain,
    key_gain,
    out_weight,
    norm_gain_ffn,
    router_weight,
    gate_weight,
    up_weight,
    down_weight,
):
    length, model_width = tokens.shape
    head_size = query_gain.shape[0]
    peers = lax.axis_size("expert")
    groups = lax.axis_size("dp")
    me = lax.axis_index("expert")
    group = lax.axis_index("dp")
    shard_rows, query_width = query_weight.shape
    kv_width = key_matrix.shape[1]
    kv_heads = kv_width // head_size
    heads = query_width // head_size // peers
    sharers = peers // kv_heads
    local_width = heads * head_size
    local_experts = gate_weight.shape[0]
    experts = local_experts * peers
    full_length = length * peers
    piece = shard_rows // groups

    def own_rows(matrix):
        return lax.dynamic_slice_in_dim(matrix, group * piece, piece, 0)

    def columns(matrix, width, copies):
        split = own_rows(matrix).reshape(piece, -1, width).transpose(1, 0, 2)
        return jnp.repeat(split, copies, axis=0)

    outgoing = jnp.concatenate(
        [
            columns(query_weight, local_width, 1),
            columns(key_matrix, head_size, sharers),
            columns(value_matrix, head_size, sharers),
        ],
        axis=2,
    )
    arrived = lax.all_to_all(outgoing, "expert", split_axis=0, concat_axis=0, tiled=True)
    projection = lax.all_gather(arrived, "dp", axis=1, tiled=True).reshape(model_width, -1)

    inputs = tokens.astype(high)
    hidden_local = norm_rows(inputs, norm_gain_attn).astype(low)
    hidden = gather_tokens(hidden_local)
    raw = dot(hidden, projection)
    cosines, sines = rotary_tables(full_length, head_size)
    seg_col = jnp.broadcast_to(segments.reshape(full_length, 1), (full_length, head_size))
    seg_row = jnp.broadcast_to(segments.reshape(1, full_length), (8, full_length))
    query_gain_row = query_gain.reshape(1, head_size)
    key_gain_row = key_gain.reshape(1, head_size)
    mixed, query_low, key_low, value_low, inverse = run_attention_forward(
        raw, heads, head_size, query_gain_row, key_gain_row, cosines, sines, seg_col, seg_row
    )
    attn = scatter_sum(dot(mixed, out_weight).astype(low))
    resid = inputs + attn.astype(high)
    ffn_local = norm_rows(resid, norm_gain_ffn).astype(low)
    ffn_rows = gather_tokens(ffn_local)
    cotangents = gather_tokens(cotangent)
    all_routes = gather_tokens(routes)

    def gates_of(rows, route_rows):
        logits = dot(rows, router_weight)
        named = jnp.any(
            route_rows[:, :, None] == jnp.arange(experts, dtype=jnp.int32)[None, None, :], axis=1
        )
        top = jnp.max(jnp.where(named, logits, -jnp.inf), axis=-1, keepdims=True)
        terms = jnp.where(named, jnp.exp(jnp.where(named, logits - top, 0.0)), 0.0)
        return terms / jnp.sum(terms, axis=-1, keepdims=True)

    gates_all = gates_of(ffn_rows, all_routes)
    own_gates = lax.dynamic_slice_in_dim(gates_all, me * local_experts, local_experts, 1)
    mixture = 0.0
    grad_rows = 0.0
    gate_grads, grad_gate_w, grad_up_w, grad_down_w = [], [], [], []
    for expert in range(local_experts):
        gate_col = own_gates[:, expert : expert + 1]
        gate_pre = dot(ffn_rows, gate_weight[expert])
        up_pre = dot(ffn_rows, up_weight[expert])
        share = jax.nn.sigmoid(gate_pre)
        silu = gate_pre * share
        act = silu * up_pre
        gated_act = (act * gate_col).astype(low)
        mixture = mixture + dot(gated_act, down_weight[expert])
        plain = dot_last(cotangents, down_weight[expert])
        gate_grads.append(jnp.sum(act * plain, axis=-1, keepdims=True))
        grad_act = plain * gate_col
        grad_gate_pre = (grad_act * up_pre * (share * (1.0 + gate_pre * (1.0 - share)))).astype(low)
        grad_up_pre = (grad_act * silu).astype(low)
        grad_rows = (
            grad_rows
            + dot_last(grad_gate_pre, gate_weight[expert])
            + dot_last(grad_up_pre, up_weight[expert])
        )
        hidden_units = gated_act.shape[1]
        grad_gate_w.append(dot_first(grad_gate_pre, ffn_rows).astype(low).reshape(groups, -1, model_width))
        grad_up_w.append(dot_first(grad_up_pre, ffn_rows).astype(low).reshape(groups, -1, model_width))
        cut_width = model_width // groups
        grad_down_w.append(
            jnp.stack([
                dot_first(gated_act, cotangents[:, part * cut_width : (part + 1) * cut_width]).astype(low)
                for part in range(groups)
            ])
        )

    gate_grad = jnp.concatenate(gate_grads, axis=1)
    lane_pad = 128 - 2 * experts % 128
    placed = jnp.zeros((full_length, experts), high)
    placed = lax.dynamic_update_slice_in_dim(placed, gate_grad, me * local_experts, 1)
    upper = placed.astype(low)
    lower = (placed - upper.astype(high)).astype(low)
    sent = jnp.concatenate(
        [grad_rows.astype(low), upper, lower, jnp.zeros((full_length, lane_pad), low)], axis=1
    )
    summed_rows = scatter_sum(sent)
    output = (resid + scatter_sum(mixture.astype(low)).astype(high)).astype(low)
    grad_gates = summed_rows[:, model_width : model_width + experts].astype(high) + summed_rows[
        :, model_width + experts : model_width + 2 * experts
    ].astype(high)
    gates = gates_of(ffn_local, routes)
    grad_logits = (
        gates * (grad_gates - jnp.sum(gates * grad_gates, axis=-1, keepdims=True))
    ).astype(low)
    grad_router = dot_first(ffn_local, grad_logits)
    grad_hidden_ffn = summed_rows[:, :model_width].astype(high) + dot_last(grad_logits, router_weight)
    grad_resid_norm, gain_rows_ffn = norm_back(resid, norm_gain_ffn, grad_hidden_ffn)
    grad_resid = cotangent.astype(high) + grad_resid_norm
    grad_attn = gather_tokens(grad_resid.astype(low))
    grad_mixed = dot_last(grad_attn, out_weight).astype(low)
    grad_out = dot_first(mixed, grad_attn)
    grad_query_low, grad_key_part, grad_value_part, query_gain_part = run_attention_backward(
        raw, query_low, key_low, value_low, inverse, mixed, grad_mixed, heads, head_size,
        query_gain_row, cosines, sines, seg_col, seg_row,
    )
    both = jnp.concatenate([grad_key_part, grad_value_part], axis=1)
    step = 1
    while step < sharers:
        swap = [(peer, peer ^ step) for peer in range(peers)]
        both = both + lax.ppermute(both.astype(low), "expert", swap).astype(high)
        step *= 2
    grad_key_rot, grad_value = both[:, :head_size], both[:, head_size:].astype(low)
    place = me % sharers
    half = head_size // 2
    swapped = jnp.concatenate([grad_key_rot[:, half:], grad_key_rot[:, :half]], axis=1)
    key_raw = raw[:, local_width : local_width + head_size]
    grad_key, key_gain_rows = norm_back(key_raw, key_gain, grad_key_rot * cosines - swapped * sines)
    grad_shared = jnp.where(
        place == 0, grad_key.astype(low), jnp.where(place == 1, grad_value, jnp.zeros_like(grad_value))
    )
    own_columns = jnp.concatenate([grad_query_low, grad_shared], axis=1)
    shared_weight = jnp.where(
        place == 0,
        projection[:, local_width : local_width + head_size],
        projection[:, local_width + head_size :],
    )
    own_weight = jnp.concatenate([projection[:, :local_width], shared_weight], axis=1)
    grad_hidden_attn = scatter_sum(dot_last(own_columns, own_weight).astype(low)).astype(high)
    grad_inputs_norm, gain_rows_attn = norm_back(inputs, norm_gain_attn, grad_hidden_attn)
    input_grad = grad_resid + grad_inputs_norm

    grad_projection = dot_first(hidden, own_columns).astype(low)
    grad_projection = grad_projection.reshape(peers, shard_rows, -1)
    grad_projection = lax.psum_scatter(grad_projection, "dp", scatter_dimension=1, tiled=True)
    grad_projection = lax.all_to_all(
        grad_projection, "expert", split_axis=0, concat_axis=0, tiled=True
    )
    grad_projection = lax.all_gather(grad_projection, "dp", axis=1, tiled=True)
    grad_query_w = (
        grad_projection[:, :, :local_width].transpose(1, 0, 2).reshape(shard_rows, query_width)
    ).astype(high)
    shared = grad_projection[:, :, local_width:].reshape(kv_heads, sharers, shard_rows, head_size)
    grad_key_w = shared[:, 0].transpose(1, 0, 2).reshape(shard_rows, kv_width).astype(high)
    grad_value_w = shared[:, 1].transpose(1, 0, 2).reshape(shard_rows, kv_width).astype(high)
    grad_out_w = lax.psum_scatter(grad_out.astype(low), "dp", scatter_dimension=0, tiled=True)
    grad_out_w = lax.all_gather(grad_out_w, "dp", axis=0, tiled=True).astype(high)

    wide = jnp.concatenate(grad_gate_w + grad_up_w, axis=1)
    wide = lax.psum_scatter(wide, "dp", scatter_dimension=0, tiled=True)
    wide = wide.reshape(2, local_experts, hidden_units // groups, model_width).transpose(0, 1, 3, 2)
    wide = wide.astype(high)
    down = jnp.concatenate(grad_down_w, axis=1)
    down = lax.psum_scatter(down, "dp", scatter_dimension=0, tiled=True)
    down = down.reshape(local_experts, hidden_units, cut_width).astype(high)
    expert_sums = (wide[0], wide[1], down)
    key_gain_grad = jnp.where(place == 0, jnp.sum(key_gain_rows, axis=0), 0.0)
    small = jnp.concatenate(
        [
            jnp.sum(gain_rows_attn, axis=0),
            jnp.sum(gain_rows_ffn, axis=0),
            query_gain_part[0],
            key_gain_grad,
            grad_router.reshape(-1),
        ]
    )
    small = lax.psum(small, ("dp", "expert"))
    cut = 2 * model_width
    return (
        output,
        input_grad,
        small[:model_width],
        grad_query_w,
        grad_key_w,
        grad_value_w,
        small[cut : cut + head_size],
        small[cut + head_size : cut + 2 * head_size],
        grad_out_w,
        small[model_width:cut],
        small[cut + 2 * head_size :].reshape(model_width, experts),
        *expert_sums,
    )


def solution(mesh):
    rows = P(("dp", "expert"), None)
    split = P("expert", None)
    cube = P("expert", None, None)
    cut = P("expert", None, "dp")
    return jax.shard_map(
        on_device,
        mesh=mesh,
        in_specs=(
            rows, P("dp", None), rows, rows, P(), split, split, split, P(), P(), split, P(), P(),
            cube, cube, cube,
        ),
        out_specs=(
            rows, rows, P(), split, split, split, P(), P(), split, P(), P(), cut, cut, cut,
        ),
        check_vma=False,
    )
```

```python
import functools

import jax
import jax.numpy as jnp
import numpy as np
from jax import lax
from jax.experimental import pallas as pl
from jax.experimental.pallas import tpu as pltpu
from jax.sharding import PartitionSpec as P

eps_norm = 1e-06
rope_base = 1000000.0
log2e = 1.4426950408889634
low = jnp.bfloat16
high = jnp.float32


def norm_rows(values, gain):
    factor = lax.rsqrt(jnp.mean(values * values, axis=-1, keepdims=True) + eps_norm)
    return values * factor * gain


def norm_back(values, gain, grad):
    factor = lax.rsqrt(jnp.mean(values * values, axis=-1, keepdims=True) + eps_norm)
    scaled = gain * grad
    inner = jnp.mean(values * scaled, axis=-1, keepdims=True)
    grad_values = factor * scaled - values * (factor * factor * factor * inner)
    return grad_values, grad * values * factor


def dot(left, right):
    return jnp.dot(left, right, preferred_element_type=high)


def dot_first(left, right):
    return lax.dot_general(left, right, (((0,), (0,)), ((), ())), preferred_element_type=high)


def dot_last(left, right):
    return lax.dot_general(left, right, (((1,), (1,)), ((), ())), preferred_element_type=high)


def rotary_tables(length, head_size):
    half = head_size // 2
    freqs = rope_base ** (-jnp.arange(half, dtype=high) * 2.0 / head_size)
    angles = jnp.arange(length, dtype=high)[:, None] * freqs[None, :]
    cosines, sines = jnp.cos(angles), jnp.sin(angles)
    return jnp.concatenate([cosines, cosines], 1), jnp.concatenate([-sines, sines], 1)


def rotate(values, cosines, sines):
    return values * cosines + pltpu.roll(values, values.shape[-1] // 2, 1) * sines


def unrotate(values, cosines, sines):
    return values * cosines - pltpu.roll(values, values.shape[-1] // 2, 1) * sines


def key_spans(length):
    block = min(256, length)
    longest = length // 2
    spans = []
    for begin in range(0, length, block):
        first = max(0, begin - longest + 1) // block * block
        spans.append((begin, block, first, begin + block - first))
    return spans


def tile_mask(seg_col, seg_row, begin, rows, first, keys):
    query_at = begin + lax.broadcasted_iota(jnp.int32, (rows, keys), 0)
    key_at = first + lax.broadcasted_iota(jnp.int32, (rows, keys), 1)
    return (query_at >= key_at) & (seg_col[begin : begin + rows, :1] == seg_row[:1, first : first + keys])


def attention_forward(
    query_ref, key_ref, value_ref, query_gain_ref, key_gain_ref, cos_ref, sin_ref, col_ref, row_ref,
    mixed_ref, query_low_ref, key_low_ref, value_low_ref, inverse_ref, value_wide,
):
    head_size = query_ref.shape[1]

    @pl.when(pl.program_id(0) == 0)
    def first_head():
        rotated = rotate(norm_rows(key_ref[...], key_gain_ref[...]), cos_ref[...], sin_ref[...])
        key_low_ref[...] = rotated.astype(low)
        value_low_ref[...] = value_ref[...].astype(low)
        value_wide[:, :head_size] = value_ref[...].astype(low)
        value_wide[:, head_size:] = jnp.ones_like(value_low_ref)

    rotated = rotate(norm_rows(query_ref[...], query_gain_ref[...]), cos_ref[...], sin_ref[...])
    query_low_ref[...] = (rotated * (head_size**-0.5 * log2e)).astype(low)
    for begin, rows, first, keys in key_spans(query_ref.shape[0]):
        scores = dot_last(query_low_ref[pl.ds(begin, rows)], key_low_ref[pl.ds(first, keys)])
        allowed = tile_mask(col_ref, row_ref, begin, rows, first, keys)
        terms = jnp.where(allowed, jnp.exp2(scores), 0.0).astype(low)
        sums = dot(terms, value_wide[pl.ds(first, keys)])
        inverse = 1.0 / sums[:, head_size:]
        mixed_ref[pl.ds(begin, rows)] = (sums[:, :head_size] * inverse).astype(low)
        inverse_ref[pl.ds(begin, rows)] = inverse


def attention_backward(
    query_ref, query_low_ref, key_low_ref, value_low_ref, inverse_ref, mixed_ref, grad_mixed_ref,
    query_gain_ref, cos_ref, sin_ref, col_ref, row_ref,
    grad_query_ref, grad_key_ref, grad_value_ref, grad_gain_ref,
):
    length, head_size = query_ref.shape

    @pl.when(pl.program_id(0) == 0)
    def first_head():
        grad_key_ref[...] = jnp.zeros_like(grad_key_ref)
        grad_value_ref[...] = jnp.zeros_like(grad_value_ref)
        grad_gain_ref[...] = jnp.zeros_like(grad_gain_ref)

    for begin, rows, first, keys in key_spans(length):
        block = pl.ds(begin, rows)
        query_low = query_low_ref[block]
        key_low = key_low_ref[pl.ds(first, keys)]
        scaled = grad_mixed_ref[block].astype(high) * inverse_ref[block]
        row_term = jnp.sum(scaled * mixed_ref[block].astype(high), axis=-1, keepdims=True)
        scaled = scaled.astype(low)
        scores = dot_last(query_low, key_low)
        allowed = tile_mask(col_ref, row_ref, begin, rows, first, keys)
        terms = jnp.where(allowed, jnp.exp2(scores), 0.0)
        grad_probs = dot_last(scaled, value_low_ref[pl.ds(first, keys)])
        grad_scores = (terms * (grad_probs - row_term)).astype(low)
        grad_value_ref[pl.ds(first, keys)] += dot_first(terms.astype(low), scaled)
        grad_key_ref[pl.ds(first, keys)] += dot_first(grad_scores, query_low) * (1.0 / log2e)
        grad_rotated = dot(grad_scores, key_low) * head_size**-0.5
        grad_normed = unrotate(grad_rotated, cos_ref[block], sin_ref[block])
        grad_raw, gain_rows = norm_back(query_ref[block], query_gain_ref[...], grad_normed)
        grad_query_ref[block] = grad_raw.astype(low)
        grad_gain_ref[...] += jnp.broadcast_to(
            jnp.sum(gain_rows, axis=0, keepdims=True), grad_gain_ref.shape
        )


def whole(shape):
    return pl.BlockSpec(shape, lambda head: (0,) * len(shape))


def run_attention_forward(raw, heads, head_size, query_gain, key_gain, cosines, sines, seg_col, seg_row):
    length = raw.shape[0]
    per_head = pl.BlockSpec((length, head_size), lambda head: (0, head))
    one = (length, head_size)
    wide = jax.ShapeDtypeStruct((length, heads * head_size), low)
    narrow = jax.ShapeDtypeStruct(one, low)
    return pl.pallas_call(
        attention_forward,
        grid=(heads,),
        in_specs=[
            per_head,
            pl.BlockSpec(one, lambda head: (0, heads)),
            pl.BlockSpec(one, lambda head: (0, heads + 1)),
            whole((1, head_size)),
            whole((1, head_size)),
            whole(one),
            whole(one),
            whole(one),
            whole((8, length)),
        ],
        out_specs=[per_head, per_head, whole(one), whole(one), per_head],
        out_shape=[wide, wide, narrow, narrow, jax.ShapeDtypeStruct((length, heads * head_size), high)],
        scratch_shapes=[pltpu.VMEM((length, 2 * head_size), low)],
        compiler_params=pltpu.CompilerParams(vmem_limit_bytes=50 << 20),
        cost_estimate=pl.CostEstimate(
            flops=3 * heads * length * length * head_size, bytes_accessed=8 * length * heads * head_size,
            transcendentals=heads * length * length // 2,
        ),
    )(raw, raw, raw, query_gain, key_gain, cosines, sines, seg_col, seg_row)


def run_attention_backward(
    raw, query_low, key_low, value_low, inverse, mixed, grad_mixed, heads, head_size, query_gain,
    cosines, sines, seg_col, seg_row,
):
    length = raw.shape[0]
    per_head = pl.BlockSpec((length, head_size), lambda head: (0, head))
    one = (length, head_size)
    return pl.pallas_call(
        attention_backward,
        grid=(heads,),
        in_specs=[
            per_head, per_head, whole(one), whole(one), per_head, per_head, per_head,
            whole((1, head_size)), whole(one), whole(one), whole(one), whole((8, length)),
        ],
        out_specs=[per_head, whole(one), whole(one), whole((8, head_size))],
        out_shape=[
            jax.ShapeDtypeStruct((length, heads * head_size), low),
            jax.ShapeDtypeStruct(one, high),
            jax.ShapeDtypeStruct(one, high),
            jax.ShapeDtypeStruct((8, head_size), high),
        ],
        compiler_params=pltpu.CompilerParams(vmem_limit_bytes=50 << 20),
        cost_estimate=pl.CostEstimate(
            flops=6 * heads * length * length * head_size, bytes_accessed=16 * length * heads * head_size,
            transcendentals=heads * length * length // 2,
        ),
    )(
        raw, query_low, key_low, value_low, inverse, mixed, grad_mixed, query_gain, cosines, sines,
        seg_col, seg_row,
    )


MESH = pl.DeviceIdType.MESH
VMEM = pl.BlockSpec(memory_space=pltpu.VMEM)
ANY = pl.BlockSpec(memory_space=pl.ANY)


def wait_all(copies):
    for copy in copies:
        copy.wait()


class Chain:
    def __init__(self):
        self.n = lax.axis_size("expert") // 2
        me = lax.axis_index("expert")
        self.z, self.c = me // 2, me % 2
        self.sibling, self.up, self.down = me + 1 - 2 * self.c, me + 2, me - 2
        self.has_up, self.has_down = self.z < self.n - 1, self.z > 0

    def greet(self):
        barrier = pltpu.get_barrier_semaphore()

        def signal(peer):
            pl.semaphore_signal(barrier, inc=1, device_id={"expert": peer}, device_id_type=MESH)

        signal(self.sibling)
        pl.when(self.has_up)(lambda: signal(self.up))
        pl.when(self.has_down)(lambda: signal(self.down))
        peers = 1 + self.has_up.astype(jnp.int32) + self.has_down.astype(jnp.int32)
        pl.semaphore_wait(barrier, peers)

    def nearest(self, step):
        turn = jnp.int32(0)
        for z in range(self.n):
            order = sorted(range(self.n), key=lambda other: (abs(other - z), other))
            for at, chip in enumerate(order):
                turn = jnp.where((self.z == z) & (step == at), chip, turn)
        return turn


class Gather:
    def __init__(self, chain, own, whole, send, recv, local):
        self.chain, self.own, self.whole = chain, own, whole
        self.send, self.recv, self.local = send, recv, local
        self.rows = own.shape[0]

    @staticmethod
    def semaphores(n):
        return [
            pltpu.SemaphoreType.DMA((3, n)),
            pltpu.SemaphoreType.DMA((2 * n,)),
            pltpu.SemaphoreType.DMA(()),
        ]

    def block(self, z, c):
        return self.whole.at[pl.ds(pl.multiple_of((2 * z + c) * self.rows, self.rows), self.rows)]

    def copy(self, source, z, way, peer):
        c = self.chain.c
        return pltpu.make_async_remote_copy(
            src_ref=source,
            dst_ref=self.block(z, c),
            send_sem=self.send.at[way, z],
            recv_sem=self.recv.at[2 * z + c],
            device_id={"expert": peer},
            device_id_type=MESH,
        )

    def wait_block(self, z, c):
        block = self.block(z, c)
        pltpu.make_async_remote_copy(
            src_ref=block,
            dst_ref=block,
            send_sem=self.send.at[0, z],
            recv_sem=self.recv.at[2 * z + c],
            device_id={"expert": self.chain.sibling},
            device_id_type=MESH,
        ).wait_recv()

    def keep(self):
        return pltpu.make_async_copy(self.own, self.block(self.chain.z, self.chain.c), self.local)

    def begin(self):
        ch = self.chain
        pl.when(ch.has_up)(lambda: self.copy(self.own, ch.z, 0, ch.up).start())
        pl.when(ch.has_down)(lambda: self.copy(self.own, ch.z, 1, ch.down).start())
        self.copy(self.own, ch.z, 2, ch.sibling).start()
        self.keep().start()

    def service(self, step):
        ch = self.chain

        def from_below():
            z = ch.z - step
            self.wait_block(z, ch.c)
            pl.when(ch.has_up)(lambda: self.copy(self.block(z, ch.c), z, 0, ch.up).start())
            self.copy(self.block(z, ch.c), z, 2, ch.sibling).start()

        def from_above():
            z = ch.z + step
            self.wait_block(z, ch.c)
            pl.when(ch.has_down)(lambda: self.copy(self.block(z, ch.c), z, 1, ch.down).start())
            self.copy(self.block(z, ch.c), z, 2, ch.sibling).start()

        pl.when(ch.z - step >= 0)(from_below)
        pl.when(ch.z + step < ch.n)(from_above)

    def wait_sibling(self, z):
        self.wait_block(z, 1 - self.chain.c)

    def finish(self):
        ch = self.chain
        for z in range(ch.n):
            at = jnp.int32(z)
            block = self.block(at, ch.c)
            pl.when(ch.has_up & (ch.z >= z))(lambda: self.copy(block, at, 0, ch.up).wait_send())
            pl.when(ch.has_down & (ch.z <= z))(lambda: self.copy(block, at, 1, ch.down).wait_send())
            self.copy(block, at, 2, ch.sibling).wait_send()


class Scatter:
    def __init__(self, chain, parts, pair, flow, pair_send, pair_recv, flow_send, flow_recv):
        self.chain, self.parts, self.pair, self.flow = chain, parts, pair, flow
        self.pair_send, self.pair_recv = pair_send, pair_recv
        self.flow_send, self.flow_recv = flow_send, flow_recv
        self.rows = pair.shape[1]

    @staticmethod
    def buffers(n, rows, width):
        return [
            pltpu.VMEM((n, rows, width), low),
            pltpu.VMEM((n + 1, rows, width), low),
            pltpu.SemaphoreType.DMA((n,)),
            pltpu.SemaphoreType.DMA((n,)),
            pltpu.SemaphoreType.DMA((n,)),
            pltpu.SemaphoreType.DMA((n + 1,)),
        ]

    def half(self, z, c):
        return self.parts.at[z, pl.ds(pl.multiple_of(c * self.rows, self.rows), self.rows)]

    def pair_copy(self, z):
        ch = self.chain
        return pltpu.make_async_remote_copy(
            src_ref=self.half(z, 1 - ch.c),
            dst_ref=self.pair.at[z],
            send_sem=self.pair_send.at[z],
            recv_sem=self.pair_recv.at[z],
            device_id={"expert": ch.sibling},
            device_id_type=MESH,
        )

    def flow_copy(self, z, slot, peer):
        return pltpu.make_async_remote_copy(
            src_ref=self.pair.at[z],
            dst_ref=self.flow.at[slot],
            send_sem=self.flow_send.at[z],
            recv_sem=self.flow_recv.at[slot],
            device_id={"expert": peer},
            device_id_type=MESH,
        )

    def wait_flow(self, slot):
        block = self.flow.at[slot]
        pltpu.make_async_remote_copy(
            src_ref=block,
            dst_ref=block,
            send_sem=self.flow_send.at[0],
            recv_sem=self.flow_recv.at[slot],
            device_id={"expert": self.chain.sibling},
            device_id_type=MESH,
        ).wait_recv()

    def start_pair(self, z):
        self.pair_copy(z).start()

    def add_pair(self, z, relayed):
        self.pair_copy(z).wait_recv()
        half = self.half(z, self.chain.c)

        def alone():
            self.pair[z] = (half[...].astype(high) + self.pair[z].astype(high)).astype(low)

        def with_flow():
            self.wait_flow(z)
            total = half[...].astype(high) + self.pair[z].astype(high) + self.flow[z].astype(high)
            self.pair[z] = total.astype(low)

        pl.when(relayed)(with_flow)
        pl.when(jnp.logical_not(relayed))(alone)

    def step(self, distance):
        ch = self.chain

        def upward():
            z = ch.z + distance
            self.add_pair(z, ch.has_down)
            self.flow_copy(z, z, ch.up).start()

        def downward():
            z = ch.z - distance
            self.add_pair(z, ch.has_up)
            self.flow_copy(z, jnp.where(distance == 1, ch.n, z), ch.down).start()

        pl.when(ch.z + distance < ch.n)(upward)
        pl.when(ch.z - distance >= 0)(downward)

    def total(self, result):
        ch = self.chain
        self.pair_copy(ch.z).wait_recv()
        result[...] = self.half(ch.z, ch.c)[...].astype(high) + self.pair[ch.z].astype(high)

        def add(slot):
            self.wait_flow(slot)
            result[...] += self.flow[slot].astype(high)

        pl.when(ch.has_down)(lambda: add(ch.z))
        pl.when(ch.has_up)(lambda: add(ch.n))

    def finish(self):
        ch = self.chain
        for z in range(ch.n):
            at = jnp.int32(z)
            self.pair_copy(at).wait_send()
            pl.when(ch.z != z)(lambda: self.flow_copy(at, at, ch.sibling).wait_send())


class Ports:
    def __init__(self, send, recv):
        self.send, self.recv, self.used, self.started = send, recv, 0, []

    def copy(self, source, target, device):
        at = self.used
        self.used += 1
        copy = pltpu.make_async_remote_copy(
            src_ref=source,
            dst_ref=target,
            send_sem=self.send.at[at],
            recv_sem=self.recv.at[at],
            device_id=device,
            device_id_type=MESH,
        )
        self.started.append(copy)
        return copy

    def finish(self):
        for copy in self.started:
            copy.wait_send()


def communicating(collective_id):
    return pltpu.CompilerParams(
        collective_id=collective_id, has_side_effects=True, vmem_limit_bytes=60 << 20
    )


def square():
    group = lax.axis_index("dp")
    y, x = group // 2, group % 2
    from_x, from_y = 2 * y + 1 - x, 2 * (1 - y) + x
    return group, y, x, from_x, from_y


def gather_kernel(
    tokens_ref, gain_ref, named_ref, query_ref, key_ref, value_ref,
    hidden_ref, all_named_ref, projection_ref, raw_ref,
    own, stage, wide_send, wide_recv, wide_local, thin_send, thin_recv, thin_local, swap_send, swap_recv,
    x_send, x_recv, y_send, y_recv, far_send, far_recv,
):
    chain = Chain()
    n = chain.n
    peers = 2 * n
    me = lax.axis_index("expert")
    group, _, _, from_x, from_y = square()
    far = 3 - group
    beside, across = {"dp": from_x}, {"dp": from_y}
    sources = [(2 * chain.nearest(step) + core, core, step) for step in range(n) for core in range(2)]
    others = [chain.sibling] + [source for source, _, step in sources if step > 0]
    barrier = pltpu.get_barrier_semaphore()
    for device in [{"expert": peer} for peer in others] + [beside, across]:
        pl.semaphore_signal(barrier, inc=1, device_id=device, device_id_type=MESH)
    rows = stage.shape[1]
    quarter = pl.ds(pl.multiple_of(group * rows, rows), rows)
    query_width = query_ref.shape[1] // peers
    head_size = key_ref.shape[1] // n
    for peer in range(peers):
        shared = pl.ds(peer // 2 * head_size, head_size)
        stage[peer, :, :query_width] = query_ref[quarter, pl.ds(peer * query_width, query_width)]
        stage[peer, :, query_width : query_width + head_size] = key_ref[quarter, shared]
        stage[peer, :, query_width + head_size :] = value_ref[quarter, shared]
    pl.semaphore_wait(barrier, peers + 1)

    def remote(source, target, send, recv, device):
        return pltpu.make_async_remote_copy(
            src_ref=source, dst_ref=target, send_sem=send, recv_sem=recv, device_id=device, device_id_type=MESH
        )

    def block(source, place):
        return projection_ref.at[source, place]

    swaps = [
        remote(stage.at[peer], block(me, group), swap_send.at[at], swap_recv.at[me], {"expert": peer})
        for at, peer in enumerate(others)
    ]
    for copy in swaps:
        copy.start()
    own[...] = norm_rows(tokens_ref[...].astype(high), gain_ref[...]).astype(low)
    wide = Gather(chain, own, hidden_ref, wide_send, wide_recv, wide_local)
    thin = Gather(chain, named_ref, all_named_ref, thin_send, thin_recv, thin_local)
    wide.begin()
    thin.begin()
    projection_ref[me, group] = stage[me]

    def to_x(at, source, place):
        part = block(source, place)
        return remote(part, part, x_send.at[at], x_recv.at[source], beside)

    def to_y(at, source, place):
        part = block(source, place)
        return remote(part, part, y_send.at[at], y_recv.at[source], across)

    def to_far(at, core, source, place):
        part = block(source, place)
        return remote(part, part, far_send.at[at], far_recv.at[source], across if core == 0 else beside)

    def wait_swap(source):
        part = block(source, group)
        remote(part, part, swap_send.at[0], swap_recv.at[source], {"expert": chain.sibling}).wait_recv()

    for at, (source, core, step) in enumerate(sources):
        if step == 0:
            pl.when(chain.c != core)(lambda: wait_swap(source))
        else:
            wait_swap(source)
        to_x(at, source, group).start()
        to_y(at, source, group).start()
        if step > 0 and core == 1:
            wide.service(step)
            thin.service(step)
    for at, (source, core, _) in enumerate(sources):
        to_x(at, source, from_x).wait_recv()
        to_y(at, source, from_y).wait_recv()
        to_far(at, core, source, from_x if core == 0 else from_y).start()
    for gather in (thin, wide):
        for z in range(n):
            gather.wait_sibling(jnp.int32(z))
        gather.keep().wait()
    for at, (source, core, _) in enumerate(sources):
        to_far(at, core, source, far).wait_recv()
    pair_rows = 2 * own.shape[0]
    shard_rows = 4 * rows

    @pl.loop(0, n)
    def each(step):
        tokens = pl.ds(pl.multiple_of(step * pair_rows, pair_rows), pair_rows)
        total = jnp.zeros((pair_rows, raw_ref.shape[1]), high)
        for source in range(peers):
            weight = projection_ref[source].reshape(shard_rows, raw_ref.shape[1])
            total = total + dot(hidden_ref[tokens, source * shard_rows : (source + 1) * shard_rows], weight)
        raw_ref[tokens] = total

    for gather in (thin, wide):
        gather.finish()
    for at, (source, core, _) in enumerate(sources):
        to_x(at, source, group).wait_send()
        to_y(at, source, group).wait_send()
        to_far(at, core, source, from_x if core == 0 else from_y).wait_send()
    for copy in swaps:
        copy.wait_send()


def run_gather(tokens, gain, named, query_weight, key_matrix, value_matrix, peers, groups):
    length, width = tokens.shape
    n = peers // 2
    shard_rows, query_columns = query_weight.shape
    columns = query_columns // peers + 2 * key_matrix.shape[1] // n
    rows = shard_rows // groups
    dma = pltpu.SemaphoreType.DMA
    hidden, all_named, projection, raw = pl.pallas_call(
        gather_kernel,
        out_shape=[
            jax.ShapeDtypeStruct((length * peers, width), low),
            jax.ShapeDtypeStruct((length * peers, named.shape[1]), named.dtype),
            jax.ShapeDtypeStruct((peers, groups, rows, columns), low),
            jax.ShapeDtypeStruct((length * peers, columns), high),
        ],
        in_specs=[VMEM] * 6,
        out_specs=[VMEM] * 4,
        scratch_shapes=[
            pltpu.VMEM((length, width), low),
            pltpu.VMEM((peers, rows, columns), low),
            *Gather.semaphores(n),
            *Gather.semaphores(n),
            dma((peers - 1,)), dma((peers,)),
            dma((peers,)), dma((peers,)), dma((peers,)), dma((peers,)), dma((peers,)), dma((peers,)),
        ],
        compiler_params=communicating(1),
        cost_estimate=pl.CostEstimate(flops=0, bytes_accessed=64 << 20, transcendentals=0),
        name="gather_hidden",
    )(tokens, gain, named, query_weight, key_matrix, value_matrix)
    return hidden, all_named, projection.reshape(width, columns), raw


def project_kernel(mixed_ref, weight_ref, tokens_ref, gain_ref, resid_ref, ffn_ref, parts, pair, flow, *sems):
    chain = Chain()
    scatter = Scatter(chain, parts, pair, flow, *sems)
    rows = parts.shape[1]

    chain.greet()

    @pl.loop(0, chain.n)
    def each(step):
        z = chain.nearest(chain.n - 1 - step)
        parts[z] = dot(mixed_ref[pl.ds(pl.multiple_of(z * rows, rows), rows)], weight_ref[...]).astype(low)
        scatter.start_pair(z)
        pl.when(step < chain.n - 1)(lambda: scatter.step(chain.n - 1 - step))

    scatter.total(resid_ref)
    resid_ref[...] += tokens_ref[...].astype(high)
    ffn_ref[...] = norm_rows(resid_ref[...], gain_ref[...]).astype(low)
    scatter.finish()


def run_project(mixed, weight, tokens, gain, peers):
    length, width = tokens.shape
    n = peers // 2
    return pl.pallas_call(
        project_kernel,
        out_shape=[
            jax.ShapeDtypeStruct((length, width), high),
            jax.ShapeDtypeStruct((length, width), low),
        ],
        in_specs=[VMEM] * 4,
        out_specs=[VMEM] * 2,
        scratch_shapes=[pltpu.VMEM((n, 2 * length, width), low)] + Scatter.buffers(n, length, width),
        compiler_params=communicating(2),
        cost_estimate=pl.CostEstimate(flops=0, bytes_accessed=64 << 20, transcendentals=0),
        name="project_and_sum",
    )(mixed, weight, tokens, gain)


def expert_block(rows, cots, gate_w, up_w, down_w, gate_col, gated, grad_gate, grad_up, block):
    hidden = gate_w.shape[1]
    chunk = hidden // 3 if hidden % 384 == 0 else hidden
    gate_grad = jnp.zeros_like(gate_col)
    for begin in range(0, hidden, chunk):
        units = pl.ds(begin, chunk)
        gate_pre = dot(rows[...], gate_w[:, units])
        up_pre = dot(rows[...], up_w[:, units])
        plain = dot_last(cots[...], down_w[units, :])
        share = 1.0 / (1.0 + jnp.exp(-gate_pre))
        silu = gate_pre * share
        act = silu * up_pre
        gate_grad = gate_grad + jnp.sum(act * plain, axis=-1, keepdims=True)
        gated[block, units] = (act * gate_col).astype(low)
        grad_act = plain * gate_col
        slope = share + silu * (1.0 - share)
        grad_gate[block, units] = (grad_act * up_pre * slope).astype(low)
        grad_up[block, units] = (grad_act * silu).astype(low)
    return gate_grad


def gate_columns(lanes, expert, gate_grad):
    sent = jnp.where(lanes == expert, gate_grad, 0.0)
    upper = sent.astype(low).astype(high)
    lower = (sent - upper).astype(low).astype(high)
    return upper + pltpu.roll(lower, 64, 1)


class Tiles:
    def __init__(self, grads, stage, sems, gated, grad_gate, grad_up, rows_all, cots):
        self.grads, self.stage, self.sems = grads, stage, sems
        self.sources = ((grad_gate, rows_all), (grad_up, rows_all), (gated, cots))
        self.groups = sems.shape[1]
        self.hidden = gated.shape[1]
        self.piece = self.hidden // self.groups
        self.tile = stage.shape[2]

    def copies(self, kind, at, slot):
        piece = self.piece
        made = []
        for part in range(self.groups):
            if kind < 2:
                target = self.grads.at[part, pl.ds(pl.multiple_of((2 * at + kind) * piece, 16), piece)]
            else:
                begin = 2 * self.hidden + part * piece
                target = self.grads.at[at, pl.ds(begin, piece)]
            source = self.stage.at[slot, pl.ds(part * piece, piece)]
            made.append(pltpu.make_async_copy(source, target, self.sems.at[slot, part]))
        return made

    def run(self, kind):
        left, right = self.sources[kind]

        @pl.loop(0, self.groups)
        def each(at):
            slot = at % 2
            if kind == 0:
                pl.when(at >= 2)(lambda: wait_all(self.copies(kind, at, slot)))
            else:
                wait_all(self.copies(kind, at, slot))
            span = pl.ds(pl.multiple_of(at * self.tile, self.tile), self.tile)
            self.stage[slot] = dot_first(left[...], right[:, span]).astype(low)
            for copy in self.copies(kind, at, slot):
                copy.start()

    def finish(self):
        for slot in range(2):
            wait_all(self.copies(0, jnp.int32(slot), slot))


def first_expert_kernel(
    ffn_ref, named_ref, router_ref, cot_hbm, gate_hbm, up_hbm, down_hbm,
    gates_ref, own_gates_ref, rows_hbm, mixture_hbm, parts_hbm, grads_hbm,
    rows_all, cots, gate_w, up_w, down_w, gated, grad_gate, grad_up, mix_stage, part_stage, tile_stage,
    load_sems, rows_sem, mix_sems, part_sems, tile_sems, gather_send, gather_recv, gather_local,
):
    chain = Chain()
    n = chain.n
    length, width = ffn_ref.shape
    pair_rows = 2 * length
    loads = [
        pltpu.make_async_copy(source, target, load_sems.at[at])
        for at, (source, target) in enumerate(
            ((gate_hbm.at[0], gate_w), (up_hbm.at[0], up_w), (cot_hbm, cots), (down_hbm.at[0], down_w))
        )
    ]
    for load in loads:
        load.start()
    chain.greet()
    gather = Gather(chain, ffn_ref, rows_all, gather_send, gather_recv, gather_local)
    gather.begin()
    gather.keep().wait()
    for load in loads:
        load.wait()
    lanes = lax.broadcasted_iota(jnp.int32, (pair_rows, 128), 1)
    expert = lax.axis_index("expert") * gate_hbm.shape[0]
    tile = tile_stage.shape[2]

    def mix_copy(z, slot):
        target = mixture_hbm.at[pl.ds(pl.multiple_of(z * pair_rows, pair_rows), pair_rows)]
        return pltpu.make_async_copy(mix_stage.at[slot], target, mix_sems.at[slot])

    def part_copy(z, slot):
        return pltpu.make_async_copy(part_stage.at[slot], parts_hbm.at[z], part_sems.at[slot])

    @pl.loop(0, n)
    def each(step):
        pl.when(step > 0)(lambda: gather.service(step))
        z = chain.nearest(step)
        gather.wait_sibling(z)
        block = pl.ds(pl.multiple_of(z * pair_rows, pair_rows), pair_rows)
        rows = rows_all.at[block]
        logits = dot_last(rows[...], router_ref[...])
        named = named_ref[block].astype(high) > 0.5
        top = jnp.max(jnp.where(named, logits, -1e30), axis=-1, keepdims=True)
        terms = jnp.where(named, jnp.exp(jnp.where(named, logits - top, 0.0)), 0.0)
        gates = terms / jnp.sum(terms, axis=-1, keepdims=True)
        gates_ref[block] = gates

        @pl.when(step == 0)
        def own_gates():
            own_gates_ref[...] = jnp.where(chain.c == 0, gates[:length], gates[length:])

        gate_col = jnp.sum(jnp.where(lanes == expert, gates, 0.0), axis=-1, keepdims=True)
        gate_grad = expert_block(
            rows, cots.at[block], gate_w, up_w, down_w, gate_col, gated, grad_gate, grad_up, block
        )
        slot = step % 2

        @pl.when(step >= 2)
        def free():
            mix_copy(z, slot).wait()
            part_copy(z, slot).wait()

        @pl.loop(0, width // tile)
        def columns(at):
            span = pl.ds(pl.multiple_of(at * tile, tile), tile)
            mix_stage[slot, :, span] = dot(gated[block], down_w[:, span]).astype(low)
            grad_rows = dot_last(grad_gate[block], gate_w[span, :]) + dot_last(grad_up[block], up_w[span, :])
            part_stage[slot, :, span] = grad_rows.astype(low)

        part_stage[slot, :, width:] = gate_columns(lanes, expert, gate_grad).astype(low)
        mix_copy(z, slot).start()
        part_copy(z, slot).start()

    rows_copy = pltpu.make_async_copy(rows_all, rows_hbm, rows_sem)
    rows_copy.start()
    tiles = Tiles(grads_hbm, tile_stage, tile_sems, gated, grad_gate, grad_up, rows_all, cots)
    for kind in range(3):
        tiles.run(kind)
    gather.finish()
    tiles.finish()
    for slot in range(2):
        mix_copy(jnp.int32(0), slot).wait()
        part_copy(jnp.int32(0), slot).wait()
    rows_copy.wait()


def second_expert_kernel(
    gates_ref, rows_hbm, cot_hbm, gate_hbm, up_hbm, down_hbm, mixture_in, parts_in,
    sum_ref, mixture_hbm, grads_hbm,
    rows_all, cots, gate_w, up_w, down_w, gated, grad_gate, grad_up, mixture, parts, tile_stage,
    load_sems, mix_sems, tile_sems, pair, flow, *scatter_sems,
):
    chain = Chain()
    n = chain.n
    pair_rows, width = parts.shape[1], rows_all.shape[1]
    loads = [
        pltpu.make_async_copy(source, target, load_sems.at[at])
        for at, (source, target) in enumerate(
            (
                (rows_hbm, rows_all), (gate_hbm.at[1], gate_w), (up_hbm.at[1], up_w), (cot_hbm, cots),
                (down_hbm.at[1], down_w), (parts_in, parts), (mixture_in, mixture),
            )
        )
    ]
    for load in loads:
        load.start()
    chain.greet()
    scatter = Scatter(chain, parts, pair, flow, *scatter_sems)
    lanes = lax.broadcasted_iota(jnp.int32, (pair_rows, 128), 1)
    expert = lax.axis_index("expert") * gate_hbm.shape[0] + 1
    tile = tile_stage.shape[2]
    for load in loads:
        load.wait()

    def mix_copy(z):
        block = pl.ds(pl.multiple_of(z * pair_rows, pair_rows), pair_rows)
        return pltpu.make_async_copy(mixture.at[block], mixture_hbm.at[block], mix_sems.at[z])

    @pl.loop(0, n)
    def each(step):
        z = chain.nearest(n - 1 - step)
        block = pl.ds(pl.multiple_of(z * pair_rows, pair_rows), pair_rows)
        gate_col = jnp.sum(jnp.where(lanes == expert, gates_ref[block], 0.0), axis=-1, keepdims=True)
        gate_grad = expert_block(
            rows_all.at[block], cots.at[block], gate_w, up_w, down_w, gate_col, gated, grad_gate, grad_up, block
        )

        @pl.loop(0, width // tile)
        def columns(at):
            span = pl.ds(pl.multiple_of(at * tile, tile), tile)
            grad_rows = dot_last(grad_gate[block], gate_w[span, :]) + dot_last(grad_up[block], up_w[span, :])
            parts[z, :, span] = (parts[z, :, span].astype(high) + grad_rows).astype(low)

        columns_sent = gate_columns(lanes, expert, gate_grad)
        parts[z, :, width:] = (parts[z, :, width:].astype(high) + columns_sent).astype(low)
        scatter.start_pair(z)

        @pl.loop(0, width // tile)
        def mixture_columns(at):
            span = pl.ds(pl.multiple_of(at * tile, tile), tile)
            added = dot(gated[block], down_w[:, span])
            mixture[block, span] = (mixture[block, span].astype(high) + added).astype(low)

        mix_copy(z).start()
        pl.when(step < n - 1)(lambda: scatter.step(n - 1 - step))

    tiles = Tiles(grads_hbm, tile_stage, tile_sems, gated, grad_gate, grad_up, rows_all, cots)
    for kind in range(3):
        tiles.run(kind)
    scatter.total(sum_ref)
    tiles.finish()
    for z in range(n):
        mix_copy(jnp.int32(z)).wait()
    scatter.finish()


def run_experts(ffn, named, router, cotangents, gate_weight, up_weight, down_weight, peers, groups):
    length, width = ffn.shape
    n = peers // 2
    full = length * peers
    _, _, hidden = gate_weight.shape
    tile = width // groups
    sent = width + 128
    dma = pltpu.SemaphoreType.DMA
    rows = pltpu.VMEM((full, width), low)
    weights = [
        pltpu.VMEM(gate_weight.shape[1:], low),
        pltpu.VMEM(up_weight.shape[1:], low),
        pltpu.VMEM(down_weight.shape[1:], low),
    ]
    acts = [pltpu.VMEM((full, hidden), low)] * 3
    grads_shape = jax.ShapeDtypeStruct((groups, 3 * hidden, tile), low)
    mixture_shape = jax.ShapeDtypeStruct((full, width), low)
    stage = pltpu.VMEM((2, hidden, tile), low)
    gates, own_gates, rows_all, mixture, parts, grads = pl.pallas_call(
        first_expert_kernel,
        out_shape=[
            jax.ShapeDtypeStruct((full, 128), high),
            jax.ShapeDtypeStruct((length, 128), high),
            jax.ShapeDtypeStruct((full, width), low),
            mixture_shape,
            jax.ShapeDtypeStruct((n, 2 * length, sent), low),
            grads_shape,
        ],
        in_specs=[VMEM, VMEM, VMEM, ANY, ANY, ANY, ANY],
        out_specs=[VMEM, VMEM, ANY, ANY, ANY, ANY],
        scratch_shapes=[
            rows, rows, *weights, *acts,
            pltpu.VMEM((2, 2 * length, width), low),
            pltpu.VMEM((2, 2 * length, sent), low),
            stage,
            dma((4,)), dma(()), dma((2,)), dma((2,)), dma((2, groups)),
            *Gather.semaphores(n),
        ],
        compiler_params=communicating(3),
        cost_estimate=pl.CostEstimate(flops=0, bytes_accessed=120 << 20, transcendentals=0),
        name="first_expert",
    )(ffn, named, router, cotangents, gate_weight, up_weight, down_weight)
    sums, mixture, more_grads = pl.pallas_call(
        second_expert_kernel,
        out_shape=[jax.ShapeDtypeStruct((length, sent), high), mixture_shape, grads_shape],
        in_specs=[VMEM] + [ANY] * 7,
        out_specs=[VMEM, ANY, ANY],
        scratch_shapes=[
            rows, rows, *weights, *acts,
            rows,
            pltpu.VMEM((n, 2 * length, sent), low),
            stage,
            dma((7,)), dma((n,)), dma((2, groups)),
            *Scatter.buffers(n, length, sent),
        ],
        compiler_params=communicating(7),
        cost_estimate=pl.CostEstimate(flops=0, bytes_accessed=120 << 20, transcendentals=0),
        name="second_expert",
    )(gates, rows_all, cotangents, gate_weight, up_weight, down_weight, mixture, parts)
    return sums, own_gates, mixture, grads, more_grads


def turn_kernel(
    sum_ref, gates_ref, ffn_ref, resid_ref, cot_ref, gain_ref, router_ref, weight_ref,
    grad_resid_ref, attn_ref, mixed_ref, router_grad_ref, gain_grad_ref,
    own, gather_send, gather_recv, gather_local,
):
    chain = Chain()
    n = chain.n
    length, width = ffn_ref.shape
    sent = sum_ref[:, width:]
    grad_gates = jnp.where(
        lax.broadcasted_iota(jnp.int32, sent.shape, 1) < 64, sent + pltpu.roll(sent, 64, 1), 0.0
    )
    gates = gates_ref[...]
    inner = jnp.sum(gates * grad_gates, axis=-1, keepdims=True)
    grad_logits = (gates * (grad_gates - inner)).astype(low)
    router_grad_ref[...] = dot_first(grad_logits, ffn_ref[...])[: router_grad_ref.shape[0]]
    grad_hidden = sum_ref[:, :width] + dot(grad_logits, router_ref[...])
    grad_rows, gain_rows = norm_back(resid_ref[...], gain_ref[...], grad_hidden)
    gain_grad_ref[...] = jnp.broadcast_to(jnp.sum(gain_rows, axis=0, keepdims=True), gain_grad_ref.shape)
    grad_resid = cot_ref[...].astype(high) + grad_rows
    grad_resid_ref[...] = grad_resid
    own[...] = grad_resid.astype(low)
    chain.greet()
    gather = Gather(chain, own, attn_ref, gather_send, gather_recv, gather_local)
    gather.begin()
    gather.keep().wait()
    pair_rows = 2 * length

    @pl.loop(0, n)
    def each(step):
        pl.when(step > 0)(lambda: gather.service(step))
        z = chain.nearest(step)
        gather.wait_sibling(z)
        block = pl.ds(pl.multiple_of(z * pair_rows, pair_rows), pair_rows)
        mixed_ref[block] = dot_last(attn_ref[block], weight_ref[...]).astype(low)

    gather.finish()


def run_turn(sums, gates, ffn, resid, cotangent, gain, router, weight, experts, peers):
    length, width = ffn.shape
    n = peers // 2
    full = length * peers
    return pl.pallas_call(
        turn_kernel,
        out_shape=[
            jax.ShapeDtypeStruct((length, width), high),
            jax.ShapeDtypeStruct((full, width), low),
            jax.ShapeDtypeStruct((full, weight.shape[0]), low),
            jax.ShapeDtypeStruct((experts, width), high),
            jax.ShapeDtypeStruct((8, width), high),
        ],
        in_specs=[VMEM] * 8,
        out_specs=[VMEM] * 5,
        scratch_shapes=[pltpu.VMEM((length, width), low), *Gather.semaphores(n)],
        compiler_params=communicating(4),
        cost_estimate=pl.CostEstimate(flops=0, bytes_accessed=64 << 20, transcendentals=0),
        name="turn_to_attention",
    )(sums, gates, ffn, resid, cotangent, gain, router, weight)


def input_kernel(
    key_part_ref, value_part_ref, raw_ref, key_gain_ref, cos_ref, sin_ref, grad_query_ref, projection_ref,
    hidden_ref, mixed_ref, attn_ref, grad_resid_ref, tokens_ref, gain_ref,
    input_grad_ref, projection_grad_ref, out_grad_ref, gain_grad_ref, key_gain_grad_ref,
    own_pair, their_pair, columns, weight, total, parts, hidden_all, mixed_all, attn_all, load_sems,
    swap_send, swap_recv, pair, flow, *scatter_sems,
):
    chain = Chain()
    n = chain.n
    loads = [
        pltpu.make_async_copy(source, target, load_sems.at[at])
        for at, (source, target) in enumerate(
            ((mixed_ref, mixed_all), (attn_ref, attn_all), (hidden_ref, hidden_all))
        )
    ]
    for load in loads:
        load.start()
    full, head_size = key_part_ref.shape
    query_width = grad_query_ref.shape[1]
    own_pair[:, :head_size] = key_part_ref[...].astype(low)
    own_pair[:, head_size:] = value_part_ref[...].astype(low)
    chain.greet()
    swap = pltpu.make_async_remote_copy(
        src_ref=own_pair,
        dst_ref=their_pair,
        send_sem=swap_send,
        recv_sem=swap_recv,
        device_id={"expert": chain.sibling},
        device_id_type=MESH,
    )
    swap.start()
    first = chain.c == 0
    weight[:, :query_width] = projection_ref[:, :query_width]
    weight[:, query_width:] = jnp.where(
        first,
        projection_ref[:, query_width : query_width + head_size],
        projection_ref[:, query_width + head_size :],
    )
    columns[:, :query_width] = grad_query_ref[...]
    swap.wait_recv()
    grad_key = key_part_ref[...] + their_pair[:, :head_size].astype(high)
    grad_value = value_part_ref[...] + their_pair[:, head_size:].astype(high)
    grad_key, gain_rows = norm_back(
        raw_ref[...], key_gain_ref[...], unrotate(grad_key, cos_ref[...], sin_ref[...])
    )
    columns[:, query_width:] = jnp.where(first, grad_key, grad_value).astype(low)
    key_gain = jnp.where(first, jnp.sum(gain_rows, axis=0, keepdims=True), 0.0)
    key_gain_grad_ref[...] = jnp.broadcast_to(key_gain, key_gain_grad_ref.shape)
    scatter = Scatter(chain, parts, pair, flow, *scatter_sems)
    pair_rows = parts.shape[1]

    for load in loads:
        load.wait()
    projection_tile = projection_grad_ref.shape[0] // n
    out_tile = out_grad_ref.shape[1] // n

    @pl.loop(0, n)
    def each(step):
        z = chain.nearest(n - 1 - step)
        rows = pl.ds(pl.multiple_of(z * pair_rows, pair_rows), pair_rows)
        parts[z] = dot_last(columns[rows], weight[...]).astype(low)
        scatter.start_pair(z)
        pl.when(step < n - 1)(lambda: scatter.step(n - 1 - step))
        span = pl.ds(pl.multiple_of(step * projection_tile, projection_tile), projection_tile)
        projection_grad_ref[span] = dot_first(hidden_all[:, span], columns[...]).astype(low)
        span = pl.ds(pl.multiple_of(step * out_tile, out_tile), out_tile)
        out_grad_ref[:, span] = dot_first(mixed_all[...], attn_all[:, span]).astype(low)

    scatter.total(total)
    grad_rows, gain_rows = norm_back(tokens_ref[...].astype(high), gain_ref[...], total[...])
    input_grad_ref[...] = grad_resid_ref[...] + grad_rows
    gain_grad_ref[...] = jnp.broadcast_to(jnp.sum(gain_rows, axis=0, keepdims=True), gain_grad_ref.shape)
    swap.wait_send()
    scatter.finish()


def run_input(
    key_part, value_part, key_raw, key_gain, cosines, sines, grad_query, projection, hidden, mixed, grad_attn,
    grad_resid, tokens, gain, peers,
):
    length, width = tokens.shape
    n = peers // 2
    full, head_size = key_part.shape
    query_width = grad_query.shape[1]
    return pl.pallas_call(
        input_kernel,
        out_shape=[
            jax.ShapeDtypeStruct((length, width), high),
            jax.ShapeDtypeStruct((width, query_width + head_size), low),
            jax.ShapeDtypeStruct((query_width, width), low),
            jax.ShapeDtypeStruct((8, width), high),
            jax.ShapeDtypeStruct((8, head_size), high),
        ],
        in_specs=[VMEM] * 8 + [ANY] * 3 + [VMEM] * 3,
        out_specs=[VMEM] * 5,
        scratch_shapes=[
            pltpu.VMEM((full, 2 * head_size), low),
            pltpu.VMEM((full, 2 * head_size), low),
            pltpu.VMEM((full, query_width + head_size), low),
            pltpu.VMEM((width, query_width + head_size), low),
            pltpu.VMEM((length, width), high),
            pltpu.VMEM((n, 2 * length, width), low),
            pltpu.VMEM(hidden.shape, low),
            pltpu.VMEM(mixed.shape, low),
            pltpu.VMEM(grad_attn.shape, low),
            pltpu.SemaphoreType.DMA((3,)),
            pltpu.SemaphoreType.DMA(()),
            pltpu.SemaphoreType.DMA(()),
            *Scatter.buffers(n, length, width),
        ],
        compiler_params=communicating(5),
        cost_estimate=pl.CostEstimate(flops=0, bytes_accessed=64 << 20, transcendentals=0),
        name="input_gradient",
    )(
        key_part, value_part, key_raw, key_gain, cosines, sines, grad_query, projection, hidden, mixed,
        grad_attn, grad_resid, tokens, gain,
    )
def weights_kernel(
    proj_ref, out_ref, attn_gain_ref, ffn_gain_ref, query_gain_ref, key_gain_ref, router_ref, resid_ref,
    mixture_ref,
    query_grad_ref, key_grad_ref, value_grad_ref, out_grad_ref, small_out_ref, output_ref,
    all_proj, first_a, first_b, out_first_a, out_first_b, second_a, second_b, out_second_a, out_second_b,
    send_a, send_b, out_send_a, out_send_b, quarter, small, got, part, small_sum, total_mixture,
    port_send, port_recv, swap_send, swap_recv, send_1, recv_1, send_2, recv_2, send_3, recv_3,
    pair, flow, *scatter_sems,
):
    peers = lax.axis_size("expert")
    me = lax.axis_index("expert")
    group, y, x, from_x, from_y = square()
    beside, across = {"dp": from_x}, {"dp": from_y}
    chain = Chain()
    scatter = Scatter(chain, mixture_ref, pair, flow, *scatter_sems)
    width = out_ref.shape[1]
    head_size = query_gain_ref.shape[1]
    small[...] = jnp.zeros_like(small)
    small[0:1] = attn_gain_ref[0:1]
    small[1:2] = ffn_gain_ref[0:1]
    small[2:3, :head_size] = query_gain_ref[0:1]
    small[3:4, :head_size] = key_gain_ref[0:1]
    small[8:] = router_ref[...]
    piece = width // peers

    def small_piece(ref, peer):
        return ref.at[:, pl.ds(pl.multiple_of(peer * piece, piece), piece)]

    barrier = pltpu.get_barrier_semaphore()
    others = [(me + shift) % peers for shift in range(1, peers)]
    groups = [(group + shift) % 4 for shift in range(1, 4)]
    for peer in others:
        pl.semaphore_signal(barrier, inc=1, device_id={"expert": peer}, device_id_type=MESH)
    for other in groups:
        pl.semaphore_signal(barrier, inc=1, device_id={"dp": other}, device_id_type=MESH)
    pl.semaphore_wait(barrier, peers + 2)

    shard_rows, columns = proj_ref.shape[1:]
    rows, half = shard_rows // 4, peers // 2
    out_rows = out_ref.shape[0] // 4
    middle = width // 2
    ports = Ports(port_send, port_recv)

    def proj_part(side, q):
        return proj_ref.at[pl.ds(side * half, half), pl.ds(pl.multiple_of(q * rows, rows), rows)]

    def out_part(ref, side, q):
        return ref.at[pl.ds(pl.multiple_of(q * out_rows, out_rows), out_rows), pl.ds(side * middle, middle)]

    def remote(source, target, send, recv, device):
        return pltpu.make_async_remote_copy(
            src_ref=source, dst_ref=target, send_sem=send, recv_sem=recv, device_id=device, device_id_type=MESH
        )

    along_x = [2 * other + 1 - x for other in range(2)]
    along_y = [2 * (1 - y) + other for other in range(2)]
    out_1a = [ports.copy(out_part(out_ref, 0, along_x[k]), out_first_a.at[k], beside) for k in range(2)]
    out_1b = [ports.copy(out_part(out_ref, 1, along_y[k]), out_first_b.at[k], across) for k in range(2)]
    proj_1a = [ports.copy(proj_part(0, along_x[k]), first_a.at[k], beside) for k in range(2)]
    proj_1b = [ports.copy(proj_part(1, along_y[k]), first_b.at[k], across) for k in range(2)]
    for copy in out_1a + out_1b + proj_1a + proj_1b:
        copy.start()

    small_1 = [
        remote(small_piece(small, peer), got.at[me], send_1.at[at], recv_1.at[me], {"expert": peer})
        for at, peer in enumerate(others)
    ]
    for copy in small_1:
        copy.start()
    got[me] = small_piece(small, me)[...]
    for z in range(chain.n):
        scatter.start_pair(jnp.int32(z))

    own = group
    for copy in out_1a + out_1b:
        copy.wait_recv()
    for_y, for_x = 2 * (1 - y) + x, 2 * y + 1 - x
    out_send_a[...] = (
        out_part(out_ref, 0, for_y)[...].astype(high) + out_first_a[1 - y].astype(high)
    ).astype(low)
    out_send_b[...] = (
        out_part(out_ref, 1, for_x)[...].astype(high) + out_first_b[1 - x].astype(high)
    ).astype(low)
    out_2a = ports.copy(out_send_a, out_second_a, across)
    out_2b = ports.copy(out_send_b, out_second_b, beside)
    out_2a.start()
    out_2b.start()
    scatter.step(3) if chain.n > 3 else None
    for copy in proj_1a + proj_1b:
        copy.wait_recv()
    send_a[...] = (proj_part(0, for_y)[...].astype(high) + first_a[1 - y].astype(high)).astype(low)
    send_b[...] = (proj_part(1, for_x)[...].astype(high) + first_b[1 - x].astype(high)).astype(low)
    proj_2a = ports.copy(send_a, second_a, across)
    proj_2b = ports.copy(send_b, second_b, beside)
    proj_2a.start()
    proj_2b.start()
    scatter.step(2) if chain.n > 2 else None

    for at, peer in enumerate(others):
        remote(got.at[peer], got.at[peer], send_1.at[at], recv_1.at[peer], {"expert": peer}).wait_recv()
    total = got[0]
    for at in range(1, peers):
        total = total + got[at]
    part[group] = total
    small_2 = [
        remote(part.at[group], part.at[group], send_2.at[at], recv_2.at[group], {"dp": other})
        for at, other in enumerate(groups)
    ]
    for copy in small_2:
        copy.start()

    out_2a.wait_recv()
    out_2b.wait_recv()
    for side, first, second, at in ((0, out_first_a, out_second_a, y), (1, out_first_b, out_second_b, x)):
        out_part(out_grad_ref, side, own)[...] = (
            out_part(out_ref, side, own)[...].astype(high) + first[at].astype(high) + second[...].astype(high)
        ).astype(low)

    def out_quarter(q):
        return out_grad_ref.at[pl.ds(pl.multiple_of(q * out_rows, out_rows), out_rows)]

    out_gx = ports.copy(out_quarter(own), out_quarter(own), beside)
    out_gy = ports.copy(out_quarter(own), out_quarter(own), across)

    proj_2a.wait_recv()
    proj_2b.wait_recv()
    for side, first, second, at in ((0, first_a, second_a, y), (1, first_b, second_b, x)):
        quarter[pl.ds(side * half, half)] = (
            proj_part(side, own)[...].astype(high) + first[at].astype(high) + second[...].astype(high)
        ).astype(low)
    swaps = [
        remote(quarter.at[peer], all_proj.at[own, me], swap_send.at[at], swap_recv.at[me], {"expert": peer})
        for at, peer in enumerate(others)
    ]
    for copy in swaps:
        copy.start()
    out_gx.start()
    out_gy.start()
    all_proj[own, me] = quarter[me]

    for at, other in enumerate(groups):
        remote(part.at[other], part.at[other], send_2.at[at], recv_2.at[other], {"dp": other}).wait_recv()
    total = part[0]
    for at in range(1, 4):
        total = total + part[at]
    small_sum[me] = total
    small_3 = [
        remote(small_sum.at[me], small_sum.at[me], send_3.at[at], recv_3.at[me], {"expert": peer})
        for at, peer in enumerate(others)
    ]
    for copy in small_3:
        copy.start()

    for at, peer in enumerate(others):
        block = all_proj.at[own, peer]
        remote(block, block, swap_send.at[at], swap_recv.at[peer], {"expert": peer}).wait_recv()
    proj_gx = ports.copy(all_proj.at[own], all_proj.at[own], beside)
    proj_gy = ports.copy(all_proj.at[own], all_proj.at[own], across)
    proj_gx.start()
    proj_gy.start()
    out_gx.wait_recv()
    out_gy.wait_recv()
    far = 3 - group
    out_fa = ports.copy(out_part(out_grad_ref, 0, from_x), out_part(out_grad_ref, 0, from_x), across)
    out_fb = ports.copy(out_part(out_grad_ref, 1, from_y), out_part(out_grad_ref, 1, from_y), beside)
    out_fa.start()
    out_fb.start()
    scatter.step(1) if chain.n > 1 else None

    def proj_half(q, side):
        return all_proj.at[q, pl.ds(side * half, half)]

    proj_gx.wait_recv()
    proj_gy.wait_recv()
    proj_fa = ports.copy(proj_half(from_x, 0), proj_half(from_x, 0), across)
    proj_fb = ports.copy(proj_half(from_y, 1), proj_half(from_y, 1), beside)
    proj_fa.start()
    proj_fb.start()
    query_width = columns - head_size

    def spread(q):
        block = pl.ds(pl.multiple_of(q * rows, rows), rows)
        for peer in range(peers):
            query_grad_ref[block, peer * query_width : (peer + 1) * query_width] = all_proj[q, peer, :, :query_width]
            shared = key_grad_ref if peer % 2 == 0 else value_grad_ref
            at = peer // 2 * head_size
            shared[block, at : at + head_size] = all_proj[q, peer, :, query_width:]

    spread(own)
    spread(from_x)
    spread(from_y)
    for at, peer in enumerate(others):
        block = small_sum.at[peer]
        remote(block, block, send_3.at[at], recv_3.at[peer], {"expert": peer}).wait_recv()
    for peer in range(peers):
        small_out_ref[:, peer * piece : (peer + 1) * piece] = small_sum[peer]
    scatter.total(total_mixture)
    output_ref[...] = (resid_ref[...] + total_mixture[...]).astype(low)
    out_fa.wait_recv()
    out_fb.wait_recv()
    proj_fa.wait_recv()
    proj_fb.wait_recv()
    spread(far)
    ports.finish()
    scatter.finish()
    for copy in small_1 + small_2 + small_3 + swaps:
        copy.wait_send()


def run_weights(
    grad_projection, grad_out, attn_gain, ffn_gain, query_gain, key_gain, router, resid, mixture, peers, kv_heads
):
    width, columns = grad_projection.shape
    head_size = query_gain.shape[1]
    length = resid.shape[0]
    n = peers // 2
    shard_rows = width // peers
    rows, half = shard_rows // 4, peers // 2
    out_rows, middle = grad_out.shape[0] // 4, grad_out.shape[1] // 2
    small_rows = 8 + router.shape[0]
    piece = (small_rows, width // peers)
    dma = pltpu.SemaphoreType.DMA
    kv_width = kv_heads * head_size
    query_width = columns - head_size

    def low_buffer(*shape):
        return pltpu.VMEM(shape, low)

    return pl.pallas_call(
        weights_kernel,
        out_shape=[
            jax.ShapeDtypeStruct((shard_rows, peers * query_width), low),
            jax.ShapeDtypeStruct((shard_rows, kv_width), low),
            jax.ShapeDtypeStruct((shard_rows, kv_width), low),
            jax.ShapeDtypeStruct(grad_out.shape, low),
            jax.ShapeDtypeStruct((small_rows, width), high),
            jax.ShapeDtypeStruct((length, width), low),
        ],
        in_specs=[VMEM] * 9,
        out_specs=[VMEM] * 6,
        scratch_shapes=[
            low_buffer(4, peers, rows, columns),
            low_buffer(2, half, rows, columns),
            low_buffer(2, half, rows, columns),
            low_buffer(2, out_rows, middle),
            low_buffer(2, out_rows, middle),
            low_buffer(half, rows, columns),
            low_buffer(half, rows, columns),
            low_buffer(out_rows, middle),
            low_buffer(out_rows, middle),
            low_buffer(half, rows, columns),
            low_buffer(half, rows, columns),
            low_buffer(out_rows, middle),
            low_buffer(out_rows, middle),
            low_buffer(peers, rows, columns),
            pltpu.VMEM((small_rows, width), high),
            pltpu.VMEM((peers, *piece), high),
            pltpu.VMEM((4, *piece), high),
            pltpu.VMEM((peers, *piece), high),
            pltpu.VMEM((length, width), high),
            dma((20,)), dma((20,)),
            dma((peers - 1,)), dma((peers,)),
            dma((peers - 1,)), dma((peers,)),
            dma((3,)), dma((4,)),
            dma((peers - 1,)), dma((peers,)),
            *Scatter.buffers(n, length, width),
        ],
        compiler_params=communicating(6),
        cost_estimate=pl.CostEstimate(flops=0, bytes_accessed=64 << 20, transcendentals=0),
        name="sum_weight_gradients",
    )(
        grad_projection.reshape(peers, shard_rows, columns), grad_out, attn_gain, ffn_gain, query_gain, key_gain,
        router, resid, mixture.reshape(n, 2 * length, width),
    )


def widen_kernel(
    wide_0, down_0, wide_1, down_1, query_in, key_in, value_in, out_in,
    gate_ref, up_ref, down_ref, query_ref, key_ref, value_ref, out_ref,
):
    for expert, (wide, down) in enumerate(((wide_0, down_0), (wide_1, down_1))):

        @pl.when(pl.program_id(0) == expert)
        def place():
            gate_ref[0] = wide[0, 0].astype(high)
            up_ref[0] = wide[0, 1].astype(high)
            down_ref[0] = down[...].astype(high)

    for source, target in ((query_in, query_ref), (key_in, key_ref), (value_in, value_ref), (out_in, out_ref)):
        target[...] = source[...].astype(high)


def run_widen(grads, weight_grads, hidden_units, model_width, groups):
    piece, tile = hidden_units // groups, model_width // groups
    operands, specs = [], []

    def of_expert(expert):
        return lambda x, j: jnp.where(x == expert, j, 0 if expert else groups - 1)

    for expert, rows in enumerate(grads):
        turn = of_expert(expert)
        operands += [rows[: 2 * hidden_units].reshape(groups, 2, piece, tile), rows[2 * hidden_units :]]
        specs += [
            pl.BlockSpec((1, 2, piece, tile), lambda x, j, turn=turn: (turn(x, j), 0, 0, 0)),
            pl.BlockSpec((piece, tile), lambda x, j, turn=turn: (turn(x, j), 0)),
        ]
    steps = 2 * groups

    def rows_of(array):
        return pl.BlockSpec((array.shape[0] // steps, array.shape[1]), lambda x, j: (x * groups + j, 0))

    return pl.pallas_call(
        widen_kernel,
        grid=(2, groups),
        out_shape=[
            jax.ShapeDtypeStruct((2, piece, model_width), high),
            jax.ShapeDtypeStruct((2, piece, model_width), high),
            jax.ShapeDtypeStruct((2, hidden_units, tile), high),
            *[jax.ShapeDtypeStruct(array.shape, high) for array in weight_grads],
        ],
        in_specs=specs + [rows_of(array) for array in weight_grads],
        out_specs=[
            pl.BlockSpec((1, piece, tile), lambda x, j: (x, 0, j)),
            pl.BlockSpec((1, piece, tile), lambda x, j: (x, 0, j)),
            pl.BlockSpec((1, piece, tile), lambda x, j: (x, j, 0)),
            *[rows_of(array) for array in weight_grads],
        ],
        compiler_params=pltpu.CompilerParams(vmem_limit_bytes=40 << 20),
        name="widen",
    )(*operands, *weight_grads)


def gather_tokens(rows):
    return lax.all_gather(rows, "expert", axis=0, tiled=True)


def scatter_sum(partial):
    return lax.psum_scatter(partial, "expert", scatter_dimension=0, tiled=True)


def projection_gradients(grad_projection, peers, kv_heads, head_size):
    width, columns = grad_projection.shape
    shard_rows = width // peers
    local_width = columns - head_size
    sharers = peers // kv_heads
    grad_projection = grad_projection.reshape(peers, shard_rows, columns)
    grad_projection = lax.psum_scatter(grad_projection, "dp", scatter_dimension=1, tiled=True)
    grad_projection = lax.all_to_all(
        grad_projection, "expert", split_axis=0, concat_axis=0, tiled=True
    )
    grad_projection = lax.all_gather(grad_projection, "dp", axis=1, tiled=True)
    grad_query_w = (
        grad_projection[:, :, :local_width].transpose(1, 0, 2).reshape(shard_rows, peers * local_width)
    ).astype(high)
    shared = grad_projection[:, :, local_width:].reshape(kv_heads, sharers, shard_rows, head_size)
    kv_width = kv_heads * head_size
    grad_key_w = shared[:, 0].transpose(1, 0, 2).reshape(shard_rows, kv_width).astype(high)
    grad_value_w = shared[:, 1].transpose(1, 0, 2).reshape(shard_rows, kv_width).astype(high)
    return grad_query_w, grad_key_w, grad_value_w


def out_gradient(grad_out):
    summed = lax.psum_scatter(grad_out, "dp", scatter_dimension=0, tiled=True)
    return lax.all_gather(summed, "dp", axis=0, tiled=True).astype(high)


def constant_tables(length, head_size):
    half = head_size // 2
    freqs = np.float32(rope_base) ** (-np.arange(half, dtype=np.float32) * np.float32(2.0 / head_size))
    angles = np.arange(length, dtype=np.float32)[:, None] * freqs[None, :]
    cosines, sines = np.cos(angles), np.sin(angles)
    return (
        jnp.asarray(np.concatenate([cosines, cosines], 1), high),
        jnp.asarray(np.concatenate([-sines, sines], 1), high),
    )


def fits_kernels(peers, groups, sharers, experts, full_length, width):
    return groups == 4 and peers % 2 == 0 and peers <= 8 and sharers == 2 and experts == 2 * peers and full_length * width <= 1 << 21


def fused_layer(
    tokens, segments, routes, cotangent, norm_gain_attn, query_weight, key_matrix, value_matrix, query_gain,
    key_gain, out_weight, norm_gain_ffn, router_weight, gate_weight, up_weight, down_weight, heads,
):
    length, model_width = tokens.shape
    head_size = query_gain.shape[0]
    peers = lax.axis_size("expert")
    groups = lax.axis_size("dp")
    local_experts, _, hidden_units = gate_weight.shape
    experts = local_experts * peers
    full_length = length * peers
    kv_heads = peers // 2
    local_width = heads * head_size
    gain_attn_row = norm_gain_attn.reshape(1, model_width)
    gain_ffn_row = norm_gain_ffn.reshape(1, model_width)

    named = jnp.any(routes[:, :, None] == jnp.arange(128, dtype=jnp.int32)[None, None, :], axis=1).astype(low)
    hidden, all_named, projection, raw = run_gather(
        tokens, gain_attn_row, named, query_weight, key_matrix, value_matrix, peers, groups
    )
    cotangent_ready, hidden = lax.optimization_barrier((cotangent, hidden))
    cotangents = lax.all_gather(cotangent_ready, "expert", axis=0, tiled=True)
    cosines, sines = constant_tables(full_length, head_size)
    seg_col = jnp.broadcast_to(segments.reshape(full_length, 1), (full_length, head_size))
    seg_row = jnp.broadcast_to(segments.reshape(1, full_length), (8, full_length))
    query_gain_row = query_gain.reshape(1, head_size)
    key_gain_row = key_gain.reshape(1, head_size)
    mixed, query_low, key_low, value_low, inverse = run_attention_forward(
        raw, heads, head_size, query_gain_row, key_gain_row, cosines, sines, seg_col, seg_row
    )
    resid, ffn_local = run_project(mixed, out_weight, tokens, gain_ffn_row, peers)
    router = jnp.concatenate([router_weight.T, jnp.zeros((128 - experts, model_width), low)], axis=0)
    sums, gates, mixture, *grads = run_experts(
        ffn_local, all_named, router, cotangents, gate_weight, up_weight, down_weight, peers, groups
    )
    grads = [
        lax.psum_scatter(each.reshape(-1, each.shape[2]), "dp", scatter_dimension=0, tiled=True) for each in grads
    ]
    grad_resid, grad_attn, grad_mixed, grad_router, gain_ffn_part = run_turn(
        sums, gates, ffn_local, resid, cotangent, gain_ffn_row, router, out_weight, experts, peers
    )
    grad_query_low, grad_key_part, grad_value_part, query_gain_part = run_attention_backward(
        raw, query_low, key_low, value_low, inverse, mixed, grad_mixed, heads, head_size,
        query_gain_row, cosines, sines, seg_col, seg_row,
    )
    input_grad, grad_projection, grad_out, gain_attn_part, key_gain_part = run_input(
        grad_key_part, grad_value_part, raw[:, local_width : local_width + head_size], key_gain_row, cosines,
        sines, grad_query_low, projection, hidden, mixed, grad_attn, grad_resid, tokens, gain_attn_row, peers,
    )
    *weight_grads, small, output = run_weights(
        grad_projection, grad_out, gain_attn_part, gain_ffn_part, query_gain_part, key_gain_part, grad_router,
        resid, mixture, peers, kv_heads,
    )
    gate_w, up_w, down_w, query_w, key_w, value_w, out_w = run_widen(
        grads, weight_grads, hidden_units, model_width, groups
    )
    return (
        output,
        input_grad,
        small[0],
        query_w,
        key_w,
        value_w,
        small[2, :head_size],
        small[3, :head_size],
        out_w,
        small[1],
        small[8:].T,
        gate_w.transpose(0, 2, 1),
        up_w.transpose(0, 2, 1),
        down_w,
    )


def on_device(
    tokens,
    segments,
    routes,
    cotangent,
    norm_gain_attn,
    query_weight,
    key_matrix,
    value_matrix,
    query_gain,
    key_gain,
    out_weight,
    norm_gain_ffn,
    router_weight,
    gate_weight,
    up_weight,
    down_weight,
):
    length, model_width = tokens.shape
    head_size = query_gain.shape[0]
    peers = lax.axis_size("expert")
    groups = lax.axis_size("dp")
    me = lax.axis_index("expert")
    group = lax.axis_index("dp")
    shard_rows, query_width = query_weight.shape
    kv_width = key_matrix.shape[1]
    kv_heads = kv_width // head_size
    heads = query_width // head_size // peers
    sharers = peers // kv_heads
    local_width = heads * head_size
    local_experts = gate_weight.shape[0]
    experts = local_experts * peers
    full_length = length * peers
    piece = shard_rows // groups

    if fits_kernels(peers, groups, sharers, experts, full_length, model_width):
        return fused_layer(
            tokens, segments, routes, cotangent, norm_gain_attn, query_weight, key_matrix, value_matrix,
            query_gain, key_gain, out_weight, norm_gain_ffn, router_weight, gate_weight, up_weight, down_weight, heads,
        )

    def own_rows(matrix):
        return lax.dynamic_slice_in_dim(matrix, group * piece, piece, 0)

    def columns(matrix, width, copies):
        split = own_rows(matrix).reshape(piece, -1, width).transpose(1, 0, 2)
        return jnp.repeat(split, copies, axis=0)

    outgoing = jnp.concatenate(
        [
            columns(query_weight, local_width, 1),
            columns(key_matrix, head_size, sharers),
            columns(value_matrix, head_size, sharers),
        ],
        axis=2,
    )
    arrived = lax.all_to_all(outgoing, "expert", split_axis=0, concat_axis=0, tiled=True)
    projection = lax.all_gather(arrived, "dp", axis=1, tiled=True).reshape(model_width, -1)

    inputs = tokens.astype(high)
    hidden_local = norm_rows(inputs, norm_gain_attn).astype(low)
    hidden = gather_tokens(hidden_local)
    raw = dot(hidden, projection)
    cosines, sines = rotary_tables(full_length, head_size)
    seg_col = jnp.broadcast_to(segments.reshape(full_length, 1), (full_length, head_size))
    seg_row = jnp.broadcast_to(segments.reshape(1, full_length), (8, full_length))
    query_gain_row = query_gain.reshape(1, head_size)
    key_gain_row = key_gain.reshape(1, head_size)
    mixed, query_low, key_low, value_low, inverse = run_attention_forward(
        raw, heads, head_size, query_gain_row, key_gain_row, cosines, sines, seg_col, seg_row
    )
    attn = scatter_sum(dot(mixed, out_weight).astype(low))
    resid = inputs + attn.astype(high)
    ffn_local = norm_rows(resid, norm_gain_ffn).astype(low)
    ffn_rows = gather_tokens(ffn_local)
    cotangents = gather_tokens(cotangent)
    all_routes = gather_tokens(routes)

    def gates_of(rows, route_rows):
        logits = dot(rows, router_weight)
        named = jnp.any(
            route_rows[:, :, None] == jnp.arange(experts, dtype=jnp.int32)[None, None, :], axis=1
        )
        top = jnp.max(jnp.where(named, logits, -jnp.inf), axis=-1, keepdims=True)
        terms = jnp.where(named, jnp.exp(jnp.where(named, logits - top, 0.0)), 0.0)
        return terms / jnp.sum(terms, axis=-1, keepdims=True)

    gates_all = gates_of(ffn_rows, all_routes)
    own_gates = lax.dynamic_slice_in_dim(gates_all, me * local_experts, local_experts, 1)
    mixture = 0.0
    grad_rows = 0.0
    gate_grads, grad_gate_w, grad_up_w, grad_down_w = [], [], [], []
    for expert in range(local_experts):
        gate_col = own_gates[:, expert : expert + 1]
        gate_pre = dot(ffn_rows, gate_weight[expert])
        up_pre = dot(ffn_rows, up_weight[expert])
        share = jax.nn.sigmoid(gate_pre)
        silu = gate_pre * share
        act = silu * up_pre
        gated_act = (act * gate_col).astype(low)
        mixture = mixture + dot(gated_act, down_weight[expert])
        plain = dot_last(cotangents, down_weight[expert])
        gate_grads.append(jnp.sum(act * plain, axis=-1, keepdims=True))
        grad_act = plain * gate_col
        grad_gate_pre = (grad_act * up_pre * (share * (1.0 + gate_pre * (1.0 - share)))).astype(low)
        grad_up_pre = (grad_act * silu).astype(low)
        grad_rows = (
            grad_rows
            + dot_last(grad_gate_pre, gate_weight[expert])
            + dot_last(grad_up_pre, up_weight[expert])
        )
        hidden_units = gated_act.shape[1]
        grad_gate_w.append(dot_first(grad_gate_pre, ffn_rows).astype(low).reshape(groups, -1, model_width))
        grad_up_w.append(dot_first(grad_up_pre, ffn_rows).astype(low).reshape(groups, -1, model_width))
        cut_width = model_width // groups
        grad_down_w.append(
            jnp.stack([
                dot_first(gated_act, cotangents[:, part * cut_width : (part + 1) * cut_width]).astype(low)
                for part in range(groups)
            ])
        )

    gate_grad = jnp.concatenate(gate_grads, axis=1)
    lane_pad = 128 - 2 * experts % 128
    placed = jnp.zeros((full_length, experts), high)
    placed = lax.dynamic_update_slice_in_dim(placed, gate_grad, me * local_experts, 1)
    upper = placed.astype(low)
    lower = (placed - upper.astype(high)).astype(low)
    sent = jnp.concatenate(
        [grad_rows.astype(low), upper, lower, jnp.zeros((full_length, lane_pad), low)], axis=1
    )
    summed_rows = scatter_sum(sent)
    output = (resid + scatter_sum(mixture.astype(low)).astype(high)).astype(low)
    grad_gates = summed_rows[:, model_width : model_width + experts].astype(high) + summed_rows[
        :, model_width + experts : model_width + 2 * experts
    ].astype(high)
    gates = gates_of(ffn_local, routes)
    grad_logits = (
        gates * (grad_gates - jnp.sum(gates * grad_gates, axis=-1, keepdims=True))
    ).astype(low)
    grad_router = dot_first(ffn_local, grad_logits)
    grad_hidden_ffn = summed_rows[:, :model_width].astype(high) + dot_last(grad_logits, router_weight)
    grad_resid_norm, gain_rows_ffn = norm_back(resid, norm_gain_ffn, grad_hidden_ffn)
    grad_resid = cotangent.astype(high) + grad_resid_norm
    grad_attn = gather_tokens(grad_resid.astype(low))
    grad_mixed = dot_last(grad_attn, out_weight).astype(low)
    grad_out = dot_first(mixed, grad_attn)
    grad_query_low, grad_key_part, grad_value_part, query_gain_part = run_attention_backward(
        raw, query_low, key_low, value_low, inverse, mixed, grad_mixed, heads, head_size,
        query_gain_row, cosines, sines, seg_col, seg_row,
    )
    both = jnp.concatenate([grad_key_part, grad_value_part], axis=1)
    step = 1
    while step < sharers:
        swap = [(peer, peer ^ step) for peer in range(peers)]
        both = both + lax.ppermute(both.astype(low), "expert", swap).astype(high)
        step *= 2
    grad_key_rot, grad_value = both[:, :head_size], both[:, head_size:].astype(low)
    place = me % sharers
    half = head_size // 2
    swapped = jnp.concatenate([grad_key_rot[:, half:], grad_key_rot[:, :half]], axis=1)
    key_raw = raw[:, local_width : local_width + head_size]
    grad_key, key_gain_rows = norm_back(key_raw, key_gain, grad_key_rot * cosines - swapped * sines)
    grad_shared = jnp.where(
        place == 0, grad_key.astype(low), jnp.where(place == 1, grad_value, jnp.zeros_like(grad_value))
    )
    own_columns = jnp.concatenate([grad_query_low, grad_shared], axis=1)
    shared_weight = jnp.where(
        place == 0,
        projection[:, local_width : local_width + head_size],
        projection[:, local_width + head_size :],
    )
    own_weight = jnp.concatenate([projection[:, :local_width], shared_weight], axis=1)
    grad_hidden_attn = scatter_sum(dot_last(own_columns, own_weight).astype(low)).astype(high)
    grad_inputs_norm, gain_rows_attn = norm_back(inputs, norm_gain_attn, grad_hidden_attn)
    input_grad = grad_resid + grad_inputs_norm

    grad_query_w, grad_key_w, grad_value_w = projection_gradients(
        dot_first(hidden, own_columns).astype(low), peers, kv_heads, head_size
    )
    grad_out_w = out_gradient(grad_out.astype(low))

    wide = jnp.concatenate(grad_gate_w + grad_up_w, axis=1)
    wide = lax.psum_scatter(wide, "dp", scatter_dimension=0, tiled=True)
    wide = wide.reshape(2, local_experts, hidden_units // groups, model_width).transpose(0, 1, 3, 2)
    wide = wide.astype(high)
    down = jnp.concatenate(grad_down_w, axis=1)
    down = lax.psum_scatter(down, "dp", scatter_dimension=0, tiled=True)
    down = down.reshape(local_experts, hidden_units, cut_width).astype(high)
    expert_sums = (wide[0], wide[1], down)
    key_gain_grad = jnp.where(place == 0, jnp.sum(key_gain_rows, axis=0), 0.0)
    small = jnp.concatenate(
        [
            jnp.sum(gain_rows_attn, axis=0),
            jnp.sum(gain_rows_ffn, axis=0),
            query_gain_part[0],
            key_gain_grad,
            grad_router.reshape(-1),
        ]
    )
    small = lax.psum(small, ("dp", "expert"))
    cut = 2 * model_width
    return (
        output,
        input_grad,
        small[:model_width],
        grad_query_w,
        grad_key_w,
        grad_value_w,
        small[cut : cut + head_size],
        small[cut + head_size : cut + 2 * head_size],
        grad_out_w,
        small[model_width:cut],
        small[cut + 2 * head_size :].reshape(model_width, experts),
        *expert_sums,
    )


def solution(mesh):
    rows = P(("dp", "expert"), None)
    split = P("expert", None)
    cube = P("expert", None, None)
    cut = P("expert", None, "dp")
    return jax.shard_map(
        on_device,
        mesh=mesh,
        in_specs=(
            rows, P("dp", None), rows, rows, P(), split, split, split, P(), P(), split, P(), P(),
            cube, cube, cube,
        ),
        out_specs=(
            rows, rows, P(), split, split, split, P(), P(), split, P(), P(), cut, cut, cut,
        ),
        check_vma=False,
    )
```

```python
import functools

import jax
import jax.numpy as jnp
import numpy as np
from jax import lax
from jax.experimental import pallas as pl
from jax.experimental.pallas import tpu as pltpu
from jax.sharding import PartitionSpec as P

eps_norm = 1e-06
rope_base = 1000000.0
log2e = 1.4426950408889634
low = jnp.bfloat16
high = jnp.float32


def norm_rows(values, gain):
    factor = lax.rsqrt(jnp.mean(values * values, axis=-1, keepdims=True) + eps_norm)
    return values * factor * gain


def norm_back(values, gain, grad):
    factor = lax.rsqrt(jnp.mean(values * values, axis=-1, keepdims=True) + eps_norm)
    scaled = gain * grad
    inner = jnp.mean(values * scaled, axis=-1, keepdims=True)
    grad_values = factor * scaled - values * (factor * factor * factor * inner)
    return grad_values, grad * values * factor


def dot(left, right):
    return jnp.dot(left, right, preferred_element_type=high)


def dot_first(left, right):
    return lax.dot_general(left, right, (((0,), (0,)), ((), ())), preferred_element_type=high)


def dot_last(left, right):
    return lax.dot_general(left, right, (((1,), (1,)), ((), ())), preferred_element_type=high)


def rotary_tables(length, head_size):
    half = head_size // 2
    freqs = rope_base ** (-jnp.arange(half, dtype=high) * 2.0 / head_size)
    angles = jnp.arange(length, dtype=high)[:, None] * freqs[None, :]
    cosines, sines = jnp.cos(angles), jnp.sin(angles)
    return jnp.concatenate([cosines, cosines], 1), jnp.concatenate([-sines, sines], 1)


def rotate(values, cosines, sines):
    return values * cosines + pltpu.roll(values, values.shape[-1] // 2, 1) * sines


def unrotate(values, cosines, sines):
    return values * cosines - pltpu.roll(values, values.shape[-1] // 2, 1) * sines


def key_spans(length):
    block = min(256, length)
    longest = length // 2
    spans = []
    for begin in range(0, length, block):
        first = max(0, begin - longest + 1) // block * block
        spans.append((begin, block, first, begin + block - first))
    return spans


def tile_mask(seg_col, seg_row, begin, rows, first, keys):
    query_at = begin + lax.broadcasted_iota(jnp.int32, (rows, keys), 0)
    key_at = first + lax.broadcasted_iota(jnp.int32, (rows, keys), 1)
    return (query_at >= key_at) & (seg_col[begin : begin + rows, :1] == seg_row[:1, first : first + keys])


def attention_forward(
    query_ref, key_ref, value_ref, query_gain_ref, key_gain_ref, cos_ref, sin_ref, col_ref, row_ref,
    mixed_ref, query_low_ref, key_low_ref, value_low_ref, inverse_ref, value_wide,
):
    head_size = query_ref.shape[1]

    @pl.when(pl.program_id(0) == 0)
    def first_head():
        rotated = rotate(norm_rows(key_ref[...], key_gain_ref[...]), cos_ref[...], sin_ref[...])
        key_low_ref[...] = rotated.astype(low)
        value_low_ref[...] = value_ref[...].astype(low)
        value_wide[:, :head_size] = value_ref[...].astype(low)
        value_wide[:, head_size:] = jnp.ones_like(value_low_ref)

    rotated = rotate(norm_rows(query_ref[...], query_gain_ref[...]), cos_ref[...], sin_ref[...])
    query_low_ref[...] = (rotated * (head_size**-0.5 * log2e)).astype(low)
    for begin, rows, first, keys in key_spans(query_ref.shape[0]):
        scores = dot_last(query_low_ref[pl.ds(begin, rows)], key_low_ref[pl.ds(first, keys)])
        allowed = tile_mask(col_ref, row_ref, begin, rows, first, keys)
        terms = jnp.where(allowed, jnp.exp2(scores), 0.0).astype(low)
        sums = dot(terms, value_wide[pl.ds(first, keys)])
        inverse = 1.0 / sums[:, head_size:]
        mixed_ref[pl.ds(begin, rows)] = (sums[:, :head_size] * inverse).astype(low)
        inverse_ref[pl.ds(begin, rows)] = inverse


def attention_backward(
    query_ref, query_low_ref, key_low_ref, value_low_ref, inverse_ref, mixed_ref, grad_mixed_ref,
    query_gain_ref, cos_ref, sin_ref, col_ref, row_ref,
    grad_query_ref, grad_key_ref, grad_value_ref, grad_gain_ref,
):
    length, head_size = query_ref.shape

    @pl.when(pl.program_id(0) == 0)
    def first_head():
        grad_key_ref[...] = jnp.zeros_like(grad_key_ref)
        grad_value_ref[...] = jnp.zeros_like(grad_value_ref)
        grad_gain_ref[...] = jnp.zeros_like(grad_gain_ref)

    for begin, rows, first, keys in key_spans(length):
        block = pl.ds(begin, rows)
        query_low = query_low_ref[block]
        key_low = key_low_ref[pl.ds(first, keys)]
        scaled = grad_mixed_ref[block].astype(high) * inverse_ref[block]
        row_term = jnp.sum(scaled * mixed_ref[block].astype(high), axis=-1, keepdims=True)
        scaled = scaled.astype(low)
        scores = dot_last(query_low, key_low)
        allowed = tile_mask(col_ref, row_ref, begin, rows, first, keys)
        terms = jnp.where(allowed, jnp.exp2(scores), 0.0)
        grad_probs = dot_last(scaled, value_low_ref[pl.ds(first, keys)])
        grad_scores = (terms * (grad_probs - row_term)).astype(low)
        grad_value_ref[pl.ds(first, keys)] += dot_first(terms.astype(low), scaled)
        grad_key_ref[pl.ds(first, keys)] += dot_first(grad_scores, query_low) * (1.0 / log2e)
        grad_rotated = dot(grad_scores, key_low) * head_size**-0.5
        grad_normed = unrotate(grad_rotated, cos_ref[block], sin_ref[block])
        grad_raw, gain_rows = norm_back(query_ref[block], query_gain_ref[...], grad_normed)
        grad_query_ref[block] = grad_raw.astype(low)
        grad_gain_ref[...] += jnp.broadcast_to(
            jnp.sum(gain_rows, axis=0, keepdims=True), grad_gain_ref.shape
        )


def whole(shape):
    return pl.BlockSpec(shape, lambda head: (0,) * len(shape))


def run_attention_forward(raw, heads, head_size, query_gain, key_gain, cosines, sines, seg_col, seg_row):
    length = raw.shape[0]
    per_head = pl.BlockSpec((length, head_size), lambda head: (0, head))
    one = (length, head_size)
    wide = jax.ShapeDtypeStruct((length, heads * head_size), low)
    narrow = jax.ShapeDtypeStruct(one, low)
    return pl.pallas_call(
        attention_forward,
        grid=(heads,),
        in_specs=[
            per_head,
            pl.BlockSpec(one, lambda head: (0, heads)),
            pl.BlockSpec(one, lambda head: (0, heads + 1)),
            whole((1, head_size)),
            whole((1, head_size)),
            whole(one),
            whole(one),
            whole(one),
            whole((8, length)),
        ],
        out_specs=[per_head, per_head, whole(one), whole(one), per_head],
        out_shape=[wide, wide, narrow, narrow, jax.ShapeDtypeStruct((length, heads * head_size), high)],
        scratch_shapes=[pltpu.VMEM((length, 2 * head_size), low)],
        compiler_params=pltpu.CompilerParams(vmem_limit_bytes=50 << 20),
        cost_estimate=pl.CostEstimate(
            flops=3 * heads * length * length * head_size, bytes_accessed=8 * length * heads * head_size,
            transcendentals=heads * length * length // 2,
        ),
    )(raw, raw, raw, query_gain, key_gain, cosines, sines, seg_col, seg_row)


def run_attention_backward(
    raw, query_low, key_low, value_low, inverse, mixed, grad_mixed, heads, head_size, query_gain,
    cosines, sines, seg_col, seg_row,
):
    length = raw.shape[0]
    per_head = pl.BlockSpec((length, head_size), lambda head: (0, head))
    one = (length, head_size)
    return pl.pallas_call(
        attention_backward,
        grid=(heads,),
        in_specs=[
            per_head, per_head, whole(one), whole(one), per_head, per_head, per_head,
            whole((1, head_size)), whole(one), whole(one), whole(one), whole((8, length)),
        ],
        out_specs=[per_head, whole(one), whole(one), whole((8, head_size))],
        out_shape=[
            jax.ShapeDtypeStruct((length, heads * head_size), low),
            jax.ShapeDtypeStruct(one, high),
            jax.ShapeDtypeStruct(one, high),
            jax.ShapeDtypeStruct((8, head_size), high),
        ],
        compiler_params=pltpu.CompilerParams(vmem_limit_bytes=50 << 20),
        cost_estimate=pl.CostEstimate(
            flops=6 * heads * length * length * head_size, bytes_accessed=16 * length * heads * head_size,
            transcendentals=heads * length * length // 2,
        ),
    )(
        raw, query_low, key_low, value_low, inverse, mixed, grad_mixed, query_gain, cosines, sines,
        seg_col, seg_row,
    )


MESH = pl.DeviceIdType.MESH
VMEM = pl.BlockSpec(memory_space=pltpu.VMEM)
ANY = pl.BlockSpec(memory_space=pl.ANY)


def wait_all(copies):
    for copy in copies:
        copy.wait()


class Chain:
    def __init__(self):
        self.n = lax.axis_size("expert") // 2
        me = lax.axis_index("expert")
        self.z, self.c = me // 2, me % 2
        self.sibling, self.up, self.down = me + 1 - 2 * self.c, me + 2, me - 2
        self.has_up, self.has_down = self.z < self.n - 1, self.z > 0

    def greet(self):
        barrier = pltpu.get_barrier_semaphore()

        def signal(peer):
            pl.semaphore_signal(barrier, inc=1, device_id={"expert": peer}, device_id_type=MESH)

        signal(self.sibling)
        pl.when(self.has_up)(lambda: signal(self.up))
        pl.when(self.has_down)(lambda: signal(self.down))
        peers = 1 + self.has_up.astype(jnp.int32) + self.has_down.astype(jnp.int32)
        pl.semaphore_wait(barrier, peers)

    def nearest(self, step):
        turn = jnp.int32(0)
        for z in range(self.n):
            order = sorted(range(self.n), key=lambda other: (abs(other - z), other))
            for at, chip in enumerate(order):
                turn = jnp.where((self.z == z) & (step == at), chip, turn)
        return turn


class Gather:
    def __init__(self, chain, own, block, send, recv, local):
        self.chain, self.own, self.block = chain, own, block
        self.send, self.recv, self.local = send, recv, local

    @staticmethod
    def semaphores(n):
        return [
            pltpu.SemaphoreType.DMA((3, n)),
            pltpu.SemaphoreType.DMA((2 * n,)),
            pltpu.SemaphoreType.DMA(()),
        ]

    def copy(self, source, z, way, peer):
        c = self.chain.c
        return pltpu.make_async_remote_copy(
            src_ref=source,
            dst_ref=self.block(z, c),
            send_sem=self.send.at[way, z],
            recv_sem=self.recv.at[2 * z + c],
            device_id={"expert": peer},
            device_id_type=MESH,
        )

    def wait_block(self, z, c):
        block = self.block(z, c)
        pltpu.make_async_remote_copy(
            src_ref=block,
            dst_ref=block,
            send_sem=self.send.at[0, z],
            recv_sem=self.recv.at[2 * z + c],
            device_id={"expert": self.chain.sibling},
            device_id_type=MESH,
        ).wait_recv()

    def keep(self):
        return pltpu.make_async_copy(self.own, self.block(self.chain.z, self.chain.c), self.local)

    def begin(self):
        ch = self.chain
        pl.when(ch.has_up)(lambda: self.copy(self.own, ch.z, 0, ch.up).start())
        pl.when(ch.has_down)(lambda: self.copy(self.own, ch.z, 1, ch.down).start())
        self.copy(self.own, ch.z, 2, ch.sibling).start()
        self.keep().start()

    def service(self, step):
        ch = self.chain

        def from_below():
            z = ch.z - step
            self.wait_block(z, ch.c)
            pl.when(ch.has_up)(lambda: self.copy(self.block(z, ch.c), z, 0, ch.up).start())
            self.copy(self.block(z, ch.c), z, 2, ch.sibling).start()

        def from_above():
            z = ch.z + step
            self.wait_block(z, ch.c)
            pl.when(ch.has_down)(lambda: self.copy(self.block(z, ch.c), z, 1, ch.down).start())
            self.copy(self.block(z, ch.c), z, 2, ch.sibling).start()

        pl.when(ch.z - step >= 0)(from_below)
        pl.when(ch.z + step < ch.n)(from_above)

    def wait_sibling(self, z):
        self.wait_block(z, 1 - self.chain.c)

    def finish(self):
        ch = self.chain
        for z in range(ch.n):
            at = jnp.int32(z)
            block = self.block(at, ch.c)
            pl.when(ch.has_up & (ch.z >= z))(lambda: self.copy(block, at, 0, ch.up).wait_send())
            pl.when(ch.has_down & (ch.z <= z))(lambda: self.copy(block, at, 1, ch.down).wait_send())
            self.copy(block, at, 2, ch.sibling).wait_send()


class NearGather(Gather):
    def __init__(self, chain, own, near, block, send, recv, local):
        super().__init__(chain, own, block, send, recv, local)
        self.near = near

    @staticmethod
    def semaphores(n):
        return Gather.semaphores(n)[:2] + [pltpu.SemaphoreType.DMA((4,))]

    def place(self, at):
        ch = self.chain
        source = self.own if at == 3 else self.near.at[at]
        z, c = ((ch.z - 1, ch.c), (ch.z + 1, ch.c), (ch.z, 1 - ch.c), (ch.z, ch.c))[at]
        return pltpu.make_async_copy(source, self.block(z, c), self.local.at[at])

    def begin(self):
        ch = self.chain

        def below():
            pl.when(ch.has_up)(lambda: self.copy(self.near.at[0], ch.z - 1, 0, ch.up).start())
            self.copy(self.near.at[0], ch.z - 1, 2, ch.sibling).start()
            self.place(0).start()

        def above():
            pl.when(ch.has_down)(lambda: self.copy(self.near.at[1], ch.z + 1, 1, ch.down).start())
            self.copy(self.near.at[1], ch.z + 1, 2, ch.sibling).start()
            self.place(1).start()

        pl.when(ch.has_down)(below)
        pl.when(ch.has_up)(above)
        self.place(2).start()
        self.place(3).start()

    def wait_placed(self):
        pl.when(self.chain.has_down)(lambda: self.place(0).wait())
        pl.when(self.chain.has_up)(lambda: self.place(1).wait())
        self.place(2).wait()
        self.place(3).wait()

    def finish(self):
        ch = self.chain
        for z in range(ch.n):
            at = jnp.int32(z)
            block = self.block(at, ch.c)
            pl.when(ch.has_up & (ch.z > z))(lambda: self.copy(block, at, 0, ch.up).wait_send())
            pl.when(ch.has_down & (ch.z < z))(lambda: self.copy(block, at, 1, ch.down).wait_send())
            pl.when(ch.z != z)(lambda: self.copy(block, at, 2, ch.sibling).wait_send())


class Scatter:
    def __init__(self, chain, half, pair, flow, pair_send, pair_recv, flow_send, flow_recv):
        self.chain, self.half, self.pair, self.flow = chain, half, pair, flow
        self.pair_send, self.pair_recv = pair_send, pair_recv
        self.flow_send, self.flow_recv = flow_send, flow_recv

    @staticmethod
    def buffers(n, rows, width):
        return [
            pltpu.VMEM((n, rows, width), low),
            pltpu.VMEM((n + 1, rows, width), low),
            pltpu.SemaphoreType.DMA((n,)),
            pltpu.SemaphoreType.DMA((n,)),
            pltpu.SemaphoreType.DMA((n,)),
            pltpu.SemaphoreType.DMA((n + 1,)),
        ]

    def pair_copy(self, z):
        ch = self.chain
        return pltpu.make_async_remote_copy(
            src_ref=self.half(z, 1 - ch.c),
            dst_ref=self.pair.at[z],
            send_sem=self.pair_send.at[z],
            recv_sem=self.pair_recv.at[z],
            device_id={"expert": ch.sibling},
            device_id_type=MESH,
        )

    def flow_copy(self, z, slot, peer):
        return pltpu.make_async_remote_copy(
            src_ref=self.pair.at[z],
            dst_ref=self.flow.at[slot],
            send_sem=self.flow_send.at[z],
            recv_sem=self.flow_recv.at[slot],
            device_id={"expert": peer},
            device_id_type=MESH,
        )

    def wait_flow(self, slot):
        block = self.flow.at[slot]
        pltpu.make_async_remote_copy(
            src_ref=block,
            dst_ref=block,
            send_sem=self.flow_send.at[0],
            recv_sem=self.flow_recv.at[slot],
            device_id={"expert": self.chain.sibling},
            device_id_type=MESH,
        ).wait_recv()

    def start_pair(self, z):
        self.pair_copy(z).start()

    def add_pair(self, z, relayed):
        self.pair_copy(z).wait_recv()
        half = self.half(z, self.chain.c)

        def alone():
            self.pair[z] = (half[...].astype(high) + self.pair[z].astype(high)).astype(low)

        def with_flow():
            self.wait_flow(z)
            total = half[...].astype(high) + self.pair[z].astype(high) + self.flow[z].astype(high)
            self.pair[z] = total.astype(low)

        pl.when(relayed)(with_flow)
        pl.when(jnp.logical_not(relayed))(alone)

    def step(self, distance):
        ch = self.chain

        def upward():
            z = ch.z + distance
            self.add_pair(z, ch.has_down)
            self.flow_copy(z, z, ch.up).start()

        def downward():
            z = ch.z - distance
            self.add_pair(z, ch.has_up)
            self.flow_copy(z, jnp.where(distance == 1, ch.n, z), ch.down).start()

        pl.when(ch.z + distance < ch.n)(upward)
        pl.when(ch.z - distance >= 0)(downward)

    def total(self, result):
        ch = self.chain
        self.pair_copy(ch.z).wait_recv()
        result[...] = self.half(ch.z, ch.c)[...].astype(high) + self.pair[ch.z].astype(high)

        def add(slot):
            self.wait_flow(slot)
            result[...] += self.flow[slot].astype(high)

        pl.when(ch.has_down)(lambda: add(ch.z))
        pl.when(ch.has_up)(lambda: add(ch.n))

    def finish(self):
        ch = self.chain
        for z in range(ch.n):
            at = jnp.int32(z)
            self.pair_copy(at).wait_send()
            pl.when(ch.z != z)(lambda: self.flow_copy(at, at, ch.sibling).wait_send())


class Ports:
    def __init__(self, send, recv):
        self.send, self.recv, self.used, self.started = send, recv, 0, []

    def copy(self, source, target, device):
        at = self.used
        self.used += 1
        copy = pltpu.make_async_remote_copy(
            src_ref=source,
            dst_ref=target,
            send_sem=self.send.at[at],
            recv_sem=self.recv.at[at],
            device_id=device,
            device_id_type=MESH,
        )
        self.started.append(copy)
        return copy

    def finish(self):
        for copy in self.started:
            copy.wait_send()


def row_block(ref, rows):
    return lambda z, c: ref.at[pl.ds(pl.multiple_of((2 * z + c) * rows, rows), rows)]


def chip_block(ref, rows):
    return lambda z, c: ref.at[z, pl.ds(pl.multiple_of(c * rows, rows), rows)]


def communicating(collective_id):
    return pltpu.CompilerParams(
        collective_id=collective_id, has_side_effects=True, vmem_limit_bytes=60 << 20
    )


def square():
    group = lax.axis_index("dp")
    y, x = group // 2, group % 2
    from_x, from_y = 2 * y + 1 - x, 2 * (1 - y) + x
    return group, y, x, from_x, from_y


def gather_kernel(
    tokens_ref, gain_ref, named_ref, cot_ref, query_hbm, key_hbm, value_hbm,
    hidden_hbm, all_named_ref, near_ref, projection_hbm, raw_hbm,
    own, stage, hidden_ref, projection_ref, raw_ref, query_ref, key_ref, value_ref,
    send_a, recv_a, local_a, send_b, recv_b, local_b, name_send, name_recv,
    swap_send, swap_recv, x_send, x_recv, y_send, y_recv, far_send, far_recv, out_sems, load_sems,
    near_send, near_recv,
):
    chain = Chain()
    n = chain.n
    peers = 2 * n
    me = lax.axis_index("expert")
    group, _, _, from_x, from_y = square()
    far = 3 - group
    beside, across = {"dp": from_x}, {"dp": from_y}
    sources = [(2 * chain.nearest(step) + core, core, step) for step in range(n) for core in range(2)]
    others = [chain.sibling] + [source for source, _, step in sources if step > 0]
    barrier = pltpu.get_barrier_semaphore()
    for device in [{"expert": peer} for peer in others] + [beside, across]:
        pl.semaphore_signal(barrier, inc=1, device_id=device, device_id_type=MESH)
    rows = stage.shape[1]
    quarter = pl.ds(pl.multiple_of(group * rows, rows), rows)
    loads = [
        pltpu.make_async_copy(source.at[quarter], target, load_sems.at[at])
        for at, (source, target) in enumerate(
            ((query_hbm, query_ref), (key_hbm, key_ref), (value_hbm, value_ref))
        )
    ]
    for load in loads:
        load.start()
    query_width = query_ref.shape[1] // peers
    head_size = key_ref.shape[1] // n
    own[...] = norm_rows(tokens_ref[...].astype(high), gain_ref[...]).astype(low)
    for load in loads:
        load.wait()
    for peer in range(peers):
        shared = pl.ds(peer // 2 * head_size, head_size)
        stage[peer, :, :query_width] = query_ref[:, pl.ds(peer * query_width, query_width)]
        stage[peer, :, query_width : query_width + head_size] = key_ref[:, shared]
        stage[peer, :, query_width + head_size :] = value_ref[:, shared]
    pl.semaphore_wait(barrier, peers + 1)

    def remote(source, target, send, recv, device):
        return pltpu.make_async_remote_copy(
            src_ref=source, dst_ref=target, send_sem=send, recv_sem=recv, device_id=device, device_id_type=MESH
        )

    def block(source, place):
        return projection_ref.at[source, place]

    swaps = [
        remote(stage.at[peer], block(me, group), swap_send.at[at], swap_recv.at[me], {"expert": peer})
        for at, peer in enumerate(others)
    ]
    for copy in swaps:
        copy.start()
    length = own.shape[0]
    piece = length // 2

    def half_block(half):
        def block_of(z, c):
            return hidden_ref.at[pl.ds(pl.multiple_of((2 * z + c) * length + half * piece, piece), piece)]

        return block_of

    wide = [
        Gather(chain, own.at[pl.ds(half * piece, piece)], half_block(half), *sems)
        for half, sems in enumerate(((send_a, recv_a, local_a), (send_b, recv_b, local_b)))
    ]
    for gather in wide:
        gather.begin()
    names = [
        remote(named_ref, all_named_ref.at[me], name_send.at[at], name_recv.at[me], {"expert": peer})
        for at, peer in enumerate(others)
    ]
    for copy in names:
        copy.start()
    all_named_ref[me] = named_ref[...]
    projection_ref[me, group] = stage[me]

    def to_x(at, source, place):
        part = block(source, place)
        return remote(part, part, x_send.at[at], x_recv.at[source], beside)

    def to_y(at, source, place):
        part = block(source, place)
        return remote(part, part, y_send.at[at], y_recv.at[source], across)

    def to_far(at, core, source, place):
        part = block(source, place)
        return remote(part, part, far_send.at[at], far_recv.at[source], across if core == 0 else beside)

    def wait_swap(source):
        part = block(source, group)
        remote(part, part, swap_send.at[0], swap_recv.at[source], {"expert": chain.sibling}).wait_recv()

    for at, (source, core, step) in enumerate(sources):
        if step == 0:
            pl.when(chain.c != core)(lambda: wait_swap(source))
        else:
            wait_swap(source)
        to_x(at, source, group).start()
        to_y(at, source, group).start()
        if step > 0 and core == 1:
            for gather in wide:
                gather.service(step)
    def near(slot, peer):
        return remote(cot_ref, near_ref.at[slot], near_send.at[slot], near_recv.at[slot], {"expert": peer})

    pl.when(chain.has_up)(lambda: near(0, chain.up).start())
    pl.when(chain.has_down)(lambda: near(1, chain.down).start())
    near(2, chain.sibling).start()
    for at, (source, core, _) in enumerate(sources):
        to_x(at, source, from_x).wait_recv()
        to_y(at, source, from_y).wait_recv()
        to_far(at, core, source, from_x if core == 0 else from_y).start()
    for gather in wide:
        for z in range(n):
            gather.wait_sibling(jnp.int32(z))
        gather.keep().wait()
    hidden_out = pltpu.make_async_copy(hidden_ref, hidden_hbm, out_sems.at[0])
    hidden_out.start()
    for at, (source, core, _) in enumerate(sources):
        to_far(at, core, source, far).wait_recv()
    projection_out = pltpu.make_async_copy(projection_ref, projection_hbm, out_sems.at[1])
    projection_out.start()
    pair_rows = 2 * own.shape[0]
    shard_rows = 4 * rows

    def raw_out(step):
        tokens = pl.ds(pl.multiple_of(step * pair_rows, pair_rows), pair_rows)
        return pltpu.make_async_copy(raw_ref.at[tokens], raw_hbm.at[tokens], out_sems.at[2 + step])

    @pl.loop(0, n)
    def each(step):
        tokens = pl.ds(pl.multiple_of(step * pair_rows, pair_rows), pair_rows)
        total = jnp.zeros((pair_rows, raw_ref.shape[1]), high)
        for source in range(peers):
            weight = projection_ref[source].reshape(shard_rows, raw_ref.shape[1])
            total = total + dot(hidden_ref[tokens, source * shard_rows : (source + 1) * shard_rows], weight)
        raw_ref[tokens] = total
        raw_out(step).start()

    for gather in wide:
        gather.finish()
    for at, peer in enumerate(others):
        part = all_named_ref.at[peer]
        remote(part, part, name_send.at[at], name_recv.at[peer], {"expert": peer}).wait_recv()
        names[at].wait_send()
    for at, (source, core, _) in enumerate(sources):
        to_x(at, source, group).wait_send()
        to_y(at, source, group).wait_send()
        to_far(at, core, source, from_x if core == 0 else from_y).wait_send()
    for copy in swaps:
        copy.wait_send()
    pl.when(chain.has_up)(lambda: near(0, chain.up).wait_send())
    pl.when(chain.has_down)(lambda: near(1, chain.down).wait_send())
    near(2, chain.sibling).wait_send()
    pl.when(chain.has_down)(lambda: near(0, chain.sibling).wait_recv())
    pl.when(chain.has_up)(lambda: near(1, chain.sibling).wait_recv())
    near(2, chain.sibling).wait_recv()
    hidden_out.wait()
    projection_out.wait()
    for step in range(n):
        raw_out(step).wait()


def run_gather(tokens, gain, named, cotangent, query_weight, key_matrix, value_matrix, peers, groups):
    length, width = tokens.shape
    n = peers // 2
    shard_rows, query_columns = query_weight.shape
    columns = query_columns // peers + 2 * key_matrix.shape[1] // n
    rows = shard_rows // groups
    dma = pltpu.SemaphoreType.DMA
    hidden, all_named, near, projection, raw = pl.pallas_call(
        gather_kernel,
        out_shape=[
            jax.ShapeDtypeStruct((length * peers, width), low),
            jax.ShapeDtypeStruct((peers, *named.shape), named.dtype),
            jax.ShapeDtypeStruct((3, length, width), low),
            jax.ShapeDtypeStruct((peers, groups, rows, columns), low),
            jax.ShapeDtypeStruct((length * peers, columns), high),
        ],
        in_specs=[VMEM] * 4 + [ANY] * 3,
        out_specs=[ANY, VMEM, VMEM, ANY, ANY],
        scratch_shapes=[
            pltpu.VMEM((length, width), low),
            pltpu.VMEM((peers, rows, columns), low),
            pltpu.VMEM((length * peers, width), low),
            pltpu.VMEM((peers, groups, rows, columns), low),
            pltpu.VMEM((length * peers, columns), high),
            pltpu.VMEM((rows, query_columns), low),
            pltpu.VMEM((rows, key_matrix.shape[1]), low),
            pltpu.VMEM((rows, key_matrix.shape[1]), low),
            *Gather.semaphores(n),
            *Gather.semaphores(n),
            dma((peers - 1,)), dma((peers,)),
            dma((peers - 1,)), dma((peers,)),
            dma((peers,)), dma((peers,)), dma((peers,)), dma((peers,)), dma((peers,)), dma((peers,)),
            dma((2 + n,)),
            dma((3,)), dma((3,)), dma((3,)),
        ],
        compiler_params=communicating(1),
        cost_estimate=pl.CostEstimate(flops=0, bytes_accessed=64 << 20, transcendentals=0),
        name="gather_hidden",
    )(tokens, gain, named, cotangent, query_weight, key_matrix, value_matrix)
    return hidden, all_named, near, projection.reshape(width, columns), raw


def attention_heads(
    raw_ref, query_gain_ref, key_gain_ref, cos_ref, sin_ref, col_ref, row_ref,
    mixed_ref, query_low_ref, key_low_ref, value_low_ref, inverse_ref, value_wide,
):
    head_size = cos_ref.shape[1]
    heads = mixed_ref.shape[1] // head_size
    key_raw = raw_ref[:, heads * head_size : (heads + 1) * head_size]
    key_low_ref[...] = rotate(norm_rows(key_raw, key_gain_ref[...]), cos_ref[...], sin_ref[...]).astype(low)
    value_low_ref[...] = raw_ref[:, (heads + 1) * head_size :].astype(low)
    value_wide[:, :head_size] = value_low_ref[...]
    value_wide[:, head_size:] = jnp.ones_like(value_low_ref)

    @pl.loop(0, heads)
    def each(head):
        columns = pl.ds(pl.multiple_of(head * head_size, head_size), head_size)
        rotated = rotate(norm_rows(raw_ref[:, columns], query_gain_ref[...]), cos_ref[...], sin_ref[...])
        query_low_ref[:, columns] = (rotated * (head_size**-0.5 * log2e)).astype(low)
        for begin, rows, first, keys in key_spans(raw_ref.shape[0]):
            block = pl.ds(begin, rows)
            scores = dot_last(query_low_ref[block, columns], key_low_ref[pl.ds(first, keys)])
            allowed = tile_mask(col_ref, row_ref, begin, rows, first, keys)
            terms = jnp.where(allowed, jnp.exp2(scores), 0.0).astype(low)
            sums = dot(terms, value_wide[pl.ds(first, keys)])
            inverse = 1.0 / sums[:, head_size:]
            mixed_ref[block, columns] = (sums[:, :head_size] * inverse).astype(low)
            inverse_ref[block, columns] = inverse


class Split:
    @staticmethod
    def take(ref, z, half, columns=slice(None)):
        block = ref[pl.ds(2 * z, 2), half, :, columns]
        return block.reshape(block.shape[0] * block.shape[1], block.shape[2])

    @staticmethod
    def put(ref, z, half, value, columns=slice(None)):
        ref[pl.ds(2 * z, 2), half, :, columns] = value.reshape(2, value.shape[0] // 2, value.shape[1])

    @staticmethod
    def every(ref, columns=slice(None)):
        block = ref[:, :, :, columns]
        return block.reshape(block.shape[0] * block.shape[1] * block.shape[2], block.shape[3])


def expert_block(rows_all, plain_of, gate_w, up_w, gate_col, gated, grad_gate, grad_up, z, half):
    hidden = gate_w.shape[1]
    chunk = hidden // 3 if hidden % 384 == 0 else hidden
    gate_grad = jnp.zeros_like(gate_col)
    for begin in range(0, hidden, chunk):
        units = pl.ds(begin, chunk)
        gate_pre = dot(Split.take(rows_all, z, half), gate_w[:, units])
        up_pre = dot(Split.take(rows_all, z, half), up_w[:, units])
        plain = plain_of(units)
        share = 1.0 / (1.0 + jnp.exp(-gate_pre))
        silu = gate_pre * share
        act = silu * up_pre
        gate_grad = gate_grad + jnp.sum(act * plain, axis=-1, keepdims=True)
        Split.put(gated, z, half, (act * gate_col).astype(low), units)
        grad_act = plain * gate_col
        slope = share + silu * (1.0 - share)
        Split.put(grad_gate, z, half, (grad_act * up_pre * slope).astype(low), units)
        Split.put(grad_up, z, half, (grad_act * silu).astype(low), units)
    return gate_grad


def gate_columns(lanes, expert, gate_grad):
    sent = jnp.where(lanes == expert, gate_grad, 0.0)
    upper = sent.astype(low).astype(high)
    lower = (sent - upper).astype(low).astype(high)
    return upper + pltpu.roll(lower, 64, 1)


class Tiles:
    def __init__(self, grads, stage, sems, gated, grad_gate, grad_up, rows_all, cots):
        self.grads, self.stage, self.sems = grads, stage, sems
        self.sources = ((grad_gate, rows_all), (grad_up, rows_all), (gated, cots))
        self.groups = sems.shape[1]
        self.hidden = gated.shape[3]
        self.piece = self.hidden // self.groups
        self.tile = stage.shape[2]

    def copies(self, kind, at, slot):
        piece = self.piece
        made = []
        for part in range(self.groups):
            if kind < 2:
                target = self.grads.at[part, pl.ds(pl.multiple_of((2 * at + kind) * piece, 16), piece)]
            else:
                begin = 2 * self.hidden + part * piece
                target = self.grads.at[at, pl.ds(begin, piece)]
            source = self.stage.at[slot, pl.ds(part * piece, piece)]
            made.append(pltpu.make_async_copy(source, target, self.sems.at[slot, part]))
        return made

    def run(self, kind):
        left, right = self.sources[kind]

        @pl.loop(0, self.groups)
        def each(at):
            slot = at % 2
            if kind == 0:
                pl.when(at >= 2)(lambda: wait_all(self.copies(kind, at, slot)))
            else:
                wait_all(self.copies(kind, at, slot))
            span = pl.ds(pl.multiple_of(at * self.tile, self.tile), self.tile)
            self.stage[slot] = dot_first(Split.every(left), Split.every(right, span)).astype(low)
            for copy in self.copies(kind, at, slot):
                copy.start()

    def finish(self):
        for slot in range(2):
            wait_all(self.copies(0, jnp.int32(slot), slot))


def first_kernel(
    query_gain_ref, key_gain_ref, row_ref, tokens_ref, gain_ref, named_ref, router_in, cot_ref, near_ref,
    raw_hbm, cos_hbm, sin_hbm, col_hbm, weight_hbm, gate_hbm, up_hbm, down_hbm,
    key_low_ref, value_low_ref, resid_ref, ffn_ref, gates_ref, own_gates_ref,
    mixed_hbm, query_low_hbm, inverse_hbm, rows_hbm, cots_hbm, mixture_hbm, parts_hbm, grads_hbm,
    raw_ref, cos_ref, sin_ref, col_ref, weight_ref, mixed_ref, query_low_ref, inverse_ref, value_wide, router_ref, plain, attn_parts, rows_all, cots, gate_w, up_w, down_w, gated, grad_gate, grad_up,
    mix_stage, part_stage, tile_stage, load_sems, rows_sems, mix_sems, part_sems, tile_sems, cot_send, cot_recv, cot_local, *transfers,
):
    chain = Chain()
    n = chain.n
    _, _, rows, width = rows_all.shape
    block_rows = 2 * rows
    loads = [
        pltpu.make_async_copy(source, target, load_sems.at[at])
        for at, (source, target) in enumerate(
            (
                (raw_hbm, raw_ref), (cos_hbm, cos_ref), (sin_hbm, sin_ref), (col_hbm, col_ref),
                (weight_hbm, weight_ref), (down_hbm.at[0], down_w), (gate_hbm.at[0], gate_w),
                (up_hbm.at[0], up_w),
            )
        )
    ]
    for load in loads:
        load.start()
    chain.greet()
    cot_gather = NearGather(
        chain, cot_ref, near_ref, lambda z, c: cots.at[2 * z + c], cot_send, cot_recv, cot_local
    )
    cot_gather.begin()
    wait_all(loads[:4])
    router_ref[...] = jnp.zeros_like(router_ref)
    router_ref[: router_in.shape[0]] = router_in[...]
    attention_heads(
        raw_ref, query_gain_ref, key_gain_ref, cos_ref, sin_ref, col_ref, row_ref,
        mixed_ref, query_low_ref, key_low_ref, value_low_ref, inverse_ref, value_wide,
    )
    attention_copies = [
        pltpu.make_async_copy(source, target, rows_sems.at[2 + at])
        for at, (source, target) in enumerate(
            ((mixed_ref, mixed_hbm), (query_low_ref, query_low_hbm), (inverse_ref, inverse_hbm))
        )
    ]
    for copy in attention_copies:
        copy.start()
    loads[4].wait()
    scatters, gathers = [], []
    for half in range(2):
        pair, flow, *rest = transfers[9 * half : 9 * half + 9]
        scatters.append(
            Scatter(chain, lambda z, c, half=half: attn_parts.at[z, c, half], pair, flow, *rest[:4])
        )
        gathers.append(
            Gather(chain, ffn_ref.at[half], lambda z, c, half=half: rows_all.at[2 * z + c, half], *rest[4:])
        )

    def plain_rows(step):
        z = chain.nearest(step)
        pl.when(step == 0)(cot_gather.wait_placed)
        pl.when(step > 0)(lambda: cot_gather.wait_sibling(z))
        cot_rows = cots[pl.ds(2 * z, 2)].reshape(4 * rows, width)
        hidden = plain.shape[3]
        plain[pl.ds(2 * z, 2)] = dot_last(cot_rows, down_w[...]).reshape(2, 2, rows, hidden)

    @pl.loop(0, n)
    def project(step):
        z = chain.nearest(n - 1 - step)
        tokens = pl.ds(pl.multiple_of(z * 4 * rows, 4 * rows), 4 * rows)
        attn_parts[z] = dot(mixed_ref[tokens], weight_ref[...]).astype(low).reshape(2, 2, rows, width)
        for scatter in scatters:
            scatter.start_pair(z)
        pl.when(step < n - 1)(lambda: scatters[0].step(n - 1 - step))
        pl.when(step == 0)(lambda: loads[5].wait())
        pl.when(step == 1)(lambda: cot_gather.service(2))
        pl.when(step < n - 1)(lambda: plain_rows(step))

    def own_rows(half):
        span = pl.ds(half * rows, rows)
        scatters[half].total(resid_ref.at[span])
        resid_ref[span] += tokens_ref[span].astype(high)
        ffn_ref[half] = norm_rows(resid_ref[span], gain_ref[...]).astype(low)
        gathers[half].begin()

    scatters[1].step(n - 1)
    own_rows(0)
    cot_gather.service(3)
    plain_rows(jnp.int32(3))
    lanes = lax.broadcasted_iota(jnp.int32, (block_rows, 128), 1)
    expert = lax.axis_index("expert") * gate_hbm.shape[0]
    tile = tile_stage.shape[2]
    wait_all(loads[6:])

    def mix_copy(z, half, slot):
        return pltpu.make_async_copy(mix_stage.at[slot], mixture_hbm.at[pl.ds(2 * z, 2), half], mix_sems.at[slot])

    def part_copy(z, half, slot):
        return pltpu.make_async_copy(part_stage.at[slot], parts_hbm.at[pl.ds(2 * z, 2), half], part_sems.at[slot])

    @pl.loop(0, 2 * n)
    def each(turn):
        for step in range(1, n - 1):

            @pl.when(turn == step)
            def early():
                scatters[1].step(n - 1 - step)
                gathers[0].service(step)

        @pl.when(turn == n - 1)
        def middle():
            own_rows(1)
            gathers[0].service(n - 1)

        pl.when((turn >= n) & (turn < 2 * n - 1))(lambda: gathers[1].service(turn - n + 1))
        half, step = turn // n, turn % n
        z = chain.nearest(step)

        def arrived(gather):
            pl.when(step == 0)(lambda: gather.keep().wait())
            gather.wait_sibling(z)

        pl.when(half == 0)(lambda: arrived(gathers[0]))
        pl.when(half == 1)(lambda: arrived(gathers[1]))
        logits = dot_last(Split.take(rows_all, z, half), router_ref[...])
        named = Split.take(named_ref, z, half).astype(high) > 0.5
        top = jnp.max(jnp.where(named, logits, -1e30), axis=-1, keepdims=True)
        terms = jnp.where(named, jnp.exp(jnp.where(named, logits - top, 0.0)), 0.0)
        gates = terms / jnp.sum(terms, axis=-1, keepdims=True)
        Split.put(gates_ref, z, half, gates)

        @pl.when(step == 0)
        def own_gates():
            own_gates_ref[half] = jnp.where(chain.c == 0, gates[:rows], gates[rows:])

        gate_col = jnp.sum(jnp.where(lanes == expert, gates, 0.0), axis=-1, keepdims=True)
        gate_grad = expert_block(
            rows_all, lambda units: Split.take(plain, z, half, units), gate_w, up_w, gate_col, gated, grad_gate,
            grad_up, z, half,
        )
        slot = turn % 2

        @pl.when(turn >= 2)
        def free():
            mix_copy(z, half, slot).wait()
            part_copy(z, half, slot).wait()

        @pl.loop(0, width // tile)
        def columns(at):
            span = pl.ds(pl.multiple_of(at * tile, tile), tile)
            mixture = dot(Split.take(gated, z, half), down_w[:, span])
            mix_stage[slot, :, :, span] = mixture.astype(low).reshape(2, rows, tile)
            grad_rows = dot_last(Split.take(grad_gate, z, half), gate_w[span, :])
            grad_rows = grad_rows + dot_last(Split.take(grad_up, z, half), up_w[span, :])
            part_stage[slot, :, :, span] = grad_rows.astype(low).reshape(2, rows, tile)

        sent = gate_columns(lanes, expert, gate_grad).astype(low)
        part_stage[slot, :, :, width:] = sent.reshape(2, rows, 128)
        mix_copy(z, half, slot).start()
        part_copy(z, half, slot).start()

    whole_copies = [
        pltpu.make_async_copy(rows_all, rows_hbm, rows_sems.at[0]),
        pltpu.make_async_copy(cots, cots_hbm, rows_sems.at[1]),
    ]
    for copy in whole_copies:
        copy.start()
    tiles = Tiles(grads_hbm, tile_stage, tile_sems, gated, grad_gate, grad_up, rows_all, cots)
    for kind in range(3):
        tiles.run(kind)
    for half in range(2):
        gathers[half].finish()
        scatters[half].finish()
    tiles.finish()
    for slot in range(2):
        mix_copy(jnp.int32(0), 0, slot).wait()
        part_copy(jnp.int32(0), 0, slot).wait()
    wait_all(whole_copies + attention_copies)
    cot_gather.finish()


def second_kernel(
    gates_ref, rows_hbm, cot_hbm, gate_hbm, up_hbm, down_hbm, mixture_in, parts_in, own_gates_ref, ffn_ref,
    resid_ref, cot_ref, gain_ref, router_in, weight_ref,
    mixture_hbm, grads_hbm, grad_resid_ref, attn_hbm, mixed_ref, router_grad_ref, gain_grad_ref,
    rows_all, cots, gate_w, up_w, down_w, gated, grad_gate, grad_up, mixture, parts, tile_stage, attn_all, own,
    sums, router_ref, load_sems, chip_sems, mix_sems, tile_sems, attn_sem, *transfers,
):
    chain = Chain()
    n = chain.n
    _, _, rows, width = rows_all.shape
    block_rows = 2 * rows
    loads = [
        pltpu.make_async_copy(source, target, load_sems.at[at])
        for at, (source, target) in enumerate(
            (
                (gate_hbm.at[1], gate_w), (up_hbm.at[1], up_w), (down_hbm.at[1], down_w), (parts_in, parts),
                (mixture_in, mixture),
            )
        )
    ]

    def chip_loads(z):
        block = pl.ds(2 * z, 2)
        return [
            pltpu.make_async_copy(rows_hbm.at[block], rows_all.at[block], chip_sems.at[0, z]),
            pltpu.make_async_copy(cot_hbm.at[block], cots.at[block], chip_sems.at[1, z]),
        ]

    for load in loads[:3]:
        load.start()
    for step in range(n):
        for load in chip_loads(chain.nearest(n - 1 - step)):
            load.start()
    for load in loads[3:]:
        load.start()
    chain.greet()
    scatters, gathers = [], []
    for half in range(2):
        pair, flow, *rest = transfers[9 * half : 9 * half + 9]
        scatters.append(Scatter(chain, lambda z, c, half=half: parts.at[2 * z + c, half], pair, flow, *rest[:4]))
        gathers.append(
            Gather(chain, own.at[half], lambda z, c, half=half: attn_all.at[2 * z + c, half], *rest[4:])
        )
    lanes = lax.broadcasted_iota(jnp.int32, (block_rows, 128), 1)
    expert = lax.axis_index("expert") * gate_hbm.shape[0] + 1
    tile = tile_stage.shape[2]
    router_ref[...] = jnp.zeros_like(router_ref)
    router_ref[: router_in.shape[0]] = router_in[...]
    wait_all(loads[:3])

    def mix_copy(z, half):
        block = pl.ds(2 * z, 2)
        return pltpu.make_async_copy(mixture.at[block, half], mixture_hbm.at[block, half], mix_sems.at[half, z])

    def own_rows(half):
        scatters[half].total(sums)
        span = pl.ds(half * rows, rows)
        sent = sums[:, width:]
        left = lax.broadcasted_iota(jnp.int32, sent.shape, 1) < 64
        grad_gates = jnp.where(left, sent + pltpu.roll(sent, 64, 1), 0.0)
        gates = own_gates_ref[half]
        inner = jnp.sum(gates * grad_gates, axis=-1, keepdims=True)
        grad_logits = (gates * (grad_gates - inner)).astype(low)
        router_grad = dot_first(grad_logits, ffn_ref[half])[: router_grad_ref.shape[0]]
        grad_hidden = sums[:, :width] + dot(grad_logits, router_ref[...])
        grad_rows, gain_rows = norm_back(resid_ref[span], gain_ref[...], grad_hidden)
        gain_grad = jnp.broadcast_to(jnp.sum(gain_rows, axis=0, keepdims=True), gain_grad_ref.shape)
        grad_resid = cot_ref[span].astype(high) + grad_rows
        grad_resid_ref[span] = grad_resid
        own[half] = grad_resid.astype(low)
        gathers[half].begin()
        if half == 0:
            router_grad_ref[...] = router_grad
            gain_grad_ref[...] = gain_grad
        else:
            router_grad_ref[...] += router_grad
            gain_grad_ref[...] += gain_grad

    @pl.loop(0, 2 * n)
    def each(turn):
        half, step = turn // n, turn % n
        z = chain.nearest(n - 1 - step)
        pl.when(half == 0)(lambda: wait_all(chip_loads(z)))
        gates = Split.take(gates_ref, z, half)
        gate_col = jnp.sum(jnp.where(lanes == expert, gates, 0.0), axis=-1, keepdims=True)
        gate_grad = expert_block(
            rows_all, lambda units: dot_last(Split.take(cots, z, half), down_w[units, :]), gate_w, up_w, gate_col,
            gated, grad_gate, grad_up, z, half,
        )

        pl.when(turn == 0)(lambda: loads[3].wait())

        @pl.loop(0, width // tile)
        def columns(at):
            span = pl.ds(pl.multiple_of(at * tile, tile), tile)
            grad_rows = dot_last(Split.take(grad_gate, z, half), gate_w[span, :])
            grad_rows = grad_rows + dot_last(Split.take(grad_up, z, half), up_w[span, :])
            Split.put(parts, z, half, (Split.take(parts, z, half, span).astype(high) + grad_rows).astype(low), span)

        last = pl.ds(width, 128)
        sent = Split.take(parts, z, half, last).astype(high) + gate_columns(lanes, expert, gate_grad)
        Split.put(parts, z, half, sent.astype(low), last)
        pl.when(half == 0)(lambda: scatters[0].start_pair(z))
        pl.when(half == 1)(lambda: scatters[1].start_pair(z))

        pl.when(turn < n - 1)(lambda: scatters[0].step(n - 1 - step))
        pl.when((turn >= n) & (turn < 2 * n - 1))(lambda: scatters[1].step(n - 1 - step))
        pl.when(turn == n)(lambda: own_rows(0))
        pl.when(turn > n)(lambda: gathers[0].service(turn - n))

    tiles = Tiles(grads_hbm, tile_stage, tile_sems, gated, grad_gate, grad_up, rows_all, cots)
    own_rows(1)
    for step in range(1, n):
        if step <= 3:
            tiles.run(step - 1)
        gathers[1].service(step)
    for kind in range(n - 1, 3):
        tiles.run(kind)
    loads[4].wait()

    @pl.loop(0, 2 * n)
    def mixture_rows(turn):
        half, z = turn // n, turn % n

        @pl.loop(0, width // tile)
        def columns(at):
            span = pl.ds(pl.multiple_of(at * tile, tile), tile)
            added = dot(Split.take(gated, z, half), down_w[:, span])
            Split.put(mixture, z, half, (Split.take(mixture, z, half, span).astype(high) + added).astype(low), span)

        mix_copy(z, half).start()

    @pl.loop(0, 2 * n)
    def mixed_rows(turn):
        half, z = turn // n, turn % n
        pl.when(half == 0)(lambda: gathers[0].wait_sibling(z))
        pl.when(half == 1)(lambda: gathers[1].wait_sibling(z))

        @pl.when(z == chain.z)
        def mine():
            pl.when(half == 0)(lambda: gathers[0].keep().wait())
            pl.when(half == 1)(lambda: gathers[1].keep().wait())

        result = dot_last(Split.take(attn_all, z, half), weight_ref[...])
        Split.put(mixed_ref, z, half, result.astype(low))

    attn_copy = pltpu.make_async_copy(attn_all, attn_hbm, attn_sem)
    attn_copy.start()
    for half in range(2):
        gathers[half].finish()
        scatters[half].finish()
        for z in range(n):
            mix_copy(jnp.int32(z), half).wait()
    tiles.finish()
    attn_copy.wait()


def split_rows(array, peers):
    return array.reshape(peers, 2, array.shape[0] // (2 * peers), array.shape[1])


def expert_scratch(gate_weight, up_weight, down_weight, peers, rows, width):
    hidden = gate_weight.shape[2]
    whole = pltpu.VMEM((peers, 2, rows, width), low)
    acts = pltpu.VMEM((peers, 2, rows, hidden), low)
    return [
        whole, whole,
        pltpu.VMEM(gate_weight.shape[1:], low),
        pltpu.VMEM(up_weight.shape[1:], low),
        pltpu.VMEM(down_weight.shape[1:], low),
        acts, acts, acts,
    ]


def run_first(
    raw, query_gain, key_gain, cosines, sines, seg_col, seg_row, weight, tokens, gain, named, router, cotangent, near, gate_weight, up_weight, down_weight,
    peers, groups,
):
    length, width = tokens.shape
    n, rows = peers // 2, length // 2
    hidden = gate_weight.shape[2]
    tile, sent = width // groups, width + 128
    full, local_width, head_size = length * peers, weight.shape[0], cosines.shape[1]
    dma = pltpu.SemaphoreType.DMA

    def split(columns, dtype):
        return jax.ShapeDtypeStruct((peers, 2, rows, columns), dtype)

    return pl.pallas_call(
        first_kernel,
        out_shape=[
            jax.ShapeDtypeStruct((full, head_size), low),
            jax.ShapeDtypeStruct((full, head_size), low),
            jax.ShapeDtypeStruct((length, width), high),
            jax.ShapeDtypeStruct((2, rows, width), low),
            split(128, high),
            jax.ShapeDtypeStruct((2, rows, 128), high),
            jax.ShapeDtypeStruct((full, local_width), low),
            jax.ShapeDtypeStruct((full, local_width), low),
            jax.ShapeDtypeStruct((full, local_width), high),
            split(width, low),
            split(width, low),
            split(width, low),
            split(sent, low),
            jax.ShapeDtypeStruct((groups, 3 * hidden, tile), low),
        ],
        in_specs=[VMEM] * 9 + [ANY] * 8,
        out_specs=[VMEM] * 6 + [ANY] * 8,
        scratch_shapes=[
            pltpu.VMEM(raw.shape, high),
            pltpu.VMEM(cosines.shape, high),
            pltpu.VMEM(sines.shape, high),
            pltpu.VMEM(seg_col.shape, jnp.int32),
            pltpu.VMEM(weight.shape, low),
            pltpu.VMEM((full, local_width), low),
            pltpu.VMEM((full, local_width), low),
            pltpu.VMEM((full, local_width), high),
            pltpu.VMEM((full, 2 * head_size), low),
            pltpu.VMEM((128, width), low),
            pltpu.VMEM((peers, 2, rows, hidden), high),
            pltpu.VMEM((n, 2, 2, rows, width), low),
            *expert_scratch(gate_weight, up_weight, down_weight, peers, rows, width),
            pltpu.VMEM((2, 2, rows, width), low),
            pltpu.VMEM((2, 2, rows, sent), low),
            pltpu.VMEM((2, hidden, tile), low),
            dma((8,)), dma((5,)), dma((2,)), dma((2,)), dma((2, groups)),
            *NearGather.semaphores(n),
            *(Scatter.buffers(n, rows, width) + Gather.semaphores(n)) * 2,
        ],
        compiler_params=communicating(3),
        cost_estimate=pl.CostEstimate(flops=0, bytes_accessed=120 << 20, transcendentals=0),
        name="attention_and_first_expert",
    )(
        query_gain, key_gain, seg_row, tokens, gain, split_rows(named.reshape(-1, 128), peers), router,
        cotangent.reshape(2, rows, width), near.reshape(3, 2, rows, width), raw, cosines, sines, seg_col, weight,
        gate_weight, up_weight, down_weight,
    )


def run_second(
    gates, rows_all, cotangents, gate_weight, up_weight, down_weight, mixture, parts, own_gates, ffn, resid,
    cotangent, gain, router, weight, experts, peers, groups,
):
    length, width = resid.shape
    n, rows = peers // 2, length // 2
    full = length * peers
    hidden = gate_weight.shape[2]
    tile, sent = width // groups, width + 128
    mixed_width = weight.shape[0]
    dma = pltpu.SemaphoreType.DMA

    def split(columns, dtype):
        return jax.ShapeDtypeStruct((peers, 2, rows, columns), dtype)

    mixture, grads, grad_resid, grad_attn, grad_mixed, grad_router, gain_grad = pl.pallas_call(
        second_kernel,
        out_shape=[
            split(width, low),
            jax.ShapeDtypeStruct((groups, 3 * hidden, tile), low),
            jax.ShapeDtypeStruct((length, width), high),
            split(width, low),
            split(mixed_width, low),
            jax.ShapeDtypeStruct((experts, width), high),
            jax.ShapeDtypeStruct((8, width), high),
        ],
        in_specs=[VMEM] + [ANY] * 7 + [VMEM] * 7,
        out_specs=[ANY, ANY, VMEM, ANY, VMEM, VMEM, VMEM],
        scratch_shapes=[
            *expert_scratch(gate_weight, up_weight, down_weight, peers, rows, width),
            pltpu.VMEM((peers, 2, rows, width), low),
            pltpu.VMEM((peers, 2, rows, sent), low),
            pltpu.VMEM((2, hidden, tile), low),
            pltpu.VMEM((peers, 2, rows, width), low),
            pltpu.VMEM((2, rows, width), low),
            pltpu.VMEM((rows, sent), high),
            pltpu.VMEM((128, width), low),
            dma((5,)), dma((2, n)), dma((2, n)), dma((2, groups)), dma(()),
            *(Scatter.buffers(n, rows, sent) + Gather.semaphores(n)) * 2,
        ],
        compiler_params=communicating(7),
        cost_estimate=pl.CostEstimate(flops=0, bytes_accessed=120 << 20, transcendentals=0),
        name="second_expert_and_turn",
    )(
        gates, rows_all, cotangents, gate_weight, up_weight, down_weight, mixture, parts,
        own_gates, ffn, resid, cotangent, gain, router, weight,
    )
    return (
        mixture.reshape(full, width), grads, grad_resid, grad_attn.reshape(full, width),
        grad_mixed.reshape(full, mixed_width), grad_router, gain_grad,
    )


def attention_heads_backward(
    raw_ref, query_low_ref, key_low_ref, value_low_ref, inverse_ref, mixed_ref, grad_mixed_ref, query_gain_ref,
    cos_ref, sin_ref, col_ref, row_ref, grad_query_ref, grad_key_ref, grad_value_ref, grad_gain_ref,
):
    length, head_size = key_low_ref.shape
    heads = query_low_ref.shape[1] // head_size
    grad_key_ref[...] = jnp.zeros_like(grad_key_ref)
    grad_value_ref[...] = jnp.zeros_like(grad_value_ref)
    grad_gain_ref[...] = jnp.zeros_like(grad_gain_ref)

    @pl.loop(0, heads)
    def each(head):
        columns = pl.ds(pl.multiple_of(head * head_size, head_size), head_size)
        for begin, rows, first, keys in key_spans(length):
            block, span = pl.ds(begin, rows), pl.ds(first, keys)
            query_low = query_low_ref[block, columns]
            key_low = key_low_ref[span]
            scaled = grad_mixed_ref[block, columns].astype(high) * inverse_ref[block, columns]
            row_term = jnp.sum(scaled * mixed_ref[block, columns].astype(high), axis=-1, keepdims=True)
            scaled = scaled.astype(low)
            scores = dot_last(query_low, key_low)
            allowed = tile_mask(col_ref, row_ref, begin, rows, first, keys)
            terms = jnp.where(allowed, jnp.exp2(scores), 0.0)
            grad_probs = dot_last(scaled, value_low_ref[span])
            grad_scores = (terms * (grad_probs - row_term)).astype(low)
            grad_value_ref[span] += dot_first(terms.astype(low), scaled)
            grad_key_ref[span] += dot_first(grad_scores, query_low) * (1.0 / log2e)
            grad_rotated = dot(grad_scores, key_low) * head_size**-0.5
            grad_normed = unrotate(grad_rotated, cos_ref[block], sin_ref[block])
            grad_raw, gain_rows = norm_back(raw_ref[block, columns], query_gain_ref[...], grad_normed)
            grad_query_ref[block, columns] = grad_raw.astype(low)
            grad_gain_ref[...] += jnp.broadcast_to(
                jnp.sum(gain_rows, axis=0, keepdims=True), grad_gain_ref.shape
            )


def input_kernel(
    query_gain_ref, key_gain_ref, row_ref, tokens_ref, gain_ref,
    raw_hbm, query_low_hbm, key_low_hbm, value_low_hbm, inverse_hbm, mixed_hbm, grad_mixed_hbm, cos_hbm, sin_hbm,
    col_hbm, projection_hbm, attn_hbm, hidden_hbm, resid_hbm,
    input_grad_ref, gain_grad_ref, query_gain_grad_ref, key_gain_grad_ref, projection_grad_hbm, out_grad_hbm,
    raw_ref, query_low_ref, key_low_ref, value_low_ref, inverse_ref, mixed_ref, grad_mixed_ref, cos_ref, sin_ref,
    col_ref, projection_ref, attn_ref, hidden_ref, resid_ref,
    own_pair, their_pair, key_part, value_part, columns, weight, total, parts, projection_grad, out_grad,
    load_sems, store_sems, swap_send, swap_recv, pair, flow, *scatter_sems,
):
    chain = Chain()
    n = chain.n
    full, head_size = key_part.shape
    sources = (
        raw_hbm, query_low_hbm, key_low_hbm, value_low_hbm, inverse_hbm, mixed_hbm, grad_mixed_hbm, cos_hbm,
        sin_hbm, col_hbm, projection_hbm, attn_hbm, hidden_hbm, resid_hbm,
    )
    targets = (
        raw_ref, query_low_ref, key_low_ref, value_low_ref, inverse_ref, mixed_ref, grad_mixed_ref, cos_ref,
        sin_ref, col_ref, projection_ref, attn_ref, hidden_ref, resid_ref,
    )
    loads = [
        pltpu.make_async_copy(source, target, load_sems.at[at])
        for at, (source, target) in enumerate(zip(sources, targets))
    ]
    for load in loads:
        load.start()
    query_width = query_low_ref.shape[1]
    wait_all(loads[:10])
    attention_heads_backward(
        raw_ref, query_low_ref, key_low_ref, value_low_ref, inverse_ref, mixed_ref, grad_mixed_ref, query_gain_ref,
        cos_ref, sin_ref, col_ref, row_ref, columns, key_part, value_part, query_gain_grad_ref,
    )
    own_pair[:, :head_size] = key_part[...].astype(low)
    own_pair[:, head_size:] = value_part[...].astype(low)
    chain.greet()
    swap = pltpu.make_async_remote_copy(
        src_ref=own_pair,
        dst_ref=their_pair,
        send_sem=swap_send,
        recv_sem=swap_recv,
        device_id={"expert": chain.sibling},
        device_id_type=MESH,
    )
    swap.start()
    first = chain.c == 0
    loads[10].wait()
    weight[:, :query_width] = projection_ref[:, :query_width]
    weight[:, query_width:] = jnp.where(
        first,
        projection_ref[:, query_width : query_width + head_size],
        projection_ref[:, query_width + head_size :],
    )
    swap.wait_recv()
    grad_key = key_part[...] + their_pair[:, :head_size].astype(high)
    grad_value = value_part[...] + their_pair[:, head_size:].astype(high)
    key_raw = raw_ref[:, query_width : query_width + head_size]
    grad_key, gain_rows = norm_back(
        key_raw, key_gain_ref[...], unrotate(grad_key, cos_ref[...], sin_ref[...])
    )
    columns[:, query_width:] = jnp.where(first, grad_key, grad_value).astype(low)
    key_gain = jnp.where(first, jnp.sum(gain_rows, axis=0, keepdims=True), 0.0)
    key_gain_grad_ref[...] = jnp.broadcast_to(key_gain, key_gain_grad_ref.shape)
    pair_rows = parts.shape[1]
    scatter = Scatter(chain, chip_block(parts, pair_rows // 2), pair, flow, *scatter_sems)
    wait_all(loads[11:])
    projection_tile = projection_grad.shape[0] // n
    out_tile = out_grad.shape[1] // n

    @pl.loop(0, n)
    def each(step):
        z = chain.nearest(n - 1 - step)
        rows = pl.ds(pl.multiple_of(z * pair_rows, pair_rows), pair_rows)
        parts[z] = dot_last(columns[rows], weight[...]).astype(low)
        scatter.start_pair(z)
        pl.when(step < n - 1)(lambda: scatter.step(n - 1 - step))
        span = pl.ds(pl.multiple_of(step * projection_tile, projection_tile), projection_tile)
        projection_grad[span] = dot_first(hidden_ref[:, span], columns[...]).astype(low)
        span = pl.ds(pl.multiple_of(step * out_tile, out_tile), out_tile)
        out_grad[:, span] = dot_first(mixed_ref[...], attn_ref[:, span]).astype(low)

    stores = [
        pltpu.make_async_copy(projection_grad, projection_grad_hbm, store_sems.at[0]),
        pltpu.make_async_copy(out_grad, out_grad_hbm, store_sems.at[1]),
    ]
    for store in stores:
        store.start()
    scatter.total(total)
    grad_rows, gain_rows = norm_back(tokens_ref[...].astype(high), gain_ref[...], total[...])
    input_grad_ref[...] = resid_ref[...] + grad_rows
    gain_grad_ref[...] = jnp.broadcast_to(jnp.sum(gain_rows, axis=0, keepdims=True), gain_grad_ref.shape)
    swap.wait_send()
    scatter.finish()
    wait_all(stores)


def run_input(
    raw, query_low, key_low, value_low, inverse, mixed, grad_mixed, query_gain, key_gain, cosines, sines, seg_col,
    seg_row, projection, hidden, grad_attn, grad_resid, tokens, gain, peers,
):
    length, width = tokens.shape
    n = peers // 2
    full, head_size = key_low.shape
    query_width = query_low.shape[1]
    loaded = [
        raw, query_low, key_low, value_low, inverse, mixed, grad_mixed, cosines, sines, seg_col, projection,
        grad_attn, hidden, grad_resid,
    ]
    dma = pltpu.SemaphoreType.DMA
    input_grad, gain_grad, query_gain_grad, key_gain_grad, projection_grad, out_grad = pl.pallas_call(
        input_kernel,
        out_shape=[
            jax.ShapeDtypeStruct((length, width), high),
            jax.ShapeDtypeStruct((8, width), high),
            jax.ShapeDtypeStruct((8, head_size), high),
            jax.ShapeDtypeStruct((8, head_size), high),
            jax.ShapeDtypeStruct((width, query_width + head_size), low),
            jax.ShapeDtypeStruct((query_width, width), low),
        ],
        in_specs=[VMEM] * 5 + [ANY] * len(loaded),
        out_specs=[VMEM] * 4 + [ANY] * 2,
        scratch_shapes=[
            *[pltpu.VMEM(array.shape, array.dtype) for array in loaded],
            pltpu.VMEM((full, 2 * head_size), low),
            pltpu.VMEM((full, 2 * head_size), low),
            pltpu.VMEM((full, head_size), high),
            pltpu.VMEM((full, head_size), high),
            pltpu.VMEM((full, query_width + head_size), low),
            pltpu.VMEM((width, query_width + head_size), low),
            pltpu.VMEM((length, width), high),
            pltpu.VMEM((n, 2 * length, width), low),
            pltpu.VMEM((width, query_width + head_size), low),
            pltpu.VMEM((query_width, width), low),
            dma((len(loaded),)), dma((2,)), dma(()), dma(()),
            *Scatter.buffers(n, length, width),
        ],
        compiler_params=communicating(5),
        cost_estimate=pl.CostEstimate(flops=0, bytes_accessed=64 << 20, transcendentals=0),
        name="attention_backward_and_input",
    )(query_gain, key_gain, seg_row, tokens, gain, *loaded)
    return input_grad, projection_grad, out_grad, gain_grad, query_gain_grad, key_gain_grad
def weights_kernel(
    proj_ref, out_ref, attn_gain_ref, ffn_gain_ref, query_gain_ref, key_gain_ref, router_ref, resid_ref,
    mixture_ref,
    query_grad_ref, key_grad_ref, value_grad_ref, out_grad_ref, small_out_ref, output_ref,
    all_proj, first_a, first_b, out_first_a, out_first_b, second_a, second_b, out_second_a, out_second_b,
    send_a, send_b, out_send_a, out_send_b, quarter, small, got, part, small_sum, total_mixture,
    port_send, port_recv, swap_send, swap_recv, send_1, recv_1, send_2, recv_2, send_3, recv_3,
    pair, flow, *scatter_sems,
):
    peers = lax.axis_size("expert")
    me = lax.axis_index("expert")
    group, y, x, from_x, from_y = square()
    beside, across = {"dp": from_x}, {"dp": from_y}
    chain = Chain()
    scatter = Scatter(chain, chip_block(mixture_ref, resid_ref.shape[0]), pair, flow, *scatter_sems)
    width = out_ref.shape[1]
    head_size = query_gain_ref.shape[1]
    small[...] = jnp.zeros_like(small)
    small[0:1] = attn_gain_ref[0:1]
    small[1:2] = ffn_gain_ref[0:1]
    small[2:3, :head_size] = query_gain_ref[0:1]
    small[3:4, :head_size] = key_gain_ref[0:1]
    small[8:] = router_ref[...]
    piece = width // peers

    def small_piece(ref, peer):
        return ref.at[:, pl.ds(pl.multiple_of(peer * piece, piece), piece)]

    barrier = pltpu.get_barrier_semaphore()
    others = [(me + shift) % peers for shift in range(1, peers)]
    groups = [(group + shift) % 4 for shift in range(1, 4)]
    for peer in others:
        pl.semaphore_signal(barrier, inc=1, device_id={"expert": peer}, device_id_type=MESH)
    for other in groups:
        pl.semaphore_signal(barrier, inc=1, device_id={"dp": other}, device_id_type=MESH)
    pl.semaphore_wait(barrier, peers + 2)

    shard_rows, columns = proj_ref.shape[1:]
    rows, half = shard_rows // 4, peers // 2
    out_rows = out_ref.shape[0] // 4
    middle = width // 2
    ports = Ports(port_send, port_recv)

    def proj_part(side, q):
        return proj_ref.at[pl.ds(side * half, half), pl.ds(pl.multiple_of(q * rows, rows), rows)]

    def out_part(ref, side, q):
        return ref.at[pl.ds(pl.multiple_of(q * out_rows, out_rows), out_rows), pl.ds(side * middle, middle)]

    def remote(source, target, send, recv, device):
        return pltpu.make_async_remote_copy(
            src_ref=source, dst_ref=target, send_sem=send, recv_sem=recv, device_id=device, device_id_type=MESH
        )

    along_x = [2 * other + 1 - x for other in range(2)]
    along_y = [2 * (1 - y) + other for other in range(2)]
    out_1a = [ports.copy(out_part(out_ref, 0, along_x[k]), out_first_a.at[k], beside) for k in range(2)]
    out_1b = [ports.copy(out_part(out_ref, 1, along_y[k]), out_first_b.at[k], across) for k in range(2)]
    proj_1a = [ports.copy(proj_part(0, along_x[k]), first_a.at[k], beside) for k in range(2)]
    proj_1b = [ports.copy(proj_part(1, along_y[k]), first_b.at[k], across) for k in range(2)]
    for copy in out_1a + out_1b + proj_1a + proj_1b:
        copy.start()

    small_1 = [
        remote(small_piece(small, peer), got.at[me], send_1.at[at], recv_1.at[me], {"expert": peer})
        for at, peer in enumerate(others)
    ]
    for copy in small_1:
        copy.start()
    got[me] = small_piece(small, me)[...]
    for z in range(chain.n):
        scatter.start_pair(jnp.int32(z))

    own = group
    for copy in out_1a + out_1b:
        copy.wait_recv()
    for_y, for_x = 2 * (1 - y) + x, 2 * y + 1 - x
    out_send_a[...] = (
        out_part(out_ref, 0, for_y)[...].astype(high) + out_first_a[1 - y].astype(high)
    ).astype(low)
    out_send_b[...] = (
        out_part(out_ref, 1, for_x)[...].astype(high) + out_first_b[1 - x].astype(high)
    ).astype(low)
    out_2a = ports.copy(out_send_a, out_second_a, across)
    out_2b = ports.copy(out_send_b, out_second_b, beside)
    out_2a.start()
    out_2b.start()
    scatter.step(3) if chain.n > 3 else None
    for copy in proj_1a + proj_1b:
        copy.wait_recv()
    send_a[...] = (proj_part(0, for_y)[...].astype(high) + first_a[1 - y].astype(high)).astype(low)
    send_b[...] = (proj_part(1, for_x)[...].astype(high) + first_b[1 - x].astype(high)).astype(low)
    proj_2a = ports.copy(send_a, second_a, across)
    proj_2b = ports.copy(send_b, second_b, beside)
    proj_2a.start()
    proj_2b.start()
    scatter.step(2) if chain.n > 2 else None

    for at, peer in enumerate(others):
        remote(got.at[peer], got.at[peer], send_1.at[at], recv_1.at[peer], {"expert": peer}).wait_recv()
    total = got[0]
    for at in range(1, peers):
        total = total + got[at]
    part[group] = total
    small_2 = [
        remote(part.at[group], part.at[group], send_2.at[at], recv_2.at[group], {"dp": other})
        for at, other in enumerate(groups)
    ]
    for copy in small_2:
        copy.start()

    out_2a.wait_recv()
    out_2b.wait_recv()
    for side, first, second, at in ((0, out_first_a, out_second_a, y), (1, out_first_b, out_second_b, x)):
        out_part(out_grad_ref, side, own)[...] = (
            out_part(out_ref, side, own)[...].astype(high) + first[at].astype(high) + second[...].astype(high)
        ).astype(low)

    def out_quarter(q):
        return out_grad_ref.at[pl.ds(pl.multiple_of(q * out_rows, out_rows), out_rows)]

    out_gx = ports.copy(out_quarter(own), out_quarter(own), beside)
    out_gy = ports.copy(out_quarter(own), out_quarter(own), across)

    proj_2a.wait_recv()
    proj_2b.wait_recv()
    for side, first, second, at in ((0, first_a, second_a, y), (1, first_b, second_b, x)):
        quarter[pl.ds(side * half, half)] = (
            proj_part(side, own)[...].astype(high) + first[at].astype(high) + second[...].astype(high)
        ).astype(low)
    swaps = [
        remote(quarter.at[peer], all_proj.at[own, me], swap_send.at[at], swap_recv.at[me], {"expert": peer})
        for at, peer in enumerate(others)
    ]
    for copy in swaps:
        copy.start()
    out_gx.start()
    out_gy.start()
    all_proj[own, me] = quarter[me]

    for at, other in enumerate(groups):
        remote(part.at[other], part.at[other], send_2.at[at], recv_2.at[other], {"dp": other}).wait_recv()
    total = part[0]
    for at in range(1, 4):
        total = total + part[at]
    small_sum[me] = total
    small_3 = [
        remote(small_sum.at[me], small_sum.at[me], send_3.at[at], recv_3.at[me], {"expert": peer})
        for at, peer in enumerate(others)
    ]
    for copy in small_3:
        copy.start()

    for at, peer in enumerate(others):
        block = all_proj.at[own, peer]
        remote(block, block, swap_send.at[at], swap_recv.at[peer], {"expert": peer}).wait_recv()
    proj_gx = ports.copy(all_proj.at[own], all_proj.at[own], beside)
    proj_gy = ports.copy(all_proj.at[own], all_proj.at[own], across)
    proj_gx.start()
    proj_gy.start()
    out_gx.wait_recv()
    out_gy.wait_recv()
    far = 3 - group
    out_fa = ports.copy(out_part(out_grad_ref, 0, from_x), out_part(out_grad_ref, 0, from_x), across)
    out_fb = ports.copy(out_part(out_grad_ref, 1, from_y), out_part(out_grad_ref, 1, from_y), beside)
    out_fa.start()
    out_fb.start()
    scatter.step(1) if chain.n > 1 else None

    def proj_half(q, side):
        return all_proj.at[q, pl.ds(side * half, half)]

    proj_gx.wait_recv()
    proj_gy.wait_recv()
    proj_fa = ports.copy(proj_half(from_x, 0), proj_half(from_x, 0), across)
    proj_fb = ports.copy(proj_half(from_y, 1), proj_half(from_y, 1), beside)
    proj_fa.start()
    proj_fb.start()
    query_width = columns - head_size

    def spread(q):
        block = pl.ds(pl.multiple_of(q * rows, rows), rows)
        for peer in range(peers):
            query_grad_ref[block, peer * query_width : (peer + 1) * query_width] = all_proj[q, peer, :, :query_width]
            shared = key_grad_ref if peer % 2 == 0 else value_grad_ref
            at = peer // 2 * head_size
            shared[block, at : at + head_size] = all_proj[q, peer, :, query_width:]

    spread(own)
    spread(from_x)
    spread(from_y)
    for at, peer in enumerate(others):
        block = small_sum.at[peer]
        remote(block, block, send_3.at[at], recv_3.at[peer], {"expert": peer}).wait_recv()
    for peer in range(peers):
        small_out_ref[:, peer * piece : (peer + 1) * piece] = small_sum[peer]
    scatter.total(total_mixture)
    output_ref[...] = (resid_ref[...] + total_mixture[...]).astype(low)
    out_fa.wait_recv()
    out_fb.wait_recv()
    proj_fa.wait_recv()
    proj_fb.wait_recv()
    spread(far)
    ports.finish()
    scatter.finish()
    for copy in small_1 + small_2 + small_3 + swaps:
        copy.wait_send()


def run_weights(
    grad_projection, grad_out, attn_gain, ffn_gain, query_gain, key_gain, router, resid, mixture, peers, kv_heads
):
    width, columns = grad_projection.shape
    head_size = query_gain.shape[1]
    length = resid.shape[0]
    n = peers // 2
    shard_rows = width // peers
    rows, half = shard_rows // 4, peers // 2
    out_rows, middle = grad_out.shape[0] // 4, grad_out.shape[1] // 2
    small_rows = 8 + router.shape[0]
    piece = (small_rows, width // peers)
    dma = pltpu.SemaphoreType.DMA
    kv_width = kv_heads * head_size
    query_width = columns - head_size

    def low_buffer(*shape):
        return pltpu.VMEM(shape, low)

    return pl.pallas_call(
        weights_kernel,
        out_shape=[
            jax.ShapeDtypeStruct((shard_rows, peers * query_width), low),
            jax.ShapeDtypeStruct((shard_rows, kv_width), low),
            jax.ShapeDtypeStruct((shard_rows, kv_width), low),
            jax.ShapeDtypeStruct(grad_out.shape, low),
            jax.ShapeDtypeStruct((small_rows, width), high),
            jax.ShapeDtypeStruct((length, width), low),
        ],
        in_specs=[VMEM] * 9,
        out_specs=[VMEM] * 6,
        scratch_shapes=[
            low_buffer(4, peers, rows, columns),
            low_buffer(2, half, rows, columns),
            low_buffer(2, half, rows, columns),
            low_buffer(2, out_rows, middle),
            low_buffer(2, out_rows, middle),
            low_buffer(half, rows, columns),
            low_buffer(half, rows, columns),
            low_buffer(out_rows, middle),
            low_buffer(out_rows, middle),
            low_buffer(half, rows, columns),
            low_buffer(half, rows, columns),
            low_buffer(out_rows, middle),
            low_buffer(out_rows, middle),
            low_buffer(peers, rows, columns),
            pltpu.VMEM((small_rows, width), high),
            pltpu.VMEM((peers, *piece), high),
            pltpu.VMEM((4, *piece), high),
            pltpu.VMEM((peers, *piece), high),
            pltpu.VMEM((length, width), high),
            dma((20,)), dma((20,)),
            dma((peers - 1,)), dma((peers,)),
            dma((peers - 1,)), dma((peers,)),
            dma((3,)), dma((4,)),
            dma((peers - 1,)), dma((peers,)),
            *Scatter.buffers(n, length, width),
        ],
        compiler_params=communicating(6),
        cost_estimate=pl.CostEstimate(flops=0, bytes_accessed=64 << 20, transcendentals=0),
        name="sum_weight_gradients",
    )(
        grad_projection.reshape(peers, shard_rows, columns), grad_out, attn_gain, ffn_gain, query_gain, key_gain,
        router, resid, mixture.reshape(n, 2 * length, width),
    )


def widen_kernel(
    wide_0, down_0, wide_1, down_1, query_in, key_in, value_in, out_in,
    gate_ref, up_ref, down_ref, query_ref, key_ref, value_ref, out_ref,
):
    for expert, (wide, down) in enumerate(((wide_0, down_0), (wide_1, down_1))):

        @pl.when(pl.program_id(0) == expert)
        def place():
            piece = gate_ref.shape[1]
            gate_ref[0] = wide[:piece].astype(high)
            up_ref[0] = wide[piece:].astype(high)
            down_ref[0] = down[...].astype(high)

    for source, target in ((query_in, query_ref), (key_in, key_ref), (value_in, value_ref), (out_in, out_ref)):
        target[...] = source[...].astype(high)


def run_widen(grads, weight_grads, hidden_units, model_width, groups):
    piece, tile = hidden_units // groups, model_width // groups
    operands, specs = [], []

    def of_expert(expert):
        return lambda x, j: jnp.where(x == expert, j, 0 if expert else groups - 1)

    for expert, rows in enumerate(grads):
        turn = of_expert(expert)
        operands += [rows, rows]
        specs += [
            pl.BlockSpec((2 * piece, tile), lambda x, j, turn=turn: (turn(x, j), 0)),
            pl.BlockSpec((piece, tile), lambda x, j, turn=turn: (2 * groups + turn(x, j), 0)),
        ]
    steps = 2 * groups

    def rows_of(array):
        return pl.BlockSpec((array.shape[0] // steps, array.shape[1]), lambda x, j: (x * groups + j, 0))

    return pl.pallas_call(
        widen_kernel,
        grid=(2, groups),
        out_shape=[
            jax.ShapeDtypeStruct((2, piece, model_width), high),
            jax.ShapeDtypeStruct((2, piece, model_width), high),
            jax.ShapeDtypeStruct((2, hidden_units, tile), high),
            *[jax.ShapeDtypeStruct(array.shape, high) for array in weight_grads],
        ],
        in_specs=specs + [rows_of(array) for array in weight_grads],
        out_specs=[
            pl.BlockSpec((1, piece, tile), lambda x, j: (x, 0, j)),
            pl.BlockSpec((1, piece, tile), lambda x, j: (x, 0, j)),
            pl.BlockSpec((1, piece, tile), lambda x, j: (x, j, 0)),
            *[rows_of(array) for array in weight_grads],
        ],
        compiler_params=pltpu.CompilerParams(vmem_limit_bytes=60 << 20),
        name="widen",
    )(*operands, *weight_grads)


def gather_tokens(rows):
    return lax.all_gather(rows, "expert", axis=0, tiled=True)


def scatter_sum(partial):
    return lax.psum_scatter(partial, "expert", scatter_dimension=0, tiled=True)


def projection_gradients(grad_projection, peers, kv_heads, head_size):
    width, columns = grad_projection.shape
    shard_rows = width // peers
    local_width = columns - head_size
    sharers = peers // kv_heads
    grad_projection = grad_projection.reshape(peers, shard_rows, columns)
    grad_projection = lax.psum_scatter(grad_projection, "dp", scatter_dimension=1, tiled=True)
    grad_projection = lax.all_to_all(
        grad_projection, "expert", split_axis=0, concat_axis=0, tiled=True
    )
    grad_projection = lax.all_gather(grad_projection, "dp", axis=1, tiled=True)
    grad_query_w = (
        grad_projection[:, :, :local_width].transpose(1, 0, 2).reshape(shard_rows, peers * local_width)
    ).astype(high)
    shared = grad_projection[:, :, local_width:].reshape(kv_heads, sharers, shard_rows, head_size)
    kv_width = kv_heads * head_size
    grad_key_w = shared[:, 0].transpose(1, 0, 2).reshape(shard_rows, kv_width).astype(high)
    grad_value_w = shared[:, 1].transpose(1, 0, 2).reshape(shard_rows, kv_width).astype(high)
    return grad_query_w, grad_key_w, grad_value_w


def out_gradient(grad_out):
    summed = lax.psum_scatter(grad_out, "dp", scatter_dimension=0, tiled=True)
    return lax.all_gather(summed, "dp", axis=0, tiled=True).astype(high)


def constant_tables(length, head_size):
    half = head_size // 2
    freqs = np.float32(rope_base) ** (-np.arange(half, dtype=np.float32) * np.float32(2.0 / head_size))
    angles = np.arange(length, dtype=np.float32)[:, None] * freqs[None, :]
    cosines, sines = np.cos(angles), np.sin(angles)
    return (
        jnp.asarray(np.concatenate([cosines, cosines], 1), high),
        jnp.asarray(np.concatenate([-sines, sines], 1), high),
    )


def fits_kernels(peers, groups, sharers, experts, full_length, width):
    return groups == 4 and peers == 8 and sharers == 2 and experts == 2 * peers and full_length * width <= 1 << 21


def fused_layer(
    tokens, segments, routes, cotangent, norm_gain_attn, query_weight, key_matrix, value_matrix, query_gain,
    key_gain, out_weight, norm_gain_ffn, router_weight, gate_weight, up_weight, down_weight, heads,
):
    length, model_width = tokens.shape
    head_size = query_gain.shape[0]
    peers = lax.axis_size("expert")
    groups = lax.axis_size("dp")
    local_experts, _, hidden_units = gate_weight.shape
    experts = local_experts * peers
    full_length = length * peers
    kv_heads = peers // 2
    local_width = heads * head_size
    gain_attn_row = norm_gain_attn.reshape(1, model_width)
    gain_ffn_row = norm_gain_ffn.reshape(1, model_width)

    named = jnp.any(routes[:, :, None] == jnp.arange(128, dtype=jnp.int32)[None, None, :], axis=1).astype(low)
    hidden, all_named, near, projection, raw = run_gather(
        tokens, gain_attn_row, named, cotangent, query_weight, key_matrix, value_matrix, peers, groups
    )
    cosines, sines = constant_tables(full_length, head_size)
    seg_col = jnp.broadcast_to(segments.reshape(full_length, 1), (full_length, head_size))
    seg_row = jnp.broadcast_to(segments.reshape(1, full_length), (8, full_length))
    query_gain_row = query_gain.reshape(1, head_size)
    key_gain_row = key_gain.reshape(1, head_size)
    router = router_weight.T
    (
        key_low, value_low, resid, ffn_local, gates, own_gates, mixed, query_low, inverse, rows_all, cotangents,
        mixture, parts, first_grads,
    ) = run_first(
        raw, query_gain_row, key_gain_row, cosines, sines, seg_col, seg_row, out_weight, tokens, gain_ffn_row,
        all_named, router, cotangent, near, gate_weight, up_weight, down_weight, peers, groups,
    )
    mixture, second_grads, grad_resid, grad_attn, grad_mixed, grad_router, gain_ffn_part = run_second(
        gates, rows_all, cotangents, gate_weight, up_weight, down_weight, mixture, parts, own_gates, ffn_local,
        resid, cotangent, gain_ffn_row, router, out_weight, experts, peers, groups,
    )
    grads = (first_grads, second_grads)
    grads = [
        lax.psum_scatter(each.reshape(-1, each.shape[2]), "dp", scatter_dimension=0, tiled=True) for each in grads
    ]
    input_grad, grad_projection, grad_out, gain_attn_part, query_gain_part, key_gain_part = run_input(
        raw, query_low, key_low, value_low, inverse, mixed, grad_mixed, query_gain_row, key_gain_row, cosines, sines,
        seg_col, seg_row, projection, hidden, grad_attn, grad_resid, tokens, gain_attn_row, peers,
    )
    *weight_grads, small, output = run_weights(
        grad_projection, grad_out, gain_attn_part, gain_ffn_part, query_gain_part, key_gain_part, grad_router,
        resid, mixture, peers, kv_heads,
    )
    gate_w, up_w, down_w, query_w, key_w, value_w, out_w = run_widen(
        grads, weight_grads, hidden_units, model_width, groups
    )
    return (
        output,
        input_grad,
        small[0],
        query_w,
        key_w,
        value_w,
        small[2, :head_size],
        small[3, :head_size],
        out_w,
        small[1],
        small[8:].T,
        gate_w.transpose(0, 2, 1),
        up_w.transpose(0, 2, 1),
        down_w,
    )


def on_device(
    tokens,
    segments,
    routes,
    cotangent,
    norm_gain_attn,
    query_weight,
    key_matrix,
    value_matrix,
    query_gain,
    key_gain,
    out_weight,
    norm_gain_ffn,
    router_weight,
    gate_weight,
    up_weight,
    down_weight,
):
    length, model_width = tokens.shape
    head_size = query_gain.shape[0]
    peers = lax.axis_size("expert")
    groups = lax.axis_size("dp")
    me = lax.axis_index("expert")
    group = lax.axis_index("dp")
    shard_rows, query_width = query_weight.shape
    kv_width = key_matrix.shape[1]
    kv_heads = kv_width // head_size
    heads = query_width // head_size // peers
    sharers = peers // kv_heads
    local_width = heads * head_size
    local_experts = gate_weight.shape[0]
    experts = local_experts * peers
    full_length = length * peers
    piece = shard_rows // groups

    if fits_kernels(peers, groups, sharers, experts, full_length, model_width):
        return fused_layer(
            tokens, segments, routes, cotangent, norm_gain_attn, query_weight, key_matrix, value_matrix,
            query_gain, key_gain, out_weight, norm_gain_ffn, router_weight, gate_weight, up_weight, down_weight, heads,
        )

    def own_rows(matrix):
        return lax.dynamic_slice_in_dim(matrix, group * piece, piece, 0)

    def columns(matrix, width, copies):
        split = own_rows(matrix).reshape(piece, -1, width).transpose(1, 0, 2)
        return jnp.repeat(split, copies, axis=0)

    outgoing = jnp.concatenate(
        [
            columns(query_weight, local_width, 1),
            columns(key_matrix, head_size, sharers),
            columns(value_matrix, head_size, sharers),
        ],
        axis=2,
    )
    arrived = lax.all_to_all(outgoing, "expert", split_axis=0, concat_axis=0, tiled=True)
    projection = lax.all_gather(arrived, "dp", axis=1, tiled=True).reshape(model_width, -1)

    inputs = tokens.astype(high)
    hidden_local = norm_rows(inputs, norm_gain_attn).astype(low)
    hidden = gather_tokens(hidden_local)
    raw = dot(hidden, projection)
    cosines, sines = rotary_tables(full_length, head_size)
    seg_col = jnp.broadcast_to(segments.reshape(full_length, 1), (full_length, head_size))
    seg_row = jnp.broadcast_to(segments.reshape(1, full_length), (8, full_length))
    query_gain_row = query_gain.reshape(1, head_size)
    key_gain_row = key_gain.reshape(1, head_size)
    mixed, query_low, key_low, value_low, inverse = run_attention_forward(
        raw, heads, head_size, query_gain_row, key_gain_row, cosines, sines, seg_col, seg_row
    )
    attn = scatter_sum(dot(mixed, out_weight).astype(low))
    resid = inputs + attn.astype(high)
    ffn_local = norm_rows(resid, norm_gain_ffn).astype(low)
    ffn_rows = gather_tokens(ffn_local)
    cotangents = gather_tokens(cotangent)
    all_routes = gather_tokens(routes)

    def gates_of(rows, route_rows):
        logits = dot(rows, router_weight)
        named = jnp.any(
            route_rows[:, :, None] == jnp.arange(experts, dtype=jnp.int32)[None, None, :], axis=1
        )
        top = jnp.max(jnp.where(named, logits, -jnp.inf), axis=-1, keepdims=True)
        terms = jnp.where(named, jnp.exp(jnp.where(named, logits - top, 0.0)), 0.0)
        return terms / jnp.sum(terms, axis=-1, keepdims=True)

    gates_all = gates_of(ffn_rows, all_routes)
    own_gates = lax.dynamic_slice_in_dim(gates_all, me * local_experts, local_experts, 1)
    mixture = 0.0
    grad_rows = 0.0
    gate_grads, grad_gate_w, grad_up_w, grad_down_w = [], [], [], []
    for expert in range(local_experts):
        gate_col = own_gates[:, expert : expert + 1]
        gate_pre = dot(ffn_rows, gate_weight[expert])
        up_pre = dot(ffn_rows, up_weight[expert])
        share = jax.nn.sigmoid(gate_pre)
        silu = gate_pre * share
        act = silu * up_pre
        gated_act = (act * gate_col).astype(low)
        mixture = mixture + dot(gated_act, down_weight[expert])
        plain = dot_last(cotangents, down_weight[expert])
        gate_grads.append(jnp.sum(act * plain, axis=-1, keepdims=True))
        grad_act = plain * gate_col
        grad_gate_pre = (grad_act * up_pre * (share * (1.0 + gate_pre * (1.0 - share)))).astype(low)
        grad_up_pre = (grad_act * silu).astype(low)
        grad_rows = (
            grad_rows
            + dot_last(grad_gate_pre, gate_weight[expert])
            + dot_last(grad_up_pre, up_weight[expert])
        )
        hidden_units = gated_act.shape[1]
        grad_gate_w.append(dot_first(grad_gate_pre, ffn_rows).astype(low).reshape(groups, -1, model_width))
        grad_up_w.append(dot_first(grad_up_pre, ffn_rows).astype(low).reshape(groups, -1, model_width))
        cut_width = model_width // groups
        grad_down_w.append(
            jnp.stack([
                dot_first(gated_act, cotangents[:, part * cut_width : (part + 1) * cut_width]).astype(low)
                for part in range(groups)
            ])
        )

    gate_grad = jnp.concatenate(gate_grads, axis=1)
    lane_pad = 128 - 2 * experts % 128
    placed = jnp.zeros((full_length, experts), high)
    placed = lax.dynamic_update_slice_in_dim(placed, gate_grad, me * local_experts, 1)
    upper = placed.astype(low)
    lower = (placed - upper.astype(high)).astype(low)
    sent = jnp.concatenate(
        [grad_rows.astype(low), upper, lower, jnp.zeros((full_length, lane_pad), low)], axis=1
    )
    summed_rows = scatter_sum(sent)
    output = (resid + scatter_sum(mixture.astype(low)).astype(high)).astype(low)
    grad_gates = summed_rows[:, model_width : model_width + experts].astype(high) + summed_rows[
        :, model_width + experts : model_width + 2 * experts
    ].astype(high)
    gates = gates_of(ffn_local, routes)
    grad_logits = (
        gates * (grad_gates - jnp.sum(gates * grad_gates, axis=-1, keepdims=True))
    ).astype(low)
    grad_router = dot_first(ffn_local, grad_logits)
    grad_hidden_ffn = summed_rows[:, :model_width].astype(high) + dot_last(grad_logits, router_weight)
    grad_resid_norm, gain_rows_ffn = norm_back(resid, norm_gain_ffn, grad_hidden_ffn)
    grad_resid = cotangent.astype(high) + grad_resid_norm
    grad_attn = gather_tokens(grad_resid.astype(low))
    grad_mixed = dot_last(grad_attn, out_weight).astype(low)
    grad_out = dot_first(mixed, grad_attn)
    grad_query_low, grad_key_part, grad_value_part, query_gain_part = run_attention_backward(
        raw, query_low, key_low, value_low, inverse, mixed, grad_mixed, heads, head_size,
        query_gain_row, cosines, sines, seg_col, seg_row,
    )
    both = jnp.concatenate([grad_key_part, grad_value_part], axis=1)
    step = 1
    while step < sharers:
        swap = [(peer, peer ^ step) for peer in range(peers)]
        both = both + lax.ppermute(both.astype(low), "expert", swap).astype(high)
        step *= 2
    grad_key_rot, grad_value = both[:, :head_size], both[:, head_size:].astype(low)
    place = me % sharers
    half = head_size // 2
    swapped = jnp.concatenate([grad_key_rot[:, half:], grad_key_rot[:, :half]], axis=1)
    key_raw = raw[:, local_width : local_width + head_size]
    grad_key, key_gain_rows = norm_back(key_raw, key_gain, grad_key_rot * cosines - swapped * sines)
    grad_shared = jnp.where(
        place == 0, grad_key.astype(low), jnp.where(place == 1, grad_value, jnp.zeros_like(grad_value))
    )
    own_columns = jnp.concatenate([grad_query_low, grad_shared], axis=1)
    shared_weight = jnp.where(
        place == 0,
        projection[:, local_width : local_width + head_size],
        projection[:, local_width + head_size :],
    )
    own_weight = jnp.concatenate([projection[:, :local_width], shared_weight], axis=1)
    grad_hidden_attn = scatter_sum(dot_last(own_columns, own_weight).astype(low)).astype(high)
    grad_inputs_norm, gain_rows_attn = norm_back(inputs, norm_gain_attn, grad_hidden_attn)
    input_grad = grad_resid + grad_inputs_norm

    grad_query_w, grad_key_w, grad_value_w = projection_gradients(
        dot_first(hidden, own_columns).astype(low), peers, kv_heads, head_size
    )
    grad_out_w = out_gradient(grad_out.astype(low))

    wide = jnp.concatenate(grad_gate_w + grad_up_w, axis=1)
    wide = lax.psum_scatter(wide, "dp", scatter_dimension=0, tiled=True)
    wide = wide.reshape(2, local_experts, hidden_units // groups, model_width).transpose(0, 1, 3, 2)
    wide = wide.astype(high)
    down = jnp.concatenate(grad_down_w, axis=1)
    down = lax.psum_scatter(down, "dp", scatter_dimension=0, tiled=True)
    down = down.reshape(local_experts, hidden_units, cut_width).astype(high)
    expert_sums = (wide[0], wide[1], down)
    key_gain_grad = jnp.where(place == 0, jnp.sum(key_gain_rows, axis=0), 0.0)
    small = jnp.concatenate(
        [
            jnp.sum(gain_rows_attn, axis=0),
            jnp.sum(gain_rows_ffn, axis=0),
            query_gain_part[0],
            key_gain_grad,
            grad_router.reshape(-1),
        ]
    )
    small = lax.psum(small, ("dp", "expert"))
    cut = 2 * model_width
    return (
        output,
        input_grad,
        small[:model_width],
        grad_query_w,
        grad_key_w,
        grad_value_w,
        small[cut : cut + head_size],
        small[cut + head_size : cut + 2 * head_size],
        grad_out_w,
        small[model_width:cut],
        small[cut + 2 * head_size :].reshape(model_width, experts),
        *expert_sums,
    )


def solution(mesh):
    rows = P(("dp", "expert"), None)
    split = P("expert", None)
    cube = P("expert", None, None)
    cut = P("expert", None, "dp")
    return jax.shard_map(
        on_device,
        mesh=mesh,
        in_specs=(
            rows, P("dp", None), rows, rows, P(), split, split, split, P(), P(), split, P(), P(),
            cube, cube, cube,
        ),
        out_specs=(
            rows, rows, P(), split, split, split, P(), P(), split, P(), P(), cut, cut, cut,
        ),
        check_vma=False,
    )
```

```python
import functools

import jax
import jax.numpy as jnp
import numpy as np
from jax import lax
from jax.experimental import pallas as pl
from jax.experimental.pallas import tpu as pltpu
from jax.sharding import PartitionSpec as P

eps_norm = 1e-06
rope_base = 1000000.0
log2e = 1.4426950408889634
low = jnp.bfloat16
high = jnp.float32


def norm_rows(values, gain):
    factor = lax.rsqrt(jnp.mean(values * values, axis=-1, keepdims=True) + eps_norm)
    return values * factor * gain


def norm_back(values, gain, grad):
    factor = lax.rsqrt(jnp.mean(values * values, axis=-1, keepdims=True) + eps_norm)
    scaled = gain * grad
    inner = jnp.mean(values * scaled, axis=-1, keepdims=True)
    grad_values = factor * scaled - values * (factor * factor * factor * inner)
    return grad_values, grad * values * factor


def dot(left, right):
    return jnp.dot(left, right, preferred_element_type=high)


def dot_first(left, right):
    return lax.dot_general(left, right, (((0,), (0,)), ((), ())), preferred_element_type=high)


def dot_last(left, right):
    return lax.dot_general(left, right, (((1,), (1,)), ((), ())), preferred_element_type=high)


def rotary_tables(length, head_size):
    half = head_size // 2
    freqs = rope_base ** (-jnp.arange(half, dtype=high) * 2.0 / head_size)
    angles = jnp.arange(length, dtype=high)[:, None] * freqs[None, :]
    cosines, sines = jnp.cos(angles), jnp.sin(angles)
    return jnp.concatenate([cosines, cosines], 1), jnp.concatenate([-sines, sines], 1)


def rotate(values, cosines, sines):
    return values * cosines + pltpu.roll(values, values.shape[-1] // 2, 1) * sines


def unrotate(values, cosines, sines):
    return values * cosines - pltpu.roll(values, values.shape[-1] // 2, 1) * sines


def key_spans(length):
    block = min(256, length)
    longest = length // 2
    spans = []
    for begin in range(0, length, block):
        first = max(0, begin - longest + 1) // block * block
        spans.append((begin, block, first, begin + block - first))
    return spans


def tile_mask(seg_col, seg_row, begin, rows, first, keys):
    query_at = begin + lax.broadcasted_iota(jnp.int32, (rows, keys), 0)
    key_at = first + lax.broadcasted_iota(jnp.int32, (rows, keys), 1)
    return (query_at >= key_at) & (seg_col[begin : begin + rows, :1] == seg_row[:1, first : first + keys])


def attention_forward(
    query_ref, key_ref, value_ref, query_gain_ref, key_gain_ref, cos_ref, sin_ref, col_ref, row_ref,
    mixed_ref, query_low_ref, key_low_ref, value_low_ref, inverse_ref, value_wide,
):
    head_size = query_ref.shape[1]

    @pl.when(pl.program_id(0) == 0)
    def first_head():
        rotated = rotate(norm_rows(key_ref[...], key_gain_ref[...]), cos_ref[...], sin_ref[...])
        key_low_ref[...] = rotated.astype(low)
        value_low_ref[...] = value_ref[...].astype(low)
        value_wide[:, :head_size] = value_ref[...].astype(low)
        value_wide[:, head_size:] = jnp.ones_like(value_low_ref)

    rotated = rotate(norm_rows(query_ref[...], query_gain_ref[...]), cos_ref[...], sin_ref[...])
    query_low_ref[...] = (rotated * (head_size**-0.5 * log2e)).astype(low)
    for begin, rows, first, keys in key_spans(query_ref.shape[0]):
        scores = dot_last(query_low_ref[pl.ds(begin, rows)], key_low_ref[pl.ds(first, keys)])
        allowed = tile_mask(col_ref, row_ref, begin, rows, first, keys)
        terms = jnp.where(allowed, jnp.exp2(scores), 0.0).astype(low)
        sums = dot(terms, value_wide[pl.ds(first, keys)])
        inverse = 1.0 / sums[:, head_size:]
        mixed_ref[pl.ds(begin, rows)] = (sums[:, :head_size] * inverse).astype(low)
        inverse_ref[pl.ds(begin, rows)] = inverse


def attention_backward(
    query_ref, query_low_ref, key_low_ref, value_low_ref, inverse_ref, mixed_ref, grad_mixed_ref,
    query_gain_ref, cos_ref, sin_ref, col_ref, row_ref,
    grad_query_ref, grad_key_ref, grad_value_ref, grad_gain_ref,
):
    length, head_size = query_ref.shape

    @pl.when(pl.program_id(0) == 0)
    def first_head():
        grad_key_ref[...] = jnp.zeros_like(grad_key_ref)
        grad_value_ref[...] = jnp.zeros_like(grad_value_ref)
        grad_gain_ref[...] = jnp.zeros_like(grad_gain_ref)

    for begin, rows, first, keys in key_spans(length):
        block = pl.ds(begin, rows)
        query_low = query_low_ref[block]
        key_low = key_low_ref[pl.ds(first, keys)]
        scaled = grad_mixed_ref[block].astype(high) * inverse_ref[block]
        row_term = jnp.sum(scaled * mixed_ref[block].astype(high), axis=-1, keepdims=True)
        scaled = scaled.astype(low)
        scores = dot_last(query_low, key_low)
        allowed = tile_mask(col_ref, row_ref, begin, rows, first, keys)
        terms = jnp.where(allowed, jnp.exp2(scores), 0.0)
        grad_probs = dot_last(scaled, value_low_ref[pl.ds(first, keys)])
        grad_scores = (terms * (grad_probs - row_term)).astype(low)
        grad_value_ref[pl.ds(first, keys)] += dot_first(terms.astype(low), scaled)
        grad_key_ref[pl.ds(first, keys)] += dot_first(grad_scores, query_low) * (1.0 / log2e)
        grad_rotated = dot(grad_scores, key_low) * head_size**-0.5
        grad_normed = unrotate(grad_rotated, cos_ref[block], sin_ref[block])
        grad_raw, gain_rows = norm_back(query_ref[block], query_gain_ref[...], grad_normed)
        grad_query_ref[block] = grad_raw.astype(low)
        grad_gain_ref[...] += jnp.broadcast_to(
            jnp.sum(gain_rows, axis=0, keepdims=True), grad_gain_ref.shape
        )


def whole(shape):
    return pl.BlockSpec(shape, lambda head: (0,) * len(shape))


def run_attention_forward(raw, heads, head_size, query_gain, key_gain, cosines, sines, seg_col, seg_row):
    length = raw.shape[0]
    per_head = pl.BlockSpec((length, head_size), lambda head: (0, head))
    one = (length, head_size)
    wide = jax.ShapeDtypeStruct((length, heads * head_size), low)
    narrow = jax.ShapeDtypeStruct(one, low)
    return pl.pallas_call(
        attention_forward,
        grid=(heads,),
        in_specs=[
            per_head,
            pl.BlockSpec(one, lambda head: (0, heads)),
            pl.BlockSpec(one, lambda head: (0, heads + 1)),
            whole((1, head_size)),
            whole((1, head_size)),
            whole(one),
            whole(one),
            whole(one),
            whole((8, length)),
        ],
        out_specs=[per_head, per_head, whole(one), whole(one), per_head],
        out_shape=[wide, wide, narrow, narrow, jax.ShapeDtypeStruct((length, heads * head_size), high)],
        scratch_shapes=[pltpu.VMEM((length, 2 * head_size), low)],
        compiler_params=pltpu.CompilerParams(vmem_limit_bytes=50 << 20),
        cost_estimate=pl.CostEstimate(
            flops=3 * heads * length * length * head_size, bytes_accessed=8 * length * heads * head_size,
            transcendentals=heads * length * length // 2,
        ),
    )(raw, raw, raw, query_gain, key_gain, cosines, sines, seg_col, seg_row)


def run_attention_backward(
    raw, query_low, key_low, value_low, inverse, mixed, grad_mixed, heads, head_size, query_gain,
    cosines, sines, seg_col, seg_row,
):
    length = raw.shape[0]
    per_head = pl.BlockSpec((length, head_size), lambda head: (0, head))
    one = (length, head_size)
    return pl.pallas_call(
        attention_backward,
        grid=(heads,),
        in_specs=[
            per_head, per_head, whole(one), whole(one), per_head, per_head, per_head,
            whole((1, head_size)), whole(one), whole(one), whole(one), whole((8, length)),
        ],
        out_specs=[per_head, whole(one), whole(one), whole((8, head_size))],
        out_shape=[
            jax.ShapeDtypeStruct((length, heads * head_size), low),
            jax.ShapeDtypeStruct(one, high),
            jax.ShapeDtypeStruct(one, high),
            jax.ShapeDtypeStruct((8, head_size), high),
        ],
        compiler_params=pltpu.CompilerParams(vmem_limit_bytes=50 << 20),
        cost_estimate=pl.CostEstimate(
            flops=6 * heads * length * length * head_size, bytes_accessed=16 * length * heads * head_size,
            transcendentals=heads * length * length // 2,
        ),
    )(
        raw, query_low, key_low, value_low, inverse, mixed, grad_mixed, query_gain, cosines, sines,
        seg_col, seg_row,
    )


MESH = pl.DeviceIdType.MESH
VMEM = pl.BlockSpec(memory_space=pltpu.VMEM)
ANY = pl.BlockSpec(memory_space=pl.ANY)


def wait_all(copies):
    for copy in copies:
        copy.wait()


class Chain:
    def __init__(self):
        self.n = lax.axis_size("expert") // 2
        me = lax.axis_index("expert")
        self.z, self.c = me // 2, me % 2
        self.sibling, self.up, self.down = me + 1 - 2 * self.c, me + 2, me - 2
        self.has_up, self.has_down = self.z < self.n - 1, self.z > 0

    def greet(self, others=()):
        barrier = pltpu.get_barrier_semaphore()

        def signal(peer):
            pl.semaphore_signal(barrier, inc=1, device_id={"expert": peer}, device_id_type=MESH)

        signal(self.sibling)
        pl.when(self.has_up)(lambda: signal(self.up))
        pl.when(self.has_down)(lambda: signal(self.down))
        for device in others:
            pl.semaphore_signal(barrier, inc=1, device_id=device, device_id_type=MESH)
        peers = 1 + len(others) + self.has_up.astype(jnp.int32) + self.has_down.astype(jnp.int32)
        pl.semaphore_wait(barrier, peers)

    def nearest(self, step):
        turn = jnp.int32(0)
        for z in range(self.n):
            order = sorted(range(self.n), key=lambda other: (abs(other - z), other))
            for at, chip in enumerate(order):
                turn = jnp.where((self.z == z) & (step == at), chip, turn)
        return turn


class Gather:
    def __init__(self, chain, own, block, send, recv, local):
        self.chain, self.own, self.block = chain, own, block
        self.send, self.recv, self.local = send, recv, local

    @staticmethod
    def semaphores(n):
        return [
            pltpu.SemaphoreType.DMA((3, n)),
            pltpu.SemaphoreType.DMA((2 * n,)),
            pltpu.SemaphoreType.DMA(()),
        ]

    def copy(self, source, z, way, peer):
        c = self.chain.c
        return pltpu.make_async_remote_copy(
            src_ref=source,
            dst_ref=self.block(z, c),
            send_sem=self.send.at[way, z],
            recv_sem=self.recv.at[2 * z + c],
            device_id={"expert": peer},
            device_id_type=MESH,
        )

    def wait_block(self, z, c):
        block = self.block(z, c)
        pltpu.make_async_remote_copy(
            src_ref=block,
            dst_ref=block,
            send_sem=self.send.at[0, z],
            recv_sem=self.recv.at[2 * z + c],
            device_id={"expert": self.chain.sibling},
            device_id_type=MESH,
        ).wait_recv()

    def keep(self):
        return pltpu.make_async_copy(self.own, self.block(self.chain.z, self.chain.c), self.local)

    def begin(self):
        ch = self.chain
        pl.when(ch.has_up)(lambda: self.copy(self.own, ch.z, 0, ch.up).start())
        pl.when(ch.has_down)(lambda: self.copy(self.own, ch.z, 1, ch.down).start())
        self.copy(self.own, ch.z, 2, ch.sibling).start()
        self.keep().start()

    def service(self, step):
        ch = self.chain

        def from_below():
            z = ch.z - step
            self.wait_block(z, ch.c)
            pl.when(ch.has_up)(lambda: self.copy(self.block(z, ch.c), z, 0, ch.up).start())
            self.copy(self.block(z, ch.c), z, 2, ch.sibling).start()

        def from_above():
            z = ch.z + step
            self.wait_block(z, ch.c)
            pl.when(ch.has_down)(lambda: self.copy(self.block(z, ch.c), z, 1, ch.down).start())
            self.copy(self.block(z, ch.c), z, 2, ch.sibling).start()

        pl.when(ch.z - step >= 0)(from_below)
        pl.when(ch.z + step < ch.n)(from_above)

    def wait_sibling(self, z):
        self.wait_block(z, 1 - self.chain.c)

    def finish(self):
        ch = self.chain
        for z in range(ch.n):
            at = jnp.int32(z)
            block = self.block(at, ch.c)
            pl.when(ch.has_up & (ch.z >= z))(lambda: self.copy(block, at, 0, ch.up).wait_send())
            pl.when(ch.has_down & (ch.z <= z))(lambda: self.copy(block, at, 1, ch.down).wait_send())
            self.copy(block, at, 2, ch.sibling).wait_send()


class NearGather(Gather):
    def __init__(self, chain, own, near, block, send, recv, local):
        super().__init__(chain, own, block, send, recv, local)
        self.near = near

    @staticmethod
    def semaphores(n):
        return Gather.semaphores(n)[:2] + [pltpu.SemaphoreType.DMA((4,))]

    def place(self, at):
        ch = self.chain
        source = self.own if at == 3 else self.near.at[at]
        z, c = ((ch.z - 1, ch.c), (ch.z + 1, ch.c), (ch.z, 1 - ch.c), (ch.z, ch.c))[at]
        return pltpu.make_async_copy(source, self.block(z, c), self.local.at[at])

    def begin(self):
        ch = self.chain

        def below():
            pl.when(ch.has_up)(lambda: self.copy(self.near.at[0], ch.z - 1, 0, ch.up).start())
            self.copy(self.near.at[0], ch.z - 1, 2, ch.sibling).start()
            self.place(0).start()

        def above():
            pl.when(ch.has_down)(lambda: self.copy(self.near.at[1], ch.z + 1, 1, ch.down).start())
            self.copy(self.near.at[1], ch.z + 1, 2, ch.sibling).start()
            self.place(1).start()

        pl.when(ch.has_down)(below)
        pl.when(ch.has_up)(above)
        self.place(2).start()
        self.place(3).start()

    def wait_placed(self):
        pl.when(self.chain.has_down)(lambda: self.place(0).wait())
        pl.when(self.chain.has_up)(lambda: self.place(1).wait())
        self.place(2).wait()
        self.place(3).wait()

    def finish(self):
        ch = self.chain
        for z in range(ch.n):
            at = jnp.int32(z)
            block = self.block(at, ch.c)
            pl.when(ch.has_up & (ch.z > z))(lambda: self.copy(block, at, 0, ch.up).wait_send())
            pl.when(ch.has_down & (ch.z < z))(lambda: self.copy(block, at, 1, ch.down).wait_send())
            pl.when(ch.z != z)(lambda: self.copy(block, at, 2, ch.sibling).wait_send())


class Scatter:
    def __init__(self, chain, half, pair, flow, pair_send, pair_recv, flow_send, flow_recv):
        self.chain, self.half, self.pair, self.flow = chain, half, pair, flow
        self.pair_send, self.pair_recv = pair_send, pair_recv
        self.flow_send, self.flow_recv = flow_send, flow_recv

    @staticmethod
    def buffers(n, rows, width):
        return [
            pltpu.VMEM((n, rows, width), low),
            pltpu.VMEM((n + 1, rows, width), low),
            pltpu.SemaphoreType.DMA((n,)),
            pltpu.SemaphoreType.DMA((n,)),
            pltpu.SemaphoreType.DMA((n,)),
            pltpu.SemaphoreType.DMA((n + 1,)),
        ]

    def pair_copy(self, z):
        ch = self.chain
        return pltpu.make_async_remote_copy(
            src_ref=self.half(z, 1 - ch.c),
            dst_ref=self.pair.at[z],
            send_sem=self.pair_send.at[z],
            recv_sem=self.pair_recv.at[z],
            device_id={"expert": ch.sibling},
            device_id_type=MESH,
        )

    def flow_copy(self, z, slot, peer):
        return pltpu.make_async_remote_copy(
            src_ref=self.pair.at[z],
            dst_ref=self.flow.at[slot],
            send_sem=self.flow_send.at[z],
            recv_sem=self.flow_recv.at[slot],
            device_id={"expert": peer},
            device_id_type=MESH,
        )

    def wait_flow(self, slot):
        block = self.flow.at[slot]
        pltpu.make_async_remote_copy(
            src_ref=block,
            dst_ref=block,
            send_sem=self.flow_send.at[0],
            recv_sem=self.flow_recv.at[slot],
            device_id={"expert": self.chain.sibling},
            device_id_type=MESH,
        ).wait_recv()

    def start_pair(self, z):
        self.pair_copy(z).start()

    def add_pair(self, z, relayed):
        self.pair_copy(z).wait_recv()
        half = self.half(z, self.chain.c)

        def alone():
            self.pair[z] = (half[...].astype(high) + self.pair[z].astype(high)).astype(low)

        def with_flow():
            self.wait_flow(z)
            total = half[...].astype(high) + self.pair[z].astype(high) + self.flow[z].astype(high)
            self.pair[z] = total.astype(low)

        pl.when(relayed)(with_flow)
        pl.when(jnp.logical_not(relayed))(alone)

    def step(self, distance):
        ch = self.chain

        def upward():
            z = ch.z + distance
            self.add_pair(z, ch.has_down)
            self.flow_copy(z, z, ch.up).start()

        def downward():
            z = ch.z - distance
            self.add_pair(z, ch.has_up)
            self.flow_copy(z, jnp.where(distance == 1, ch.n, z), ch.down).start()

        pl.when(ch.z + distance < ch.n)(upward)
        pl.when(ch.z - distance >= 0)(downward)

    def total(self, result):
        ch = self.chain
        self.pair_copy(ch.z).wait_recv()
        result[...] = self.half(ch.z, ch.c)[...].astype(high) + self.pair[ch.z].astype(high)

        def add(slot):
            self.wait_flow(slot)
            result[...] += self.flow[slot].astype(high)

        pl.when(ch.has_down)(lambda: add(ch.z))
        pl.when(ch.has_up)(lambda: add(ch.n))

    def finish(self):
        ch = self.chain
        for z in range(ch.n):
            at = jnp.int32(z)
            self.pair_copy(at).wait_send()
            pl.when(ch.z != z)(lambda: self.flow_copy(at, at, ch.sibling).wait_send())


class Ports:
    def __init__(self, send, recv):
        self.send, self.recv, self.used, self.started = send, recv, 0, []

    def copy(self, source, target, device):
        at = self.used
        self.used += 1
        copy = pltpu.make_async_remote_copy(
            src_ref=source,
            dst_ref=target,
            send_sem=self.send.at[at],
            recv_sem=self.recv.at[at],
            device_id=device,
            device_id_type=MESH,
        )
        self.started.append(copy)
        return copy

    def finish(self):
        for copy in self.started:
            copy.wait_send()


def square():
    group = lax.axis_index("dp")
    y, x = group // 2, group % 2
    from_x, from_y = 2 * y + 1 - x, 2 * (1 - y) + x
    return group, y, x, from_x, from_y


class SquareSum:
    def __init__(self, source, result, first_a, first_b, second_a, second_b, send_a, send_b, ports):
        self.source, self.result = source, result
        self.own, self.y, self.x, self.from_x, self.from_y = square()
        self.first_a, self.first_b, self.second_a, self.second_b = first_a, first_b, second_a, second_b
        self.send_a, self.send_b = send_a, send_b
        self.rows, self.middle = source.shape[0] // 4, source.shape[1] // 2
        beside, across = {"dp": self.from_x}, {"dp": self.from_y}
        self.first = []
        for k in range(2):
            self.first.append(ports.copy(self.part(source, 0, 2 * k + 1 - self.x), first_a.at[k], beside))
            self.first.append(ports.copy(self.part(source, 1, 2 * (1 - self.y) + k), first_b.at[k], across))
        self.second = [ports.copy(send_a, second_a, across), ports.copy(send_b, second_b, beside)]

    @staticmethod
    def buffers(rows, columns):
        quarter = (rows // 4, columns // 2)
        return [pltpu.VMEM((2, *quarter), low)] * 2 + [pltpu.VMEM(quarter, low)] * 4

    def part(self, ref, side, quarter):
        rows = pl.ds(pl.multiple_of(quarter * self.rows, self.rows), self.rows)
        return ref.at[rows, pl.ds(side * self.middle, self.middle)]

    @staticmethod
    def start(copies):
        for copy in copies:
            copy.start()

    @staticmethod
    def arrive(copies):
        for copy in copies:
            copy.wait_recv()

    def begin(self):
        self.start(self.first)

    def exchange(self):
        self.arrive(self.first)
        along_y = self.part(self.source, 0, self.from_y)[...].astype(high)
        self.send_a[...] = (along_y + self.first_a[1 - self.y].astype(high)).astype(low)
        along_x = self.part(self.source, 1, self.from_x)[...].astype(high)
        self.send_b[...] = (along_x + self.first_b[1 - self.x].astype(high)).astype(low)
        self.start(self.second)

    def settle(self):
        self.arrive(self.second)
        for side, first, second in (
            (0, self.first_a[self.y], self.second_a), (1, self.first_b[self.x], self.second_b)
        ):
            total = self.part(self.source, side, self.own)[...].astype(high) + first.astype(high)
            columns = pl.ds(side * self.middle, self.middle)
            self.result[:, columns] = (total + second[...].astype(high)).astype(low)


class SquareCopy:
    def __init__(self, mine, result, ports):
        own, _, _, from_x, from_y = square()
        rows, middle = mine.shape[0], mine.shape[1] // 2
        beside, across = {"dp": from_x}, {"dp": from_y}

        def quarter(at):
            return pl.ds(pl.multiple_of(at * rows, rows), rows)

        target = result.at[quarter(own)]
        self.mine, self.target = mine, target
        self.near = [ports.copy(mine, target, beside), ports.copy(mine, target, across)]
        left = result.at[quarter(from_x), pl.ds(0, middle)]
        right = result.at[quarter(from_y), pl.ds(middle, middle)]
        self.far = [ports.copy(left, left, across), ports.copy(right, right, beside)]

    def begin(self):
        SquareSum.start(self.near)
        self.target[...] = self.mine[...]

    def hand_on(self):
        SquareSum.arrive(self.near)
        SquareSum.start(self.far)

    def finish(self):
        SquareSum.arrive(self.far)


def row_block(ref, rows):
    return lambda z, c: ref.at[pl.ds(pl.multiple_of((2 * z + c) * rows, rows), rows)]


def chip_block(ref, rows):
    return lambda z, c: ref.at[z, pl.ds(pl.multiple_of(c * rows, rows), rows)]


def communicating(collective_id):
    return pltpu.CompilerParams(
        collective_id=collective_id, has_side_effects=True, vmem_limit_bytes=60 << 20
    )


def gather_kernel(
    tokens_ref, gain_ref, named_ref, cot_ref, query_hbm, key_hbm, value_hbm,
    hidden_hbm, all_named_ref, near_ref, projection_hbm, raw_hbm,
    own, stage, hidden_ref, projection_ref, raw_ref, query_ref, key_ref, value_ref,
    send_a, recv_a, local_a, send_b, recv_b, local_b, name_send, name_recv,
    swap_send, swap_recv, x_send, x_recv, y_send, y_recv, far_send, far_recv, out_sems, load_sems,
    near_send, near_recv,
):
    chain = Chain()
    n = chain.n
    peers = 2 * n
    me = lax.axis_index("expert")
    group, _, _, from_x, from_y = square()
    far = 3 - group
    beside, across = {"dp": from_x}, {"dp": from_y}
    sources = [(2 * chain.nearest(step) + core, core, step) for step in range(n) for core in range(2)]
    others = [chain.sibling] + [source for source, _, step in sources if step > 0]
    barrier = pltpu.get_barrier_semaphore()
    for device in [{"expert": peer} for peer in others] + [beside, across]:
        pl.semaphore_signal(barrier, inc=1, device_id=device, device_id_type=MESH)
    rows = stage.shape[1]
    quarter = pl.ds(pl.multiple_of(group * rows, rows), rows)
    loads = [
        pltpu.make_async_copy(source.at[quarter], target, load_sems.at[at])
        for at, (source, target) in enumerate(
            ((query_hbm, query_ref), (key_hbm, key_ref), (value_hbm, value_ref))
        )
    ]
    for load in loads:
        load.start()
    query_width = query_ref.shape[1] // peers
    head_size = key_ref.shape[1] // n
    own[...] = norm_rows(tokens_ref[...].astype(high), gain_ref[...]).astype(low)
    for load in loads:
        load.wait()
    for peer in range(peers):
        shared = pl.ds(peer // 2 * head_size, head_size)
        stage[peer, :, :query_width] = query_ref[:, pl.ds(peer * query_width, query_width)]
        stage[peer, :, query_width : query_width + head_size] = key_ref[:, shared]
        stage[peer, :, query_width + head_size :] = value_ref[:, shared]
    pl.semaphore_wait(barrier, peers + 1)

    def remote(source, target, send, recv, device):
        return pltpu.make_async_remote_copy(
            src_ref=source, dst_ref=target, send_sem=send, recv_sem=recv, device_id=device, device_id_type=MESH
        )

    def block(source, place):
        return projection_ref.at[source, place]

    swaps = [
        remote(stage.at[peer], block(me, group), swap_send.at[at], swap_recv.at[me], {"expert": peer})
        for at, peer in enumerate(others)
    ]
    for copy in swaps:
        copy.start()
    length = own.shape[0]
    piece = length // 2

    def half_block(half):
        def block_of(z, c):
            return hidden_ref.at[pl.ds(pl.multiple_of((2 * z + c) * length + half * piece, piece), piece)]

        return block_of

    wide = [
        Gather(chain, own.at[pl.ds(half * piece, piece)], half_block(half), *sems)
        for half, sems in enumerate(((send_a, recv_a, local_a), (send_b, recv_b, local_b)))
    ]
    for gather in wide:
        gather.begin()
    names = [
        remote(named_ref, all_named_ref.at[me], name_send.at[at], name_recv.at[me], {"expert": peer})
        for at, peer in enumerate(others)
    ]
    for copy in names:
        copy.start()
    all_named_ref[me] = named_ref[...]
    projection_ref[me, group] = stage[me]

    def to_x(at, source, place):
        part = block(source, place)
        return remote(part, part, x_send.at[at], x_recv.at[source], beside)

    def to_y(at, source, place):
        part = block(source, place)
        return remote(part, part, y_send.at[at], y_recv.at[source], across)

    def to_far(at, core, source, place):
        part = block(source, place)
        return remote(part, part, far_send.at[at], far_recv.at[source], across if core == 0 else beside)

    def wait_swap(source):
        part = block(source, group)
        remote(part, part, swap_send.at[0], swap_recv.at[source], {"expert": chain.sibling}).wait_recv()

    for at, (source, core, step) in enumerate(sources):
        if step == 0:
            pl.when(chain.c != core)(lambda: wait_swap(source))
        else:
            wait_swap(source)
        to_x(at, source, group).start()
        to_y(at, source, group).start()
    for gather in wide:
        gather.service(1)
    for at, (source, core, _) in enumerate(sources):
        to_x(at, source, from_x).wait_recv()
        to_y(at, source, from_y).wait_recv()
        to_far(at, core, source, from_x if core == 0 else from_y).start()
    for step in range(2, n):
        for gather in wide:
            gather.service(step)

    def near(slot, peer):
        return remote(cot_ref, near_ref.at[slot], near_send.at[slot], near_recv.at[slot], {"expert": peer})

    pl.when(chain.has_up)(lambda: near(0, chain.up).start())
    pl.when(chain.has_down)(lambda: near(1, chain.down).start())
    near(2, chain.sibling).start()
    for gather in wide:
        for z in range(n):
            gather.wait_sibling(jnp.int32(z))
        gather.keep().wait()
    hidden_out = pltpu.make_async_copy(hidden_ref, hidden_hbm, out_sems.at[0])
    hidden_out.start()
    for at, (source, core, _) in enumerate(sources):
        to_far(at, core, source, far).wait_recv()
    projection_out = pltpu.make_async_copy(projection_ref, projection_hbm, out_sems.at[1])
    projection_out.start()
    pair_rows = 2 * own.shape[0]
    shard_rows = 4 * rows

    def raw_out(step):
        tokens = pl.ds(pl.multiple_of(step * pair_rows, pair_rows), pair_rows)
        return pltpu.make_async_copy(raw_ref.at[tokens], raw_hbm.at[tokens], out_sems.at[2 + step])

    @pl.loop(0, n)
    def each(step):
        tokens = pl.ds(pl.multiple_of(step * pair_rows, pair_rows), pair_rows)
        total = jnp.zeros((pair_rows, raw_ref.shape[1]), high)
        for source in range(peers):
            weight = projection_ref[source].reshape(shard_rows, raw_ref.shape[1])
            total = total + dot(hidden_ref[tokens, source * shard_rows : (source + 1) * shard_rows], weight)
        raw_ref[tokens] = total
        raw_out(step).start()

    for gather in wide:
        gather.finish()
    for at, peer in enumerate(others):
        part = all_named_ref.at[peer]
        remote(part, part, name_send.at[at], name_recv.at[peer], {"expert": peer}).wait_recv()
        names[at].wait_send()
    for at, (source, core, _) in enumerate(sources):
        to_x(at, source, group).wait_send()
        to_y(at, source, group).wait_send()
        to_far(at, core, source, from_x if core == 0 else from_y).wait_send()
    for copy in swaps:
        copy.wait_send()
    pl.when(chain.has_up)(lambda: near(0, chain.up).wait_send())
    pl.when(chain.has_down)(lambda: near(1, chain.down).wait_send())
    near(2, chain.sibling).wait_send()
    pl.when(chain.has_down)(lambda: near(0, chain.sibling).wait_recv())
    pl.when(chain.has_up)(lambda: near(1, chain.sibling).wait_recv())
    near(2, chain.sibling).wait_recv()
    hidden_out.wait()
    projection_out.wait()
    for step in range(n):
        raw_out(step).wait()


def run_gather(tokens, gain, named, cotangent, query_weight, key_matrix, value_matrix, peers, groups):
    length, width = tokens.shape
    n = peers // 2
    shard_rows, query_columns = query_weight.shape
    columns = query_columns // peers + 2 * key_matrix.shape[1] // n
    rows = shard_rows // groups
    dma = pltpu.SemaphoreType.DMA
    hidden, all_named, near, projection, raw = pl.pallas_call(
        gather_kernel,
        out_shape=[
            jax.ShapeDtypeStruct((length * peers, width), low),
            jax.ShapeDtypeStruct((peers, *named.shape), named.dtype),
            jax.ShapeDtypeStruct((3, length, width), low),
            jax.ShapeDtypeStruct((peers, groups, rows, columns), low),
            jax.ShapeDtypeStruct((length * peers, columns), high),
        ],
        in_specs=[VMEM] * 4 + [ANY] * 3,
        out_specs=[ANY, VMEM, VMEM, ANY, ANY],
        scratch_shapes=[
            pltpu.VMEM((length, width), low),
            pltpu.VMEM((peers, rows, columns), low),
            pltpu.VMEM((length * peers, width), low),
            pltpu.VMEM((peers, groups, rows, columns), low),
            pltpu.VMEM((length * peers, columns), high),
            pltpu.VMEM((rows, query_columns), low),
            pltpu.VMEM((rows, key_matrix.shape[1]), low),
            pltpu.VMEM((rows, key_matrix.shape[1]), low),
            *Gather.semaphores(n),
            *Gather.semaphores(n),
            dma((peers - 1,)), dma((peers,)),
            dma((peers - 1,)), dma((peers,)),
            dma((peers,)), dma((peers,)), dma((peers,)), dma((peers,)), dma((peers,)), dma((peers,)),
            dma((2 + n,)),
            dma((3,)), dma((3,)), dma((3,)),
        ],
        compiler_params=communicating(1),
        cost_estimate=pl.CostEstimate(flops=0, bytes_accessed=64 << 20, transcendentals=0),
        name="gather_hidden",
    )(tokens, gain, named, cotangent, query_weight, key_matrix, value_matrix)
    return hidden, all_named, near, projection.reshape(width, columns), raw


def attention_heads(
    raw_ref, query_gain_ref, key_gain_ref, cos_ref, sin_ref, col_ref, row_ref,
    mixed_ref, query_low_ref, key_low_ref, value_low_ref, inverse_ref, value_wide,
):
    head_size = cos_ref.shape[1]
    heads = mixed_ref.shape[1] // head_size
    key_raw = raw_ref[:, heads * head_size : (heads + 1) * head_size]
    key_low_ref[...] = rotate(norm_rows(key_raw, key_gain_ref[...]), cos_ref[...], sin_ref[...]).astype(low)
    value_low_ref[...] = raw_ref[:, (heads + 1) * head_size :].astype(low)
    value_wide[:, :head_size] = value_low_ref[...]
    value_wide[:, head_size:] = jnp.ones_like(value_low_ref)

    @pl.loop(0, heads)
    def each(head):
        columns = pl.ds(pl.multiple_of(head * head_size, head_size), head_size)
        rotated = rotate(norm_rows(raw_ref[:, columns], query_gain_ref[...]), cos_ref[...], sin_ref[...])
        query_low_ref[:, columns] = (rotated * (head_size**-0.5 * log2e)).astype(low)
        for begin, rows, first, keys in key_spans(raw_ref.shape[0]):
            block = pl.ds(begin, rows)
            scores = dot_last(query_low_ref[block, columns], key_low_ref[pl.ds(first, keys)])
            allowed = tile_mask(col_ref, row_ref, begin, rows, first, keys)
            terms = jnp.where(allowed, jnp.exp2(scores), 0.0).astype(low)
            sums = dot(terms, value_wide[pl.ds(first, keys)])
            inverse = 1.0 / sums[:, head_size:]
            mixed_ref[block, columns] = (sums[:, :head_size] * inverse).astype(low)
            inverse_ref[block, columns] = inverse


class Split:
    both = slice(None)

    @staticmethod
    def take(ref, z, half, columns=slice(None)):
        block = ref[pl.ds(2 * z, 2), half, :, columns]
        return block.reshape(-1, block.shape[-1])

    @staticmethod
    def put(ref, z, half, value, columns=slice(None)):
        halves = (2, 2) if half is Split.both else (2,)
        ref[pl.ds(2 * z, 2), half, :, columns] = value.reshape(*halves, ref.shape[2], value.shape[1])

    @staticmethod
    def every(ref, columns=slice(None)):
        block = ref[:, :, :, columns]
        return block.reshape(block.shape[0] * block.shape[1] * block.shape[2], block.shape[3])


def expert_block(rows_all, plain_of, gate_w, up_w, gate_col, gated, grad_gate, grad_up, z, half):
    hidden = gate_w.shape[1]
    chunk = hidden // 3 if hidden % 384 == 0 else hidden
    gate_grad = jnp.zeros_like(gate_col)
    for begin in range(0, hidden, chunk):
        units = pl.ds(begin, chunk)
        gate_pre = dot(Split.take(rows_all, z, half), gate_w[:, units])
        up_pre = dot(Split.take(rows_all, z, half), up_w[:, units])
        plain = plain_of(units)
        share = 1.0 / (1.0 + jnp.exp(-gate_pre))
        silu = gate_pre * share
        act = silu * up_pre
        gate_grad = gate_grad + jnp.sum(act * plain, axis=-1, keepdims=True)
        Split.put(gated, z, half, (act * gate_col).astype(low), units)
        grad_act = plain * gate_col
        slope = share + silu * (1.0 - share)
        Split.put(grad_gate, z, half, (grad_act * up_pre * slope).astype(low), units)
        Split.put(grad_up, z, half, (grad_act * silu).astype(low), units)
    return gate_grad


def gate_columns(lanes, expert, gate_grad):
    sent = jnp.where(lanes == expert, gate_grad, 0.0)
    upper = sent.astype(low).astype(high)
    lower = (sent - upper).astype(low).astype(high)
    return upper + pltpu.roll(lower, 64, 1)


class Tiles:
    def __init__(self, grads, stage, sems, gated, grad_gate, grad_up, rows_all, cots):
        self.grads, self.stage, self.sems = grads, stage, sems
        self.sources = ((grad_gate, rows_all), (grad_up, rows_all), (gated, cots))
        self.groups = sems.shape[1]
        self.hidden = gated.shape[3]
        self.piece = self.hidden // self.groups
        self.tile = stage.shape[2]

    def copies(self, kind, at, slot):
        piece = self.piece
        made = []
        for part in range(self.groups):
            if kind < 2:
                target = self.grads.at[part, pl.ds(pl.multiple_of((2 * at + kind) * piece, 16), piece)]
            else:
                begin = 2 * self.hidden + part * piece
                target = self.grads.at[at, pl.ds(begin, piece)]
            source = self.stage.at[slot, pl.ds(part * piece, piece)]
            made.append(pltpu.make_async_copy(source, target, self.sems.at[slot, part]))
        return made

    def run(self, kind):
        left, right = self.sources[kind]

        @pl.loop(0, self.groups)
        def each(at):
            slot = at % 2
            if kind == 0:
                pl.when(at >= 2)(lambda: wait_all(self.copies(kind, at, slot)))
            else:
                wait_all(self.copies(kind, at, slot))
            span = pl.ds(pl.multiple_of(at * self.tile, self.tile), self.tile)
            self.stage[slot] = dot_first(Split.every(left), Split.every(right, span)).astype(low)
            for copy in self.copies(kind, at, slot):
                copy.start()

    def finish(self):
        for slot in range(2):
            wait_all(self.copies(0, jnp.int32(slot), slot))


def first_kernel(
    query_gain_ref, key_gain_ref, row_ref, tokens_ref, gain_ref, named_ref, router_in, cot_ref, near_ref,
    raw_hbm, cos_hbm, sin_hbm, col_hbm, weight_hbm, gate_hbm, up_hbm, down_hbm,
    key_low_ref, value_low_ref, resid_ref, ffn_ref, gates_ref, own_gates_ref,
    mixed_hbm, query_low_hbm, inverse_hbm, rows_hbm, cots_hbm, gated_hbm, parts_hbm, grads_hbm,
    raw_ref, cos_ref, sin_ref, col_ref, weight_ref, mixed_ref, query_low_ref, inverse_ref, value_wide, router_ref, plain, attn_parts, rows_all, cots, gate_w, up_w, down_w, gated, grad_gate, grad_up,
    part_stage, tile_stage, load_sems, rows_sems, part_sems, tile_sems, cot_send, cot_recv, cot_local, *transfers,
):
    chain = Chain()
    n = chain.n
    _, _, rows, width = rows_all.shape
    block_rows = 2 * rows
    loads = [
        pltpu.make_async_copy(source, target, load_sems.at[at])
        for at, (source, target) in enumerate(
            (
                (raw_hbm, raw_ref), (cos_hbm, cos_ref), (sin_hbm, sin_ref), (col_hbm, col_ref),
                (weight_hbm, weight_ref), (down_hbm.at[0], down_w), (gate_hbm.at[0], gate_w),
                (up_hbm.at[0], up_w),
            )
        )
    ]
    for load in loads:
        load.start()
    chain.greet()
    cot_gather = NearGather(
        chain, cot_ref, near_ref, lambda z, c: cots.at[2 * z + c], cot_send, cot_recv, cot_local
    )
    cot_gather.begin()
    wait_all(loads[:4])
    router_ref[...] = jnp.zeros_like(router_ref)
    router_ref[: router_in.shape[0]] = router_in[...]
    attention_heads(
        raw_ref, query_gain_ref, key_gain_ref, cos_ref, sin_ref, col_ref, row_ref,
        mixed_ref, query_low_ref, key_low_ref, value_low_ref, inverse_ref, value_wide,
    )
    attention_copies = [
        pltpu.make_async_copy(source, target, rows_sems.at[2 + at])
        for at, (source, target) in enumerate(
            ((mixed_ref, mixed_hbm), (query_low_ref, query_low_hbm), (inverse_ref, inverse_hbm))
        )
    ]
    for copy in attention_copies:
        copy.start()
    loads[4].wait()
    scatters, gathers = [], []
    for half in range(2):
        pair, flow, *rest = transfers[9 * half : 9 * half + 9]
        scatters.append(
            Scatter(chain, lambda z, c, half=half: attn_parts.at[z, c, half], pair, flow, *rest[:4])
        )
        gathers.append(
            Gather(chain, ffn_ref.at[half], lambda z, c, half=half: rows_all.at[2 * z + c, half], *rest[4:])
        )

    def plain_rows(step):
        z = chain.nearest(step)
        pl.when(step == 0)(cot_gather.wait_placed)
        pl.when(step > 0)(lambda: cot_gather.wait_sibling(z))
        cot_rows = cots[pl.ds(2 * z, 2)].reshape(4 * rows, width)
        hidden = plain.shape[3]
        plain[pl.ds(2 * z, 2)] = dot_last(cot_rows, down_w[...]).reshape(2, 2, rows, hidden)

    @pl.loop(0, n)
    def project(step):
        z = chain.nearest(n - 1 - step)
        tokens = pl.ds(pl.multiple_of(z * 4 * rows, 4 * rows), 4 * rows)
        attn_parts[z] = dot(mixed_ref[tokens], weight_ref[...]).astype(low).reshape(2, 2, rows, width)
        for scatter in scatters:
            scatter.start_pair(z)
        pl.when(step < n - 1)(lambda: scatters[0].step(n - 1 - step))
        pl.when(step == 0)(lambda: loads[5].wait())
        pl.when(step == 1)(lambda: cot_gather.service(2))
        pl.when(step < n - 1)(lambda: plain_rows(step))

    def own_rows(half):
        span = pl.ds(half * rows, rows)
        scatters[half].total(resid_ref.at[span])
        resid_ref[span] += tokens_ref[span].astype(high)
        ffn_ref[half] = norm_rows(resid_ref[span], gain_ref[...]).astype(low)
        gathers[half].begin()

    scatters[1].step(n - 1)
    own_rows(0)
    scatters[1].step(n - 2)
    cot_gather.service(3)
    plain_rows(jnp.int32(3))
    lanes = lax.broadcasted_iota(jnp.int32, (block_rows, 128), 1)
    expert = lax.axis_index("expert") * gate_hbm.shape[0]
    tile = tile_stage.shape[2]
    wait_all(loads[6:])

    def part_copy(z, half, slot):
        return pltpu.make_async_copy(part_stage.at[slot], parts_hbm.at[pl.ds(2 * z, 2), half], part_sems.at[slot])

    @pl.loop(0, 2 * n)
    def each(turn):
        pl.when((turn >= 1) & (turn < n - 1))(lambda: gathers[0].service(turn))
        pl.when((turn >= 1) & (turn < n - 2))(lambda: scatters[1].step(n - 2 - turn))

        @pl.when(turn == n - 1)
        def middle():
            own_rows(1)
            gathers[0].service(n - 1)

        pl.when((turn >= n) & (turn < 2 * n - 1))(lambda: gathers[1].service(turn - n + 1))
        half, step = turn // n, turn % n
        z = chain.nearest(step)

        def arrived(gather):
            pl.when(step == 0)(lambda: gather.keep().wait())
            gather.wait_sibling(z)

        pl.when(half == 0)(lambda: arrived(gathers[0]))
        pl.when(half == 1)(lambda: arrived(gathers[1]))
        logits = dot_last(Split.take(rows_all, z, half), router_ref[...])
        named = Split.take(named_ref, z, half).astype(high) > 0.5
        top = jnp.max(jnp.where(named, logits, -1e30), axis=-1, keepdims=True)
        terms = jnp.where(named, jnp.exp(jnp.where(named, logits - top, 0.0)), 0.0)
        gates = terms / jnp.sum(terms, axis=-1, keepdims=True)
        Split.put(gates_ref, z, half, gates)

        @pl.when(step == 0)
        def own_gates():
            own_gates_ref[half] = jnp.where(chain.c == 0, gates[:rows], gates[rows:])

        gate_col = jnp.sum(jnp.where(lanes == expert, gates, 0.0), axis=-1, keepdims=True)
        gate_grad = expert_block(
            rows_all, lambda units: Split.take(plain, z, half, units), gate_w, up_w, gate_col, gated, grad_gate,
            grad_up, z, half,
        )
        slot = turn % 2

        pl.when(turn >= 2)(lambda: part_copy(z, half, slot).wait())

        @pl.loop(0, width // tile)
        def columns(at):
            span = pl.ds(pl.multiple_of(at * tile, tile), tile)
            grad_rows = dot_last(Split.take(grad_gate, z, half), gate_w[span, :])
            grad_rows = grad_rows + dot_last(Split.take(grad_up, z, half), up_w[span, :])
            part_stage[slot, :, :, span] = grad_rows.astype(low).reshape(2, rows, tile)

        sent = gate_columns(lanes, expert, gate_grad).astype(low)
        part_stage[slot, :, :, width:] = sent.reshape(2, rows, 128)
        part_copy(z, half, slot).start()

    whole_copies = [
        pltpu.make_async_copy(rows_all, rows_hbm, rows_sems.at[0]),
        pltpu.make_async_copy(cots, cots_hbm, rows_sems.at[1]),
        pltpu.make_async_copy(gated, gated_hbm, rows_sems.at[5]),
    ]
    for copy in whole_copies:
        copy.start()
    tiles = Tiles(grads_hbm, tile_stage, tile_sems, gated, grad_gate, grad_up, rows_all, cots)
    for kind in range(3):
        tiles.run(kind)
    for half in range(2):
        gathers[half].finish()
        scatters[half].finish()
    tiles.finish()
    for slot in range(2):
        part_copy(jnp.int32(0), 0, slot).wait()
    wait_all(whole_copies + attention_copies)
    cot_gather.finish()


def second_kernel(
    gates_ref, rows_hbm, cot_hbm, gate_hbm, up_hbm, down_hbm, parts_in,
    sum_ref, gated_hbm, grads_hbm,
    rows_all, cots, gate_w, up_w, down_w, gated, grad_gate, grad_up, parts, tile_stage, load_sems, chip_sems,
    tile_sems, out_sem, pair, flow, *scatter_sems,
):
    chain = Chain()
    n = chain.n
    width = rows_all.shape[3]
    block_rows = parts.shape[1]
    loads = [
        pltpu.make_async_copy(source, target, load_sems.at[at])
        for at, (source, target) in enumerate(
            (
                (gate_hbm.at[1], gate_w), (up_hbm.at[1], up_w), (down_hbm.at[1], down_w), (parts_in, parts),
            )
        )
    ]

    def chip_loads(z):
        block = pl.ds(2 * z, 2)
        return [
            pltpu.make_async_copy(rows_hbm.at[block], rows_all.at[block], chip_sems.at[0, z]),
            pltpu.make_async_copy(cot_hbm.at[block], cots.at[block], chip_sems.at[1, z]),
        ]

    for load in loads[:3]:
        load.start()
    for step in range(n):
        for load in chip_loads(chain.nearest(n - 1 - step)):
            load.start()
    loads[3].start()
    chain.greet()
    scatter = Scatter(chain, chip_block(parts, block_rows // 2), pair, flow, *scatter_sems)
    lanes = lax.broadcasted_iota(jnp.int32, (block_rows, 128), 1)
    expert = lax.axis_index("expert") * gate_hbm.shape[0] + 1
    tile = tile_stage.shape[2]
    wait_all(loads[:3])

    @pl.loop(0, n)
    def each(step):
        z = chain.nearest(n - 1 - step)
        wait_all(chip_loads(z))
        gates = Split.take(gates_ref, z, Split.both)
        gate_col = jnp.sum(jnp.where(lanes == expert, gates, 0.0), axis=-1, keepdims=True)
        gate_grad = expert_block(
            rows_all, lambda units: dot_last(Split.take(cots, z, Split.both), down_w[units, :]), gate_w, up_w,
            gate_col, gated, grad_gate, grad_up, z, Split.both,
        )
        pl.when(step == 0)(lambda: loads[3].wait())

        @pl.loop(0, width // tile)
        def columns(at):
            span = pl.ds(pl.multiple_of(at * tile, tile), tile)
            grad_rows = dot_last(Split.take(grad_gate, z, Split.both), gate_w[span, :])
            grad_rows = grad_rows + dot_last(Split.take(grad_up, z, Split.both), up_w[span, :])
            parts[z, :, span] = (parts[z, :, span].astype(high) + grad_rows).astype(low)

        sent = parts[z, :, width:].astype(high) + gate_columns(lanes, expert, gate_grad)
        parts[z, :, width:] = sent.astype(low)
        scatter.start_pair(z)
        pl.when(step < n - 1)(lambda: scatter.step(n - 1 - step))

    gated_copy = pltpu.make_async_copy(gated, gated_hbm, out_sem)
    gated_copy.start()
    tiles = Tiles(grads_hbm, tile_stage, tile_sems, gated, grad_gate, grad_up, rows_all, cots)
    for kind in range(3):
        tiles.run(kind)
    scatter.total(sum_ref)
    scatter.finish()
    tiles.finish()
    gated_copy.wait()


def split_rows(array, peers):
    return array.reshape(peers, 2, array.shape[0] // (2 * peers), array.shape[1])


def expert_scratch(gate_weight, up_weight, down_weight, peers, rows, width):
    hidden = gate_weight.shape[2]
    whole = pltpu.VMEM((peers, 2, rows, width), low)
    acts = pltpu.VMEM((peers, 2, rows, hidden), low)
    return [
        whole, whole,
        pltpu.VMEM(gate_weight.shape[1:], low),
        pltpu.VMEM(up_weight.shape[1:], low),
        pltpu.VMEM(down_weight.shape[1:], low),
        acts, acts, acts,
    ]


def run_first(
    raw, query_gain, key_gain, cosines, sines, seg_col, seg_row, weight, tokens, gain, named, router, cotangent, near, gate_weight, up_weight, down_weight,
    peers, groups,
):
    length, width = tokens.shape
    n, rows = peers // 2, length // 2
    hidden = gate_weight.shape[2]
    tile, sent = width // groups, width + 128
    full, local_width, head_size = length * peers, weight.shape[0], cosines.shape[1]
    dma = pltpu.SemaphoreType.DMA

    def split(columns, dtype):
        return jax.ShapeDtypeStruct((peers, 2, rows, columns), dtype)

    return pl.pallas_call(
        first_kernel,
        out_shape=[
            jax.ShapeDtypeStruct((full, head_size), low),
            jax.ShapeDtypeStruct((full, head_size), low),
            jax.ShapeDtypeStruct((length, width), high),
            jax.ShapeDtypeStruct((2, rows, width), low),
            split(128, high),
            jax.ShapeDtypeStruct((2, rows, 128), high),
            jax.ShapeDtypeStruct((full, local_width), low),
            jax.ShapeDtypeStruct((full, local_width), low),
            jax.ShapeDtypeStruct((full, local_width), high),
            split(width, low),
            split(width, low),
            split(hidden, low),
            split(sent, low),
            jax.ShapeDtypeStruct((groups, 3 * hidden, tile), low),
        ],
        in_specs=[VMEM] * 9 + [ANY] * 8,
        out_specs=[VMEM] * 6 + [ANY] * 8,
        scratch_shapes=[
            pltpu.VMEM(raw.shape, high),
            pltpu.VMEM(cosines.shape, high),
            pltpu.VMEM(sines.shape, high),
            pltpu.VMEM(seg_col.shape, jnp.int32),
            pltpu.VMEM(weight.shape, low),
            pltpu.VMEM((full, local_width), low),
            pltpu.VMEM((full, local_width), low),
            pltpu.VMEM((full, local_width), high),
            pltpu.VMEM((full, 2 * head_size), low),
            pltpu.VMEM((128, width), low),
            pltpu.VMEM((peers, 2, rows, hidden), high),
            pltpu.VMEM((n, 2, 2, rows, width), low),
            *expert_scratch(gate_weight, up_weight, down_weight, peers, rows, width),
            pltpu.VMEM((2, 2, rows, sent), low),
            pltpu.VMEM((2, hidden, tile), low),
            dma((8,)), dma((6,)), dma((2,)), dma((2, groups)),
            *NearGather.semaphores(n),
            *(Scatter.buffers(n, rows, width) + Gather.semaphores(n)) * 2,
        ],
        compiler_params=communicating(3),
        cost_estimate=pl.CostEstimate(flops=0, bytes_accessed=120 << 20, transcendentals=0),
        name="attention_and_first_expert",
    )(
        query_gain, key_gain, seg_row, tokens, gain, split_rows(named.reshape(-1, 128), peers), router,
        cotangent.reshape(2, rows, width), near.reshape(3, 2, rows, width), raw, cosines, sines, seg_col, weight,
        gate_weight, up_weight, down_weight,
    )


def run_second(gates, rows_all, cotangents, gate_weight, up_weight, down_weight, parts, peers, groups):
    _, _, rows, width = rows_all.shape
    n, length = peers // 2, 2 * rows
    hidden = gate_weight.shape[2]
    tile, sent = width // groups, width + 128
    dma = pltpu.SemaphoreType.DMA
    return pl.pallas_call(
        second_kernel,
        out_shape=[
            jax.ShapeDtypeStruct((length, sent), high),
            jax.ShapeDtypeStruct((peers, 2, rows, hidden), low),
            jax.ShapeDtypeStruct((groups, 3 * hidden, tile), low),
        ],
        in_specs=[VMEM] + [ANY] * 6,
        out_specs=[VMEM, ANY, ANY],
        scratch_shapes=[
            *expert_scratch(gate_weight, up_weight, down_weight, peers, rows, width),
            pltpu.VMEM((n, 2 * length, sent), low),
            pltpu.VMEM((2, hidden, tile), low),
            dma((4,)), dma((2, n)), dma((2, groups)), dma(()),
            *Scatter.buffers(n, length, sent),
        ],
        compiler_params=communicating(7),
        cost_estimate=pl.CostEstimate(flops=0, bytes_accessed=120 << 20, transcendentals=0),
        name="second_expert",
    )(gates, rows_all, cotangents, gate_weight, up_weight, down_weight, parts.reshape(n, 2 * length, sent))


def attention_block_backward(
    span_of, raw_ref, query_low_ref, key_low_ref, value_low_ref, inverse_ref, mixed_ref, grad_mixed_ref,
    query_gain_ref, cos_ref, sin_ref, col_ref, row_ref, grad_query_ref, grad_key_ref, grad_value_ref, grad_gain_ref,
):
    begin, rows, first, keys = span_of
    head_size = key_low_ref.shape[1]
    heads = query_low_ref.shape[1] // head_size
    block, span = pl.ds(begin, rows), pl.ds(first, keys)

    @pl.loop(0, heads)
    def each(head):
        columns = pl.ds(pl.multiple_of(head * head_size, head_size), head_size)
        query_low = query_low_ref[block, columns]
        key_low = key_low_ref[span]
        scaled = grad_mixed_ref[block, columns].astype(high) * inverse_ref[block, columns]
        row_term = jnp.sum(scaled * mixed_ref[block, columns].astype(high), axis=-1, keepdims=True)
        scaled = scaled.astype(low)
        scores = dot_last(query_low, key_low)
        allowed = tile_mask(col_ref, row_ref, begin, rows, first, keys)
        terms = jnp.where(allowed, jnp.exp2(scores), 0.0)
        grad_probs = dot_last(scaled, value_low_ref[span])
        grad_scores = (terms * (grad_probs - row_term)).astype(low)
        grad_value_ref[span] += dot_first(terms.astype(low), scaled)
        grad_key_ref[span] += dot_first(grad_scores, query_low) * (1.0 / log2e)
        grad_rotated = dot(grad_scores, key_low) * head_size**-0.5
        grad_normed = unrotate(grad_rotated, cos_ref[block], sin_ref[block])
        grad_raw, gain_rows = norm_back(raw_ref[block, columns], query_gain_ref[...], grad_normed)
        grad_query_ref[block, columns] = grad_raw.astype(low)
        grad_gain_ref[...] += jnp.broadcast_to(jnp.sum(gain_rows, axis=0, keepdims=True), grad_gain_ref.shape)


def input_kernel(
    sums_ref, own_gates_ref, ffn_ref, resid_ref, cot_ref, gain_ffn_ref, router_in, weight_ref,
    query_gain_ref, key_gain_ref, row_ref, tokens_ref, gain_ref,
    raw_hbm, query_low_hbm, key_low_hbm, value_low_hbm, inverse_hbm, mixed_hbm, cos_hbm, sin_hbm, col_hbm,
    projection_hbm, hidden_hbm,
    input_grad_ref, out_own_ref, gain_grad_ref, ffn_gain_grad_ref, query_gain_grad_ref, key_gain_grad_ref,
    router_grad_ref, projection_grad_hbm,
    raw_ref, query_low_ref, key_low_ref, value_low_ref, inverse_ref, mixed_ref, cos_ref, sin_ref, col_ref,
    projection_ref, hidden_ref,
    router_ref, own, attn_ref, grad_mixed, grad_resid, own_pair, their_pair, key_part, value_part, columns, weight,
    total, parts, projection_grad, out_grad, load_sems, store_sem, swap_send, swap_recv, port_send, port_recv,
    send_a, recv_a, local_a, send_b, recv_b, local_b, pair, flow, *rest,
):
    chain = Chain()
    n = chain.n
    scatter_sems, square_buffers = rest[:4], rest[4:]
    full, head_size = key_part.shape
    _, _, rows, width = attn_ref.shape
    query_width = query_low_ref.shape[1]
    sources = (
        raw_hbm, query_low_hbm, key_low_hbm, value_low_hbm, inverse_hbm, mixed_hbm, cos_hbm, sin_hbm, col_hbm,
        projection_hbm, hidden_hbm,
    )
    targets = (
        raw_ref, query_low_ref, key_low_ref, value_low_ref, inverse_ref, mixed_ref, cos_ref, sin_ref, col_ref,
        projection_ref, hidden_ref,
    )
    loads = [
        pltpu.make_async_copy(source, target, load_sems.at[at])
        for at, (source, target) in enumerate(zip(sources, targets))
    ]
    for load in loads:
        load.start()
    _, _, _, from_x, from_y = square()
    router_ref[...] = jnp.zeros_like(router_ref)
    router_ref[: router_in.shape[0]] = router_in[...]
    sent = sums_ref[:, width:]
    left = lax.broadcasted_iota(jnp.int32, sent.shape, 1) < 64
    grad_gates = jnp.where(left, sent + pltpu.roll(sent, 64, 1), 0.0)
    gates = own_gates_ref[...]
    inner = jnp.sum(gates * grad_gates, axis=-1, keepdims=True)
    grad_logits = (gates * (grad_gates - inner)).astype(low)
    grad_hidden = sums_ref[:, :width] + dot(grad_logits, router_ref[...])
    grad_rows, gain_rows = norm_back(resid_ref[...], gain_ffn_ref[...], grad_hidden)
    grad_resid[...] = cot_ref[...].astype(high) + grad_rows
    own[...] = grad_resid[...].astype(low).reshape(2, rows, width)
    chain.greet([{"dp": from_x}, {"dp": from_y}])
    gathers = [
        Gather(chain, own.at[half], lambda z, c, half=half: attn_ref.at[2 * z + c, half], *sems)
        for half, sems in enumerate(((send_a, recv_a, local_a), (send_b, recv_b, local_b)))
    ]
    for gather in gathers:
        gather.begin()
    router_grad_ref[...] = dot_first(grad_logits, ffn_ref[...])[: router_grad_ref.shape[0]]
    ffn_gain_grad_ref[...] = jnp.broadcast_to(
        jnp.sum(gain_rows, axis=0, keepdims=True), ffn_gain_grad_ref.shape
    )
    key_part[...] = jnp.zeros_like(key_part)
    value_part[...] = jnp.zeros_like(value_part)
    query_gain_grad_ref[...] = jnp.zeros_like(query_gain_grad_ref)
    wait_all(loads[:9])
    spans = key_spans(full)

    @pl.loop(0, n)
    def blocks(step):
        z = chain.nearest(step)
        for gather in gathers:
            pl.when(step > 0)(lambda: gather.service(step))
        for gather in gathers:
            pl.when(step == 0)(lambda: gather.keep().wait())
            gather.wait_sibling(z)
        tokens = pl.ds(pl.multiple_of(z * 4 * rows, 4 * rows), 4 * rows)
        grad_mixed[tokens] = dot_last(Split.take(attn_ref, z, Split.both), weight_ref[...]).astype(low)
        for at, span_of in enumerate(spans):

            @pl.when(z == at)
            def backward():
                attention_block_backward(
                    span_of, raw_ref, query_low_ref, key_low_ref, value_low_ref, inverse_ref, mixed_ref, grad_mixed,
                    query_gain_ref, cos_ref, sin_ref, col_ref, row_ref, columns, key_part, value_part,
                    query_gain_grad_ref,
                )

    own_pair[:, :head_size] = key_part[...].astype(low)
    own_pair[:, head_size:] = value_part[...].astype(low)
    swap = pltpu.make_async_remote_copy(
        src_ref=own_pair,
        dst_ref=their_pair,
        send_sem=swap_send,
        recv_sem=swap_recv,
        device_id={"expert": chain.sibling},
        device_id_type=MESH,
    )
    swap.start()
    first = chain.c == 0
    wait_all(loads[9:])
    weight[:, :query_width] = projection_ref[:, :query_width]
    weight[:, query_width:] = jnp.where(
        first,
        projection_ref[:, query_width : query_width + head_size],
        projection_ref[:, query_width + head_size :],
    )
    swap.wait_recv()
    grad_key = key_part[...] + their_pair[:, :head_size].astype(high)
    grad_value = value_part[...] + their_pair[:, head_size:].astype(high)
    key_raw = raw_ref[:, query_width : query_width + head_size]
    grad_key, gain_rows = norm_back(
        key_raw, key_gain_ref[...], unrotate(grad_key, cos_ref[...], sin_ref[...])
    )
    columns[:, query_width:] = jnp.where(first, grad_key, grad_value).astype(low)
    key_gain = jnp.where(first, jnp.sum(gain_rows, axis=0, keepdims=True), 0.0)
    key_gain_grad_ref[...] = jnp.broadcast_to(key_gain, key_gain_grad_ref.shape)
    pair_rows = parts.shape[1]
    scatter = Scatter(chain, chip_block(parts, pair_rows // 2), pair, flow, *scatter_sems)
    ports = Ports(port_send, port_recv)
    out_total = SquareSum(out_grad, out_own_ref, *square_buffers, ports)
    projection_tile = projection_grad.shape[0] // n
    out_tile = width // n

    @pl.loop(0, n)
    def each(step):
        z = chain.nearest(n - 1 - step)
        tokens = pl.ds(pl.multiple_of(z * pair_rows, pair_rows), pair_rows)
        parts[z] = dot_last(columns[tokens], weight[...]).astype(low)
        scatter.start_pair(z)
        pl.when(step < n - 1)(lambda: scatter.step(n - 1 - step))

        @pl.when(step == 0)
        def out_gradient():
            @pl.loop(0, n)
            def tiles(at):
                span = pl.ds(pl.multiple_of(at * out_tile, out_tile), out_tile)
                out_grad[:, span] = dot_first(mixed_ref[...], Split.every(attn_ref, span)).astype(low)

            out_total.begin()

        span = pl.ds(pl.multiple_of(step * projection_tile, projection_tile), projection_tile)
        projection_grad[span] = dot_first(hidden_ref[:, span], columns[...]).astype(low)

    projection_store = pltpu.make_async_copy(projection_grad, projection_grad_hbm, store_sem)
    projection_store.start()
    out_total.exchange()
    scatter.total(total)
    grad_rows, gain_rows = norm_back(tokens_ref[...].astype(high), gain_ref[...], total[...])
    input_grad_ref[...] = grad_resid[...] + grad_rows
    gain_grad_ref[...] = jnp.broadcast_to(jnp.sum(gain_rows, axis=0, keepdims=True), gain_grad_ref.shape)
    out_total.settle()
    swap.wait_send()
    for gather in gathers:
        gather.finish()
    scatter.finish()
    ports.finish()
    projection_store.wait()


def run_input(
    sums, own_gates, ffn, resid, cotangent, gain_ffn, router, out_weight, raw, query_low, key_low, value_low,
    inverse, mixed, query_gain, key_gain, cosines, sines, seg_col, seg_row, projection, hidden, tokens, gain,
    experts, peers,
):
    length, width = tokens.shape
    n, rows = peers // 2, length // 2
    full, head_size = key_low.shape
    query_width = query_low.shape[1]
    loaded = [
        raw, query_low, key_low, value_low, inverse, mixed, cosines, sines, seg_col, projection, hidden,
    ]
    dma = pltpu.SemaphoreType.DMA
    input_grad, out_own, gain_grad, ffn_gain_grad, query_gain_grad, key_gain_grad, router_grad, projection_grad = (
        pl.pallas_call(
            input_kernel,
            out_shape=[
                jax.ShapeDtypeStruct((length, width), high),
                jax.ShapeDtypeStruct((query_width // 4, width), low),
                jax.ShapeDtypeStruct((8, width), high),
                jax.ShapeDtypeStruct((8, width), high),
                jax.ShapeDtypeStruct((8, head_size), high),
                jax.ShapeDtypeStruct((8, head_size), high),
                jax.ShapeDtypeStruct((experts, width), high),
                jax.ShapeDtypeStruct((width, query_width + head_size), low),
            ],
            in_specs=[VMEM] * 13 + [ANY] * len(loaded),
            out_specs=[VMEM] * 7 + [ANY],
            scratch_shapes=[
                *[pltpu.VMEM(array.shape, array.dtype) for array in loaded],
                pltpu.VMEM((128, width), low),
                pltpu.VMEM((2, rows, width), low),
                pltpu.VMEM((peers, 2, rows, width), low),
                pltpu.VMEM((full, query_width), low),
                pltpu.VMEM((length, width), high),
                pltpu.VMEM((full, 2 * head_size), low),
                pltpu.VMEM((full, 2 * head_size), low),
                pltpu.VMEM((full, head_size), high),
                pltpu.VMEM((full, head_size), high),
                pltpu.VMEM((full, query_width + head_size), low),
                pltpu.VMEM((width, query_width + head_size), low),
                pltpu.VMEM((length, width), high),
                pltpu.VMEM((n, 2 * length, width), low),
                pltpu.VMEM((width, query_width + head_size), low),
                pltpu.VMEM((query_width, width), low),
                dma((len(loaded),)), dma(()), dma(()), dma(()), dma((6,)), dma((6,)),
                *Gather.semaphores(n) * 2,
                *Scatter.buffers(n, length, width),
                *SquareSum.buffers(query_width, width),
            ],
            compiler_params=communicating(5),
            cost_estimate=pl.CostEstimate(flops=0, bytes_accessed=64 << 20, transcendentals=0),
            name="attention_backward_and_input",
        )(
            sums, own_gates.reshape(length, 128), ffn.reshape(length, width), resid, cotangent, gain_ffn, router,
            out_weight, query_gain, key_gain, seg_row, tokens, gain, *loaded,
        )
    )
    return (
        input_grad, projection_grad, out_own, gain_grad, ffn_gain_grad, query_gain_grad, key_gain_grad, router_grad,
    )
def weights_kernel(
    attn_gain_ref, ffn_gain_ref, query_gain_ref, key_gain_ref, router_ref, out_own_ref, proj_hbm, resid_hbm,
    gated_0, gated_1, down_hbm,
    query_grad_ref, key_grad_ref, value_grad_ref, out_grad_ref, small_out_ref, output_ref,
    proj_ref, resid_ref, gated, down_w, mixture, load_sems, all_proj, first_a, first_b, second_a, second_b,
    send_a, send_b, quarter, small, got, part, small_sum, total_mixture,
    port_send, port_recv, swap_send, swap_recv, send_1, recv_1, send_2, recv_2, send_3, recv_3,
    pair, flow, *scatter_sems,
):
    peers = lax.axis_size("expert")
    me = lax.axis_index("expert")
    group, y, x, from_x, from_y = square()
    beside, across = {"dp": from_x}, {"dp": from_y}
    chain = Chain()
    scatter = Scatter(chain, chip_block(mixture, resid_ref.shape[0]), pair, flow, *scatter_sems)
    loads = [
        pltpu.make_async_copy(source, target, load_sems.at[at])
        for at, (source, target) in enumerate(
            (
                (proj_hbm, proj_ref), (gated_0, gated.at[0]), (gated_1, gated.at[1]),
                (down_hbm, down_w), (resid_hbm, resid_ref),
            )
        )
    ]
    for load in loads:
        load.start()
    width = resid_ref.shape[1]
    head_size = query_gain_ref.shape[1]
    small[...] = jnp.zeros_like(small)
    small[0:1] = attn_gain_ref[0:1]
    small[1:2] = ffn_gain_ref[0:1]
    small[2:3, :head_size] = query_gain_ref[0:1]
    small[3:4, :head_size] = key_gain_ref[0:1]
    small[8:] = router_ref[...]
    piece = width // peers

    def small_piece(ref, peer):
        return ref.at[:, pl.ds(pl.multiple_of(peer * piece, piece), piece)]

    barrier = pltpu.get_barrier_semaphore()
    others = [(me + shift) % peers for shift in range(1, peers)]
    groups = [(group + shift) % 4 for shift in range(1, 4)]
    for peer in others:
        pl.semaphore_signal(barrier, inc=1, device_id={"expert": peer}, device_id_type=MESH)
    for other in groups:
        pl.semaphore_signal(barrier, inc=1, device_id={"dp": other}, device_id_type=MESH)
    pl.semaphore_wait(barrier, peers + 2)

    shard_rows, columns = proj_ref.shape[1:]
    rows, half = shard_rows // 4, peers // 2
    ports = Ports(port_send, port_recv)

    def proj_part(side, q, ref=proj_ref):
        return ref.at[pl.ds(side * half, half), pl.ds(pl.multiple_of(q * rows, rows), rows)]

    def remote(source, target, send, recv, device):
        return pltpu.make_async_remote_copy(
            src_ref=source, dst_ref=target, send_sem=send, recv_sem=recv, device_id=device, device_id_type=MESH
        )

    along_x = [2 * other + 1 - x for other in range(2)]
    along_y = [2 * (1 - y) + other for other in range(2)]
    proj_1a = [ports.copy(proj_part(0, along_x[k], proj_hbm), first_a.at[k], beside) for k in range(2)]
    proj_1b = [ports.copy(proj_part(1, along_y[k], proj_hbm), first_b.at[k], across) for k in range(2)]
    for copy in proj_1a + proj_1b:
        copy.start()
    out_copy = SquareCopy(out_own_ref, out_grad_ref, ports)
    out_copy.begin()

    small_1 = [
        remote(small_piece(small, peer), got.at[me], send_1.at[at], recv_1.at[me], {"expert": peer})
        for at, peer in enumerate(others)
    ]
    for copy in small_1:
        copy.start()
    got[me] = small_piece(small, me)[...]
    wait_all(loads)

    def mixture_rows(step):
        z = chain.nearest(chain.n - 1 - step)

        @pl.loop(0, 4)
        def columns(at):
            span = pl.ds(pl.multiple_of(at * (width // 4), width // 4), width // 4)
            mixture[z, :, span] = (dot(gated[0, z], down_w[0, :, span]) + dot(gated[1, z], down_w[1, :, span])).astype(low)

        scatter.start_pair(z)

    @pl.loop(0, chain.n)
    def each_chip(step):
        mixture_rows(step)


    own = group
    for_y, for_x = 2 * (1 - y) + x, 2 * y + 1 - x
    scatter.step(3) if chain.n > 3 else None
    for copy in proj_1a + proj_1b:
        copy.wait_recv()
    send_a[...] = (proj_part(0, for_y)[...].astype(high) + first_a[1 - y].astype(high)).astype(low)
    send_b[...] = (proj_part(1, for_x)[...].astype(high) + first_b[1 - x].astype(high)).astype(low)
    proj_2a = ports.copy(send_a, second_a, across)
    proj_2b = ports.copy(send_b, second_b, beside)
    proj_2a.start()
    proj_2b.start()
    scatter.step(2) if chain.n > 2 else None
    out_copy.hand_on()

    for at, peer in enumerate(others):
        remote(got.at[peer], got.at[peer], send_1.at[at], recv_1.at[peer], {"expert": peer}).wait_recv()
    total = got[0]
    for at in range(1, peers):
        total = total + got[at]
    part[group] = total
    small_2 = [
        remote(part.at[group], part.at[group], send_2.at[at], recv_2.at[group], {"dp": other})
        for at, other in enumerate(groups)
    ]
    for copy in small_2:
        copy.start()

    proj_2a.wait_recv()
    proj_2b.wait_recv()
    for side, first, second, at in ((0, first_a, second_a, y), (1, first_b, second_b, x)):
        quarter[pl.ds(side * half, half)] = (
            proj_part(side, own)[...].astype(high) + first[at].astype(high) + second[...].astype(high)
        ).astype(low)
    swaps = [
        remote(quarter.at[peer], all_proj.at[own, me], swap_send.at[at], swap_recv.at[me], {"expert": peer})
        for at, peer in enumerate(others)
    ]
    for copy in swaps:
        copy.start()
    all_proj[own, me] = quarter[me]

    for at, other in enumerate(groups):
        remote(part.at[other], part.at[other], send_2.at[at], recv_2.at[other], {"dp": other}).wait_recv()
    total = part[0]
    for at in range(1, 4):
        total = total + part[at]
    small_sum[me] = total
    small_3 = [
        remote(small_sum.at[me], small_sum.at[me], send_3.at[at], recv_3.at[me], {"expert": peer})
        for at, peer in enumerate(others)
    ]
    for copy in small_3:
        copy.start()

    for at, peer in enumerate(others):
        block = all_proj.at[own, peer]
        remote(block, block, swap_send.at[at], swap_recv.at[peer], {"expert": peer}).wait_recv()
    proj_gx = ports.copy(all_proj.at[own], all_proj.at[own], beside)
    proj_gy = ports.copy(all_proj.at[own], all_proj.at[own], across)
    proj_gx.start()
    proj_gy.start()
    far = 3 - group
    scatter.step(1) if chain.n > 1 else None

    def proj_half(q, side):
        return all_proj.at[q, pl.ds(side * half, half)]

    proj_gx.wait_recv()
    proj_gy.wait_recv()
    proj_fa = ports.copy(proj_half(from_x, 0), proj_half(from_x, 0), across)
    proj_fb = ports.copy(proj_half(from_y, 1), proj_half(from_y, 1), beside)
    proj_fa.start()
    proj_fb.start()
    query_width = columns - head_size

    def spread(q):
        block = pl.ds(pl.multiple_of(q * rows, rows), rows)
        for peer in range(peers):
            query_grad_ref[block, peer * query_width : (peer + 1) * query_width] = all_proj[q, peer, :, :query_width]
            shared = key_grad_ref if peer % 2 == 0 else value_grad_ref
            at = peer // 2 * head_size
            shared[block, at : at + head_size] = all_proj[q, peer, :, query_width:]

    spread(own)
    spread(from_x)
    spread(from_y)
    for at, peer in enumerate(others):
        block = small_sum.at[peer]
        remote(block, block, send_3.at[at], recv_3.at[peer], {"expert": peer}).wait_recv()
    for peer in range(peers):
        small_out_ref[:, peer * piece : (peer + 1) * piece] = small_sum[peer]
    scatter.total(total_mixture)
    output_ref[...] = (resid_ref[...] + total_mixture[...]).astype(low)
    out_copy.finish()
    proj_fa.wait_recv()
    proj_fb.wait_recv()
    spread(far)
    ports.finish()
    scatter.finish()
    for copy in small_1 + small_2 + small_3 + swaps:
        copy.wait_send()


def run_weights(
    grad_projection, out_own, attn_gain, ffn_gain, query_gain, key_gain, router, resid, first_gated, second_gated,
    down_weight, peers, kv_heads,
):
    width, columns = grad_projection.shape
    head_size = query_gain.shape[1]
    length = resid.shape[0]
    n = peers // 2
    shard_rows = width // peers
    rows, half = shard_rows // 4, peers // 2
    small_rows = 8 + router.shape[0]
    piece = (small_rows, width // peers)
    hidden = down_weight.shape[1]
    dma = pltpu.SemaphoreType.DMA
    kv_width = kv_heads * head_size
    query_width = columns - head_size

    def low_buffer(*shape):
        return pltpu.VMEM(shape, low)

    return pl.pallas_call(
        weights_kernel,
        out_shape=[
            jax.ShapeDtypeStruct((shard_rows, peers * query_width), low),
            jax.ShapeDtypeStruct((shard_rows, kv_width), low),
            jax.ShapeDtypeStruct((shard_rows, kv_width), low),
            jax.ShapeDtypeStruct((4 * out_own.shape[0], width), low),
            jax.ShapeDtypeStruct((small_rows, width), high),
            jax.ShapeDtypeStruct((length, width), low),
        ],
        in_specs=[VMEM] * 6 + [ANY] * 5,
        out_specs=[VMEM] * 6,
        scratch_shapes=[
            low_buffer(peers, shard_rows, columns),
            pltpu.VMEM(resid.shape, high),
            low_buffer(2, n, 2 * length, hidden),
            low_buffer(*down_weight.shape),
            low_buffer(n, 2 * length, width),
            dma((5,)),
            low_buffer(4, peers, rows, columns),
            low_buffer(2, half, rows, columns),
            low_buffer(2, half, rows, columns),
            low_buffer(half, rows, columns),
            low_buffer(half, rows, columns),
            low_buffer(half, rows, columns),
            low_buffer(half, rows, columns),
            low_buffer(peers, rows, columns),
            pltpu.VMEM((small_rows, width), high),
            pltpu.VMEM((peers, *piece), high),
            pltpu.VMEM((4, *piece), high),
            pltpu.VMEM((peers, *piece), high),
            pltpu.VMEM((length, width), high),
            dma((14,)), dma((14,)),
            dma((peers - 1,)), dma((peers,)),
            dma((peers - 1,)), dma((peers,)),
            dma((3,)), dma((4,)),
            dma((peers - 1,)), dma((peers,)),
            *Scatter.buffers(n, length, width),
        ],
        compiler_params=communicating(6),
        cost_estimate=pl.CostEstimate(flops=0, bytes_accessed=64 << 20, transcendentals=0),
        name="sum_weight_gradients",
    )(
        attn_gain, ffn_gain, query_gain, key_gain, router, out_own, grad_projection.reshape(peers, shard_rows, columns),
        resid, first_gated.reshape(n, 2 * length, hidden), second_gated.reshape(n, 2 * length, hidden),
        down_weight,
    )


def widen_kernel(
    wide_0, down_0, wide_1, down_1, query_in, key_in, value_in, out_in, small_ref,
    gate_ref, up_ref, down_ref, query_ref, key_ref, value_ref, out_ref,
    attn_gain_ref, ffn_gain_ref, query_gain_ref, key_gain_ref, router_ref,
):
    for expert, (wide, down) in enumerate(((wide_0, down_0), (wide_1, down_1))):

        @pl.when(pl.program_id(0) == expert)
        def place():
            piece = gate_ref.shape[1]
            gate_ref[0] = wide[:piece].astype(high)
            up_ref[0] = wide[piece:].astype(high)
            down_ref[0] = down[...].astype(high)

    for source, target in ((query_in, query_ref), (key_in, key_ref), (value_in, value_ref), (out_in, out_ref)):
        target[...] = source[...].astype(high)

    @pl.when((pl.program_id(0) == 0) & (pl.program_id(1) == 0))
    def small():
        attn_gain_ref[...] = small_ref[0]
        ffn_gain_ref[...] = small_ref[1]
        query_gain_ref[...] = small_ref[2, : query_gain_ref.shape[0]]
        key_gain_ref[...] = small_ref[3, : key_gain_ref.shape[0]]
        router_ref[...] = small_ref[8:]


def run_widen(grads, weight_grads, small, head_size, hidden_units, model_width, groups):
    piece, tile = hidden_units // groups, model_width // groups
    operands, specs = [], []

    def of_expert(expert):
        return lambda x, j: jnp.where(x == expert, j, 0 if expert else groups - 1)

    for expert, rows in enumerate(grads):
        turn = of_expert(expert)
        operands += [rows, rows]
        specs += [
            pl.BlockSpec((2 * piece, tile), lambda x, j, turn=turn: (turn(x, j), 0)),
            pl.BlockSpec((piece, tile), lambda x, j, turn=turn: (2 * groups + turn(x, j), 0)),
        ]
    steps = 2 * groups
    small_shapes = [
        (model_width,), (model_width,), (head_size,), (head_size,), (small.shape[0] - 8, model_width),
    ]

    def rows_of(array):
        return pl.BlockSpec((array.shape[0] // steps, array.shape[1]), lambda x, j: (x * groups + j, 0))

    return pl.pallas_call(
        widen_kernel,
        grid=(2, groups),
        out_shape=[
            jax.ShapeDtypeStruct((2, piece, model_width), high),
            jax.ShapeDtypeStruct((2, piece, model_width), high),
            jax.ShapeDtypeStruct((2, hidden_units, tile), high),
            *[jax.ShapeDtypeStruct(array.shape, high) for array in weight_grads],
            *[jax.ShapeDtypeStruct(shape, high) for shape in small_shapes],
        ],
        in_specs=specs + [rows_of(array) for array in weight_grads] + [pl.BlockSpec(small.shape, lambda x, j: (0, 0))],
        out_specs=[
            pl.BlockSpec((1, piece, tile), lambda x, j: (x, 0, j)),
            pl.BlockSpec((1, piece, tile), lambda x, j: (x, 0, j)),
            pl.BlockSpec((1, piece, tile), lambda x, j: (x, j, 0)),
            *[rows_of(array) for array in weight_grads],
            *[pl.BlockSpec(shape, lambda x, j, rank=len(shape): (0,) * rank) for shape in small_shapes],
        ],
        compiler_params=pltpu.CompilerParams(vmem_limit_bytes=60 << 20),
        name="widen",
    )(*operands, *weight_grads, small)


def gather_tokens(rows):
    return lax.all_gather(rows, "expert", axis=0, tiled=True)


def scatter_sum(partial):
    return lax.psum_scatter(partial, "expert", scatter_dimension=0, tiled=True)


def projection_gradients(grad_projection, peers, kv_heads, head_size):
    width, columns = grad_projection.shape
    shard_rows = width // peers
    local_width = columns - head_size
    sharers = peers // kv_heads
    grad_projection = grad_projection.reshape(peers, shard_rows, columns)
    grad_projection = lax.psum_scatter(grad_projection, "dp", scatter_dimension=1, tiled=True)
    grad_projection = lax.all_to_all(
        grad_projection, "expert", split_axis=0, concat_axis=0, tiled=True
    )
    grad_projection = lax.all_gather(grad_projection, "dp", axis=1, tiled=True)
    grad_query_w = (
        grad_projection[:, :, :local_width].transpose(1, 0, 2).reshape(shard_rows, peers * local_width)
    ).astype(high)
    shared = grad_projection[:, :, local_width:].reshape(kv_heads, sharers, shard_rows, head_size)
    kv_width = kv_heads * head_size
    grad_key_w = shared[:, 0].transpose(1, 0, 2).reshape(shard_rows, kv_width).astype(high)
    grad_value_w = shared[:, 1].transpose(1, 0, 2).reshape(shard_rows, kv_width).astype(high)
    return grad_query_w, grad_key_w, grad_value_w


def out_gradient(grad_out):
    summed = lax.psum_scatter(grad_out, "dp", scatter_dimension=0, tiled=True)
    return lax.all_gather(summed, "dp", axis=0, tiled=True).astype(high)


def constant_tables(length, head_size):
    half = head_size // 2
    freqs = np.float32(rope_base) ** (-np.arange(half, dtype=np.float32) * np.float32(2.0 / head_size))
    angles = np.arange(length, dtype=np.float32)[:, None] * freqs[None, :]
    cosines, sines = np.cos(angles), np.sin(angles)
    return (
        jnp.asarray(np.concatenate([cosines, cosines], 1), high),
        jnp.asarray(np.concatenate([-sines, sines], 1), high),
    )


def fits_kernels(peers, groups, sharers, experts, full_length, width):
    return groups == 4 and peers == 8 and sharers == 2 and experts == 2 * peers and full_length * width <= 1 << 21


def fused_layer(
    tokens, segments, routes, cotangent, norm_gain_attn, query_weight, key_matrix, value_matrix, query_gain,
    key_gain, out_weight, norm_gain_ffn, router_weight, gate_weight, up_weight, down_weight, heads,
):
    length, model_width = tokens.shape
    head_size = query_gain.shape[0]
    peers = lax.axis_size("expert")
    groups = lax.axis_size("dp")
    local_experts, _, hidden_units = gate_weight.shape
    experts = local_experts * peers
    full_length = length * peers
    kv_heads = peers // 2
    local_width = heads * head_size
    gain_attn_row = norm_gain_attn.reshape(1, model_width)
    gain_ffn_row = norm_gain_ffn.reshape(1, model_width)

    named = jnp.any(routes[:, :, None] == jnp.arange(128, dtype=jnp.int32)[None, None, :], axis=1).astype(low)
    hidden, all_named, near, projection, raw = run_gather(
        tokens, gain_attn_row, named, cotangent, query_weight, key_matrix, value_matrix, peers, groups
    )
    cosines, sines = constant_tables(full_length, head_size)
    seg_col = jnp.broadcast_to(segments.reshape(full_length, 1), (full_length, head_size))
    seg_row = jnp.broadcast_to(segments.reshape(1, full_length), (8, full_length))
    query_gain_row = query_gain.reshape(1, head_size)
    key_gain_row = key_gain.reshape(1, head_size)
    router = router_weight.T
    (
        key_low, value_low, resid, ffn_local, gates, own_gates, mixed, query_low, inverse, rows_all, cotangents,
        first_gated, parts, first_grads,
    ) = run_first(
        raw, query_gain_row, key_gain_row, cosines, sines, seg_col, seg_row, out_weight, tokens, gain_ffn_row,
        all_named, router, cotangent, near, gate_weight, up_weight, down_weight, peers, groups,
    )
    sums, second_gated, second_grads = run_second(
        gates, rows_all, cotangents, gate_weight, up_weight, down_weight, parts, peers, groups
    )
    grads = [
        lax.psum_scatter(each.reshape(-1, each.shape[2]), "dp", scatter_dimension=0, tiled=True)
        for each in (first_grads, second_grads)
    ]
    input_grad, grad_projection, out_own, gain_attn_part, gain_ffn_part, query_gain_part, key_gain_part, grad_router = (
        run_input(
            sums, own_gates, ffn_local, resid, cotangent, gain_ffn_row, router, out_weight, raw, query_low, key_low,
            value_low, inverse, mixed, query_gain_row, key_gain_row, cosines, sines, seg_col, seg_row, projection,
            hidden, tokens, gain_attn_row, experts, peers,
        )
    )
    grads[0], grad_projection = lax.optimization_barrier((grads[0], grad_projection))
    *weight_grads, small, output = run_weights(
        grad_projection, out_own, gain_attn_part, gain_ffn_part, query_gain_part, key_gain_part, grad_router,
        resid, first_gated, second_gated, down_weight, peers, kv_heads,
    )
    gate_w, up_w, down_w, query_w, key_w, value_w, out_w, *sums = run_widen(
        grads, weight_grads, small, head_size, hidden_units, model_width, groups
    )
    gain_attn_grad, gain_ffn_grad, query_gain_grad, key_gain_grad, router_grad = sums
    return (
        output,
        input_grad,
        gain_attn_grad,
        query_w,
        key_w,
        value_w,
        query_gain_grad,
        key_gain_grad,
        out_w,
        gain_ffn_grad,
        router_grad.T,
        gate_w.transpose(0, 2, 1),
        up_w.transpose(0, 2, 1),
        down_w,
    )


def on_device(
    tokens,
    segments,
    routes,
    cotangent,
    norm_gain_attn,
    query_weight,
    key_matrix,
    value_matrix,
    query_gain,
    key_gain,
    out_weight,
    norm_gain_ffn,
    router_weight,
    gate_weight,
    up_weight,
    down_weight,
):
    length, model_width = tokens.shape
    head_size = query_gain.shape[0]
    peers = lax.axis_size("expert")
    groups = lax.axis_size("dp")
    me = lax.axis_index("expert")
    group = lax.axis_index("dp")
    shard_rows, query_width = query_weight.shape
    kv_width = key_matrix.shape[1]
    kv_heads = kv_width // head_size
    heads = query_width // head_size // peers
    sharers = peers // kv_heads
    local_width = heads * head_size
    local_experts = gate_weight.shape[0]
    experts = local_experts * peers
    full_length = length * peers
    piece = shard_rows // groups

    if fits_kernels(peers, groups, sharers, experts, full_length, model_width):
        return fused_layer(
            tokens, segments, routes, cotangent, norm_gain_attn, query_weight, key_matrix, value_matrix,
            query_gain, key_gain, out_weight, norm_gain_ffn, router_weight, gate_weight, up_weight, down_weight, heads,
        )

    def own_rows(matrix):
        return lax.dynamic_slice_in_dim(matrix, group * piece, piece, 0)

    def columns(matrix, width, copies):
        split = own_rows(matrix).reshape(piece, -1, width).transpose(1, 0, 2)
        return jnp.repeat(split, copies, axis=0)

    outgoing = jnp.concatenate(
        [
            columns(query_weight, local_width, 1),
            columns(key_matrix, head_size, sharers),
            columns(value_matrix, head_size, sharers),
        ],
        axis=2,
    )
    arrived = lax.all_to_all(outgoing, "expert", split_axis=0, concat_axis=0, tiled=True)
    projection = lax.all_gather(arrived, "dp", axis=1, tiled=True).reshape(model_width, -1)

    inputs = tokens.astype(high)
    hidden_local = norm_rows(inputs, norm_gain_attn).astype(low)
    hidden = gather_tokens(hidden_local)
    raw = dot(hidden, projection)
    cosines, sines = rotary_tables(full_length, head_size)
    seg_col = jnp.broadcast_to(segments.reshape(full_length, 1), (full_length, head_size))
    seg_row = jnp.broadcast_to(segments.reshape(1, full_length), (8, full_length))
    query_gain_row = query_gain.reshape(1, head_size)
    key_gain_row = key_gain.reshape(1, head_size)
    mixed, query_low, key_low, value_low, inverse = run_attention_forward(
        raw, heads, head_size, query_gain_row, key_gain_row, cosines, sines, seg_col, seg_row
    )
    attn = scatter_sum(dot(mixed, out_weight).astype(low))
    resid = inputs + attn.astype(high)
    ffn_local = norm_rows(resid, norm_gain_ffn).astype(low)
    ffn_rows = gather_tokens(ffn_local)
    cotangents = gather_tokens(cotangent)
    all_routes = gather_tokens(routes)

    def gates_of(rows, route_rows):
        logits = dot(rows, router_weight)
        named = jnp.any(
            route_rows[:, :, None] == jnp.arange(experts, dtype=jnp.int32)[None, None, :], axis=1
        )
        top = jnp.max(jnp.where(named, logits, -jnp.inf), axis=-1, keepdims=True)
        terms = jnp.where(named, jnp.exp(jnp.where(named, logits - top, 0.0)), 0.0)
        return terms / jnp.sum(terms, axis=-1, keepdims=True)

    gates_all = gates_of(ffn_rows, all_routes)
    own_gates = lax.dynamic_slice_in_dim(gates_all, me * local_experts, local_experts, 1)
    mixture = 0.0
    grad_rows = 0.0
    gate_grads, grad_gate_w, grad_up_w, grad_down_w = [], [], [], []
    for expert in range(local_experts):
        gate_col = own_gates[:, expert : expert + 1]
        gate_pre = dot(ffn_rows, gate_weight[expert])
        up_pre = dot(ffn_rows, up_weight[expert])
        share = jax.nn.sigmoid(gate_pre)
        silu = gate_pre * share
        act = silu * up_pre
        gated_act = (act * gate_col).astype(low)
        mixture = mixture + dot(gated_act, down_weight[expert])
        plain = dot_last(cotangents, down_weight[expert])
        gate_grads.append(jnp.sum(act * plain, axis=-1, keepdims=True))
        grad_act = plain * gate_col
        grad_gate_pre = (grad_act * up_pre * (share * (1.0 + gate_pre * (1.0 - share)))).astype(low)
        grad_up_pre = (grad_act * silu).astype(low)
        grad_rows = (
            grad_rows
            + dot_last(grad_gate_pre, gate_weight[expert])
            + dot_last(grad_up_pre, up_weight[expert])
        )
        hidden_units = gated_act.shape[1]
        grad_gate_w.append(dot_first(grad_gate_pre, ffn_rows).astype(low).reshape(groups, -1, model_width))
        grad_up_w.append(dot_first(grad_up_pre, ffn_rows).astype(low).reshape(groups, -1, model_width))
        cut_width = model_width // groups
        grad_down_w.append(
            jnp.stack([
                dot_first(gated_act, cotangents[:, part * cut_width : (part + 1) * cut_width]).astype(low)
                for part in range(groups)
            ])
        )

    gate_grad = jnp.concatenate(gate_grads, axis=1)
    lane_pad = 128 - 2 * experts % 128
    placed = jnp.zeros((full_length, experts), high)
    placed = lax.dynamic_update_slice_in_dim(placed, gate_grad, me * local_experts, 1)
    upper = placed.astype(low)
    lower = (placed - upper.astype(high)).astype(low)
    sent = jnp.concatenate(
        [grad_rows.astype(low), upper, lower, jnp.zeros((full_length, lane_pad), low)], axis=1
    )
    summed_rows = scatter_sum(sent)
    output = (resid + scatter_sum(mixture.astype(low)).astype(high)).astype(low)
    grad_gates = summed_rows[:, model_width : model_width + experts].astype(high) + summed_rows[
        :, model_width + experts : model_width + 2 * experts
    ].astype(high)
    gates = gates_of(ffn_local, routes)
    grad_logits = (
        gates * (grad_gates - jnp.sum(gates * grad_gates, axis=-1, keepdims=True))
    ).astype(low)
    grad_router = dot_first(ffn_local, grad_logits)
    grad_hidden_ffn = summed_rows[:, :model_width].astype(high) + dot_last(grad_logits, router_weight)
    grad_resid_norm, gain_rows_ffn = norm_back(resid, norm_gain_ffn, grad_hidden_ffn)
    grad_resid = cotangent.astype(high) + grad_resid_norm
    grad_attn = gather_tokens(grad_resid.astype(low))
    grad_mixed = dot_last(grad_attn, out_weight).astype(low)
    grad_out = dot_first(mixed, grad_attn)
    grad_query_low, grad_key_part, grad_value_part, query_gain_part = run_attention_backward(
        raw, query_low, key_low, value_low, inverse, mixed, grad_mixed, heads, head_size,
        query_gain_row, cosines, sines, seg_col, seg_row,
    )
    both = jnp.concatenate([grad_key_part, grad_value_part], axis=1)
    step = 1
    while step < sharers:
        swap = [(peer, peer ^ step) for peer in range(peers)]
        both = both + lax.ppermute(both.astype(low), "expert", swap).astype(high)
        step *= 2
    grad_key_rot, grad_value = both[:, :head_size], both[:, head_size:].astype(low)
    place = me % sharers
    half = head_size // 2
    swapped = jnp.concatenate([grad_key_rot[:, half:], grad_key_rot[:, :half]], axis=1)
    key_raw = raw[:, local_width : local_width + head_size]
    grad_key, key_gain_rows = norm_back(key_raw, key_gain, grad_key_rot * cosines - swapped * sines)
    grad_shared = jnp.where(
        place == 0, grad_key.astype(low), jnp.where(place == 1, grad_value, jnp.zeros_like(grad_value))
    )
    own_columns = jnp.concatenate([grad_query_low, grad_shared], axis=1)
    shared_weight = jnp.where(
        place == 0,
        projection[:, local_width : local_width + head_size],
        projection[:, local_width + head_size :],
    )
    own_weight = jnp.concatenate([projection[:, :local_width], shared_weight], axis=1)
    grad_hidden_attn = scatter_sum(dot_last(own_columns, own_weight).astype(low)).astype(high)
    grad_inputs_norm, gain_rows_attn = norm_back(inputs, norm_gain_attn, grad_hidden_attn)
    input_grad = grad_resid + grad_inputs_norm

    grad_query_w, grad_key_w, grad_value_w = projection_gradients(
        dot_first(hidden, own_columns).astype(low), peers, kv_heads, head_size
    )
    grad_out_w = out_gradient(grad_out.astype(low))

    wide = jnp.concatenate(grad_gate_w + grad_up_w, axis=1)
    wide = lax.psum_scatter(wide, "dp", scatter_dimension=0, tiled=True)
    wide = wide.reshape(2, local_experts, hidden_units // groups, model_width).transpose(0, 1, 3, 2)
    wide = wide.astype(high)
    down = jnp.concatenate(grad_down_w, axis=1)
    down = lax.psum_scatter(down, "dp", scatter_dimension=0, tiled=True)
    down = down.reshape(local_experts, hidden_units, cut_width).astype(high)
    expert_sums = (wide[0], wide[1], down)
    key_gain_grad = jnp.where(place == 0, jnp.sum(key_gain_rows, axis=0), 0.0)
    small = jnp.concatenate(
        [
            jnp.sum(gain_rows_attn, axis=0),
            jnp.sum(gain_rows_ffn, axis=0),
            query_gain_part[0],
            key_gain_grad,
            grad_router.reshape(-1),
        ]
    )
    small = lax.psum(small, ("dp", "expert"))
    cut = 2 * model_width
    return (
        output,
        input_grad,
        small[:model_width],
        grad_query_w,
        grad_key_w,
        grad_value_w,
        small[cut : cut + head_size],
        small[cut + head_size : cut + 2 * head_size],
        grad_out_w,
        small[model_width:cut],
        small[cut + 2 * head_size :].reshape(model_width, experts),
        *expert_sums,
    )


def solution(mesh):
    rows = P(("dp", "expert"), None)
    split = P("expert", None)
    cube = P("expert", None, None)
    cut = P("expert", None, "dp")
    return jax.shard_map(
        on_device,
        mesh=mesh,
        in_specs=(
            rows, P("dp", None), rows, rows, P(), split, split, split, P(), P(), split, P(), P(),
            cube, cube, cube,
        ),
        out_specs=(
            rows, rows, P(), split, split, split, P(), P(), split, P(), P(), cut, cut, cut,
        ),
        check_vma=False,
    )
```

```python
import functools

import jax
import jax.numpy as jnp
import numpy as np
from jax import lax
from jax.experimental import pallas as pl
from jax.experimental.pallas import tpu as pltpu
from jax.sharding import PartitionSpec as P

eps_norm = 1e-06
rope_base = 1000000.0
log2e = 1.4426950408889634
low = jnp.bfloat16
high = jnp.float32


def norm_rows(values, gain):
    factor = lax.rsqrt(jnp.mean(values * values, axis=-1, keepdims=True) + eps_norm)
    return values * factor * gain


def norm_back(values, gain, grad):
    factor = lax.rsqrt(jnp.mean(values * values, axis=-1, keepdims=True) + eps_norm)
    scaled = gain * grad
    inner = jnp.mean(values * scaled, axis=-1, keepdims=True)
    grad_values = factor * scaled - values * (factor * factor * factor * inner)
    return grad_values, grad * values * factor


def dot(left, right):
    return jnp.dot(left, right, preferred_element_type=high)


def dot_first(left, right):
    return lax.dot_general(left, right, (((0,), (0,)), ((), ())), preferred_element_type=high)


def dot_last(left, right):
    return lax.dot_general(left, right, (((1,), (1,)), ((), ())), preferred_element_type=high)


def rotary_tables(length, head_size):
    half = head_size // 2
    freqs = rope_base ** (-jnp.arange(half, dtype=high) * 2.0 / head_size)
    angles = jnp.arange(length, dtype=high)[:, None] * freqs[None, :]
    cosines, sines = jnp.cos(angles), jnp.sin(angles)
    return jnp.concatenate([cosines, cosines], 1), jnp.concatenate([-sines, sines], 1)


def rotate(values, cosines, sines):
    return values * cosines + pltpu.roll(values, values.shape[-1] // 2, 1) * sines


def unrotate(values, cosines, sines):
    return values * cosines - pltpu.roll(values, values.shape[-1] // 2, 1) * sines


def key_spans(length):
    block = min(256, length)
    longest = length // 2
    spans = []
    for begin in range(0, length, block):
        first = max(0, begin - longest + 1) // block * block
        spans.append((begin, block, first, begin + block - first))
    return spans


def tile_mask(seg_col, seg_row, begin, rows, first, keys):
    query_at = begin + lax.broadcasted_iota(jnp.int32, (rows, keys), 0)
    key_at = first + lax.broadcasted_iota(jnp.int32, (rows, keys), 1)
    return (query_at >= key_at) & (seg_col[begin : begin + rows, :1] == seg_row[:1, first : first + keys])


def attention_forward(
    query_ref, key_ref, value_ref, query_gain_ref, key_gain_ref, cos_ref, sin_ref, col_ref, row_ref,
    mixed_ref, query_low_ref, key_low_ref, value_low_ref, inverse_ref, value_wide,
):
    head_size = query_ref.shape[1]

    @pl.when(pl.program_id(0) == 0)
    def first_head():
        rotated = rotate(norm_rows(key_ref[...], key_gain_ref[...]), cos_ref[...], sin_ref[...])
        key_low_ref[...] = rotated.astype(low)
        value_low_ref[...] = value_ref[...].astype(low)
        value_wide[:, :head_size] = value_ref[...].astype(low)
        value_wide[:, head_size:] = jnp.ones_like(value_low_ref)

    rotated = rotate(norm_rows(query_ref[...], query_gain_ref[...]), cos_ref[...], sin_ref[...])
    query_low_ref[...] = (rotated * (head_size**-0.5 * log2e)).astype(low)
    for begin, rows, first, keys in key_spans(query_ref.shape[0]):
        scores = dot_last(query_low_ref[pl.ds(begin, rows)], key_low_ref[pl.ds(first, keys)])
        allowed = tile_mask(col_ref, row_ref, begin, rows, first, keys)
        terms = jnp.where(allowed, jnp.exp2(scores), 0.0).astype(low)
        sums = dot(terms, value_wide[pl.ds(first, keys)])
        inverse = 1.0 / sums[:, head_size:]
        mixed_ref[pl.ds(begin, rows)] = (sums[:, :head_size] * inverse).astype(low)
        inverse_ref[pl.ds(begin, rows)] = inverse


def attention_backward(
    query_ref, query_low_ref, key_low_ref, value_low_ref, inverse_ref, mixed_ref, grad_mixed_ref,
    query_gain_ref, cos_ref, sin_ref, col_ref, row_ref,
    grad_query_ref, grad_key_ref, grad_value_ref, grad_gain_ref,
):
    length, head_size = query_ref.shape

    @pl.when(pl.program_id(0) == 0)
    def first_head():
        grad_key_ref[...] = jnp.zeros_like(grad_key_ref)
        grad_value_ref[...] = jnp.zeros_like(grad_value_ref)
        grad_gain_ref[...] = jnp.zeros_like(grad_gain_ref)

    for begin, rows, first, keys in key_spans(length):
        block = pl.ds(begin, rows)
        query_low = query_low_ref[block]
        key_low = key_low_ref[pl.ds(first, keys)]
        scaled = grad_mixed_ref[block].astype(high) * inverse_ref[block]
        row_term = jnp.sum(scaled * mixed_ref[block].astype(high), axis=-1, keepdims=True)
        scaled = scaled.astype(low)
        scores = dot_last(query_low, key_low)
        allowed = tile_mask(col_ref, row_ref, begin, rows, first, keys)
        terms = jnp.where(allowed, jnp.exp2(scores), 0.0)
        grad_probs = dot_last(scaled, value_low_ref[pl.ds(first, keys)])
        grad_scores = (terms * (grad_probs - row_term)).astype(low)
        grad_value_ref[pl.ds(first, keys)] += dot_first(terms.astype(low), scaled)
        grad_key_ref[pl.ds(first, keys)] += dot_first(grad_scores, query_low) * (1.0 / log2e)
        grad_rotated = dot(grad_scores, key_low) * head_size**-0.5
        grad_normed = unrotate(grad_rotated, cos_ref[block], sin_ref[block])
        grad_raw, gain_rows = norm_back(query_ref[block], query_gain_ref[...], grad_normed)
        grad_query_ref[block] = grad_raw.astype(low)
        grad_gain_ref[...] += jnp.broadcast_to(
            jnp.sum(gain_rows, axis=0, keepdims=True), grad_gain_ref.shape
        )


def whole(shape):
    return pl.BlockSpec(shape, lambda head: (0,) * len(shape))


def run_attention_forward(raw, heads, head_size, query_gain, key_gain, cosines, sines, seg_col, seg_row):
    length = raw.shape[0]
    per_head = pl.BlockSpec((length, head_size), lambda head: (0, head))
    one = (length, head_size)
    wide = jax.ShapeDtypeStruct((length, heads * head_size), low)
    narrow = jax.ShapeDtypeStruct(one, low)
    return pl.pallas_call(
        attention_forward,
        grid=(heads,),
        in_specs=[
            per_head,
            pl.BlockSpec(one, lambda head: (0, heads)),
            pl.BlockSpec(one, lambda head: (0, heads + 1)),
            whole((1, head_size)),
            whole((1, head_size)),
            whole(one),
            whole(one),
            whole(one),
            whole((8, length)),
        ],
        out_specs=[per_head, per_head, whole(one), whole(one), per_head],
        out_shape=[wide, wide, narrow, narrow, jax.ShapeDtypeStruct((length, heads * head_size), high)],
        scratch_shapes=[pltpu.VMEM((length, 2 * head_size), low)],
        compiler_params=pltpu.CompilerParams(vmem_limit_bytes=50 << 20),
        cost_estimate=pl.CostEstimate(
            flops=3 * heads * length * length * head_size, bytes_accessed=8 * length * heads * head_size,
            transcendentals=heads * length * length // 2,
        ),
    )(raw, raw, raw, query_gain, key_gain, cosines, sines, seg_col, seg_row)


def run_attention_backward(
    raw, query_low, key_low, value_low, inverse, mixed, grad_mixed, heads, head_size, query_gain,
    cosines, sines, seg_col, seg_row,
):
    length = raw.shape[0]
    per_head = pl.BlockSpec((length, head_size), lambda head: (0, head))
    one = (length, head_size)
    return pl.pallas_call(
        attention_backward,
        grid=(heads,),
        in_specs=[
            per_head, per_head, whole(one), whole(one), per_head, per_head, per_head,
            whole((1, head_size)), whole(one), whole(one), whole(one), whole((8, length)),
        ],
        out_specs=[per_head, whole(one), whole(one), whole((8, head_size))],
        out_shape=[
            jax.ShapeDtypeStruct((length, heads * head_size), low),
            jax.ShapeDtypeStruct(one, high),
            jax.ShapeDtypeStruct(one, high),
            jax.ShapeDtypeStruct((8, head_size), high),
        ],
        compiler_params=pltpu.CompilerParams(vmem_limit_bytes=50 << 20),
        cost_estimate=pl.CostEstimate(
            flops=6 * heads * length * length * head_size, bytes_accessed=16 * length * heads * head_size,
            transcendentals=heads * length * length // 2,
        ),
    )(
        raw, query_low, key_low, value_low, inverse, mixed, grad_mixed, query_gain, cosines, sines,
        seg_col, seg_row,
    )


MESH = pl.DeviceIdType.MESH
VMEM = pl.BlockSpec(memory_space=pltpu.VMEM)
ANY = pl.BlockSpec(memory_space=pl.ANY)


def wait_all(copies):
    for copy in copies:
        copy.wait()


class Chain:
    def __init__(self):
        self.n = lax.axis_size("expert") // 2
        me = lax.axis_index("expert")
        self.z, self.c = me // 2, me % 2
        self.sibling, self.up, self.down = me + 1 - 2 * self.c, me + 2, me - 2
        self.has_up, self.has_down = self.z < self.n - 1, self.z > 0

    def greet(self, others=()):
        barrier = pltpu.get_barrier_semaphore()

        def signal(peer):
            pl.semaphore_signal(barrier, inc=1, device_id={"expert": peer}, device_id_type=MESH)

        signal(self.sibling)
        pl.when(self.has_up)(lambda: signal(self.up))
        pl.when(self.has_down)(lambda: signal(self.down))
        for device in others:
            pl.semaphore_signal(barrier, inc=1, device_id=device, device_id_type=MESH)
        peers = 1 + len(others) + self.has_up.astype(jnp.int32) + self.has_down.astype(jnp.int32)
        pl.semaphore_wait(barrier, peers)

    def nearest(self, step):
        turn = jnp.int32(0)
        for z in range(self.n):
            order = sorted(range(self.n), key=lambda other: (abs(other - z), other))
            for at, chip in enumerate(order):
                turn = jnp.where((self.z == z) & (step == at), chip, turn)
        return turn


class Gather:
    def __init__(self, chain, own, block, send, recv, local):
        self.chain, self.own, self.block = chain, own, block
        self.send, self.recv, self.local = send, recv, local

    @staticmethod
    def semaphores(n):
        return [
            pltpu.SemaphoreType.DMA((3, n)),
            pltpu.SemaphoreType.DMA((2 * n,)),
            pltpu.SemaphoreType.DMA(()),
        ]

    def copy(self, source, z, way, peer):
        c = self.chain.c
        return pltpu.make_async_remote_copy(
            src_ref=source,
            dst_ref=self.block(z, c),
            send_sem=self.send.at[way, z],
            recv_sem=self.recv.at[2 * z + c],
            device_id={"expert": peer},
            device_id_type=MESH,
        )

    def wait_block(self, z, c):
        block = self.block(z, c)
        pltpu.make_async_remote_copy(
            src_ref=block,
            dst_ref=block,
            send_sem=self.send.at[0, z],
            recv_sem=self.recv.at[2 * z + c],
            device_id={"expert": self.chain.sibling},
            device_id_type=MESH,
        ).wait_recv()

    def keep(self):
        return pltpu.make_async_copy(self.own, self.block(self.chain.z, self.chain.c), self.local)

    def begin(self):
        ch = self.chain
        pl.when(ch.has_up)(lambda: self.copy(self.own, ch.z, 0, ch.up).start())
        pl.when(ch.has_down)(lambda: self.copy(self.own, ch.z, 1, ch.down).start())
        self.copy(self.own, ch.z, 2, ch.sibling).start()
        self.keep().start()

    def service(self, step):
        ch = self.chain

        def from_below():
            z = ch.z - step
            self.wait_block(z, ch.c)
            pl.when(ch.has_up)(lambda: self.copy(self.block(z, ch.c), z, 0, ch.up).start())
            self.copy(self.block(z, ch.c), z, 2, ch.sibling).start()

        def from_above():
            z = ch.z + step
            self.wait_block(z, ch.c)
            pl.when(ch.has_down)(lambda: self.copy(self.block(z, ch.c), z, 1, ch.down).start())
            self.copy(self.block(z, ch.c), z, 2, ch.sibling).start()

        pl.when(ch.z - step >= 0)(from_below)
        pl.when(ch.z + step < ch.n)(from_above)

    def wait_sibling(self, z):
        self.wait_block(z, 1 - self.chain.c)

    def finish(self):
        ch = self.chain
        for z in range(ch.n):
            at = jnp.int32(z)
            block = self.block(at, ch.c)
            pl.when(ch.has_up & (ch.z >= z))(lambda: self.copy(block, at, 0, ch.up).wait_send())
            pl.when(ch.has_down & (ch.z <= z))(lambda: self.copy(block, at, 1, ch.down).wait_send())
            self.copy(block, at, 2, ch.sibling).wait_send()


class NearGather(Gather):
    def __init__(self, chain, own, near, block, send, recv, local):
        super().__init__(chain, own, block, send, recv, local)
        self.near = near

    @staticmethod
    def semaphores(n):
        return Gather.semaphores(n)[:2] + [pltpu.SemaphoreType.DMA((4,))]

    def place(self, at):
        ch = self.chain
        source = self.own if at == 3 else self.near.at[at]
        z, c = ((ch.z - 1, ch.c), (ch.z + 1, ch.c), (ch.z, 1 - ch.c), (ch.z, ch.c))[at]
        return pltpu.make_async_copy(source, self.block(z, c), self.local.at[at])

    def begin(self):
        ch = self.chain

        def below():
            pl.when(ch.has_up)(lambda: self.copy(self.near.at[0], ch.z - 1, 0, ch.up).start())
            self.copy(self.near.at[0], ch.z - 1, 2, ch.sibling).start()
            self.place(0).start()

        def above():
            pl.when(ch.has_down)(lambda: self.copy(self.near.at[1], ch.z + 1, 1, ch.down).start())
            self.copy(self.near.at[1], ch.z + 1, 2, ch.sibling).start()
            self.place(1).start()

        pl.when(ch.has_down)(below)
        pl.when(ch.has_up)(above)
        self.place(2).start()
        self.place(3).start()

    def wait_placed(self):
        pl.when(self.chain.has_down)(lambda: self.place(0).wait())
        pl.when(self.chain.has_up)(lambda: self.place(1).wait())
        self.place(2).wait()
        self.place(3).wait()

    def finish(self):
        ch = self.chain
        for z in range(ch.n):
            at = jnp.int32(z)
            block = self.block(at, ch.c)
            pl.when(ch.has_up & (ch.z > z))(lambda: self.copy(block, at, 0, ch.up).wait_send())
            pl.when(ch.has_down & (ch.z < z))(lambda: self.copy(block, at, 1, ch.down).wait_send())
            pl.when(ch.z != z)(lambda: self.copy(block, at, 2, ch.sibling).wait_send())


class Scatter:
    def __init__(self, chain, half, pair, flow, pair_send, pair_recv, flow_send, flow_recv):
        self.chain, self.half, self.pair, self.flow = chain, half, pair, flow
        self.pair_send, self.pair_recv = pair_send, pair_recv
        self.flow_send, self.flow_recv = flow_send, flow_recv

    @staticmethod
    def buffers(n, rows, width):
        return [
            pltpu.VMEM((n, rows, width), low),
            pltpu.VMEM((n + 1, rows, width), low),
            pltpu.SemaphoreType.DMA((n,)),
            pltpu.SemaphoreType.DMA((n,)),
            pltpu.SemaphoreType.DMA((n,)),
            pltpu.SemaphoreType.DMA((n + 1,)),
        ]

    def pair_copy(self, z):
        ch = self.chain
        return pltpu.make_async_remote_copy(
            src_ref=self.half(z, 1 - ch.c),
            dst_ref=self.pair.at[z],
            send_sem=self.pair_send.at[z],
            recv_sem=self.pair_recv.at[z],
            device_id={"expert": ch.sibling},
            device_id_type=MESH,
        )

    def flow_copy(self, z, slot, peer):
        return pltpu.make_async_remote_copy(
            src_ref=self.pair.at[z],
            dst_ref=self.flow.at[slot],
            send_sem=self.flow_send.at[z],
            recv_sem=self.flow_recv.at[slot],
            device_id={"expert": peer},
            device_id_type=MESH,
        )

    def wait_flow(self, slot):
        block = self.flow.at[slot]
        pltpu.make_async_remote_copy(
            src_ref=block,
            dst_ref=block,
            send_sem=self.flow_send.at[0],
            recv_sem=self.flow_recv.at[slot],
            device_id={"expert": self.chain.sibling},
            device_id_type=MESH,
        ).wait_recv()

    def start_pair(self, z):
        self.pair_copy(z).start()

    def add_pair(self, z, relayed):
        self.pair_copy(z).wait_recv()
        half = self.half(z, self.chain.c)

        def alone():
            self.pair[z] = (half[...].astype(high) + self.pair[z].astype(high)).astype(low)

        def with_flow():
            self.wait_flow(z)
            total = half[...].astype(high) + self.pair[z].astype(high) + self.flow[z].astype(high)
            self.pair[z] = total.astype(low)

        pl.when(relayed)(with_flow)
        pl.when(jnp.logical_not(relayed))(alone)

    def step(self, distance):
        ch = self.chain

        def upward():
            z = ch.z + distance
            self.add_pair(z, ch.has_down)
            self.flow_copy(z, z, ch.up).start()

        def downward():
            z = ch.z - distance
            self.add_pair(z, ch.has_up)
            self.flow_copy(z, jnp.where(distance == 1, ch.n, z), ch.down).start()

        pl.when(ch.z + distance < ch.n)(upward)
        pl.when(ch.z - distance >= 0)(downward)

    def total(self, result):
        ch = self.chain
        self.pair_copy(ch.z).wait_recv()
        result[...] = self.half(ch.z, ch.c)[...].astype(high) + self.pair[ch.z].astype(high)

        def add(slot):
            self.wait_flow(slot)
            result[...] += self.flow[slot].astype(high)

        pl.when(ch.has_down)(lambda: add(ch.z))
        pl.when(ch.has_up)(lambda: add(ch.n))

    def finish(self):
        ch = self.chain
        for z in range(ch.n):
            at = jnp.int32(z)
            self.pair_copy(at).wait_send()
            pl.when(ch.z != z)(lambda: self.flow_copy(at, at, ch.sibling).wait_send())


class Ports:
    def __init__(self, send, recv):
        self.send, self.recv, self.used, self.started = send, recv, 0, []

    def copy(self, source, target, device):
        at = self.used
        self.used += 1
        copy = pltpu.make_async_remote_copy(
            src_ref=source,
            dst_ref=target,
            send_sem=self.send.at[at],
            recv_sem=self.recv.at[at],
            device_id=device,
            device_id_type=MESH,
        )
        self.started.append(copy)
        return copy

    def finish(self):
        for copy in self.started:
            copy.wait_send()


def square():
    group = lax.axis_index("dp")
    y, x = group // 2, group % 2
    from_x, from_y = 2 * y + 1 - x, 2 * (1 - y) + x
    return group, y, x, from_x, from_y


class SquareSum:
    def __init__(self, source, result, first_a, first_b, second_a, second_b, send_a, send_b, ports):
        self.source, self.result = source, result
        self.own, self.y, self.x, self.from_x, self.from_y = square()
        self.first_a, self.first_b, self.second_a, self.second_b = first_a, first_b, second_a, second_b
        self.send_a, self.send_b = send_a, send_b
        self.rows, self.middle = source.shape[0] // 4, source.shape[1] // 2
        beside, across = {"dp": self.from_x}, {"dp": self.from_y}
        self.first = []
        for k in range(2):
            self.first.append(ports.copy(self.part(source, 0, 2 * k + 1 - self.x), first_a.at[k], beside))
            self.first.append(ports.copy(self.part(source, 1, 2 * (1 - self.y) + k), first_b.at[k], across))
        self.second = [ports.copy(send_a, second_a, across), ports.copy(send_b, second_b, beside)]

    @staticmethod
    def buffers(rows, columns):
        quarter = (rows // 4, columns // 2)
        return [pltpu.VMEM((2, *quarter), low)] * 2 + [pltpu.VMEM(quarter, low)] * 4

    def part(self, ref, side, quarter):
        rows = pl.ds(pl.multiple_of(quarter * self.rows, self.rows), self.rows)
        return ref.at[rows, pl.ds(side * self.middle, self.middle)]

    @staticmethod
    def start(copies):
        for copy in copies:
            copy.start()

    @staticmethod
    def arrive(copies):
        for copy in copies:
            copy.wait_recv()

    def begin(self):
        self.start(self.first)

    def exchange(self):
        self.arrive(self.first)
        along_y = self.part(self.source, 0, self.from_y)[...].astype(high)
        self.send_a[...] = (along_y + self.first_a[1 - self.y].astype(high)).astype(low)
        along_x = self.part(self.source, 1, self.from_x)[...].astype(high)
        self.send_b[...] = (along_x + self.first_b[1 - self.x].astype(high)).astype(low)
        self.start(self.second)

    def settle(self):
        self.arrive(self.second)
        for side, first, second in (
            (0, self.first_a[self.y], self.second_a), (1, self.first_b[self.x], self.second_b)
        ):
            total = self.part(self.source, side, self.own)[...].astype(high) + first.astype(high)
            columns = pl.ds(side * self.middle, self.middle)
            self.result[:, columns] = (total + second[...].astype(high)).astype(low)


class WideSum:
    def __init__(self, grads):
        self.grads = grads
        self.own, self.y, self.x, self.from_x, self.from_y = square()
        self.middle = grads.shape[2] // 2
        self.beside, self.across = {"dp": self.from_x}, {"dp": self.from_y}

    def part(self, side, quarter):
        return self.grads.at[quarter, :, pl.ds(side * self.middle, self.middle)]

    def first(self, first_a, first_b, ports):
        copies = []
        for k in range(2):
            copies.append(ports.copy(self.part(0, 2 * k + 1 - self.x), first_a.at[k], self.beside))
            copies.append(ports.copy(self.part(1, 2 * (1 - self.y) + k), first_b.at[k], self.across))
        return copies

    def load(self, first_a, first_b, left, right, sems):
        pairs = (
            (self.part(0, self.from_y), left.at[0]), (first_a.at[1 - self.y], left.at[1]),
            (self.part(1, self.from_x), right.at[0]), (first_b.at[1 - self.x], right.at[1]),
        )
        return [pltpu.make_async_copy(source, target, sems.at[at]) for at, (source, target) in enumerate(pairs)]

    def second(self, left, right, second_a, second_b, ports):
        for both in (left, right):
            both[0] = (both[0].astype(high) + both[1].astype(high)).astype(low)
        return [
            ports.copy(left.at[0], second_a, self.across),
            ports.copy(right.at[0], second_b, self.beside),
        ]


def wide_shapes(grads):
    _, rows, columns = grads.shape
    first = jax.ShapeDtypeStruct((2, rows, columns // 2), low)
    second = jax.ShapeDtypeStruct((rows, columns // 2), low)
    return [first, first], [second, second]


class SquareCopy:
    def __init__(self, mine, result, ports):
        own, _, _, from_x, from_y = square()
        rows, middle = mine.shape[0], mine.shape[1] // 2
        beside, across = {"dp": from_x}, {"dp": from_y}

        def quarter(at):
            return pl.ds(pl.multiple_of(at * rows, rows), rows)

        target = result.at[quarter(own)]
        self.mine, self.target = mine, target
        self.near = [ports.copy(mine, target, beside), ports.copy(mine, target, across)]
        left = result.at[quarter(from_x), pl.ds(0, middle)]
        right = result.at[quarter(from_y), pl.ds(middle, middle)]
        self.far = [ports.copy(left, left, across), ports.copy(right, right, beside)]

    def begin(self):
        SquareSum.start(self.near)
        self.target[...] = self.mine[...]

    def hand_on(self):
        SquareSum.arrive(self.near)
        SquareSum.start(self.far)

    def finish(self):
        SquareSum.arrive(self.far)


def row_block(ref, rows):
    return lambda z, c: ref.at[pl.ds(pl.multiple_of((2 * z + c) * rows, rows), rows)]


def chip_block(ref, rows):
    return lambda z, c: ref.at[z, pl.ds(pl.multiple_of(c * rows, rows), rows)]


def communicating(collective_id, mebibytes=60):
    return pltpu.CompilerParams(
        collective_id=collective_id, has_side_effects=True, vmem_limit_bytes=mebibytes << 20
    )


def gather_kernel(
    tokens_ref, gain_ref, routes_ref, segments_ref, cot_ref, query_hbm, key_hbm, value_hbm,
    hidden_hbm, all_named_ref, near_ref, col_ref, projection_hbm, raw_hbm,
    named_ref, own, stage, hidden_ref, projection_ref, raw_ref, query_ref, key_ref, value_ref,
    send_a, recv_a, local_a, send_b, recv_b, local_b, name_send, name_recv,
    swap_send, swap_recv, x_send, x_recv, y_send, y_recv, far_send, far_recv, out_sems, load_sems,
    near_send, near_recv,
):
    chain = Chain()
    n = chain.n
    peers = 2 * n
    me = lax.axis_index("expert")
    group, _, _, from_x, from_y = square()
    far = 3 - group
    beside, across = {"dp": from_x}, {"dp": from_y}
    sources = [(2 * chain.nearest(step) + core, core, step) for step in range(n) for core in range(2)]
    others = [chain.sibling] + [source for source, _, step in sources if step > 0]
    barrier = pltpu.get_barrier_semaphore()
    for device in [{"expert": peer} for peer in others] + [beside, across]:
        pl.semaphore_signal(barrier, inc=1, device_id=device, device_id_type=MESH)
    rows = stage.shape[1]
    quarter = pl.ds(pl.multiple_of(group * rows, rows), rows)
    loads = [
        pltpu.make_async_copy(source.at[quarter], target, load_sems.at[at])
        for at, (source, target) in enumerate(
            ((query_hbm, query_ref), (key_hbm, key_ref), (value_hbm, value_ref))
        )
    ]
    for load in loads:
        load.start()
    query_width = query_ref.shape[1] // peers
    head_size = key_ref.shape[1] // n
    own[...] = norm_rows(tokens_ref[...].astype(high), gain_ref[...]).astype(low)
    lanes = lax.broadcasted_iota(jnp.int32, named_ref.shape, 1)
    named = jnp.zeros(named_ref.shape, high)
    routes = routes_ref[...].astype(high).T.astype(jnp.int32)
    for at in range(routes.shape[1]):
        named = jnp.where(routes[:, at : at + 1] == lanes, 1.0, named)
    named_ref[...] = named.astype(low)
    for load in loads:
        load.wait()
    for peer in range(peers):
        shared = pl.ds(peer // 2 * head_size, head_size)
        stage[peer, :, :query_width] = query_ref[:, pl.ds(peer * query_width, query_width)]
        stage[peer, :, query_width : query_width + head_size] = key_ref[:, shared]
        stage[peer, :, query_width + head_size :] = value_ref[:, shared]
    pl.semaphore_wait(barrier, peers + 1)

    def remote(source, target, send, recv, device):
        return pltpu.make_async_remote_copy(
            src_ref=source, dst_ref=target, send_sem=send, recv_sem=recv, device_id=device, device_id_type=MESH
        )

    def block(source, place):
        return projection_ref.at[source, place]

    swaps = [
        remote(stage.at[peer], block(me, group), swap_send.at[at], swap_recv.at[me], {"expert": peer})
        for at, peer in enumerate(others)
    ]
    for copy in swaps:
        copy.start()
    length = own.shape[0]
    piece = length // 2

    def half_block(half):
        def block_of(z, c):
            return hidden_ref.at[pl.ds(pl.multiple_of((2 * z + c) * length + half * piece, piece), piece)]

        return block_of

    wide = [
        Gather(chain, own.at[pl.ds(half * piece, piece)], half_block(half), *sems)
        for half, sems in enumerate(((send_a, recv_a, local_a), (send_b, recv_b, local_b)))
    ]
    for gather in wide:
        gather.begin()
    names = [
        remote(named_ref, all_named_ref.at[me], name_send.at[at], name_recv.at[me], {"expert": peer})
        for at, peer in enumerate(others)
    ]
    for copy in names:
        copy.start()
    all_named_ref[me] = named_ref[...]
    row = jnp.broadcast_to(segments_ref[...].astype(high), (col_ref.shape[1], col_ref.shape[0]))
    col_ref[...] = row.T.astype(jnp.int32)
    projection_ref[me, group] = stage[me]

    def to_x(at, source, place):
        part = block(source, place)
        return remote(part, part, x_send.at[at], x_recv.at[source], beside)

    def to_y(at, source, place):
        part = block(source, place)
        return remote(part, part, y_send.at[at], y_recv.at[source], across)

    def to_far(at, core, source, place):
        part = block(source, place)
        return remote(part, part, far_send.at[at], far_recv.at[source], across if core == 0 else beside)

    def wait_swap(source):
        part = block(source, group)
        remote(part, part, swap_send.at[0], swap_recv.at[source], {"expert": chain.sibling}).wait_recv()

    for at, (source, core, step) in enumerate(sources):
        if step == 0:
            pl.when(chain.c != core)(lambda: wait_swap(source))
        else:
            wait_swap(source)
        to_x(at, source, group).start()
        to_y(at, source, group).start()
    for gather in wide:
        gather.service(1)
    for at, (source, core, _) in enumerate(sources):
        to_x(at, source, from_x).wait_recv()
        to_y(at, source, from_y).wait_recv()
        to_far(at, core, source, from_x if core == 0 else from_y).start()
    for step in range(2, n):
        for gather in wide:
            gather.service(step)

    def near(slot, peer):
        return remote(cot_ref, near_ref.at[slot], near_send.at[slot], near_recv.at[slot], {"expert": peer})

    pl.when(chain.has_up)(lambda: near(0, chain.up).start())
    pl.when(chain.has_down)(lambda: near(1, chain.down).start())
    near(2, chain.sibling).start()
    for gather in wide:
        for z in range(n):
            gather.wait_sibling(jnp.int32(z))
        gather.keep().wait()
    hidden_out = pltpu.make_async_copy(hidden_ref, hidden_hbm, out_sems.at[0])
    hidden_out.start()
    for at, (source, core, _) in enumerate(sources):
        to_far(at, core, source, far).wait_recv()
    projection_out = pltpu.make_async_copy(projection_ref, projection_hbm, out_sems.at[1])
    projection_out.start()
    pair_rows = 2 * own.shape[0]
    shard_rows = 4 * rows

    def raw_out(step):
        tokens = pl.ds(pl.multiple_of(step * pair_rows, pair_rows), pair_rows)
        return pltpu.make_async_copy(raw_ref.at[tokens], raw_hbm.at[tokens], out_sems.at[2 + step])

    @pl.loop(0, n)
    def each(step):
        tokens = pl.ds(pl.multiple_of(step * pair_rows, pair_rows), pair_rows)
        total = jnp.zeros((pair_rows, raw_ref.shape[1]), high)
        for source in range(peers):
            weight = projection_ref[source].reshape(shard_rows, raw_ref.shape[1])
            total = total + dot(hidden_ref[tokens, source * shard_rows : (source + 1) * shard_rows], weight)
        raw_ref[tokens] = total
        raw_out(step).start()

    for gather in wide:
        gather.finish()
    for at, peer in enumerate(others):
        part = all_named_ref.at[peer]
        remote(part, part, name_send.at[at], name_recv.at[peer], {"expert": peer}).wait_recv()
        names[at].wait_send()
    for at, (source, core, _) in enumerate(sources):
        to_x(at, source, group).wait_send()
        to_y(at, source, group).wait_send()
        to_far(at, core, source, from_x if core == 0 else from_y).wait_send()
    for copy in swaps:
        copy.wait_send()
    pl.when(chain.has_up)(lambda: near(0, chain.up).wait_send())
    pl.when(chain.has_down)(lambda: near(1, chain.down).wait_send())
    near(2, chain.sibling).wait_send()
    pl.when(chain.has_down)(lambda: near(0, chain.sibling).wait_recv())
    pl.when(chain.has_up)(lambda: near(1, chain.sibling).wait_recv())
    near(2, chain.sibling).wait_recv()
    hidden_out.wait()
    projection_out.wait()
    for step in range(n):
        raw_out(step).wait()


def run_gather(tokens, gain, routes, segments, cotangent, query_weight, key_matrix, value_matrix, peers, groups):
    length, width = tokens.shape
    n = peers // 2
    shard_rows, query_columns = query_weight.shape
    columns = query_columns // peers + 2 * key_matrix.shape[1] // n
    rows = shard_rows // groups
    dma = pltpu.SemaphoreType.DMA
    hidden, all_named, near, seg_col, projection, raw = pl.pallas_call(
        gather_kernel,
        out_shape=[
            jax.ShapeDtypeStruct((length * peers, width), low),
            jax.ShapeDtypeStruct((peers, length, 128), low),
            jax.ShapeDtypeStruct((3, length, width), low),
            jax.ShapeDtypeStruct((length * peers, 128), jnp.int32),
            jax.ShapeDtypeStruct((peers, groups, rows, columns), low),
            jax.ShapeDtypeStruct((length * peers, columns), high),
        ],
        in_specs=[VMEM] * 5 + [ANY] * 3,
        out_specs=[ANY, VMEM, VMEM, VMEM, ANY, ANY],
        scratch_shapes=[
            pltpu.VMEM((length, 128), low),
            pltpu.VMEM((length, width), low),
            pltpu.VMEM((peers, rows, columns), low),
            pltpu.VMEM((length * peers, width), low),
            pltpu.VMEM((peers, groups, rows, columns), low),
            pltpu.VMEM((length * peers, columns), high),
            pltpu.VMEM((rows, query_columns), low),
            pltpu.VMEM((rows, key_matrix.shape[1]), low),
            pltpu.VMEM((rows, key_matrix.shape[1]), low),
            *Gather.semaphores(n),
            *Gather.semaphores(n),
            dma((peers - 1,)), dma((peers,)),
            dma((peers - 1,)), dma((peers,)),
            dma((peers,)), dma((peers,)), dma((peers,)), dma((peers,)), dma((peers,)), dma((peers,)),
            dma((2 + n,)),
            dma((3,)), dma((3,)), dma((3,)),
        ],
        compiler_params=communicating(1),
        cost_estimate=pl.CostEstimate(flops=0, bytes_accessed=64 << 20, transcendentals=0),
        name="gather_hidden",
    )(tokens, gain, routes, segments, cotangent, query_weight, key_matrix, value_matrix)
    return hidden, all_named, near, seg_col, projection.reshape(width, columns), raw


def attention_heads(
    raw_ref, query_gain_ref, key_gain_ref, cos_ref, sin_ref, col_ref, row_ref,
    mixed_ref, query_low_ref, key_low_ref, value_low_ref, inverse_ref, value_wide,
):
    head_size = cos_ref.shape[1]
    heads = mixed_ref.shape[1] // head_size
    key_raw = raw_ref[:, heads * head_size : (heads + 1) * head_size]
    key_low_ref[...] = rotate(norm_rows(key_raw, key_gain_ref[...]), cos_ref[...], sin_ref[...]).astype(low)
    value_low_ref[...] = raw_ref[:, (heads + 1) * head_size :].astype(low)
    value_wide[:, :head_size] = value_low_ref[...]
    value_wide[:, head_size:] = jnp.ones_like(value_low_ref)

    @pl.loop(0, heads)
    def each(head):
        columns = pl.ds(pl.multiple_of(head * head_size, head_size), head_size)
        rotated = rotate(norm_rows(raw_ref[:, columns], query_gain_ref[...]), cos_ref[...], sin_ref[...])
        query_low_ref[:, columns] = (rotated * (head_size**-0.5 * log2e)).astype(low)
        for begin, rows, first, keys in key_spans(raw_ref.shape[0]):
            block = pl.ds(begin, rows)
            scores = dot_last(query_low_ref[block, columns], key_low_ref[pl.ds(first, keys)])
            allowed = tile_mask(col_ref, row_ref, begin, rows, first, keys)
            terms = jnp.where(allowed, jnp.exp2(scores), 0.0).astype(low)
            sums = dot(terms, value_wide[pl.ds(first, keys)])
            inverse = 1.0 / sums[:, head_size:]
            mixed_ref[block, columns] = (sums[:, :head_size] * inverse).astype(low)
            inverse_ref[block, columns] = inverse


class Split:
    both = slice(None)

    @staticmethod
    def take(ref, z, half, columns=slice(None)):
        block = ref[pl.ds(2 * z, 2), half, :, columns]
        return block.reshape(-1, block.shape[-1])

    @staticmethod
    def put(ref, z, half, value, columns=slice(None)):
        halves = (2, 2) if half is Split.both else (2,)
        ref[pl.ds(2 * z, 2), half, :, columns] = value.reshape(*halves, ref.shape[2], value.shape[1])

    @staticmethod
    def every(ref, columns=slice(None)):
        block = ref[:, :, :, columns]
        return block.reshape(block.shape[0] * block.shape[1] * block.shape[2], block.shape[3])


def expert_block(rows_all, plain_of, gate_w, up_w, gate_col, gated, grad_gate, grad_up, z, half):
    hidden = gate_w.shape[1]
    chunk = hidden // 3 if hidden % 384 == 0 else hidden
    gate_grad = jnp.zeros_like(gate_col)
    for begin in range(0, hidden, chunk):
        units = pl.ds(begin, chunk)
        gate_pre = dot(Split.take(rows_all, z, half), gate_w[:, units])
        up_pre = dot(Split.take(rows_all, z, half), up_w[:, units])
        plain = plain_of(units)
        share = 1.0 / (1.0 + jnp.exp(-gate_pre))
        silu = gate_pre * share
        act = silu * up_pre
        gate_grad = gate_grad + jnp.sum(act * plain, axis=-1, keepdims=True)
        Split.put(gated, z, half, (act * gate_col).astype(low), units)
        grad_act = plain * gate_col
        slope = share + silu * (1.0 - share)
        Split.put(grad_gate, z, half, (grad_act * up_pre * slope).astype(low), units)
        Split.put(grad_up, z, half, (grad_act * silu).astype(low), units)
    return gate_grad


def gate_columns(lanes, expert, gate_grad):
    sent = jnp.where(lanes == expert, gate_grad, 0.0)
    upper = sent.astype(low).astype(high)
    lower = (sent - upper).astype(low).astype(high)
    return upper + pltpu.roll(lower, 64, 1)


class Tiles:
    def __init__(self, grads, stage, sems, gated, grad_gate, grad_up, rows_all, cots):
        self.grads, self.stage, self.sems = grads, stage, sems
        self.sources = ((grad_gate, rows_all), (grad_up, rows_all), (gated, cots))
        self.groups = sems.shape[1]
        self.hidden = gated.shape[3]
        self.piece = self.hidden // self.groups
        self.tile = stage.shape[2]

    def copies(self, kind, at, slot):
        piece = self.piece
        made = []
        for part in range(self.groups):
            if kind < 2:
                columns = pl.ds(pl.multiple_of(at * self.tile, self.tile), self.tile)
                target = self.grads.at[part, pl.ds(kind * piece, piece), columns]
            else:
                columns = pl.ds(part * self.tile, self.tile)
                target = self.grads.at[at, pl.ds(2 * piece, piece), columns]
            source = self.stage.at[slot, pl.ds(part * piece, piece)]
            made.append(pltpu.make_async_copy(source, target, self.sems.at[slot, part]))
        return made

    def run(self, kind):
        left, right = self.sources[kind]

        @pl.loop(0, self.groups)
        def each(at):
            slot = at % 2
            if kind == 0:
                pl.when(at >= 2)(lambda: wait_all(self.copies(kind, at, slot)))
            else:
                wait_all(self.copies(kind, at, slot))
            span = pl.ds(pl.multiple_of(at * self.tile, self.tile), self.tile)
            self.stage[slot] = dot_first(Split.every(left), Split.every(right, span)).astype(low)
            for copy in self.copies(kind, at, slot):
                copy.start()

    def finish(self):
        for slot in range(2):
            wait_all(self.copies(0, jnp.int32(slot), slot))


def first_kernel(
    query_gain_ref, key_gain_ref, row_ref, tokens_ref, gain_ref, named_ref, router_in, cot_ref, near_ref,
    raw_hbm, cos_hbm, sin_hbm, col_hbm, weight_hbm, gate_hbm, up_hbm, down_hbm,
    key_low_ref, value_low_ref, own_gates_ref, resid_hbm, ffn_hbm, gates_hbm,
    mixed_hbm, query_low_hbm, inverse_hbm, rows_hbm, cots_hbm, gated_hbm, parts_hbm, grads_hbm,
    resid_ref, ffn_ref, gates_ref,
    raw_ref, cos_ref, sin_ref, col_ref, weight_ref, mixed_ref, query_low_ref, inverse_ref, value_wide, router_ref, plain, attn_parts, rows_all, cots, gate_w, up_w, down_w, gated, grad_gate, grad_up,
    part_stage, tile_stage, load_sems, rows_sems, part_sems, tile_sems, cot_send, cot_recv, cot_local, *transfers,
):
    chain = Chain()
    n = chain.n
    _, _, rows, width = rows_all.shape
    block_rows = 2 * rows
    loads = [
        pltpu.make_async_copy(source, target, load_sems.at[at])
        for at, (source, target) in enumerate(
            (
                (raw_hbm, raw_ref), (cos_hbm, cos_ref), (sin_hbm, sin_ref), (col_hbm, col_ref),
                (weight_hbm, weight_ref), (down_hbm.at[0], down_w), (gate_hbm.at[0], gate_w),
                (up_hbm.at[0], up_w),
            )
        )
    ]
    for load in loads:
        load.start()
    chain.greet()
    cot_gather = NearGather(
        chain, cot_ref, near_ref, lambda z, c: cots.at[2 * z + c], cot_send, cot_recv, cot_local
    )
    cot_gather.begin()
    wait_all(loads[:4])
    router_ref[...] = jnp.zeros_like(router_ref)
    router_ref[: router_in.shape[0]] = router_in[...]
    attention_heads(
        raw_ref, query_gain_ref, key_gain_ref, cos_ref, sin_ref, col_ref, row_ref,
        mixed_ref, query_low_ref, key_low_ref, value_low_ref, inverse_ref, value_wide,
    )
    attention_copies = [
        pltpu.make_async_copy(source, target, rows_sems.at[2 + at])
        for at, (source, target) in enumerate(
            ((mixed_ref, mixed_hbm), (query_low_ref, query_low_hbm), (inverse_ref, inverse_hbm))
        )
    ]
    for copy in attention_copies:
        copy.start()
    loads[4].wait()
    scatters, gathers = [], []
    for half in range(2):
        pair, flow, *rest = transfers[9 * half : 9 * half + 9]
        scatters.append(
            Scatter(chain, lambda z, c, half=half: attn_parts.at[z, c, half], pair, flow, *rest[:4])
        )
        gathers.append(
            Gather(chain, ffn_ref.at[half], lambda z, c, half=half: rows_all.at[2 * z + c, half], *rest[4:])
        )

    def plain_rows(step):
        z = chain.nearest(step)
        pl.when(step == 0)(cot_gather.wait_placed)
        pl.when(step > 0)(lambda: cot_gather.wait_sibling(z))
        cot_rows = cots[pl.ds(2 * z, 2)].reshape(4 * rows, width)
        hidden = plain.shape[3]
        plain[pl.ds(2 * z, 2)] = dot_last(cot_rows, down_w[...]).reshape(2, 2, rows, hidden)

    @pl.loop(0, n)
    def project(step):
        z = chain.nearest(n - 1 - step)
        tokens = pl.ds(pl.multiple_of(z * 4 * rows, 4 * rows), 4 * rows)
        attn_parts[z] = dot(mixed_ref[tokens], weight_ref[...]).astype(low).reshape(2, 2, rows, width)
        for scatter in scatters:
            scatter.start_pair(z)
        pl.when(step < n - 1)(lambda: scatters[0].step(n - 1 - step))
        pl.when(step == 0)(lambda: loads[5].wait())
        pl.when(step == 1)(lambda: cot_gather.service(2))
        pl.when(step < n - 1)(lambda: plain_rows(step))

    def own_rows(half):
        span = pl.ds(half * rows, rows)
        scatters[half].total(resid_ref.at[span])
        resid_ref[span] += tokens_ref[span].astype(high)
        ffn_ref[half] = norm_rows(resid_ref[span], gain_ref[...]).astype(low)
        gathers[half].begin()

    scatters[1].step(n - 1)
    own_rows(0)
    scatters[1].step(n - 2)
    cot_gather.service(3)
    plain_rows(jnp.int32(3))
    lanes = lax.broadcasted_iota(jnp.int32, (block_rows, 128), 1)
    expert = lax.axis_index("expert") * gate_hbm.shape[0]
    tile = tile_stage.shape[2]
    wait_all(loads[6:])

    def part_copy(z, half, slot):
        return pltpu.make_async_copy(part_stage.at[slot], parts_hbm.at[pl.ds(2 * z, 2), half], part_sems.at[slot])

    @pl.loop(0, 2 * n)
    def each(turn):
        pl.when((turn >= 1) & (turn < n - 1))(lambda: gathers[0].service(turn))
        pl.when((turn >= 1) & (turn < n - 2))(lambda: scatters[1].step(n - 2 - turn))

        @pl.when(turn == n - 1)
        def middle():
            own_rows(1)
            gathers[0].service(n - 1)

        pl.when((turn >= n) & (turn < 2 * n - 1))(lambda: gathers[1].service(turn - n + 1))
        half, step = turn // n, turn % n
        z = chain.nearest(step)

        def arrived(gather):
            pl.when(step == 0)(lambda: gather.keep().wait())
            gather.wait_sibling(z)

        pl.when(half == 0)(lambda: arrived(gathers[0]))
        pl.when(half == 1)(lambda: arrived(gathers[1]))
        logits = dot_last(Split.take(rows_all, z, half), router_ref[...])
        named = Split.take(named_ref, z, half).astype(high) > 0.5
        top = jnp.max(jnp.where(named, logits, -1e30), axis=-1, keepdims=True)
        terms = jnp.where(named, jnp.exp(jnp.where(named, logits - top, 0.0)), 0.0)
        gates = terms / jnp.sum(terms, axis=-1, keepdims=True)
        Split.put(gates_ref, z, half, gates)

        @pl.when(step == 0)
        def own_gates():
            own_gates_ref[half] = jnp.where(chain.c == 0, gates[:rows], gates[rows:])

        gate_col = jnp.sum(jnp.where(lanes == expert, gates, 0.0), axis=-1, keepdims=True)
        gate_grad = expert_block(
            rows_all, lambda units: Split.take(plain, z, half, units), gate_w, up_w, gate_col, gated, grad_gate,
            grad_up, z, half,
        )
        slot = turn % 2

        pl.when(turn >= 2)(lambda: part_copy(z, half, slot).wait())

        @pl.loop(0, width // tile)
        def columns(at):
            span = pl.ds(pl.multiple_of(at * tile, tile), tile)
            grad_rows = dot_last(Split.take(grad_gate, z, half), gate_w[span, :])
            grad_rows = grad_rows + dot_last(Split.take(grad_up, z, half), up_w[span, :])
            part_stage[slot, :, :, span] = grad_rows.astype(low).reshape(2, rows, tile)

        sent = gate_columns(lanes, expert, gate_grad).astype(low)
        part_stage[slot, :, :, width:] = sent.reshape(2, rows, 128)
        part_copy(z, half, slot).start()

    whole_copies = [
        pltpu.make_async_copy(rows_all, rows_hbm, rows_sems.at[0]),
        pltpu.make_async_copy(cots, cots_hbm, rows_sems.at[1]),
        pltpu.make_async_copy(gated, gated_hbm, rows_sems.at[5]),
        pltpu.make_async_copy(resid_ref, resid_hbm, rows_sems.at[6]),
        pltpu.make_async_copy(ffn_ref, ffn_hbm, rows_sems.at[7]),
        pltpu.make_async_copy(gates_ref, gates_hbm, rows_sems.at[8]),
    ]
    for copy in whole_copies:
        copy.start()
    tiles = Tiles(grads_hbm, tile_stage, tile_sems, gated, grad_gate, grad_up, rows_all, cots)
    for kind in range(3):
        tiles.run(kind)
    for half in range(2):
        gathers[half].finish()
        scatters[half].finish()
    tiles.finish()
    for slot in range(2):
        part_copy(jnp.int32(0), 0, slot).wait()
    wait_all(whole_copies + attention_copies)
    cot_gather.finish()


def second_kernel(
    gates_ref, rows_hbm, cot_hbm, gate_hbm, up_hbm, down_hbm, parts_in, wide_hbm,
    sum_ref, gated_hbm, grads_hbm, first_a, first_b,
    rows_all, cots, gate_w, up_w, down_w, gated, grad_gate, grad_up, parts, tile_stage, load_sems, chip_sems,
    tile_sems, out_sem, port_send, port_recv, pair, flow, *scatter_sems,
):
    chain = Chain()
    n = chain.n
    width = rows_all.shape[3]
    block_rows = parts.shape[1]
    loads = [
        pltpu.make_async_copy(source, target, load_sems.at[at])
        for at, (source, target) in enumerate(
            (
                (gate_hbm.at[1], gate_w), (up_hbm.at[1], up_w), (down_hbm.at[1], down_w), (parts_in, parts),
            )
        )
    ]

    def chip_loads(z):
        block = pl.ds(2 * z, 2)
        return [
            pltpu.make_async_copy(rows_hbm.at[block], rows_all.at[block], chip_sems.at[0, z]),
            pltpu.make_async_copy(cot_hbm.at[block], cots.at[block], chip_sems.at[1, z]),
        ]

    for load in loads[:3]:
        load.start()
    for step in range(n):
        for load in chip_loads(chain.nearest(n - 1 - step)):
            load.start()
    loads[3].start()
    wide = WideSum(wide_hbm)
    chain.greet([wide.beside, wide.across])
    ports = Ports(port_send, port_recv)
    wide_sent = wide.first(first_a, first_b, ports)
    SquareSum.start(wide_sent)
    scatter = Scatter(chain, chip_block(parts, block_rows // 2), pair, flow, *scatter_sems)
    lanes = lax.broadcasted_iota(jnp.int32, (block_rows, 128), 1)
    expert = lax.axis_index("expert") * gate_hbm.shape[0] + 1
    tile = tile_stage.shape[2]
    wait_all(loads[:3])

    @pl.loop(0, n)
    def each(step):
        z = chain.nearest(n - 1 - step)
        wait_all(chip_loads(z))
        gates = Split.take(gates_ref, z, Split.both)
        gate_col = jnp.sum(jnp.where(lanes == expert, gates, 0.0), axis=-1, keepdims=True)
        gate_grad = expert_block(
            rows_all, lambda units: dot_last(Split.take(cots, z, Split.both), down_w[units, :]), gate_w, up_w,
            gate_col, gated, grad_gate, grad_up, z, Split.both,
        )
        pl.when(step == 0)(lambda: loads[3].wait())

        @pl.loop(0, width // tile)
        def columns(at):
            span = pl.ds(pl.multiple_of(at * tile, tile), tile)
            grad_rows = dot_last(Split.take(grad_gate, z, Split.both), gate_w[span, :])
            grad_rows = grad_rows + dot_last(Split.take(grad_up, z, Split.both), up_w[span, :])
            parts[z, :, span] = (parts[z, :, span].astype(high) + grad_rows).astype(low)

        sent = parts[z, :, width:].astype(high) + gate_columns(lanes, expert, gate_grad)
        parts[z, :, width:] = sent.astype(low)
        scatter.start_pair(z)
        pl.when(step < n - 1)(lambda: scatter.step(n - 1 - step))

    gated_copy = pltpu.make_async_copy(gated, gated_hbm, out_sem)
    gated_copy.start()
    tiles = Tiles(grads_hbm, tile_stage, tile_sems, gated, grad_gate, grad_up, rows_all, cots)
    for kind in range(3):
        tiles.run(kind)
    scatter.total(sum_ref)
    scatter.finish()
    tiles.finish()
    gated_copy.wait()
    SquareSum.arrive(wide_sent)
    ports.finish()


def split_rows(array, peers):
    return array.reshape(peers, 2, array.shape[0] // (2 * peers), array.shape[1])


def expert_scratch(gate_weight, up_weight, down_weight, peers, rows, width):
    hidden = gate_weight.shape[2]
    whole = pltpu.VMEM((peers, 2, rows, width), low)
    acts = pltpu.VMEM((peers, 2, rows, hidden), low)
    return [
        whole, whole,
        pltpu.VMEM(gate_weight.shape[1:], low),
        pltpu.VMEM(up_weight.shape[1:], low),
        pltpu.VMEM(down_weight.shape[1:], low),
        acts, acts, acts,
    ]


def run_first(
    raw, query_gain, key_gain, cosines, sines, seg_col, seg_row, weight, tokens, gain, named, router, cotangent, near, gate_weight, up_weight, down_weight,
    peers, groups,
):
    length, width = tokens.shape
    n, rows = peers // 2, length // 2
    hidden = gate_weight.shape[2]
    tile, sent = width // groups, width + 128
    full, local_width, head_size = length * peers, weight.shape[0], cosines.shape[1]
    dma = pltpu.SemaphoreType.DMA

    def split(columns, dtype):
        return jax.ShapeDtypeStruct((peers, 2, rows, columns), dtype)

    return pl.pallas_call(
        first_kernel,
        out_shape=[
            jax.ShapeDtypeStruct((full, head_size), low),
            jax.ShapeDtypeStruct((full, head_size), low),
            jax.ShapeDtypeStruct((2, rows, 128), high),
            jax.ShapeDtypeStruct((length, width), high),
            jax.ShapeDtypeStruct((2, rows, width), low),
            split(128, high),
            jax.ShapeDtypeStruct((full, local_width), low),
            jax.ShapeDtypeStruct((full, local_width), low),
            jax.ShapeDtypeStruct((full, local_width), high),
            split(width, low),
            split(width, low),
            split(hidden, low),
            split(sent, low),
            jax.ShapeDtypeStruct((groups, 3 * hidden // groups, width), low),
        ],
        in_specs=[VMEM] * 9 + [ANY] * 8,
        out_specs=[VMEM] * 3 + [ANY] * 11,
        scratch_shapes=[
            pltpu.VMEM((length, width), high),
            pltpu.VMEM((2, rows, width), low),
            pltpu.VMEM((peers, 2, rows, 128), high),
            pltpu.VMEM(raw.shape, high),
            pltpu.VMEM(cosines.shape, high),
            pltpu.VMEM(sines.shape, high),
            pltpu.VMEM(seg_col.shape, jnp.int32),
            pltpu.VMEM(weight.shape, low),
            pltpu.VMEM((full, local_width), low),
            pltpu.VMEM((full, local_width), low),
            pltpu.VMEM((full, local_width), high),
            pltpu.VMEM((full, 2 * head_size), low),
            pltpu.VMEM((128, width), low),
            pltpu.VMEM((peers, 2, rows, hidden), high),
            pltpu.VMEM((n, 2, 2, rows, width), low),
            *expert_scratch(gate_weight, up_weight, down_weight, peers, rows, width),
            pltpu.VMEM((2, 2, rows, sent), low),
            pltpu.VMEM((2, hidden, tile), low),
            dma((8,)), dma((9,)), dma((2,)), dma((2, groups)),
            *NearGather.semaphores(n),
            *(Scatter.buffers(n, rows, width) + Gather.semaphores(n)) * 2,
        ],
        compiler_params=communicating(3),
        cost_estimate=pl.CostEstimate(flops=0, bytes_accessed=120 << 20, transcendentals=0),
        name="attention_and_first_expert",
    )(
        query_gain, key_gain, seg_row, tokens, gain, split_rows(named.reshape(-1, 128), peers), router,
        cotangent.reshape(2, rows, width), near.reshape(3, 2, rows, width), raw, cosines, sines, seg_col, weight,
        gate_weight, up_weight, down_weight,
    )


def run_second(gates, rows_all, cotangents, gate_weight, up_weight, down_weight, parts, first_grads, peers, groups):
    _, _, rows, width = rows_all.shape
    n, length = peers // 2, 2 * rows
    hidden = gate_weight.shape[2]
    tile, sent = width // groups, width + 128
    dma = pltpu.SemaphoreType.DMA
    return pl.pallas_call(
        second_kernel,
        out_shape=[
            jax.ShapeDtypeStruct((length, sent), high),
            jax.ShapeDtypeStruct((peers, 2, rows, hidden), low),
            jax.ShapeDtypeStruct((groups, 3 * hidden // groups, width), low),
            *wide_shapes(first_grads)[0],
        ],
        in_specs=[VMEM] + [ANY] * 7,
        out_specs=[VMEM, ANY, ANY, ANY, ANY],
        scratch_shapes=[
            *expert_scratch(gate_weight, up_weight, down_weight, peers, rows, width),
            pltpu.VMEM((n, 2 * length, sent), low),
            pltpu.VMEM((2, hidden, tile), low),
            dma((4,)), dma((2, n)), dma((2, groups)), dma(()), dma((4,)), dma((4,)),
            *Scatter.buffers(n, length, sent),
        ],
        compiler_params=communicating(7),
        cost_estimate=pl.CostEstimate(flops=0, bytes_accessed=120 << 20, transcendentals=0),
        name="second_expert",
    )(
        gates, rows_all, cotangents, gate_weight, up_weight, down_weight, parts.reshape(n, 2 * length, sent),
        first_grads,
    )


def attention_block_backward(
    span_of, raw_ref, query_low_ref, key_low_ref, value_low_ref, inverse_ref, mixed_ref, grad_mixed_ref,
    query_gain_ref, cos_ref, sin_ref, col_ref, row_ref, grad_query_ref, grad_key_ref, grad_value_ref, grad_gain_ref,
):
    begin, rows, first, keys = span_of
    head_size = key_low_ref.shape[1]
    heads = query_low_ref.shape[1] // head_size
    block, span = pl.ds(begin, rows), pl.ds(first, keys)

    @pl.loop(0, heads)
    def each(head):
        columns = pl.ds(pl.multiple_of(head * head_size, head_size), head_size)
        query_low = query_low_ref[block, columns]
        key_low = key_low_ref[span]
        scaled = grad_mixed_ref[block, columns].astype(high) * inverse_ref[block, columns]
        row_term = jnp.sum(scaled * mixed_ref[block, columns].astype(high), axis=-1, keepdims=True)
        scaled = scaled.astype(low)
        scores = dot_last(query_low, key_low)
        allowed = tile_mask(col_ref, row_ref, begin, rows, first, keys)
        terms = jnp.where(allowed, jnp.exp2(scores), 0.0)
        grad_probs = dot_last(scaled, value_low_ref[span])
        grad_scores = (terms * (grad_probs - row_term)).astype(low)
        grad_value_ref[span] += dot_first(terms.astype(low), scaled)
        grad_key_ref[span] += dot_first(grad_scores, query_low) * (1.0 / log2e)
        grad_rotated = dot(grad_scores, key_low) * head_size**-0.5
        grad_normed = unrotate(grad_rotated, cos_ref[block], sin_ref[block])
        grad_raw, gain_rows = norm_back(raw_ref[block, columns], query_gain_ref[...], grad_normed)
        grad_query_ref[block, columns] = grad_raw.astype(low)
        grad_gain_ref[...] += jnp.broadcast_to(jnp.sum(gain_rows, axis=0, keepdims=True), grad_gain_ref.shape)


def input_kernel(
    sums_ref, own_gates_ref, ffn_ref, resid_ref, cot_ref, gain_ffn_ref, router_in, weight_ref,
    query_gain_ref, key_gain_ref, row_ref, tokens_ref, gain_ref,
    raw_hbm, query_low_hbm, key_low_hbm, value_low_hbm, inverse_hbm, mixed_hbm, cos_hbm, sin_hbm, col_hbm,
    projection_hbm, hidden_hbm, wide_0, wide_0a, wide_0b, wide_1,
    input_grad_ref, out_own_ref, gain_grad_ref, ffn_gain_grad_ref, query_gain_grad_ref, key_gain_grad_ref,
    router_grad_ref, projection_grad_hbm, second_a, second_b, first_a, first_b,
    raw_ref, query_low_ref, key_low_ref, value_low_ref, inverse_ref, mixed_ref, cos_ref, sin_ref, col_ref,
    projection_ref, hidden_ref,
    router_ref, own, attn_ref, grad_mixed, grad_resid, own_pair, their_pair, key_part, value_part, columns,
    parts, projection_grad, out_grad, load_sems, store_sem, swap_send, swap_recv, port_send, port_recv,
    wide_left, wide_right, wide_sems,
    send_a, recv_a, local_a, send_b, recv_b, local_b, pair, flow, *rest,
):
    chain = Chain()
    n = chain.n
    scatter_sems, square_buffers = rest[:4], rest[4:]
    full, head_size = key_part.shape
    _, _, rows, width = attn_ref.shape
    query_width = query_low_ref.shape[1]
    sources = (
        raw_hbm.at[:, pl.ds(0, query_width + head_size)], query_low_hbm, key_low_hbm, value_low_hbm, inverse_hbm, mixed_hbm, cos_hbm, sin_hbm, col_hbm,
        projection_hbm, hidden_hbm,
    )
    targets = (
        raw_ref, query_low_ref, key_low_ref, value_low_ref, inverse_ref, mixed_ref, cos_ref, sin_ref, col_ref,
        projection_ref, hidden_ref,
    )
    loads = [
        pltpu.make_async_copy(source, target, load_sems.at[at])
        for at, (source, target) in enumerate(zip(sources, targets))
    ]
    wide = WideSum(wide_0)
    wide_loads = wide.load(wide_0a, wide_0b, wide_left, wide_right, wide_sems)
    for load in wide_loads + loads:
        load.start()
    chain.greet([wide.beside, wide.across])
    ports = Ports(port_send, port_recv)
    wide_first = WideSum(wide_1).first(first_a, first_b, ports)
    SquareSum.start(wide_first)
    router_ref[...] = jnp.zeros_like(router_ref)
    router_ref[: router_in.shape[0]] = router_in[...]
    sent = sums_ref[:, width:]
    left = lax.broadcasted_iota(jnp.int32, sent.shape, 1) < 64
    grad_gates = jnp.where(left, sent + pltpu.roll(sent, 64, 1), 0.0)
    gates = own_gates_ref[...]
    inner = jnp.sum(gates * grad_gates, axis=-1, keepdims=True)
    grad_logits = (gates * (grad_gates - inner)).astype(low)
    grad_hidden = sums_ref[:, :width] + dot(grad_logits, router_ref[...])
    grad_rows, gain_rows = norm_back(resid_ref[...], gain_ffn_ref[...], grad_hidden)
    grad_resid[...] = cot_ref[...].astype(high) + grad_rows
    own[...] = grad_resid[...].astype(low).reshape(2, rows, width)
    gathers = [
        Gather(chain, own.at[half], lambda z, c, half=half: attn_ref.at[2 * z + c, half], *sems)
        for half, sems in enumerate(((send_a, recv_a, local_a), (send_b, recv_b, local_b)))
    ]
    for gather in gathers:
        gather.begin()
    wait_all(wide_loads)
    wide_second = wide.second(wide_left, wide_right, second_a, second_b, ports)
    SquareSum.start(wide_second)
    router_grad_ref[...] = dot_first(grad_logits, ffn_ref[...])[: router_grad_ref.shape[0]]
    ffn_gain_grad_ref[...] = jnp.broadcast_to(
        jnp.sum(gain_rows, axis=0, keepdims=True), ffn_gain_grad_ref.shape
    )
    key_part[...] = jnp.zeros_like(key_part)
    value_part[...] = jnp.zeros_like(value_part)
    query_gain_grad_ref[...] = jnp.zeros_like(query_gain_grad_ref)
    wait_all(loads[:9])
    spans = key_spans(full)

    @pl.loop(0, n)
    def blocks(step):
        z = chain.nearest(step)
        for gather in gathers:
            pl.when(step > 0)(lambda: gather.service(step))
        for gather in gathers:
            pl.when(step == 0)(lambda: gather.keep().wait())
            gather.wait_sibling(z)
        tokens = pl.ds(pl.multiple_of(z * 4 * rows, 4 * rows), 4 * rows)
        grad_mixed[tokens] = dot_last(Split.take(attn_ref, z, Split.both), weight_ref[...]).astype(low)
        for at, span_of in enumerate(spans):

            @pl.when(z == at)
            def backward():
                attention_block_backward(
                    span_of, raw_ref, query_low_ref, key_low_ref, value_low_ref, inverse_ref, mixed_ref, grad_mixed,
                    query_gain_ref, cos_ref, sin_ref, col_ref, row_ref, columns, key_part, value_part,
                    query_gain_grad_ref,
                )

    own_pair[:, :head_size] = key_part[...].astype(low)
    own_pair[:, head_size:] = value_part[...].astype(low)
    swap = pltpu.make_async_remote_copy(
        src_ref=own_pair,
        dst_ref=their_pair,
        send_sem=swap_send,
        recv_sem=swap_recv,
        device_id={"expert": chain.sibling},
        device_id_type=MESH,
    )
    swap.start()
    first = chain.c == 0
    wait_all(loads[9:])
    shared = pl.ds(query_width, head_size)
    projection_ref[:, shared] = jnp.where(
        first, projection_ref[:, shared], projection_ref[:, query_width + head_size :]
    )
    own_width = query_width + head_size
    swap.wait_recv()
    grad_key = key_part[...] + their_pair[:, :head_size].astype(high)
    grad_value = value_part[...] + their_pair[:, head_size:].astype(high)
    key_raw = raw_ref[:, query_width:]
    grad_key, gain_rows = norm_back(
        key_raw, key_gain_ref[...], unrotate(grad_key, cos_ref[...], sin_ref[...])
    )
    columns[:, query_width:] = jnp.where(first, grad_key, grad_value).astype(low)
    key_gain = jnp.where(first, jnp.sum(gain_rows, axis=0, keepdims=True), 0.0)
    key_gain_grad_ref[...] = jnp.broadcast_to(key_gain, key_gain_grad_ref.shape)
    pair_rows = parts.shape[1]
    scatter = Scatter(chain, chip_block(parts, pair_rows // 2), pair, flow, *scatter_sems)
    out_total = SquareSum(out_grad, out_own_ref, *square_buffers, ports)
    projection_tile = projection_grad.shape[0] // n
    out_tile = width // n

    @pl.loop(0, n)
    def each(step):
        z = chain.nearest(n - 1 - step)
        tokens = pl.ds(pl.multiple_of(z * pair_rows, pair_rows), pair_rows)
        parts[z] = dot_last(columns[tokens], projection_ref[:, :own_width]).astype(low)
        scatter.start_pair(z)
        pl.when(step < n - 1)(lambda: scatter.step(n - 1 - step))

        @pl.when(step == 0)
        def out_gradient():
            @pl.loop(0, n)
            def tiles(at):
                span = pl.ds(pl.multiple_of(at * out_tile, out_tile), out_tile)
                out_grad[:, span] = dot_first(mixed_ref[...], Split.every(attn_ref, span)).astype(low)

            out_total.begin()

        span = pl.ds(pl.multiple_of(step * projection_tile, projection_tile), projection_tile)
        projection_grad[span] = dot_first(hidden_ref[:, span], columns[...]).astype(low)

    projection_store = pltpu.make_async_copy(projection_grad, projection_grad_hbm, store_sem)
    projection_store.start()
    out_total.exchange()
    scatter.total(input_grad_ref)
    grad_rows, gain_rows = norm_back(tokens_ref[...].astype(high), gain_ref[...], input_grad_ref[...])
    input_grad_ref[...] = grad_resid[...] + grad_rows
    gain_grad_ref[...] = jnp.broadcast_to(jnp.sum(gain_rows, axis=0, keepdims=True), gain_grad_ref.shape)
    out_total.settle()
    SquareSum.arrive(wide_first + wide_second)
    swap.wait_send()
    for gather in gathers:
        gather.finish()
    scatter.finish()
    ports.finish()
    projection_store.wait()


def run_input(
    sums, own_gates, ffn, resid, cotangent, gain_ffn, router, out_weight, raw, query_low, key_low, value_low,
    inverse, mixed, query_gain, key_gain, cosines, sines, seg_col, seg_row, projection, hidden, tokens, gain,
    first_wide, second_grads, experts, peers,
):
    length, width = tokens.shape
    n, rows = peers // 2, length // 2
    full, head_size = key_low.shape
    query_width = query_low.shape[1]
    loaded = [
        raw, query_low, key_low, value_low, inverse, mixed, cosines, sines, seg_col, projection, hidden,
    ]
    dma = pltpu.SemaphoreType.DMA
    wide_first, wide_second = wide_shapes(second_grads)
    half = (2, *wide_second[0].shape)
    (
        input_grad, out_own, gain_grad, ffn_gain_grad, query_gain_grad, key_gain_grad, router_grad, projection_grad,
        *wide,
    ) = (
        pl.pallas_call(
            input_kernel,
            out_shape=[
                jax.ShapeDtypeStruct((length, width), high),
                jax.ShapeDtypeStruct((query_width // 4, width), low),
                jax.ShapeDtypeStruct((8, width), high),
                jax.ShapeDtypeStruct((8, width), high),
                jax.ShapeDtypeStruct((8, head_size), high),
                jax.ShapeDtypeStruct((8, head_size), high),
                jax.ShapeDtypeStruct((experts, width), high),
                jax.ShapeDtypeStruct((width, query_width + head_size), low),
                *wide_second,
                *wide_first,
            ],
            in_specs=[VMEM] * 13 + [ANY] * (len(loaded) + 4),
            out_specs=[VMEM] * 7 + [ANY] * 5,
            scratch_shapes=[
                pltpu.VMEM((full, query_width + head_size), high),
                *[pltpu.VMEM(array.shape, array.dtype) for array in loaded[1:]],
                pltpu.VMEM((128, width), low),
                pltpu.VMEM((2, rows, width), low),
                pltpu.VMEM((peers, 2, rows, width), low),
                pltpu.VMEM((full, query_width), low),
                pltpu.VMEM((length, width), high),
                pltpu.VMEM((full, 2 * head_size), low),
                pltpu.VMEM((full, 2 * head_size), low),
                pltpu.VMEM((full, head_size), high),
                pltpu.VMEM((full, head_size), high),
                pltpu.VMEM((full, query_width + head_size), low),
                pltpu.VMEM((n, 2 * length, width), low),
                pltpu.VMEM((width, query_width + head_size), low),
                pltpu.VMEM((query_width, width), low),
                dma((len(loaded),)), dma(()), dma(()), dma(()), dma((12,)), dma((12,)),
                pltpu.VMEM(half, low), pltpu.VMEM(half, low), dma((4,)),
                *Gather.semaphores(n) * 2,
                *Scatter.buffers(n, length, width),
                *SquareSum.buffers(query_width, width),
            ],
            compiler_params=communicating(5, 62),
            cost_estimate=pl.CostEstimate(flops=0, bytes_accessed=64 << 20, transcendentals=0),
            name="attention_backward_and_input",
        )(
            sums, own_gates.reshape(length, 128), ffn.reshape(length, width), resid, cotangent, gain_ffn, router,
            out_weight, query_gain, key_gain, seg_row, tokens, gain, *loaded, *first_wide, second_grads,
        )
    )
    return (
        input_grad, projection_grad, out_own, gain_grad, ffn_gain_grad, query_gain_grad, key_gain_grad, router_grad,
        wide[:2], wide[2:],
    )
def weights_kernel(
    attn_gain_ref, ffn_gain_ref, query_gain_ref, key_gain_ref, router_ref, out_own_ref, proj_hbm, resid_hbm,
    gated_0, gated_1, down_hbm, wide_hbm, wide_a, wide_b,
    query_grad_ref, key_grad_ref, value_grad_ref, out_grad_ref, small_out_ref, output_ref, wide_second_a, wide_second_b,
    proj_ref, resid_ref, gated, down_w, mixture, load_sems, all_proj, first_a, first_b, second_a, second_b,
    send_a, send_b, quarter, small, got, part, small_sum, total_mixture,
    port_send, port_recv, swap_send, swap_recv, send_1, recv_1, send_2, recv_2, send_3, recv_3,
    wide_left, wide_right, wide_sems, pair, flow, *scatter_sems,
):
    peers = lax.axis_size("expert")
    me = lax.axis_index("expert")
    group, y, x, from_x, from_y = square()
    beside, across = {"dp": from_x}, {"dp": from_y}
    chain = Chain()
    scatter = Scatter(chain, chip_block(mixture, resid_ref.shape[0]), pair, flow, *scatter_sems)
    loads = [
        pltpu.make_async_copy(source, target, load_sems.at[at])
        for at, (source, target) in enumerate(
            (
                (proj_hbm, proj_ref), (gated_0, gated.at[0]), (gated_1, gated.at[1]),
                (down_hbm, down_w), (resid_hbm, resid_ref),
            )
        )
    ]
    wide = WideSum(wide_hbm)
    wide_loads = wide.load(wide_a, wide_b, wide_left, wide_right, wide_sems)
    for load in wide_loads + loads:
        load.start()
    width = resid_ref.shape[1]
    head_size = query_gain_ref.shape[1]
    small[...] = jnp.zeros_like(small)
    small[0:1] = attn_gain_ref[0:1]
    small[1:2] = ffn_gain_ref[0:1]
    small[2:3, :head_size] = query_gain_ref[0:1]
    small[3:4, :head_size] = key_gain_ref[0:1]
    small[8:] = router_ref[...]
    piece = width // peers

    def small_piece(ref, peer):
        return ref.at[:, pl.ds(pl.multiple_of(peer * piece, piece), piece)]

    barrier = pltpu.get_barrier_semaphore()
    others = [(me + shift) % peers for shift in range(1, peers)]
    groups = [(group + shift) % 4 for shift in range(1, 4)]
    for peer in others:
        pl.semaphore_signal(barrier, inc=1, device_id={"expert": peer}, device_id_type=MESH)
    for other in groups:
        pl.semaphore_signal(barrier, inc=1, device_id={"dp": other}, device_id_type=MESH)
    pl.semaphore_wait(barrier, peers + 2)

    shard_rows, columns = proj_ref.shape[1:]
    rows, half = shard_rows // 4, peers // 2
    ports = Ports(port_send, port_recv)

    def proj_part(side, q, ref=proj_ref):
        return ref.at[pl.ds(side * half, half), pl.ds(pl.multiple_of(q * rows, rows), rows)]

    def remote(source, target, send, recv, device):
        return pltpu.make_async_remote_copy(
            src_ref=source, dst_ref=target, send_sem=send, recv_sem=recv, device_id=device, device_id_type=MESH
        )

    along_x = [2 * other + 1 - x for other in range(2)]
    along_y = [2 * (1 - y) + other for other in range(2)]
    proj_1a = [ports.copy(proj_part(0, along_x[k], proj_hbm), first_a.at[k], beside) for k in range(2)]
    proj_1b = [ports.copy(proj_part(1, along_y[k], proj_hbm), first_b.at[k], across) for k in range(2)]
    for copy in proj_1a + proj_1b:
        copy.start()

    small_1 = [
        remote(small_piece(small, peer), got.at[me], send_1.at[at], recv_1.at[me], {"expert": peer})
        for at, peer in enumerate(others)
    ]
    for copy in small_1:
        copy.start()
    got[me] = small_piece(small, me)[...]
    wait_all(loads)

    def mixture_rows(step):
        z = chain.nearest(chain.n - 1 - step)

        @pl.loop(0, 4)
        def columns(at):
            span = pl.ds(pl.multiple_of(at * (width // 4), width // 4), width // 4)
            mixture[z, :, span] = (dot(gated[0, z], down_w[0, :, span]) + dot(gated[1, z], down_w[1, :, span])).astype(low)

        scatter.start_pair(z)

    @pl.loop(0, chain.n)
    def each_chip(step):
        mixture_rows(step)


    own = group
    for_y, for_x = 2 * (1 - y) + x, 2 * y + 1 - x
    scatter.step(3) if chain.n > 3 else None
    for copy in proj_1a + proj_1b:
        copy.wait_recv()
    send_a[...] = (proj_part(0, for_y)[...].astype(high) + first_a[1 - y].astype(high)).astype(low)
    send_b[...] = (proj_part(1, for_x)[...].astype(high) + first_b[1 - x].astype(high)).astype(low)
    proj_2a = ports.copy(send_a, second_a, across)
    proj_2b = ports.copy(send_b, second_b, beside)
    proj_2a.start()
    proj_2b.start()
    wait_all(wide_loads)
    wide_sent = wide.second(wide_left, wide_right, wide_second_a, wide_second_b, ports)
    SquareSum.start(wide_sent)
    out_copy = SquareCopy(out_own_ref, out_grad_ref, ports)
    out_copy.begin()
    scatter.step(2) if chain.n > 2 else None

    for at, peer in enumerate(others):
        remote(got.at[peer], got.at[peer], send_1.at[at], recv_1.at[peer], {"expert": peer}).wait_recv()
    total = got[0]
    for at in range(1, peers):
        total = total + got[at]
    part[group] = total
    small_2 = [
        remote(part.at[group], part.at[group], send_2.at[at], recv_2.at[group], {"dp": other})
        for at, other in enumerate(groups)
    ]
    for copy in small_2:
        copy.start()

    proj_2a.wait_recv()
    proj_2b.wait_recv()
    for side, first, second, at in ((0, first_a, second_a, y), (1, first_b, second_b, x)):
        quarter[pl.ds(side * half, half)] = (
            proj_part(side, own)[...].astype(high) + first[at].astype(high) + second[...].astype(high)
        ).astype(low)
    swaps = [
        remote(quarter.at[peer], all_proj.at[own, me], swap_send.at[at], swap_recv.at[me], {"expert": peer})
        for at, peer in enumerate(others)
    ]
    for copy in swaps:
        copy.start()
    all_proj[own, me] = quarter[me]

    for at, other in enumerate(groups):
        remote(part.at[other], part.at[other], send_2.at[at], recv_2.at[other], {"dp": other}).wait_recv()
    total = part[0]
    for at in range(1, 4):
        total = total + part[at]
    small_sum[me] = total
    small_3 = [
        remote(small_sum.at[me], small_sum.at[me], send_3.at[at], recv_3.at[me], {"expert": peer})
        for at, peer in enumerate(others)
    ]
    for copy in small_3:
        copy.start()

    for at, peer in enumerate(others):
        block = all_proj.at[own, peer]
        remote(block, block, swap_send.at[at], swap_recv.at[peer], {"expert": peer}).wait_recv()
    proj_gx = ports.copy(all_proj.at[own], all_proj.at[own], beside)
    proj_gy = ports.copy(all_proj.at[own], all_proj.at[own], across)
    proj_gx.start()
    proj_gy.start()
    far = 3 - group
    scatter.step(1) if chain.n > 1 else None
    out_copy.hand_on()

    def proj_half(q, side):
        return all_proj.at[q, pl.ds(side * half, half)]

    proj_gx.wait_recv()
    proj_gy.wait_recv()
    proj_fa = ports.copy(proj_half(from_x, 0), proj_half(from_x, 0), across)
    proj_fb = ports.copy(proj_half(from_y, 1), proj_half(from_y, 1), beside)
    proj_fa.start()
    proj_fb.start()
    query_width = columns - head_size

    def spread(q):
        block = pl.ds(pl.multiple_of(q * rows, rows), rows)
        for peer in range(peers):
            query_grad_ref[block, peer * query_width : (peer + 1) * query_width] = all_proj[q, peer, :, :query_width]
            shared = key_grad_ref if peer % 2 == 0 else value_grad_ref
            at = peer // 2 * head_size
            shared[block, at : at + head_size] = all_proj[q, peer, :, query_width:]

    spread(own)
    spread(from_x)
    spread(from_y)
    for at, peer in enumerate(others):
        block = small_sum.at[peer]
        remote(block, block, send_3.at[at], recv_3.at[peer], {"expert": peer}).wait_recv()
    for peer in range(peers):
        small_out_ref[:, peer * piece : (peer + 1) * piece] = small_sum[peer]
    scatter.total(total_mixture)
    output_ref[...] = (resid_ref[...] + total_mixture[...]).astype(low)
    out_copy.finish()
    SquareSum.arrive(wide_sent)
    proj_fa.wait_recv()
    proj_fb.wait_recv()
    spread(far)
    ports.finish()
    scatter.finish()
    for copy in small_1 + small_2 + small_3 + swaps:
        copy.wait_send()


def run_weights(
    grad_projection, out_own, attn_gain, ffn_gain, query_gain, key_gain, router, resid, first_gated, second_gated,
    down_weight, second_wide, peers, kv_heads,
):
    width, columns = grad_projection.shape
    head_size = query_gain.shape[1]
    length = resid.shape[0]
    n = peers // 2
    shard_rows = width // peers
    rows, half = shard_rows // 4, peers // 2
    small_rows = 8 + router.shape[0]
    piece = (small_rows, width // peers)
    hidden = down_weight.shape[1]
    dma = pltpu.SemaphoreType.DMA
    kv_width = kv_heads * head_size
    query_width = columns - head_size

    _, wide_second = wide_shapes(second_wide[0])
    wide_half = (2, *wide_second[0].shape)

    def low_buffer(*shape):
        return pltpu.VMEM(shape, low)

    return pl.pallas_call(
        weights_kernel,
        out_shape=[
            jax.ShapeDtypeStruct((shard_rows, peers * query_width), low),
            jax.ShapeDtypeStruct((shard_rows, kv_width), low),
            jax.ShapeDtypeStruct((shard_rows, kv_width), low),
            jax.ShapeDtypeStruct((4 * out_own.shape[0], width), low),
            jax.ShapeDtypeStruct((small_rows, width), high),
            jax.ShapeDtypeStruct((length, width), low),
            *wide_second,
        ],
        in_specs=[VMEM] * 6 + [ANY] * 8,
        out_specs=[VMEM] * 6 + [ANY] * 2,
        scratch_shapes=[
            low_buffer(peers, shard_rows, columns),
            pltpu.VMEM(resid.shape, high),
            low_buffer(2, n, 2 * length, hidden),
            low_buffer(*down_weight.shape),
            low_buffer(n, 2 * length, width),
            dma((5,)),
            low_buffer(4, peers, rows, columns),
            low_buffer(2, half, rows, columns),
            low_buffer(2, half, rows, columns),
            low_buffer(half, rows, columns),
            low_buffer(half, rows, columns),
            low_buffer(half, rows, columns),
            low_buffer(half, rows, columns),
            low_buffer(peers, rows, columns),
            pltpu.VMEM((small_rows, width), high),
            pltpu.VMEM((peers, *piece), high),
            pltpu.VMEM((4, *piece), high),
            pltpu.VMEM((peers, *piece), high),
            pltpu.VMEM((length, width), high),
            dma((16,)), dma((16,)),
            dma((peers - 1,)), dma((peers,)),
            dma((peers - 1,)), dma((peers,)),
            dma((3,)), dma((4,)),
            dma((peers - 1,)), dma((peers,)),
            low_buffer(*wide_half), low_buffer(*wide_half), dma((4,)),
            *Scatter.buffers(n, length, width),
        ],
        compiler_params=communicating(6),
        cost_estimate=pl.CostEstimate(flops=0, bytes_accessed=64 << 20, transcendentals=0),
        name="sum_weight_gradients",
    )(
        attn_gain, ffn_gain, query_gain, key_gain, router, out_own, grad_projection.reshape(peers, shard_rows, columns),
        resid, first_gated.reshape(n, 2 * length, hidden), second_gated.reshape(n, 2 * length, hidden),
        down_weight, *second_wide,
    )


def widen_kernel(*refs):
    sums, refs = refs[1:31], refs[31:]
    sources, small_ref, refs = refs[:4], refs[4], refs[5:]
    gate_ref, up_ref, down_ref, *targets = refs[:7]
    attn_gain_ref, ffn_gain_ref, query_gain_ref, key_gain_ref, router_ref = refs[7:]
    tile = down_ref.shape[3]
    middle = gate_ref.shape[2] // 2
    for expert in range(2):

        @pl.when(pl.program_id(0) == expert)
        def place():
            for kind, target in enumerate((gate_ref, up_ref, down_ref)):
                at = 15 * expert + 5 * kind
                grads, first_a, first_b, second_a, second_b = sums[at : at + 5]
                for side, first, second in ((0, first_a, second_a), (1, first_b, second_b)):
                    columns = pl.ds(side * middle, middle)
                    total = grads[0, :, columns].astype(high) + first[0].astype(high) + second[...].astype(high)
                    if kind < 2:
                        target[0, :, columns] = total
                    else:
                        for part in range(middle // tile):
                            target[0, side * (middle // tile) + part] = total[:, part * tile : (part + 1) * tile]

    for source, target in zip(sources, targets):
        target[...] = source[...].astype(high)

    @pl.when((pl.program_id(0) == 0) & (pl.program_id(1) == 0))
    def small():
        attn_gain_ref[...] = small_ref[0]
        ffn_gain_ref[...] = small_ref[1]
        query_gain_ref[...] = small_ref[2, : query_gain_ref.shape[0]]
        key_gain_ref[...] = small_ref[3, : key_gain_ref.shape[0]]
        router_ref[...] = small_ref[8:]


def run_widen(sums, weight_grads, small, head_size, hidden_units, model_width, groups):
    piece, tile = hidden_units // groups, model_width // groups
    operands, specs = [], []
    block, middle = piece // groups, model_width // 2
    group = lax.axis_index("dp").astype(jnp.int32).reshape(1)

    def of_expert(expert):
        return lambda x, j: jnp.where(x == expert, j, 0 if expert else groups - 1)

    for expert, (grads, (first_a, first_b), (second_a, second_b)) in enumerate(sums):
        turn = of_expert(expert)
        for at in range(3):

            def row(x, j, turn=turn, at=at):
                return at * groups + turn(x, j)

            operands += [grads, first_a, first_b, second_a, second_b]
            specs += [
                pl.BlockSpec((1, block, model_width), lambda x, j, g, row=row: (g[0], row(x, j), 0)),
                pl.BlockSpec((1, block, middle), lambda x, j, g, row=row: (g[0] // 2, row(x, j), 0)),
                pl.BlockSpec((1, block, middle), lambda x, j, g, row=row: (g[0] % 2, row(x, j), 0)),
                pl.BlockSpec((block, middle), lambda x, j, g, row=row: (row(x, j), 0)),
                pl.BlockSpec((block, middle), lambda x, j, g, row=row: (row(x, j), 0)),
            ]
    steps = 2 * groups
    small_shapes = [
        (model_width,), (model_width,), (head_size,), (head_size,), (small.shape[0] - 8, model_width),
    ]

    def rows_of(array):
        return pl.BlockSpec((array.shape[0] // steps, array.shape[1]), lambda x, j, g: (x * groups + j, 0))

    return pl.pallas_call(
        widen_kernel,
        out_shape=[
            jax.ShapeDtypeStruct((2, piece, model_width), high),
            jax.ShapeDtypeStruct((2, piece, model_width), high),
            jax.ShapeDtypeStruct((2, groups, piece, tile), high),
            *[jax.ShapeDtypeStruct(array.shape, high) for array in weight_grads],
            *[jax.ShapeDtypeStruct(shape, high) for shape in small_shapes],
        ],
        grid_spec=pltpu.PrefetchScalarGridSpec(
            num_scalar_prefetch=1,
            grid=(2, groups),
            in_specs=specs
            + [rows_of(array) for array in weight_grads]
            + [pl.BlockSpec(small.shape, lambda x, j, g: (0, 0))],
            out_specs=[
                pl.BlockSpec((1, block, model_width), lambda x, j, g: (x, j, 0)),
                pl.BlockSpec((1, block, model_width), lambda x, j, g: (x, j, 0)),
                pl.BlockSpec((1, groups, block, tile), lambda x, j, g: (x, 0, j, 0)),
                *[rows_of(array) for array in weight_grads],
                *[pl.BlockSpec(shape, lambda x, j, g, rank=len(shape): (0,) * rank) for shape in small_shapes],
            ],
        ),
        compiler_params=pltpu.CompilerParams(vmem_limit_bytes=60 << 20),
        name="widen",
    )(group, *operands, *weight_grads, small)


def gather_tokens(rows):
    return lax.all_gather(rows, "expert", axis=0, tiled=True)


def scatter_sum(partial):
    return lax.psum_scatter(partial, "expert", scatter_dimension=0, tiled=True)


def projection_gradients(grad_projection, peers, kv_heads, head_size):
    width, columns = grad_projection.shape
    shard_rows = width // peers
    local_width = columns - head_size
    sharers = peers // kv_heads
    grad_projection = grad_projection.reshape(peers, shard_rows, columns)
    grad_projection = lax.psum_scatter(grad_projection, "dp", scatter_dimension=1, tiled=True)
    grad_projection = lax.all_to_all(
        grad_projection, "expert", split_axis=0, concat_axis=0, tiled=True
    )
    grad_projection = lax.all_gather(grad_projection, "dp", axis=1, tiled=True)
    grad_query_w = (
        grad_projection[:, :, :local_width].transpose(1, 0, 2).reshape(shard_rows, peers * local_width)
    ).astype(high)
    shared = grad_projection[:, :, local_width:].reshape(kv_heads, sharers, shard_rows, head_size)
    kv_width = kv_heads * head_size
    grad_key_w = shared[:, 0].transpose(1, 0, 2).reshape(shard_rows, kv_width).astype(high)
    grad_value_w = shared[:, 1].transpose(1, 0, 2).reshape(shard_rows, kv_width).astype(high)
    return grad_query_w, grad_key_w, grad_value_w


def out_gradient(grad_out):
    summed = lax.psum_scatter(grad_out, "dp", scatter_dimension=0, tiled=True)
    return lax.all_gather(summed, "dp", axis=0, tiled=True).astype(high)


def constant_tables(length, head_size):
    half = head_size // 2
    freqs = np.float32(rope_base) ** (-np.arange(half, dtype=np.float32) * np.float32(2.0 / head_size))
    angles = np.arange(length, dtype=np.float32)[:, None] * freqs[None, :]
    cosines, sines = np.cos(angles), np.sin(angles)
    return (
        jnp.asarray(np.concatenate([cosines, cosines], 1), high),
        jnp.asarray(np.concatenate([-sines, sines], 1), high),
    )


def fits_kernels(peers, groups, sharers, experts, full_length, width):
    return groups == 4 and peers == 8 and sharers == 2 and experts == 2 * peers and full_length * width <= 1 << 21


def fused_layer(
    tokens, segments, routes, cotangent, norm_gain_attn, query_weight, key_matrix, value_matrix, query_gain,
    key_gain, out_weight, norm_gain_ffn, router_weight, gate_weight, up_weight, down_weight, heads,
):
    length, model_width = tokens.shape
    head_size = query_gain.shape[0]
    peers = lax.axis_size("expert")
    groups = lax.axis_size("dp")
    local_experts, _, hidden_units = gate_weight.shape
    experts = local_experts * peers
    full_length = length * peers
    kv_heads = peers // 2
    local_width = heads * head_size
    gain_attn_row = norm_gain_attn.reshape(1, model_width)
    gain_ffn_row = norm_gain_ffn.reshape(1, model_width)

    hidden, all_named, near, seg_col, projection, raw = run_gather(
        tokens, gain_attn_row, routes.T, segments, cotangent, query_weight, key_matrix, value_matrix, peers, groups
    )
    cosines, sines = constant_tables(full_length, head_size)
    seg_row = segments
    query_gain_row = query_gain.reshape(1, head_size)
    key_gain_row = key_gain.reshape(1, head_size)
    router = router_weight.T
    (
        key_low, value_low, own_gates, resid, ffn_local, gates, mixed, query_low, inverse, rows_all, cotangents,
        first_gated, parts, first_grads,
    ) = run_first(
        raw, query_gain_row, key_gain_row, cosines, sines, seg_col, seg_row, out_weight, tokens, gain_ffn_row,
        all_named, router, cotangent, near, gate_weight, up_weight, down_weight, peers, groups,
    )
    sums, second_gated, second_grads, *first_step = run_second(
        gates, rows_all, cotangents, gate_weight, up_weight, down_weight, parts, first_grads, peers, groups
    )
    (
        input_grad, grad_projection, out_own, gain_attn_part, gain_ffn_part, query_gain_part, key_gain_part,
        grad_router, first_end, second_step,
    ) = run_input(
        sums, own_gates, ffn_local, resid, cotangent, gain_ffn_row, router, out_weight, raw, query_low, key_low,
        value_low, inverse, mixed, query_gain_row, key_gain_row, cosines, sines, seg_col, seg_row, projection,
        hidden, tokens, gain_attn_row, (first_grads, *first_step), second_grads, experts, peers,
    )
    *weight_grads, small, output, second_a, second_b = run_weights(
        grad_projection, out_own, gain_attn_part, gain_ffn_part, query_gain_part, key_gain_part, grad_router,
        resid, first_gated, second_gated, down_weight, (second_grads, *second_step), peers, kv_heads,
    )
    grads = ((first_grads, first_step, first_end), (second_grads, second_step, (second_a, second_b)))
    gate_w, up_w, down_w, query_w, key_w, value_w, out_w, *sums = run_widen(
        grads, weight_grads, small, head_size, hidden_units, model_width, groups
    )
    gain_attn_grad, gain_ffn_grad, query_gain_grad, key_gain_grad, router_grad = sums
    return (
        output,
        input_grad,
        gain_attn_grad,
        query_w,
        key_w,
        value_w,
        query_gain_grad,
        key_gain_grad,
        out_w,
        gain_ffn_grad,
        router_grad.T,
        gate_w.transpose(0, 2, 1),
        up_w.transpose(0, 2, 1),
        down_w.reshape(local_experts, hidden_units, model_width // groups),
    )


def on_device(
    tokens,
    segments,
    routes,
    cotangent,
    norm_gain_attn,
    query_weight,
    key_matrix,
    value_matrix,
    query_gain,
    key_gain,
    out_weight,
    norm_gain_ffn,
    router_weight,
    gate_weight,
    up_weight,
    down_weight,
):
    length, model_width = tokens.shape
    head_size = query_gain.shape[0]
    peers = lax.axis_size("expert")
    groups = lax.axis_size("dp")
    me = lax.axis_index("expert")
    group = lax.axis_index("dp")
    shard_rows, query_width = query_weight.shape
    kv_width = key_matrix.shape[1]
    kv_heads = kv_width // head_size
    heads = query_width // head_size // peers
    sharers = peers // kv_heads
    local_width = heads * head_size
    local_experts = gate_weight.shape[0]
    experts = local_experts * peers
    full_length = length * peers
    piece = shard_rows // groups

    if fits_kernels(peers, groups, sharers, experts, full_length, model_width):
        return fused_layer(
            tokens, segments, routes, cotangent, norm_gain_attn, query_weight, key_matrix, value_matrix,
            query_gain, key_gain, out_weight, norm_gain_ffn, router_weight, gate_weight, up_weight, down_weight, heads,
        )

    def own_rows(matrix):
        return lax.dynamic_slice_in_dim(matrix, group * piece, piece, 0)

    def columns(matrix, width, copies):
        split = own_rows(matrix).reshape(piece, -1, width).transpose(1, 0, 2)
        return jnp.repeat(split, copies, axis=0)

    outgoing = jnp.concatenate(
        [
            columns(query_weight, local_width, 1),
            columns(key_matrix, head_size, sharers),
            columns(value_matrix, head_size, sharers),
        ],
        axis=2,
    )
    arrived = lax.all_to_all(outgoing, "expert", split_axis=0, concat_axis=0, tiled=True)
    projection = lax.all_gather(arrived, "dp", axis=1, tiled=True).reshape(model_width, -1)

    inputs = tokens.astype(high)
    hidden_local = norm_rows(inputs, norm_gain_attn).astype(low)
    hidden = gather_tokens(hidden_local)
    raw = dot(hidden, projection)
    cosines, sines = rotary_tables(full_length, head_size)
    seg_col = jnp.broadcast_to(segments.reshape(full_length, 1), (full_length, head_size))
    seg_row = jnp.broadcast_to(segments.reshape(1, full_length), (8, full_length))
    query_gain_row = query_gain.reshape(1, head_size)
    key_gain_row = key_gain.reshape(1, head_size)
    mixed, query_low, key_low, value_low, inverse = run_attention_forward(
        raw, heads, head_size, query_gain_row, key_gain_row, cosines, sines, seg_col, seg_row
    )
    attn = scatter_sum(dot(mixed, out_weight).astype(low))
    resid = inputs + attn.astype(high)
    ffn_local = norm_rows(resid, norm_gain_ffn).astype(low)
    ffn_rows = gather_tokens(ffn_local)
    cotangents = gather_tokens(cotangent)
    all_routes = gather_tokens(routes)

    def gates_of(rows, route_rows):
        logits = dot(rows, router_weight)
        named = jnp.any(
            route_rows[:, :, None] == jnp.arange(experts, dtype=jnp.int32)[None, None, :], axis=1
        )
        top = jnp.max(jnp.where(named, logits, -jnp.inf), axis=-1, keepdims=True)
        terms = jnp.where(named, jnp.exp(jnp.where(named, logits - top, 0.0)), 0.0)
        return terms / jnp.sum(terms, axis=-1, keepdims=True)

    gates_all = gates_of(ffn_rows, all_routes)
    own_gates = lax.dynamic_slice_in_dim(gates_all, me * local_experts, local_experts, 1)
    mixture = 0.0
    grad_rows = 0.0
    gate_grads, grad_gate_w, grad_up_w, grad_down_w = [], [], [], []
    for expert in range(local_experts):
        gate_col = own_gates[:, expert : expert + 1]
        gate_pre = dot(ffn_rows, gate_weight[expert])
        up_pre = dot(ffn_rows, up_weight[expert])
        share = jax.nn.sigmoid(gate_pre)
        silu = gate_pre * share
        act = silu * up_pre
        gated_act = (act * gate_col).astype(low)
        mixture = mixture + dot(gated_act, down_weight[expert])
        plain = dot_last(cotangents, down_weight[expert])
        gate_grads.append(jnp.sum(act * plain, axis=-1, keepdims=True))
        grad_act = plain * gate_col
        grad_gate_pre = (grad_act * up_pre * (share * (1.0 + gate_pre * (1.0 - share)))).astype(low)
        grad_up_pre = (grad_act * silu).astype(low)
        grad_rows = (
            grad_rows
            + dot_last(grad_gate_pre, gate_weight[expert])
            + dot_last(grad_up_pre, up_weight[expert])
        )
        hidden_units = gated_act.shape[1]
        grad_gate_w.append(dot_first(grad_gate_pre, ffn_rows).astype(low).reshape(groups, -1, model_width))
        grad_up_w.append(dot_first(grad_up_pre, ffn_rows).astype(low).reshape(groups, -1, model_width))
        cut_width = model_width // groups
        grad_down_w.append(
            jnp.stack([
                dot_first(gated_act, cotangents[:, part * cut_width : (part + 1) * cut_width]).astype(low)
                for part in range(groups)
            ])
        )

    gate_grad = jnp.concatenate(gate_grads, axis=1)
    lane_pad = 128 - 2 * experts % 128
    placed = jnp.zeros((full_length, experts), high)
    placed = lax.dynamic_update_slice_in_dim(placed, gate_grad, me * local_experts, 1)
    upper = placed.astype(low)
    lower = (placed - upper.astype(high)).astype(low)
    sent = jnp.concatenate(
        [grad_rows.astype(low), upper, lower, jnp.zeros((full_length, lane_pad), low)], axis=1
    )
    summed_rows = scatter_sum(sent)
    output = (resid + scatter_sum(mixture.astype(low)).astype(high)).astype(low)
    grad_gates = summed_rows[:, model_width : model_width + experts].astype(high) + summed_rows[
        :, model_width + experts : model_width + 2 * experts
    ].astype(high)
    gates = gates_of(ffn_local, routes)
    grad_logits = (
        gates * (grad_gates - jnp.sum(gates * grad_gates, axis=-1, keepdims=True))
    ).astype(low)
    grad_router = dot_first(ffn_local, grad_logits)
    grad_hidden_ffn = summed_rows[:, :model_width].astype(high) + dot_last(grad_logits, router_weight)
    grad_resid_norm, gain_rows_ffn = norm_back(resid, norm_gain_ffn, grad_hidden_ffn)
    grad_resid = cotangent.astype(high) + grad_resid_norm
    grad_attn = gather_tokens(grad_resid.astype(low))
    grad_mixed = dot_last(grad_attn, out_weight).astype(low)
    grad_out = dot_first(mixed, grad_attn)
    grad_query_low, grad_key_part, grad_value_part, query_gain_part = run_attention_backward(
        raw, query_low, key_low, value_low, inverse, mixed, grad_mixed, heads, head_size,
        query_gain_row, cosines, sines, seg_col, seg_row,
    )
    both = jnp.concatenate([grad_key_part, grad_value_part], axis=1)
    step = 1
    while step < sharers:
        swap = [(peer, peer ^ step) for peer in range(peers)]
        both = both + lax.ppermute(both.astype(low), "expert", swap).astype(high)
        step *= 2
    grad_key_rot, grad_value = both[:, :head_size], both[:, head_size:].astype(low)
    place = me % sharers
    half = head_size // 2
    swapped = jnp.concatenate([grad_key_rot[:, half:], grad_key_rot[:, :half]], axis=1)
    key_raw = raw[:, local_width : local_width + head_size]
    grad_key, key_gain_rows = norm_back(key_raw, key_gain, grad_key_rot * cosines - swapped * sines)
    grad_shared = jnp.where(
        place == 0, grad_key.astype(low), jnp.where(place == 1, grad_value, jnp.zeros_like(grad_value))
    )
    own_columns = jnp.concatenate([grad_query_low, grad_shared], axis=1)
    shared_weight = jnp.where(
        place == 0,
        projection[:, local_width : local_width + head_size],
        projection[:, local_width + head_size :],
    )
    own_weight = jnp.concatenate([projection[:, :local_width], shared_weight], axis=1)
    grad_hidden_attn = scatter_sum(dot_last(own_columns, own_weight).astype(low)).astype(high)
    grad_inputs_norm, gain_rows_attn = norm_back(inputs, norm_gain_attn, grad_hidden_attn)
    input_grad = grad_resid + grad_inputs_norm

    grad_query_w, grad_key_w, grad_value_w = projection_gradients(
        dot_first(hidden, own_columns).astype(low), peers, kv_heads, head_size
    )
    grad_out_w = out_gradient(grad_out.astype(low))

    wide = jnp.concatenate(grad_gate_w + grad_up_w, axis=1)
    wide = lax.psum_scatter(wide, "dp", scatter_dimension=0, tiled=True)
    wide = wide.reshape(2, local_experts, hidden_units // groups, model_width).transpose(0, 1, 3, 2)
    wide = wide.astype(high)
    down = jnp.concatenate(grad_down_w, axis=1)
    down = lax.psum_scatter(down, "dp", scatter_dimension=0, tiled=True)
    down = down.reshape(local_experts, hidden_units, cut_width).astype(high)
    expert_sums = (wide[0], wide[1], down)
    key_gain_grad = jnp.where(place == 0, jnp.sum(key_gain_rows, axis=0), 0.0)
    small = jnp.concatenate(
        [
            jnp.sum(gain_rows_attn, axis=0),
            jnp.sum(gain_rows_ffn, axis=0),
            query_gain_part[0],
            key_gain_grad,
            grad_router.reshape(-1),
        ]
    )
    small = lax.psum(small, ("dp", "expert"))
    cut = 2 * model_width
    return (
        output,
        input_grad,
        small[:model_width],
        grad_query_w,
        grad_key_w,
        grad_value_w,
        small[cut : cut + head_size],
        small[cut + head_size : cut + 2 * head_size],
        grad_out_w,
        small[model_width:cut],
        small[cut + 2 * head_size :].reshape(model_width, experts),
        *expert_sums,
    )


def solution(mesh):
    rows = P(("dp", "expert"), None)
    split = P("expert", None)
    cube = P("expert", None, None)
    cut = P("expert", None, "dp")
    return jax.shard_map(
        on_device,
        mesh=mesh,
        in_specs=(
            rows, P("dp", None), rows, rows, P(), split, split, split, P(), P(), split, P(), P(),
            cube, cube, cube,
        ),
        out_specs=(
            rows, rows, P(), split, split, split, P(), P(), split, P(), P(), cut, cut, cut,
        ),
        check_vma=False,
    )
```

```python
import functools

import jax
import jax.numpy as jnp
import numpy as np
from jax import lax
from jax.experimental import pallas as pl
from jax.experimental.pallas import tpu as pltpu
from jax.sharding import PartitionSpec as P

eps_norm = 1e-06
rope_base = 1000000.0
log2e = 1.4426950408889634
low = jnp.bfloat16
high = jnp.float32


def norm_rows(values, gain):
    factor = lax.rsqrt(jnp.mean(values * values, axis=-1, keepdims=True) + eps_norm)
    return values * factor * gain


def norm_back(values, gain, grad):
    factor = lax.rsqrt(jnp.mean(values * values, axis=-1, keepdims=True) + eps_norm)
    scaled = gain * grad
    inner = jnp.mean(values * scaled, axis=-1, keepdims=True)
    grad_values = factor * scaled - values * (factor * factor * factor * inner)
    return grad_values, grad * values * factor


def dot(left, right):
    return jnp.dot(left, right, preferred_element_type=high)


def dot_first(left, right):
    return lax.dot_general(left, right, (((0,), (0,)), ((), ())), preferred_element_type=high)


def dot_last(left, right):
    return lax.dot_general(left, right, (((1,), (1,)), ((), ())), preferred_element_type=high)


def rotary_tables(length, head_size):
    half = head_size // 2
    freqs = rope_base ** (-jnp.arange(half, dtype=high) * 2.0 / head_size)
    angles = jnp.arange(length, dtype=high)[:, None] * freqs[None, :]
    cosines, sines = jnp.cos(angles), jnp.sin(angles)
    return jnp.concatenate([cosines, cosines], 1), jnp.concatenate([-sines, sines], 1)


def rotate(values, cosines, sines):
    return values * cosines + pltpu.roll(values, values.shape[-1] // 2, 1) * sines


def unrotate(values, cosines, sines):
    return values * cosines - pltpu.roll(values, values.shape[-1] // 2, 1) * sines


def key_spans(length):
    block = min(256, length)
    longest = length // 2
    spans = []
    for begin in range(0, length, block):
        first = max(0, begin - longest + 1) // block * block
        spans.append((begin, block, first, begin + block - first))
    return spans


def tile_mask(seg_col, seg_row, begin, rows, first, keys):
    query_at = begin + lax.broadcasted_iota(jnp.int32, (rows, keys), 0)
    key_at = first + lax.broadcasted_iota(jnp.int32, (rows, keys), 1)
    return (query_at >= key_at) & (seg_col[begin : begin + rows, :1] == seg_row[:1, first : first + keys])


def attention_forward(
    query_ref, key_ref, value_ref, query_gain_ref, key_gain_ref, cos_ref, sin_ref, col_ref, row_ref,
    mixed_ref, query_low_ref, key_low_ref, value_low_ref, inverse_ref, value_wide,
):
    head_size = query_ref.shape[1]

    @pl.when(pl.program_id(0) == 0)
    def first_head():
        rotated = rotate(norm_rows(key_ref[...], key_gain_ref[...]), cos_ref[...], sin_ref[...])
        key_low_ref[...] = rotated.astype(low)
        value_low_ref[...] = value_ref[...].astype(low)
        value_wide[:, :head_size] = value_ref[...].astype(low)
        value_wide[:, head_size:] = jnp.ones_like(value_low_ref)

    rotated = rotate(norm_rows(query_ref[...], query_gain_ref[...]), cos_ref[...], sin_ref[...])
    query_low_ref[...] = (rotated * (head_size**-0.5 * log2e)).astype(low)
    for begin, rows, first, keys in key_spans(query_ref.shape[0]):
        scores = dot_last(query_low_ref[pl.ds(begin, rows)], key_low_ref[pl.ds(first, keys)])
        allowed = tile_mask(col_ref, row_ref, begin, rows, first, keys)
        terms = jnp.where(allowed, jnp.exp2(scores), 0.0).astype(low)
        sums = dot(terms, value_wide[pl.ds(first, keys)])
        inverse = 1.0 / sums[:, head_size:]
        mixed_ref[pl.ds(begin, rows)] = (sums[:, :head_size] * inverse).astype(low)
        inverse_ref[pl.ds(begin, rows)] = inverse


def attention_backward(
    query_ref, query_low_ref, key_low_ref, value_low_ref, inverse_ref, mixed_ref, grad_mixed_ref,
    query_gain_ref, cos_ref, sin_ref, col_ref, row_ref,
    grad_query_ref, grad_key_ref, grad_value_ref, grad_gain_ref,
):
    length, head_size = query_ref.shape

    @pl.when(pl.program_id(0) == 0)
    def first_head():
        grad_key_ref[...] = jnp.zeros_like(grad_key_ref)
        grad_value_ref[...] = jnp.zeros_like(grad_value_ref)
        grad_gain_ref[...] = jnp.zeros_like(grad_gain_ref)

    for begin, rows, first, keys in key_spans(length):
        block = pl.ds(begin, rows)
        query_low = query_low_ref[block]
        key_low = key_low_ref[pl.ds(first, keys)]
        scaled = grad_mixed_ref[block].astype(high) * inverse_ref[block]
        row_term = jnp.sum(scaled * mixed_ref[block].astype(high), axis=-1, keepdims=True)
        scaled = scaled.astype(low)
        scores = dot_last(query_low, key_low)
        allowed = tile_mask(col_ref, row_ref, begin, rows, first, keys)
        terms = jnp.where(allowed, jnp.exp2(scores), 0.0)
        grad_probs = dot_last(scaled, value_low_ref[pl.ds(first, keys)])
        grad_scores = (terms * (grad_probs - row_term)).astype(low)
        grad_value_ref[pl.ds(first, keys)] += dot_first(terms.astype(low), scaled)
        grad_key_ref[pl.ds(first, keys)] += dot_first(grad_scores, query_low) * (1.0 / log2e)
        grad_rotated = dot(grad_scores, key_low) * head_size**-0.5
        grad_normed = unrotate(grad_rotated, cos_ref[block], sin_ref[block])
        grad_raw, gain_rows = norm_back(query_ref[block], query_gain_ref[...], grad_normed)
        grad_query_ref[block] = grad_raw.astype(low)
        grad_gain_ref[...] += jnp.broadcast_to(
            jnp.sum(gain_rows, axis=0, keepdims=True), grad_gain_ref.shape
        )


def whole(shape):
    return pl.BlockSpec(shape, lambda head: (0,) * len(shape))


def run_attention_forward(raw, heads, head_size, query_gain, key_gain, cosines, sines, seg_col, seg_row):
    length = raw.shape[0]
    per_head = pl.BlockSpec((length, head_size), lambda head: (0, head))
    one = (length, head_size)
    wide = jax.ShapeDtypeStruct((length, heads * head_size), low)
    narrow = jax.ShapeDtypeStruct(one, low)
    return pl.pallas_call(
        attention_forward,
        grid=(heads,),
        in_specs=[
            per_head,
            pl.BlockSpec(one, lambda head: (0, heads)),
            pl.BlockSpec(one, lambda head: (0, heads + 1)),
            whole((1, head_size)),
            whole((1, head_size)),
            whole(one),
            whole(one),
            whole(one),
            whole((8, length)),
        ],
        out_specs=[per_head, per_head, whole(one), whole(one), per_head],
        out_shape=[wide, wide, narrow, narrow, jax.ShapeDtypeStruct((length, heads * head_size), high)],
        scratch_shapes=[pltpu.VMEM((length, 2 * head_size), low)],
        compiler_params=pltpu.CompilerParams(vmem_limit_bytes=50 << 20),
        cost_estimate=pl.CostEstimate(
            flops=3 * heads * length * length * head_size, bytes_accessed=8 * length * heads * head_size,
            transcendentals=heads * length * length // 2,
        ),
    )(raw, raw, raw, query_gain, key_gain, cosines, sines, seg_col, seg_row)


def run_attention_backward(
    raw, query_low, key_low, value_low, inverse, mixed, grad_mixed, heads, head_size, query_gain,
    cosines, sines, seg_col, seg_row,
):
    length = raw.shape[0]
    per_head = pl.BlockSpec((length, head_size), lambda head: (0, head))
    one = (length, head_size)
    return pl.pallas_call(
        attention_backward,
        grid=(heads,),
        in_specs=[
            per_head, per_head, whole(one), whole(one), per_head, per_head, per_head,
            whole((1, head_size)), whole(one), whole(one), whole(one), whole((8, length)),
        ],
        out_specs=[per_head, whole(one), whole(one), whole((8, head_size))],
        out_shape=[
            jax.ShapeDtypeStruct((length, heads * head_size), low),
            jax.ShapeDtypeStruct(one, high),
            jax.ShapeDtypeStruct(one, high),
            jax.ShapeDtypeStruct((8, head_size), high),
        ],
        compiler_params=pltpu.CompilerParams(vmem_limit_bytes=50 << 20),
        cost_estimate=pl.CostEstimate(
            flops=6 * heads * length * length * head_size, bytes_accessed=16 * length * heads * head_size,
            transcendentals=heads * length * length // 2,
        ),
    )(
        raw, query_low, key_low, value_low, inverse, mixed, grad_mixed, query_gain, cosines, sines,
        seg_col, seg_row,
    )


MESH = pl.DeviceIdType.MESH
VMEM = pl.BlockSpec(memory_space=pltpu.VMEM)
ANY = pl.BlockSpec(memory_space=pl.ANY)


def wait_all(copies):
    for copy in copies:
        copy.wait()


class Chain:
    def __init__(self):
        self.n = lax.axis_size("expert") // 2
        me = lax.axis_index("expert")
        self.z, self.c = me // 2, me % 2
        self.sibling, self.up, self.down = me + 1 - 2 * self.c, me + 2, me - 2
        self.has_up, self.has_down = self.z < self.n - 1, self.z > 0

    def greet(self, others=()):
        barrier = pltpu.get_barrier_semaphore()

        def signal(peer):
            pl.semaphore_signal(barrier, inc=1, device_id={"expert": peer}, device_id_type=MESH)

        signal(self.sibling)
        pl.when(self.has_up)(lambda: signal(self.up))
        pl.when(self.has_down)(lambda: signal(self.down))
        for device in others:
            pl.semaphore_signal(barrier, inc=1, device_id=device, device_id_type=MESH)
        peers = 1 + len(others) + self.has_up.astype(jnp.int32) + self.has_down.astype(jnp.int32)
        pl.semaphore_wait(barrier, peers)

    def nearest(self, step):
        turn = jnp.int32(0)
        for z in range(self.n):
            order = sorted(range(self.n), key=lambda other: (abs(other - z), other))
            for at, chip in enumerate(order):
                turn = jnp.where((self.z == z) & (step == at), chip, turn)
        return turn


class Gather:
    def __init__(self, chain, own, block, send, recv, local):
        self.chain, self.own, self.block = chain, own, block
        self.send, self.recv, self.local = send, recv, local

    @staticmethod
    def semaphores(n):
        return [
            pltpu.SemaphoreType.DMA((3, n)),
            pltpu.SemaphoreType.DMA((2 * n,)),
            pltpu.SemaphoreType.DMA(()),
        ]

    def copy(self, source, z, way, peer):
        c = self.chain.c
        return pltpu.make_async_remote_copy(
            src_ref=source,
            dst_ref=self.block(z, c),
            send_sem=self.send.at[way, z],
            recv_sem=self.recv.at[2 * z + c],
            device_id={"expert": peer},
            device_id_type=MESH,
        )

    def wait_block(self, z, c):
        block = self.block(z, c)
        pltpu.make_async_remote_copy(
            src_ref=block,
            dst_ref=block,
            send_sem=self.send.at[0, z],
            recv_sem=self.recv.at[2 * z + c],
            device_id={"expert": self.chain.sibling},
            device_id_type=MESH,
        ).wait_recv()

    def keep(self):
        return pltpu.make_async_copy(self.own, self.block(self.chain.z, self.chain.c), self.local)

    def begin(self):
        ch = self.chain
        pl.when(ch.has_up)(lambda: self.copy(self.own, ch.z, 0, ch.up).start())
        pl.when(ch.has_down)(lambda: self.copy(self.own, ch.z, 1, ch.down).start())
        self.copy(self.own, ch.z, 2, ch.sibling).start()
        self.keep().start()

    def service(self, step):
        ch = self.chain

        def from_below():
            z = ch.z - step
            self.wait_block(z, ch.c)
            pl.when(ch.has_up)(lambda: self.copy(self.block(z, ch.c), z, 0, ch.up).start())
            self.copy(self.block(z, ch.c), z, 2, ch.sibling).start()

        def from_above():
            z = ch.z + step
            self.wait_block(z, ch.c)
            pl.when(ch.has_down)(lambda: self.copy(self.block(z, ch.c), z, 1, ch.down).start())
            self.copy(self.block(z, ch.c), z, 2, ch.sibling).start()

        pl.when(ch.z - step >= 0)(from_below)
        pl.when(ch.z + step < ch.n)(from_above)

    def wait_sibling(self, z):
        self.wait_block(z, 1 - self.chain.c)

    def finish(self):
        ch = self.chain
        for z in range(ch.n):
            at = jnp.int32(z)
            block = self.block(at, ch.c)
            pl.when(ch.has_up & (ch.z >= z))(lambda: self.copy(block, at, 0, ch.up).wait_send())
            pl.when(ch.has_down & (ch.z <= z))(lambda: self.copy(block, at, 1, ch.down).wait_send())
            self.copy(block, at, 2, ch.sibling).wait_send()


class NearGather(Gather):
    def __init__(self, chain, own, near, block, send, recv, local):
        super().__init__(chain, own, block, send, recv, local)
        self.near = near

    @staticmethod
    def semaphores(n):
        return Gather.semaphores(n)[:2] + [pltpu.SemaphoreType.DMA((4,))]

    def place(self, at):
        ch = self.chain
        source = self.own if at == 3 else self.near.at[at]
        z, c = ((ch.z - 1, ch.c), (ch.z + 1, ch.c), (ch.z, 1 - ch.c), (ch.z, ch.c))[at]
        return pltpu.make_async_copy(source, self.block(z, c), self.local.at[at])

    def begin(self):
        ch = self.chain

        def below():
            pl.when(ch.has_up)(lambda: self.copy(self.near.at[0], ch.z - 1, 0, ch.up).start())
            self.copy(self.near.at[0], ch.z - 1, 2, ch.sibling).start()
            self.place(0).start()

        def above():
            pl.when(ch.has_down)(lambda: self.copy(self.near.at[1], ch.z + 1, 1, ch.down).start())
            self.copy(self.near.at[1], ch.z + 1, 2, ch.sibling).start()
            self.place(1).start()

        pl.when(ch.has_down)(below)
        pl.when(ch.has_up)(above)
        self.place(2).start()
        self.place(3).start()

    def wait_placed(self):
        pl.when(self.chain.has_down)(lambda: self.place(0).wait())
        pl.when(self.chain.has_up)(lambda: self.place(1).wait())
        self.place(2).wait()
        self.place(3).wait()

    def finish(self):
        ch = self.chain
        for z in range(ch.n):
            at = jnp.int32(z)
            block = self.block(at, ch.c)
            pl.when(ch.has_up & (ch.z > z))(lambda: self.copy(block, at, 0, ch.up).wait_send())
            pl.when(ch.has_down & (ch.z < z))(lambda: self.copy(block, at, 1, ch.down).wait_send())
            pl.when(ch.z != z)(lambda: self.copy(block, at, 2, ch.sibling).wait_send())


class Scatter:
    def __init__(self, chain, half, pair, flow, pair_send, pair_recv, flow_send, flow_recv):
        self.chain, self.half, self.pair, self.flow = chain, half, pair, flow
        self.pair_send, self.pair_recv = pair_send, pair_recv
        self.flow_send, self.flow_recv = flow_send, flow_recv

    @staticmethod
    def buffers(n, rows, width):
        return [
            pltpu.VMEM((n, rows, width), low),
            pltpu.VMEM((n + 1, rows, width), low),
            pltpu.SemaphoreType.DMA((n,)),
            pltpu.SemaphoreType.DMA((n,)),
            pltpu.SemaphoreType.DMA((n,)),
            pltpu.SemaphoreType.DMA((n + 1,)),
        ]

    def pair_copy(self, z):
        ch = self.chain
        return pltpu.make_async_remote_copy(
            src_ref=self.half(z, 1 - ch.c),
            dst_ref=self.pair.at[z],
            send_sem=self.pair_send.at[z],
            recv_sem=self.pair_recv.at[z],
            device_id={"expert": ch.sibling},
            device_id_type=MESH,
        )

    def flow_copy(self, z, slot, peer):
        return pltpu.make_async_remote_copy(
            src_ref=self.pair.at[z],
            dst_ref=self.flow.at[slot],
            send_sem=self.flow_send.at[z],
            recv_sem=self.flow_recv.at[slot],
            device_id={"expert": peer},
            device_id_type=MESH,
        )

    def wait_flow(self, slot):
        block = self.flow.at[slot]
        pltpu.make_async_remote_copy(
            src_ref=block,
            dst_ref=block,
            send_sem=self.flow_send.at[0],
            recv_sem=self.flow_recv.at[slot],
            device_id={"expert": self.chain.sibling},
            device_id_type=MESH,
        ).wait_recv()

    def start_pair(self, z):
        self.pair_copy(z).start()

    def add_pair(self, z, relayed):
        self.pair_copy(z).wait_recv()
        half = self.half(z, self.chain.c)

        def alone():
            self.pair[z] = (half[...].astype(high) + self.pair[z].astype(high)).astype(low)

        def with_flow():
            self.wait_flow(z)
            total = half[...].astype(high) + self.pair[z].astype(high) + self.flow[z].astype(high)
            self.pair[z] = total.astype(low)

        pl.when(relayed)(with_flow)
        pl.when(jnp.logical_not(relayed))(alone)

    def step(self, distance):
        ch = self.chain

        def upward():
            z = ch.z + distance
            self.add_pair(z, ch.has_down)
            self.flow_copy(z, z, ch.up).start()

        def downward():
            z = ch.z - distance
            self.add_pair(z, ch.has_up)
            self.flow_copy(z, jnp.where(distance == 1, ch.n, z), ch.down).start()

        pl.when(ch.z + distance < ch.n)(upward)
        pl.when(ch.z - distance >= 0)(downward)

    def total(self, result):
        ch = self.chain
        self.pair_copy(ch.z).wait_recv()
        result[...] = self.half(ch.z, ch.c)[...].astype(high) + self.pair[ch.z].astype(high)

        def add(slot):
            self.wait_flow(slot)
            result[...] += self.flow[slot].astype(high)

        pl.when(ch.has_down)(lambda: add(ch.z))
        pl.when(ch.has_up)(lambda: add(ch.n))

    def finish(self):
        ch = self.chain
        for z in range(ch.n):
            at = jnp.int32(z)
            self.pair_copy(at).wait_send()
            pl.when(ch.z != z)(lambda: self.flow_copy(at, at, ch.sibling).wait_send())


class Ports:
    def __init__(self, send, recv):
        self.send, self.recv, self.used, self.started = send, recv, 0, []

    def copy(self, source, target, device):
        at = self.used
        self.used += 1
        copy = pltpu.make_async_remote_copy(
            src_ref=source,
            dst_ref=target,
            send_sem=self.send.at[at],
            recv_sem=self.recv.at[at],
            device_id=device,
            device_id_type=MESH,
        )
        self.started.append(copy)
        return copy

    def finish(self):
        for copy in self.started:
            copy.wait_send()


def square():
    group = lax.axis_index("dp")
    y, x = group // 2, group % 2
    from_x, from_y = 2 * y + 1 - x, 2 * (1 - y) + x
    return group, y, x, from_x, from_y


class SquareSum:
    def __init__(self, source, result, first_a, first_b, second_a, second_b, send_a, send_b, ports):
        self.source, self.result = source, result
        self.own, self.y, self.x, self.from_x, self.from_y = square()
        self.first_a, self.first_b, self.second_a, self.second_b = first_a, first_b, second_a, second_b
        self.send_a, self.send_b = send_a, send_b
        self.rows, self.middle = source.shape[0] // 4, source.shape[1] // 2
        beside, across = {"dp": self.from_x}, {"dp": self.from_y}
        self.first = []
        for k in range(2):
            self.first.append(ports.copy(self.part(source, 0, 2 * k + 1 - self.x), first_a.at[k], beside))
            self.first.append(ports.copy(self.part(source, 1, 2 * (1 - self.y) + k), first_b.at[k], across))
        self.second = [ports.copy(send_a, second_a, across), ports.copy(send_b, second_b, beside)]

    @staticmethod
    def buffers(rows, columns):
        quarter = (rows // 4, columns // 2)
        return [pltpu.VMEM((2, *quarter), low)] * 2 + [pltpu.VMEM(quarter, low)] * 4

    def part(self, ref, side, quarter):
        rows = pl.ds(pl.multiple_of(quarter * self.rows, self.rows), self.rows)
        return ref.at[rows, pl.ds(side * self.middle, self.middle)]

    @staticmethod
    def start(copies):
        for copy in copies:
            copy.start()

    @staticmethod
    def arrive(copies):
        for copy in copies:
            copy.wait_recv()

    def begin(self):
        self.start(self.first)

    def exchange(self):
        self.arrive(self.first)
        along_y = self.part(self.source, 0, self.from_y)[...].astype(high)
        self.send_a[...] = (along_y + self.first_a[1 - self.y].astype(high)).astype(low)
        along_x = self.part(self.source, 1, self.from_x)[...].astype(high)
        self.send_b[...] = (along_x + self.first_b[1 - self.x].astype(high)).astype(low)
        self.start(self.second)

    def settle(self):
        self.arrive(self.second)
        for side, first, second in (
            (0, self.first_a[self.y], self.second_a), (1, self.first_b[self.x], self.second_b)
        ):
            total = self.part(self.source, side, self.own)[...].astype(high) + first.astype(high)
            columns = pl.ds(side * self.middle, self.middle)
            self.result[:, columns] = (total + second[...].astype(high)).astype(low)


class WideSum:
    def __init__(self, grads):
        self.grads = grads
        self.own, self.y, self.x, self.from_x, self.from_y = square()
        self.middle = grads.shape[2] // 2
        self.beside, self.across = {"dp": self.from_x}, {"dp": self.from_y}

    def part(self, side, quarter):
        return self.grads.at[quarter, :, pl.ds(side * self.middle, self.middle)]

    def first(self, first_a, first_b, ports):
        copies = []
        for k in range(2):
            copies.append(ports.copy(self.part(0, 2 * k + 1 - self.x), first_a.at[k], self.beside))
            copies.append(ports.copy(self.part(1, 2 * (1 - self.y) + k), first_b.at[k], self.across))
        return copies

    def load(self, first_a, first_b, left, right, sems):
        pairs = (
            (self.part(0, self.from_y), left.at[0]), (first_a.at[1 - self.y], left.at[1]),
            (self.part(1, self.from_x), right.at[0]), (first_b.at[1 - self.x], right.at[1]),
        )
        return [pltpu.make_async_copy(source, target, sems.at[at]) for at, (source, target) in enumerate(pairs)]

    def second(self, left, right, second_a, second_b, ports):
        for both in (left, right):
            both[0] = (both[0].astype(high) + both[1].astype(high)).astype(low)
        return [
            ports.copy(left.at[0], second_a, self.across),
            ports.copy(right.at[0], second_b, self.beside),
        ]


def wide_shapes(grads):
    _, rows, columns = grads.shape
    first = jax.ShapeDtypeStruct((2, rows, columns // 2), low)
    second = jax.ShapeDtypeStruct((rows, columns // 2), low)
    return [first, first], [second, second]


class SquareCopy:
    def __init__(self, mine, result, ports):
        own, _, _, from_x, from_y = square()
        rows, middle = mine.shape[0], mine.shape[1] // 2
        beside, across = {"dp": from_x}, {"dp": from_y}

        def quarter(at):
            return pl.ds(pl.multiple_of(at * rows, rows), rows)

        target = result.at[quarter(own)]
        self.mine, self.target = mine, target
        self.near = [ports.copy(mine, target, beside), ports.copy(mine, target, across)]
        left = result.at[quarter(from_x), pl.ds(0, middle)]
        right = result.at[quarter(from_y), pl.ds(middle, middle)]
        self.far = [ports.copy(left, left, across), ports.copy(right, right, beside)]

    def begin(self):
        SquareSum.start(self.near)
        self.target[...] = self.mine[...]

    def hand_on(self):
        SquareSum.arrive(self.near)
        SquareSum.start(self.far)

    def finish(self):
        SquareSum.arrive(self.far)


def row_block(ref, rows):
    return lambda z, c: ref.at[pl.ds(pl.multiple_of((2 * z + c) * rows, rows), rows)]


def chip_block(ref, rows):
    return lambda z, c: ref.at[z, pl.ds(pl.multiple_of(c * rows, rows), rows)]


def communicating(collective_id, mebibytes=60):
    return pltpu.CompilerParams(
        collective_id=collective_id, has_side_effects=True, vmem_limit_bytes=mebibytes << 20
    )


def gather_kernel(
    tokens_ref, gain_ref, routes_ref, segments_ref, cot_ref, query_hbm, key_hbm, value_hbm,
    hidden_hbm, all_named_ref, near_ref, col_ref, projection_hbm, raw_hbm,
    named_ref, own, stage, hidden_ref, projection_ref, raw_ref, query_ref, key_ref, value_ref,
    send_a, recv_a, local_a, send_b, recv_b, local_b, name_send, name_recv,
    swap_send, swap_recv, x_send, x_recv, y_send, y_recv, far_send, far_recv, out_sems, load_sems,
    near_send, near_recv,
):
    chain = Chain()
    n = chain.n
    peers = 2 * n
    me = lax.axis_index("expert")
    group, _, _, from_x, from_y = square()
    far = 3 - group
    beside, across = {"dp": from_x}, {"dp": from_y}
    sources = [(2 * chain.nearest(step) + core, core, step) for step in range(n) for core in range(2)]
    others = [chain.sibling] + [source for source, _, step in sources if step > 0]
    barrier = pltpu.get_barrier_semaphore()
    for device in [{"expert": peer} for peer in others] + [beside, across]:
        pl.semaphore_signal(barrier, inc=1, device_id=device, device_id_type=MESH)
    rows = stage.shape[1]
    quarter = pl.ds(pl.multiple_of(group * rows, rows), rows)
    loads = [
        pltpu.make_async_copy(source.at[quarter], target, load_sems.at[at])
        for at, (source, target) in enumerate(
            ((query_hbm, query_ref), (key_hbm, key_ref), (value_hbm, value_ref))
        )
    ]
    for load in loads:
        load.start()
    query_width = query_ref.shape[1] // peers
    head_size = key_ref.shape[1] // n
    own[...] = norm_rows(tokens_ref[...].astype(high), gain_ref[...]).astype(low)
    lanes = lax.broadcasted_iota(jnp.int32, named_ref.shape, 1)
    named = jnp.zeros(named_ref.shape, high)
    routes = routes_ref[...].astype(high).T.astype(jnp.int32)
    for at in range(routes.shape[1]):
        named = jnp.where(routes[:, at : at + 1] == lanes, 1.0, named)
    named_ref[...] = named.astype(low)
    for load in loads:
        load.wait()
    for peer in range(peers):
        shared = pl.ds(peer // 2 * head_size, head_size)
        stage[peer, :, :query_width] = query_ref[:, pl.ds(peer * query_width, query_width)]
        stage[peer, :, query_width : query_width + head_size] = key_ref[:, shared]
        stage[peer, :, query_width + head_size :] = value_ref[:, shared]
    pl.semaphore_wait(barrier, peers + 1)

    def remote(source, target, send, recv, device):
        return pltpu.make_async_remote_copy(
            src_ref=source, dst_ref=target, send_sem=send, recv_sem=recv, device_id=device, device_id_type=MESH
        )

    def block(source, place):
        return projection_ref.at[source, place]

    swaps = [
        remote(stage.at[peer], block(me, group), swap_send.at[at], swap_recv.at[me], {"expert": peer})
        for at, peer in enumerate(others)
    ]
    for copy in swaps:
        copy.start()
    length = own.shape[0]
    piece = length // 2

    def half_block(half):
        def block_of(z, c):
            return hidden_ref.at[pl.ds(pl.multiple_of((2 * z + c) * length + half * piece, piece), piece)]

        return block_of

    wide = [
        Gather(chain, own.at[pl.ds(half * piece, piece)], half_block(half), *sems)
        for half, sems in enumerate(((send_a, recv_a, local_a), (send_b, recv_b, local_b)))
    ]
    for gather in wide:
        gather.begin()
    names = [
        remote(named_ref, all_named_ref.at[me], name_send.at[at], name_recv.at[me], {"expert": peer})
        for at, peer in enumerate(others)
    ]
    for copy in names:
        copy.start()
    all_named_ref[me] = named_ref[...]
    row = jnp.broadcast_to(segments_ref[...].astype(high), (col_ref.shape[1], col_ref.shape[0]))
    col_ref[...] = row.T.astype(jnp.int32)
    projection_ref[me, group] = stage[me]

    def to_x(at, source, place):
        part = block(source, place)
        return remote(part, part, x_send.at[at], x_recv.at[source], beside)

    def to_y(at, source, place):
        part = block(source, place)
        return remote(part, part, y_send.at[at], y_recv.at[source], across)

    def to_far(at, core, source, place):
        part = block(source, place)
        return remote(part, part, far_send.at[at], far_recv.at[source], across if core == 0 else beside)

    def wait_swap(source):
        part = block(source, group)
        remote(part, part, swap_send.at[0], swap_recv.at[source], {"expert": chain.sibling}).wait_recv()

    for at, (source, core, step) in enumerate(sources):
        if step == 0:
            pl.when(chain.c != core)(lambda: wait_swap(source))
        else:
            wait_swap(source)
        to_x(at, source, group).start()
        to_y(at, source, group).start()
    for gather in wide:
        gather.service(1)
    for at, (source, core, _) in enumerate(sources):
        to_x(at, source, from_x).wait_recv()
        to_y(at, source, from_y).wait_recv()
        to_far(at, core, source, from_x if core == 0 else from_y).start()
    for step in range(2, n):
        for gather in wide:
            gather.service(step)

    def near(slot, peer):
        return remote(cot_ref, near_ref.at[slot], near_send.at[slot], near_recv.at[slot], {"expert": peer})

    pl.when(chain.has_up)(lambda: near(0, chain.up).start())
    pl.when(chain.has_down)(lambda: near(1, chain.down).start())
    near(2, chain.sibling).start()
    for gather in wide:
        for z in range(n):
            gather.wait_sibling(jnp.int32(z))
        gather.keep().wait()
    hidden_out = pltpu.make_async_copy(hidden_ref, hidden_hbm, out_sems.at[0])
    hidden_out.start()
    for at, (source, core, _) in enumerate(sources):
        to_far(at, core, source, far).wait_recv()
    projection_out = pltpu.make_async_copy(projection_ref, projection_hbm, out_sems.at[1])
    projection_out.start()
    pair_rows = 2 * own.shape[0]
    shard_rows = 4 * rows

    def raw_out(step):
        tokens = pl.ds(pl.multiple_of(step * pair_rows, pair_rows), pair_rows)
        return pltpu.make_async_copy(raw_ref.at[tokens], raw_hbm.at[tokens], out_sems.at[2 + step])

    @pl.loop(0, n)
    def each(step):
        tokens = pl.ds(pl.multiple_of(step * pair_rows, pair_rows), pair_rows)
        total = jnp.zeros((pair_rows, raw_ref.shape[1]), high)
        for source in range(peers):
            weight = projection_ref[source].reshape(shard_rows, raw_ref.shape[1])
            total = total + dot(hidden_ref[tokens, source * shard_rows : (source + 1) * shard_rows], weight)
        raw_ref[tokens] = total
        raw_out(step).start()

    for gather in wide:
        gather.finish()
    for at, peer in enumerate(others):
        part = all_named_ref.at[peer]
        remote(part, part, name_send.at[at], name_recv.at[peer], {"expert": peer}).wait_recv()
        names[at].wait_send()
    for at, (source, core, _) in enumerate(sources):
        to_x(at, source, group).wait_send()
        to_y(at, source, group).wait_send()
        to_far(at, core, source, from_x if core == 0 else from_y).wait_send()
    for copy in swaps:
        copy.wait_send()
    pl.when(chain.has_up)(lambda: near(0, chain.up).wait_send())
    pl.when(chain.has_down)(lambda: near(1, chain.down).wait_send())
    near(2, chain.sibling).wait_send()
    pl.when(chain.has_down)(lambda: near(0, chain.sibling).wait_recv())
    pl.when(chain.has_up)(lambda: near(1, chain.sibling).wait_recv())
    near(2, chain.sibling).wait_recv()
    hidden_out.wait()
    projection_out.wait()
    for step in range(n):
        raw_out(step).wait()


def run_gather(tokens, gain, routes, segments, cotangent, query_weight, key_matrix, value_matrix, peers, groups):
    length, width = tokens.shape
    n = peers // 2
    shard_rows, query_columns = query_weight.shape
    columns = query_columns // peers + 2 * key_matrix.shape[1] // n
    rows = shard_rows // groups
    dma = pltpu.SemaphoreType.DMA
    hidden, all_named, near, seg_col, projection, raw = pl.pallas_call(
        gather_kernel,
        out_shape=[
            jax.ShapeDtypeStruct((length * peers, width), low),
            jax.ShapeDtypeStruct((peers, length, 128), low),
            jax.ShapeDtypeStruct((3, length, width), low),
            jax.ShapeDtypeStruct((length * peers, 128), jnp.int32),
            jax.ShapeDtypeStruct((peers, groups, rows, columns), low),
            jax.ShapeDtypeStruct((length * peers, columns), high),
        ],
        in_specs=[VMEM] * 5 + [ANY] * 3,
        out_specs=[ANY, VMEM, VMEM, VMEM, ANY, ANY],
        scratch_shapes=[
            pltpu.VMEM((length, 128), low),
            pltpu.VMEM((length, width), low),
            pltpu.VMEM((peers, rows, columns), low),
            pltpu.VMEM((length * peers, width), low),
            pltpu.VMEM((peers, groups, rows, columns), low),
            pltpu.VMEM((length * peers, columns), high),
            pltpu.VMEM((rows, query_columns), low),
            pltpu.VMEM((rows, key_matrix.shape[1]), low),
            pltpu.VMEM((rows, key_matrix.shape[1]), low),
            *Gather.semaphores(n),
            *Gather.semaphores(n),
            dma((peers - 1,)), dma((peers,)),
            dma((peers - 1,)), dma((peers,)),
            dma((peers,)), dma((peers,)), dma((peers,)), dma((peers,)), dma((peers,)), dma((peers,)),
            dma((2 + n,)),
            dma((3,)), dma((3,)), dma((3,)),
        ],
        compiler_params=communicating(1),
        cost_estimate=pl.CostEstimate(flops=0, bytes_accessed=64 << 20, transcendentals=0),
        name="gather_hidden",
    )(tokens, gain, routes, segments, cotangent, query_weight, key_matrix, value_matrix)
    return hidden, all_named, near, seg_col, projection.reshape(width, columns), raw


def attention_heads(
    raw_ref, query_gain_ref, key_gain_ref, cos_ref, sin_ref, col_ref, row_ref,
    mixed_ref, query_low_ref, key_low_ref, value_low_ref, inverse_ref, value_wide,
):
    head_size = cos_ref.shape[1]
    heads = mixed_ref.shape[1] // head_size
    key_raw = raw_ref[:, heads * head_size : (heads + 1) * head_size]
    key_low_ref[...] = rotate(norm_rows(key_raw, key_gain_ref[...]), cos_ref[...], sin_ref[...]).astype(low)
    value_low_ref[...] = raw_ref[:, (heads + 1) * head_size :].astype(low)
    value_wide[:, :head_size] = value_low_ref[...]
    value_wide[:, head_size:] = jnp.ones_like(value_low_ref)

    @pl.loop(0, heads)
    def each(head):
        columns = pl.ds(pl.multiple_of(head * head_size, head_size), head_size)
        rotated = rotate(norm_rows(raw_ref[:, columns], query_gain_ref[...]), cos_ref[...], sin_ref[...])
        query_low_ref[:, columns] = (rotated * (head_size**-0.5 * log2e)).astype(low)
        for begin, rows, first, keys in key_spans(raw_ref.shape[0]):
            block = pl.ds(begin, rows)
            scores = dot_last(query_low_ref[block, columns], key_low_ref[pl.ds(first, keys)])
            allowed = tile_mask(col_ref, row_ref, begin, rows, first, keys)
            terms = jnp.where(allowed, jnp.exp2(scores), 0.0).astype(low)
            sums = dot(terms, value_wide[pl.ds(first, keys)])
            inverse = 1.0 / sums[:, head_size:]
            mixed_ref[block, columns] = (sums[:, :head_size] * inverse).astype(low)
            inverse_ref[block, columns] = inverse


class Split:
    both = slice(None)

    @staticmethod
    def take(ref, z, half, columns=slice(None)):
        block = ref[pl.ds(2 * z, 2), half, :, columns]
        return block.reshape(-1, block.shape[-1])

    @staticmethod
    def put(ref, z, half, value, columns=slice(None)):
        halves = (2, 2) if half is Split.both else (2,)
        ref[pl.ds(2 * z, 2), half, :, columns] = value.reshape(*halves, ref.shape[2], value.shape[1])

    @staticmethod
    def every(ref, columns=slice(None)):
        block = ref[:, :, :, columns]
        return block.reshape(block.shape[0] * block.shape[1] * block.shape[2], block.shape[3])


def expert_block(rows_all, plain_of, gate_w, up_w, gate_col, gated, grad_gate, grad_up, z, half):
    hidden = gate_w.shape[1]
    chunk = hidden // 3 if hidden % 384 == 0 else hidden
    gate_grad = jnp.zeros_like(gate_col)
    for begin in range(0, hidden, chunk):
        units = pl.ds(begin, chunk)
        gate_pre = dot(Split.take(rows_all, z, half), gate_w[:, units])
        up_pre = dot(Split.take(rows_all, z, half), up_w[:, units])
        plain = plain_of(units)
        share = 1.0 / (1.0 + jnp.exp(-gate_pre))
        silu = gate_pre * share
        act = silu * up_pre
        gate_grad = gate_grad + jnp.sum(act * plain, axis=-1, keepdims=True)
        Split.put(gated, z, half, (act * gate_col).astype(low), units)
        grad_act = plain * gate_col
        slope = share + silu * (1.0 - share)
        Split.put(grad_gate, z, half, (grad_act * up_pre * slope).astype(low), units)
        Split.put(grad_up, z, half, (grad_act * silu).astype(low), units)
    return gate_grad


def gate_columns(lanes, expert, gate_grad):
    sent = jnp.where(lanes == expert, gate_grad, 0.0)
    upper = sent.astype(low).astype(high)
    lower = (sent - upper).astype(low).astype(high)
    return upper + pltpu.roll(lower, 64, 1)


class Tiles:
    def __init__(self, grads, stage, sems, gated, grad_gate, grad_up, rows_all, cots):
        self.grads, self.stage, self.sems = grads, stage, sems
        self.sources = ((grad_gate, rows_all), (grad_up, rows_all), (gated, cots))
        self.groups = sems.shape[1]
        self.hidden = gated.shape[3]
        self.piece = self.hidden // self.groups
        self.tile = stage.shape[2]

    def copies(self, kind, at, slot):
        piece = self.piece
        made = []
        for part in range(self.groups):
            if kind < 2:
                columns = pl.ds(pl.multiple_of(at * self.tile, self.tile), self.tile)
                target = self.grads.at[part, pl.ds(kind * piece, piece), columns]
            else:
                columns = pl.ds(part * self.tile, self.tile)
                target = self.grads.at[at, pl.ds(2 * piece, piece), columns]
            source = self.stage.at[slot, pl.ds(part * piece, piece)]
            made.append(pltpu.make_async_copy(source, target, self.sems.at[slot, part]))
        return made

    def run(self, kind):
        left, right = self.sources[kind]

        @pl.loop(0, self.groups)
        def each(at):
            slot = at % 2
            if kind == 0:
                pl.when(at >= 2)(lambda: wait_all(self.copies(kind, at, slot)))
            else:
                wait_all(self.copies(kind, at, slot))
            span = pl.ds(pl.multiple_of(at * self.tile, self.tile), self.tile)
            self.stage[slot] = dot_first(Split.every(left), Split.every(right, span)).astype(low)
            for copy in self.copies(kind, at, slot):
                copy.start()

    def finish(self):
        for slot in range(2):
            wait_all(self.copies(0, jnp.int32(slot), slot))


def first_kernel(
    query_gain_ref, key_gain_ref, row_ref, tokens_ref, gain_ref, named_ref, router_in, cot_ref, near_ref,
    raw_hbm, cos_hbm, sin_hbm, col_hbm, weight_hbm, gate_hbm, up_hbm, down_hbm,
    key_low_ref, value_low_ref, own_gates_ref, resid_hbm, ffn_hbm, gates_hbm,
    mixed_hbm, query_low_hbm, inverse_hbm, rows_hbm, cots_hbm, gated_hbm, parts_hbm, grads_hbm,
    resid_ref, ffn_ref, gates_ref,
    raw_ref, cos_ref, sin_ref, col_ref, weight_ref, mixed_ref, query_low_ref, inverse_ref, value_wide, router_ref, plain, attn_parts, rows_all, cots, gate_w, up_w, down_w, gated, grad_gate, grad_up,
    part_stage, tile_stage, load_sems, rows_sems, part_sems, tile_sems, cot_send, cot_recv, cot_local, *transfers,
):
    chain = Chain()
    n = chain.n
    _, _, rows, width = rows_all.shape
    block_rows = 2 * rows
    loads = [
        pltpu.make_async_copy(source, target, load_sems.at[at])
        for at, (source, target) in enumerate(
            (
                (raw_hbm, raw_ref), (cos_hbm, cos_ref), (sin_hbm, sin_ref), (col_hbm, col_ref),
                (weight_hbm, weight_ref), (down_hbm.at[0], down_w), (gate_hbm.at[0], gate_w),
                (up_hbm.at[0], up_w),
            )
        )
    ]
    for load in loads:
        load.start()
    chain.greet()
    cot_gather = NearGather(
        chain, cot_ref, near_ref, lambda z, c: cots.at[2 * z + c], cot_send, cot_recv, cot_local
    )
    cot_gather.begin()
    wait_all(loads[:4])
    router_ref[...] = jnp.zeros_like(router_ref)
    router_ref[: router_in.shape[0]] = router_in[...]
    attention_heads(
        raw_ref, query_gain_ref, key_gain_ref, cos_ref, sin_ref, col_ref, row_ref,
        mixed_ref, query_low_ref, key_low_ref, value_low_ref, inverse_ref, value_wide,
    )
    attention_copies = [
        pltpu.make_async_copy(source, target, rows_sems.at[2 + at])
        for at, (source, target) in enumerate(
            ((mixed_ref, mixed_hbm), (query_low_ref, query_low_hbm), (inverse_ref, inverse_hbm))
        )
    ]
    for copy in attention_copies:
        copy.start()
    loads[4].wait()
    scatters, gathers = [], []
    for half in range(2):
        pair, flow, *rest = transfers[9 * half : 9 * half + 9]
        scatters.append(
            Scatter(chain, lambda z, c, half=half: attn_parts.at[z, c, half], pair, flow, *rest[:4])
        )
        gathers.append(
            Gather(chain, ffn_ref.at[half], lambda z, c, half=half: rows_all.at[2 * z + c, half], *rest[4:])
        )

    def plain_rows(step):
        z = chain.nearest(step)
        pl.when(step == 0)(cot_gather.wait_placed)
        pl.when(step > 0)(lambda: cot_gather.wait_sibling(z))
        cot_rows = cots[pl.ds(2 * z, 2)].reshape(4 * rows, width)
        hidden = plain.shape[3]
        plain[pl.ds(2 * z, 2)] = dot_last(cot_rows, down_w[...]).reshape(2, 2, rows, hidden)

    @pl.loop(0, n)
    def project(step):
        z = chain.nearest(n - 1 - step)
        tokens = pl.ds(pl.multiple_of(z * 4 * rows, 4 * rows), 4 * rows)
        attn_parts[z] = dot(mixed_ref[tokens], weight_ref[...]).astype(low).reshape(2, 2, rows, width)
        for scatter in scatters:
            scatter.start_pair(z)
        pl.when(step < n - 1)(lambda: scatters[0].step(n - 1 - step))
        pl.when(step == 0)(lambda: loads[5].wait())
        pl.when(step == 1)(lambda: cot_gather.service(2))
        pl.when(step < n - 1)(lambda: plain_rows(step))

    def own_rows(half):
        span = pl.ds(half * rows, rows)
        scatters[half].total(resid_ref.at[span])
        resid_ref[span] += tokens_ref[span].astype(high)
        ffn_ref[half] = norm_rows(resid_ref[span], gain_ref[...]).astype(low)
        gathers[half].begin()

    scatters[1].step(n - 1)
    own_rows(0)
    scatters[1].step(n - 2)
    cot_gather.service(3)
    plain_rows(jnp.int32(3))
    lanes = lax.broadcasted_iota(jnp.int32, (block_rows, 128), 1)
    expert = lax.axis_index("expert") * gate_hbm.shape[0]
    tile = tile_stage.shape[2]
    wait_all(loads[6:])

    def part_copy(z, half, slot):
        return pltpu.make_async_copy(part_stage.at[slot], parts_hbm.at[pl.ds(2 * z, 2), half], part_sems.at[slot])

    @pl.loop(0, 2 * n)
    def each(turn):
        pl.when((turn >= 1) & (turn < n - 1))(lambda: gathers[0].service(turn))
        pl.when((turn >= 1) & (turn < n - 2))(lambda: scatters[1].step(n - 2 - turn))

        @pl.when(turn == n - 1)
        def middle():
            own_rows(1)
            gathers[0].service(n - 1)

        pl.when((turn >= n) & (turn < 2 * n - 1))(lambda: gathers[1].service(turn - n + 1))
        half, step = turn // n, turn % n
        z = chain.nearest(step)

        def arrived(gather):
            pl.when(step == 0)(lambda: gather.keep().wait())
            gather.wait_sibling(z)

        pl.when(half == 0)(lambda: arrived(gathers[0]))
        pl.when(half == 1)(lambda: arrived(gathers[1]))
        logits = dot_last(Split.take(rows_all, z, half), router_ref[...])
        named = Split.take(named_ref, z, half).astype(high) > 0.5
        top = jnp.max(jnp.where(named, logits, -1e30), axis=-1, keepdims=True)
        terms = jnp.where(named, jnp.exp(jnp.where(named, logits - top, 0.0)), 0.0)
        gates = terms / jnp.sum(terms, axis=-1, keepdims=True)
        Split.put(gates_ref, z, half, gates)

        @pl.when(step == 0)
        def own_gates():
            own_gates_ref[half] = jnp.where(chain.c == 0, gates[:rows], gates[rows:])

        gate_col = jnp.sum(jnp.where(lanes == expert, gates, 0.0), axis=-1, keepdims=True)
        gate_grad = expert_block(
            rows_all, lambda units: Split.take(plain, z, half, units), gate_w, up_w, gate_col, gated, grad_gate,
            grad_up, z, half,
        )
        slot = turn % 2

        pl.when(turn >= 2)(lambda: part_copy(z, half, slot).wait())

        @pl.loop(0, width // tile)
        def columns(at):
            span = pl.ds(pl.multiple_of(at * tile, tile), tile)
            grad_rows = dot_last(Split.take(grad_gate, z, half), gate_w[span, :])
            grad_rows = grad_rows + dot_last(Split.take(grad_up, z, half), up_w[span, :])
            part_stage[slot, :, :, span] = grad_rows.astype(low).reshape(2, rows, tile)

        sent = gate_columns(lanes, expert, gate_grad).astype(low)
        part_stage[slot, :, :, width:] = sent.reshape(2, rows, 128)
        part_copy(z, half, slot).start()

    whole_copies = [
        pltpu.make_async_copy(rows_all, rows_hbm, rows_sems.at[0]),
        pltpu.make_async_copy(cots, cots_hbm, rows_sems.at[1]),
        pltpu.make_async_copy(gated, gated_hbm, rows_sems.at[5]),
        pltpu.make_async_copy(resid_ref, resid_hbm, rows_sems.at[6]),
        pltpu.make_async_copy(ffn_ref, ffn_hbm, rows_sems.at[7]),
        pltpu.make_async_copy(gates_ref, gates_hbm, rows_sems.at[8]),
    ]
    for copy in whole_copies:
        copy.start()
    tiles = Tiles(grads_hbm, tile_stage, tile_sems, gated, grad_gate, grad_up, rows_all, cots)
    for kind in range(3):
        tiles.run(kind)
    for half in range(2):
        gathers[half].finish()
        scatters[half].finish()
    tiles.finish()
    for slot in range(2):
        part_copy(jnp.int32(0), 0, slot).wait()
    wait_all(whole_copies + attention_copies)
    cot_gather.finish()


def second_kernel(
    gates_ref, rows_hbm, cot_hbm, gate_hbm, up_hbm, down_hbm, parts_in, wide_hbm,
    sum_ref, gated_hbm, grads_hbm, first_a, first_b,
    rows_all, cots, gate_w, up_w, down_w, gated, grad_gate, grad_up, parts, tile_stage, load_sems, chip_sems,
    tile_sems, out_sem, port_send, port_recv, pair, flow, *scatter_sems,
):
    chain = Chain()
    n = chain.n
    width = rows_all.shape[3]
    block_rows = parts.shape[1]
    loads = [
        pltpu.make_async_copy(source, target, load_sems.at[at])
        for at, (source, target) in enumerate(
            (
                (gate_hbm.at[1], gate_w), (up_hbm.at[1], up_w), (down_hbm.at[1], down_w), (parts_in, parts),
            )
        )
    ]

    def chip_loads(z):
        block = pl.ds(2 * z, 2)
        return [
            pltpu.make_async_copy(rows_hbm.at[block], rows_all.at[block], chip_sems.at[0, z]),
            pltpu.make_async_copy(cot_hbm.at[block], cots.at[block], chip_sems.at[1, z]),
        ]

    for load in loads[:3]:
        load.start()
    for step in range(n):
        for load in chip_loads(chain.nearest(n - 1 - step)):
            load.start()
    loads[3].start()
    wide = WideSum(wide_hbm)
    chain.greet([wide.beside, wide.across])
    ports = Ports(port_send, port_recv)
    wide_sent = wide.first(first_a, first_b, ports)
    SquareSum.start(wide_sent)
    scatter = Scatter(chain, chip_block(parts, block_rows // 2), pair, flow, *scatter_sems)
    lanes = lax.broadcasted_iota(jnp.int32, (block_rows, 128), 1)
    expert = lax.axis_index("expert") * gate_hbm.shape[0] + 1
    tile = tile_stage.shape[2]
    wait_all(loads[:3])

    @pl.loop(0, n)
    def each(step):
        z = chain.nearest(n - 1 - step)
        wait_all(chip_loads(z))
        gates = Split.take(gates_ref, z, Split.both)
        gate_col = jnp.sum(jnp.where(lanes == expert, gates, 0.0), axis=-1, keepdims=True)
        gate_grad = expert_block(
            rows_all, lambda units: dot_last(Split.take(cots, z, Split.both), down_w[units, :]), gate_w, up_w,
            gate_col, gated, grad_gate, grad_up, z, Split.both,
        )
        pl.when(step == 0)(lambda: loads[3].wait())

        @pl.loop(0, width // tile)
        def columns(at):
            span = pl.ds(pl.multiple_of(at * tile, tile), tile)
            grad_rows = dot_last(Split.take(grad_gate, z, Split.both), gate_w[span, :])
            grad_rows = grad_rows + dot_last(Split.take(grad_up, z, Split.both), up_w[span, :])
            parts[z, :, span] = (parts[z, :, span].astype(high) + grad_rows).astype(low)

        sent = parts[z, :, width:].astype(high) + gate_columns(lanes, expert, gate_grad)
        parts[z, :, width:] = sent.astype(low)
        scatter.start_pair(z)
        pl.when(step < n - 1)(lambda: scatter.step(n - 1 - step))

    gated_copy = pltpu.make_async_copy(gated, gated_hbm, out_sem)
    gated_copy.start()
    tiles = Tiles(grads_hbm, tile_stage, tile_sems, gated, grad_gate, grad_up, rows_all, cots)
    for kind in range(3):
        tiles.run(kind)
    scatter.total(sum_ref)
    scatter.finish()
    tiles.finish()
    gated_copy.wait()
    SquareSum.arrive(wide_sent)
    ports.finish()


def split_rows(array, peers):
    return array.reshape(peers, 2, array.shape[0] // (2 * peers), array.shape[1])


def expert_scratch(gate_weight, up_weight, down_weight, peers, rows, width):
    hidden = gate_weight.shape[2]
    whole = pltpu.VMEM((peers, 2, rows, width), low)
    acts = pltpu.VMEM((peers, 2, rows, hidden), low)
    return [
        whole, whole,
        pltpu.VMEM(gate_weight.shape[1:], low),
        pltpu.VMEM(up_weight.shape[1:], low),
        pltpu.VMEM(down_weight.shape[1:], low),
        acts, acts, acts,
    ]


def run_first(
    raw, query_gain, key_gain, cosines, sines, seg_col, seg_row, weight, tokens, gain, named, router, cotangent, near, gate_weight, up_weight, down_weight,
    peers, groups,
):
    length, width = tokens.shape
    n, rows = peers // 2, length // 2
    hidden = gate_weight.shape[2]
    tile, sent = width // groups, width + 128
    full, local_width, head_size = length * peers, weight.shape[0], cosines.shape[1]
    dma = pltpu.SemaphoreType.DMA

    def split(columns, dtype):
        return jax.ShapeDtypeStruct((peers, 2, rows, columns), dtype)

    return pl.pallas_call(
        first_kernel,
        out_shape=[
            jax.ShapeDtypeStruct((full, head_size), low),
            jax.ShapeDtypeStruct((full, head_size), low),
            jax.ShapeDtypeStruct((2, rows, 128), high),
            jax.ShapeDtypeStruct((length, width), high),
            jax.ShapeDtypeStruct((2, rows, width), low),
            split(128, high),
            jax.ShapeDtypeStruct((full, local_width), low),
            jax.ShapeDtypeStruct((full, local_width), low),
            jax.ShapeDtypeStruct((full, local_width), high),
            split(width, low),
            split(width, low),
            split(hidden, low),
            split(sent, low),
            jax.ShapeDtypeStruct((groups, 3 * hidden // groups, width), low),
        ],
        in_specs=[VMEM] * 9 + [ANY] * 8,
        out_specs=[VMEM] * 3 + [ANY] * 11,
        scratch_shapes=[
            pltpu.VMEM((length, width), high),
            pltpu.VMEM((2, rows, width), low),
            pltpu.VMEM((peers, 2, rows, 128), high),
            pltpu.VMEM(raw.shape, high),
            pltpu.VMEM(cosines.shape, high),
            pltpu.VMEM(sines.shape, high),
            pltpu.VMEM(seg_col.shape, jnp.int32),
            pltpu.VMEM(weight.shape, low),
            pltpu.VMEM((full, local_width), low),
            pltpu.VMEM((full, local_width), low),
            pltpu.VMEM((full, local_width), high),
            pltpu.VMEM((full, 2 * head_size), low),
            pltpu.VMEM((128, width), low),
            pltpu.VMEM((peers, 2, rows, hidden), high),
            pltpu.VMEM((n, 2, 2, rows, width), low),
            *expert_scratch(gate_weight, up_weight, down_weight, peers, rows, width),
            pltpu.VMEM((2, 2, rows, sent), low),
            pltpu.VMEM((2, hidden, tile), low),
            dma((8,)), dma((9,)), dma((2,)), dma((2, groups)),
            *NearGather.semaphores(n),
            *(Scatter.buffers(n, rows, width) + Gather.semaphores(n)) * 2,
        ],
        compiler_params=communicating(3),
        cost_estimate=pl.CostEstimate(flops=0, bytes_accessed=120 << 20, transcendentals=0),
        name="attention_and_first_expert",
    )(
        query_gain, key_gain, seg_row, tokens, gain, split_rows(named.reshape(-1, 128), peers), router,
        cotangent.reshape(2, rows, width), near.reshape(3, 2, rows, width), raw, cosines, sines, seg_col, weight,
        gate_weight, up_weight, down_weight,
    )


def run_second(gates, rows_all, cotangents, gate_weight, up_weight, down_weight, parts, first_grads, peers, groups):
    _, _, rows, width = rows_all.shape
    n, length = peers // 2, 2 * rows
    hidden = gate_weight.shape[2]
    tile, sent = width // groups, width + 128
    dma = pltpu.SemaphoreType.DMA
    return pl.pallas_call(
        second_kernel,
        out_shape=[
            jax.ShapeDtypeStruct((length, sent), high),
            jax.ShapeDtypeStruct((peers, 2, rows, hidden), low),
            jax.ShapeDtypeStruct((groups, 3 * hidden // groups, width), low),
            *wide_shapes(first_grads)[0],
        ],
        in_specs=[VMEM] + [ANY] * 7,
        out_specs=[VMEM, ANY, ANY, ANY, ANY],
        scratch_shapes=[
            *expert_scratch(gate_weight, up_weight, down_weight, peers, rows, width),
            pltpu.VMEM((n, 2 * length, sent), low),
            pltpu.VMEM((2, hidden, tile), low),
            dma((4,)), dma((2, n)), dma((2, groups)), dma(()), dma((4,)), dma((4,)),
            *Scatter.buffers(n, length, sent),
        ],
        compiler_params=communicating(7),
        cost_estimate=pl.CostEstimate(flops=0, bytes_accessed=120 << 20, transcendentals=0),
        name="second_expert",
    )(
        gates, rows_all, cotangents, gate_weight, up_weight, down_weight, parts.reshape(n, 2 * length, sent),
        first_grads,
    )


def attention_block_backward(
    span_of, raw_ref, query_low_ref, key_low_ref, value_low_ref, inverse_ref, mixed_ref, grad_mixed_ref,
    query_gain_ref, cos_ref, sin_ref, col_ref, row_ref, grad_query_ref, grad_key_ref, grad_value_ref, grad_gain_ref,
):
    begin, rows, first, keys = span_of
    head_size = key_low_ref.shape[1]
    heads = query_low_ref.shape[1] // head_size
    block, span = pl.ds(begin, rows), pl.ds(first, keys)

    @pl.loop(0, heads)
    def each(head):
        columns = pl.ds(pl.multiple_of(head * head_size, head_size), head_size)
        query_low = query_low_ref[block, columns]
        key_low = key_low_ref[span]
        scaled = grad_mixed_ref[block, columns].astype(high) * inverse_ref[block, columns]
        row_term = jnp.sum(scaled * mixed_ref[block, columns].astype(high), axis=-1, keepdims=True)
        scaled = scaled.astype(low)
        scores = dot_last(query_low, key_low)
        allowed = tile_mask(col_ref, row_ref, begin, rows, first, keys)
        terms = jnp.where(allowed, jnp.exp2(scores), 0.0)
        grad_probs = dot_last(scaled, value_low_ref[span])
        grad_scores = (terms * (grad_probs - row_term)).astype(low)
        grad_value_ref[span] += dot_first(terms.astype(low), scaled)
        grad_key_ref[span] += dot_first(grad_scores, query_low) * (1.0 / log2e)
        grad_rotated = dot(grad_scores, key_low) * head_size**-0.5
        grad_normed = unrotate(grad_rotated, cos_ref[block], sin_ref[block])
        grad_raw, gain_rows = norm_back(raw_ref[block, columns], query_gain_ref[...], grad_normed)
        grad_query_ref[block, columns] = grad_raw.astype(low)
        grad_gain_ref[...] += jnp.broadcast_to(jnp.sum(gain_rows, axis=0, keepdims=True), grad_gain_ref.shape)


def input_kernel(
    sums_ref, own_gates_ref, ffn_ref, resid_ref, cot_ref, gain_ffn_ref, router_in, weight_ref,
    query_gain_ref, key_gain_ref, row_ref, tokens_ref, gain_ref,
    raw_hbm, query_low_hbm, key_low_hbm, value_low_hbm, inverse_hbm, mixed_hbm, cos_hbm, sin_hbm, col_hbm,
    projection_hbm, hidden_hbm, wide_0, wide_0a, wide_0b, wide_1,
    input_grad_ref, out_own_ref, gain_grad_ref, ffn_gain_grad_ref, query_gain_grad_ref, key_gain_grad_ref,
    router_grad_ref, projection_grad_hbm, second_a, second_b, first_a, first_b,
    raw_ref, query_low_ref, key_low_ref, value_low_ref, inverse_ref, mixed_ref, cos_ref, sin_ref, col_ref,
    projection_ref, hidden_ref,
    router_ref, own, attn_ref, grad_mixed, grad_resid, own_pair, their_pair, key_part, value_part, columns,
    parts, projection_grad, out_grad, load_sems, store_sem, swap_send, swap_recv, port_send, port_recv,
    wide_left, wide_right, wide_sems,
    send_a, recv_a, local_a, send_b, recv_b, local_b, pair, flow, *rest,
):
    chain = Chain()
    n = chain.n
    scatter_sems, square_buffers = rest[:4], rest[4:]
    full, head_size = key_part.shape
    _, _, rows, width = attn_ref.shape
    query_width = query_low_ref.shape[1]
    sources = (
        raw_hbm.at[:, pl.ds(0, query_width + head_size)], query_low_hbm, key_low_hbm, value_low_hbm, inverse_hbm, mixed_hbm, cos_hbm, sin_hbm, col_hbm,
        projection_hbm, hidden_hbm,
    )
    targets = (
        raw_ref, query_low_ref, key_low_ref, value_low_ref, inverse_ref, mixed_ref, cos_ref, sin_ref, col_ref,
        projection_ref, hidden_ref,
    )
    loads = [
        pltpu.make_async_copy(source, target, load_sems.at[at])
        for at, (source, target) in enumerate(zip(sources, targets))
    ]
    wide = WideSum(wide_0)
    wide_loads = wide.load(wide_0a, wide_0b, wide_left, wide_right, wide_sems)
    for load in wide_loads + loads:
        load.start()
    chain.greet([wide.beside, wide.across])
    ports = Ports(port_send, port_recv)
    wide_first = WideSum(wide_1).first(first_a, first_b, ports)
    SquareSum.start(wide_first)
    router_ref[...] = jnp.zeros_like(router_ref)
    router_ref[: router_in.shape[0]] = router_in[...]
    sent = sums_ref[:, width:]
    left = lax.broadcasted_iota(jnp.int32, sent.shape, 1) < 64
    grad_gates = jnp.where(left, sent + pltpu.roll(sent, 64, 1), 0.0)
    gates = own_gates_ref[...]
    inner = jnp.sum(gates * grad_gates, axis=-1, keepdims=True)
    grad_logits = (gates * (grad_gates - inner)).astype(low)
    grad_hidden = sums_ref[:, :width] + dot(grad_logits, router_ref[...])
    grad_rows, gain_rows = norm_back(resid_ref[...], gain_ffn_ref[...], grad_hidden)
    grad_resid[...] = cot_ref[...].astype(high) + grad_rows
    own[...] = grad_resid[...].astype(low).reshape(2, rows, width)
    gathers = [
        Gather(chain, own.at[half], lambda z, c, half=half: attn_ref.at[2 * z + c, half], *sems)
        for half, sems in enumerate(((send_a, recv_a, local_a), (send_b, recv_b, local_b)))
    ]
    for gather in gathers:
        gather.begin()
    wait_all(wide_loads)
    wide_second = wide.second(wide_left, wide_right, second_a, second_b, ports)
    router_grad_ref[...] = dot_first(grad_logits, ffn_ref[...])[: router_grad_ref.shape[0]]
    ffn_gain_grad_ref[...] = jnp.broadcast_to(
        jnp.sum(gain_rows, axis=0, keepdims=True), ffn_gain_grad_ref.shape
    )
    key_part[...] = jnp.zeros_like(key_part)
    value_part[...] = jnp.zeros_like(value_part)
    query_gain_grad_ref[...] = jnp.zeros_like(query_gain_grad_ref)
    wait_all(loads[:9])
    spans = key_spans(full)

    @pl.loop(0, n)
    def blocks(step):
        z = chain.nearest(step)
        for gather in gathers:
            pl.when(step > 0)(lambda: gather.service(step))
        for gather in gathers:
            pl.when(step == 0)(lambda: gather.keep().wait())
            gather.wait_sibling(z)
        tokens = pl.ds(pl.multiple_of(z * 4 * rows, 4 * rows), 4 * rows)
        grad_mixed[tokens] = dot_last(Split.take(attn_ref, z, Split.both), weight_ref[...]).astype(low)
        for at, span_of in enumerate(spans):

            @pl.when(z == at)
            def backward():
                attention_block_backward(
                    span_of, raw_ref, query_low_ref, key_low_ref, value_low_ref, inverse_ref, mixed_ref, grad_mixed,
                    query_gain_ref, cos_ref, sin_ref, col_ref, row_ref, columns, key_part, value_part,
                    query_gain_grad_ref,
                )

    own_pair[:, :head_size] = key_part[...].astype(low)
    own_pair[:, head_size:] = value_part[...].astype(low)
    swap = pltpu.make_async_remote_copy(
        src_ref=own_pair,
        dst_ref=their_pair,
        send_sem=swap_send,
        recv_sem=swap_recv,
        device_id={"expert": chain.sibling},
        device_id_type=MESH,
    )
    swap.start()
    first = chain.c == 0
    wait_all(loads[9:])
    shared = pl.ds(query_width, head_size)
    projection_ref[:, shared] = jnp.where(
        first, projection_ref[:, shared], projection_ref[:, query_width + head_size :]
    )
    own_width = query_width + head_size
    swap.wait_recv()
    grad_key = key_part[...] + their_pair[:, :head_size].astype(high)
    grad_value = value_part[...] + their_pair[:, head_size:].astype(high)
    key_raw = raw_ref[:, query_width:]
    grad_key, gain_rows = norm_back(
        key_raw, key_gain_ref[...], unrotate(grad_key, cos_ref[...], sin_ref[...])
    )
    columns[:, query_width:] = jnp.where(first, grad_key, grad_value).astype(low)
    key_gain = jnp.where(first, jnp.sum(gain_rows, axis=0, keepdims=True), 0.0)
    key_gain_grad_ref[...] = jnp.broadcast_to(key_gain, key_gain_grad_ref.shape)
    pair_rows = parts.shape[1]
    scatter = Scatter(chain, chip_block(parts, pair_rows // 2), pair, flow, *scatter_sems)
    out_total = SquareSum(out_grad, out_own_ref, *square_buffers, ports)
    projection_tile = projection_grad.shape[0] // n
    out_tile = width // n

    @pl.loop(0, n)
    def each(step):
        z = chain.nearest(n - 1 - step)
        tokens = pl.ds(pl.multiple_of(z * pair_rows, pair_rows), pair_rows)
        parts[z] = dot_last(columns[tokens], projection_ref[:, :own_width]).astype(low)
        scatter.start_pair(z)
        pl.when(step < n - 1)(lambda: scatter.step(n - 1 - step))

        @pl.when(step == 0)
        def out_gradient():
            @pl.loop(0, n)
            def tiles(at):
                span = pl.ds(pl.multiple_of(at * out_tile, out_tile), out_tile)
                out_grad[:, span] = dot_first(mixed_ref[...], Split.every(attn_ref, span)).astype(low)

            out_total.begin()
            SquareSum.start(wide_second)

        span = pl.ds(pl.multiple_of(step * projection_tile, projection_tile), projection_tile)
        projection_grad[span] = dot_first(hidden_ref[:, span], columns[...]).astype(low)

    projection_store = pltpu.make_async_copy(projection_grad, projection_grad_hbm, store_sem)
    projection_store.start()
    out_total.exchange()
    scatter.total(input_grad_ref)
    grad_rows, gain_rows = norm_back(tokens_ref[...].astype(high), gain_ref[...], input_grad_ref[...])
    input_grad_ref[...] = grad_resid[...] + grad_rows
    gain_grad_ref[...] = jnp.broadcast_to(jnp.sum(gain_rows, axis=0, keepdims=True), gain_grad_ref.shape)
    out_total.settle()
    SquareSum.arrive(wide_first + wide_second)
    swap.wait_send()
    for gather in gathers:
        gather.finish()
    scatter.finish()
    ports.finish()
    projection_store.wait()


def run_input(
    sums, own_gates, ffn, resid, cotangent, gain_ffn, router, out_weight, raw, query_low, key_low, value_low,
    inverse, mixed, query_gain, key_gain, cosines, sines, seg_col, seg_row, projection, hidden, tokens, gain,
    first_wide, second_grads, experts, peers,
):
    length, width = tokens.shape
    n, rows = peers // 2, length // 2
    full, head_size = key_low.shape
    query_width = query_low.shape[1]
    loaded = [
        raw, query_low, key_low, value_low, inverse, mixed, cosines, sines, seg_col, projection, hidden,
    ]
    dma = pltpu.SemaphoreType.DMA
    wide_first, wide_second = wide_shapes(second_grads)
    half = (2, *wide_second[0].shape)
    (
        input_grad, out_own, gain_grad, ffn_gain_grad, query_gain_grad, key_gain_grad, router_grad, projection_grad,
        *wide,
    ) = (
        pl.pallas_call(
            input_kernel,
            out_shape=[
                jax.ShapeDtypeStruct((length, width), high),
                jax.ShapeDtypeStruct((query_width // 4, width), low),
                jax.ShapeDtypeStruct((8, width), high),
                jax.ShapeDtypeStruct((8, width), high),
                jax.ShapeDtypeStruct((8, head_size), high),
                jax.ShapeDtypeStruct((8, head_size), high),
                jax.ShapeDtypeStruct((experts, width), high),
                jax.ShapeDtypeStruct((width, query_width + head_size), low),
                *wide_second,
                *wide_first,
            ],
            in_specs=[VMEM] * 13 + [ANY] * (len(loaded) + 4),
            out_specs=[VMEM] * 7 + [ANY] * 5,
            scratch_shapes=[
                pltpu.VMEM((full, query_width + head_size), high),
                *[pltpu.VMEM(array.shape, array.dtype) for array in loaded[1:]],
                pltpu.VMEM((128, width), low),
                pltpu.VMEM((2, rows, width), low),
                pltpu.VMEM((peers, 2, rows, width), low),
                pltpu.VMEM((full, query_width), low),
                pltpu.VMEM((length, width), high),
                pltpu.VMEM((full, 2 * head_size), low),
                pltpu.VMEM((full, 2 * head_size), low),
                pltpu.VMEM((full, head_size), high),
                pltpu.VMEM((full, head_size), high),
                pltpu.VMEM((full, query_width + head_size), low),
                pltpu.VMEM((n, 2 * length, width), low),
                pltpu.VMEM((width, query_width + head_size), low),
                pltpu.VMEM((query_width, width), low),
                dma((len(loaded),)), dma(()), dma(()), dma(()), dma((12,)), dma((12,)),
                pltpu.VMEM(half, low), pltpu.VMEM(half, low), dma((4,)),
                *Gather.semaphores(n) * 2,
                *Scatter.buffers(n, length, width),
                *SquareSum.buffers(query_width, width),
            ],
            compiler_params=communicating(5, 62),
            cost_estimate=pl.CostEstimate(flops=0, bytes_accessed=64 << 20, transcendentals=0),
            name="attention_backward_and_input",
        )(
            sums, own_gates.reshape(length, 128), ffn.reshape(length, width), resid, cotangent, gain_ffn, router,
            out_weight, query_gain, key_gain, seg_row, tokens, gain, *loaded, *first_wide, second_grads,
        )
    )
    return (
        input_grad, projection_grad, out_own, gain_grad, ffn_gain_grad, query_gain_grad, key_gain_grad, router_grad,
        wide[:2], wide[2:],
    )
def weights_kernel(
    attn_gain_ref, ffn_gain_ref, query_gain_ref, key_gain_ref, router_ref, out_own_ref, proj_hbm, resid_hbm,
    gated_0, gated_1, down_hbm, wide_hbm, wide_a, wide_b, done_hbm, done_a, done_b, done_second_a, done_second_b,
    query_grad_ref, key_grad_ref, value_grad_ref, out_grad_ref, small_out_ref, output_ref, wide_second_a, wide_second_b, sum_0, sum_1,
    proj_ref, resid_ref, gated, down_w, mixture, load_sems, all_proj, first_a, first_b, second_a, second_b,
    send_a, send_b, quarter, small, got, part, small_sum, total_mixture,
    port_send, port_recv, swap_send, swap_recv, send_1, recv_1, send_2, recv_2, send_3, recv_3,
    wide_left, wide_right, wide_sems, last, last_sems, pair, flow, *scatter_sems,
):
    peers = lax.axis_size("expert")
    me = lax.axis_index("expert")
    group, y, x, from_x, from_y = square()
    beside, across = {"dp": from_x}, {"dp": from_y}
    chain = Chain()
    scatter = Scatter(chain, chip_block(mixture, resid_ref.shape[0]), pair, flow, *scatter_sems)
    loads = [
        pltpu.make_async_copy(source, target, load_sems.at[at])
        for at, (source, target) in enumerate(
            (
                (proj_hbm, proj_ref), (gated_0, gated.at[0]), (gated_1, gated.at[1]),
                (down_hbm, down_w), (resid_hbm, resid_ref),
            )
        )
    ]
    wide = WideSum(wide_hbm)
    wide_loads = wide.load(wide_a, wide_b, wide_left, wide_right, wide_sems)
    for load in wide_loads + loads:
        load.start()
    width = resid_ref.shape[1]
    head_size = query_gain_ref.shape[1]
    small[...] = jnp.zeros_like(small)
    small[0:1] = attn_gain_ref[0:1]
    small[1:2] = ffn_gain_ref[0:1]
    small[2:3, :head_size] = query_gain_ref[0:1]
    small[3:4, :head_size] = key_gain_ref[0:1]
    small[8:] = router_ref[...]
    piece = width // peers

    def small_piece(ref, peer):
        return ref.at[:, pl.ds(pl.multiple_of(peer * piece, piece), piece)]

    barrier = pltpu.get_barrier_semaphore()
    others = [(me + shift) % peers for shift in range(1, peers)]
    groups = [(group + shift) % 4 for shift in range(1, 4)]
    for peer in others:
        pl.semaphore_signal(barrier, inc=1, device_id={"expert": peer}, device_id_type=MESH)
    for other in groups:
        pl.semaphore_signal(barrier, inc=1, device_id={"dp": other}, device_id_type=MESH)
    pl.semaphore_wait(barrier, peers + 2)

    shard_rows, columns = proj_ref.shape[1:]
    rows, half = shard_rows // 4, peers // 2
    ports = Ports(port_send, port_recv)

    def proj_part(side, q, ref=proj_ref):
        return ref.at[pl.ds(side * half, half), pl.ds(pl.multiple_of(q * rows, rows), rows)]

    def remote(source, target, send, recv, device):
        return pltpu.make_async_remote_copy(
            src_ref=source, dst_ref=target, send_sem=send, recv_sem=recv, device_id=device, device_id_type=MESH
        )

    def close(grads, first_a, first_b, second_a, second_b, total):
        middle = width // 2
        for side, first, second in ((0, first_a.at[y], second_a), (1, first_b.at[x], second_b)):
            columns = pl.ds(side * middle, middle)
            pieces = [
                pltpu.make_async_copy(source, last.at[at], last_sems.at[at])
                for at, source in enumerate((grads.at[group, :, columns], first, second))
            ]
            for copy in pieces:
                copy.start()
            wait_all(pieces)
            last[0] = (last[0].astype(high) + last[1].astype(high) + last[2].astype(high)).astype(low)
            store = pltpu.make_async_copy(last.at[0], total.at[:, columns], last_sems.at[3])
            store.start()
            store.wait()

    along_x = [2 * other + 1 - x for other in range(2)]
    along_y = [2 * (1 - y) + other for other in range(2)]
    proj_1a = [ports.copy(proj_part(0, along_x[k], proj_hbm), first_a.at[k], beside) for k in range(2)]
    proj_1b = [ports.copy(proj_part(1, along_y[k], proj_hbm), first_b.at[k], across) for k in range(2)]
    for copy in proj_1a + proj_1b:
        copy.start()
    out_copy = SquareCopy(out_own_ref, out_grad_ref, ports)
    out_copy.begin()

    small_1 = [
        remote(small_piece(small, peer), got.at[me], send_1.at[at], recv_1.at[me], {"expert": peer})
        for at, peer in enumerate(others)
    ]
    for copy in small_1:
        copy.start()
    got[me] = small_piece(small, me)[...]
    wait_all(loads)

    def mixture_rows(step):
        z = chain.nearest(chain.n - 1 - step)

        @pl.loop(0, 4)
        def columns(at):
            span = pl.ds(pl.multiple_of(at * (width // 4), width // 4), width // 4)
            mixture[z, :, span] = (dot(gated[0, z], down_w[0, :, span]) + dot(gated[1, z], down_w[1, :, span])).astype(low)

        scatter.start_pair(z)

    @pl.loop(0, chain.n)
    def each_chip(step):
        mixture_rows(step)


    own = group
    for_y, for_x = 2 * (1 - y) + x, 2 * y + 1 - x
    scatter.step(3) if chain.n > 3 else None
    for copy in proj_1a + proj_1b:
        copy.wait_recv()
    send_a[...] = (proj_part(0, for_y)[...].astype(high) + first_a[1 - y].astype(high)).astype(low)
    send_b[...] = (proj_part(1, for_x)[...].astype(high) + first_b[1 - x].astype(high)).astype(low)
    proj_2a = ports.copy(send_a, second_a, across)
    proj_2b = ports.copy(send_b, second_b, beside)
    proj_2a.start()
    proj_2b.start()
    wait_all(wide_loads)
    wide_sent = wide.second(wide_left, wide_right, wide_second_a, wide_second_b, ports)
    SquareSum.start(wide_sent)
    close(done_hbm, done_a, done_b, done_second_a, done_second_b, sum_0)
    scatter.step(2) if chain.n > 2 else None

    for at, peer in enumerate(others):
        remote(got.at[peer], got.at[peer], send_1.at[at], recv_1.at[peer], {"expert": peer}).wait_recv()
    total = got[0]
    for at in range(1, peers):
        total = total + got[at]
    part[group] = total
    small_2 = [
        remote(part.at[group], part.at[group], send_2.at[at], recv_2.at[group], {"dp": other})
        for at, other in enumerate(groups)
    ]
    for copy in small_2:
        copy.start()

    proj_2a.wait_recv()
    proj_2b.wait_recv()
    for side, first, second, at in ((0, first_a, second_a, y), (1, first_b, second_b, x)):
        quarter[pl.ds(side * half, half)] = (
            proj_part(side, own)[...].astype(high) + first[at].astype(high) + second[...].astype(high)
        ).astype(low)
    swaps = [
        remote(quarter.at[peer], all_proj.at[own, me], swap_send.at[at], swap_recv.at[me], {"expert": peer})
        for at, peer in enumerate(others)
    ]
    for copy in swaps:
        copy.start()
    all_proj[own, me] = quarter[me]

    for at, other in enumerate(groups):
        remote(part.at[other], part.at[other], send_2.at[at], recv_2.at[other], {"dp": other}).wait_recv()
    total = part[0]
    for at in range(1, 4):
        total = total + part[at]
    small_sum[me] = total
    small_3 = [
        remote(small_sum.at[me], small_sum.at[me], send_3.at[at], recv_3.at[me], {"expert": peer})
        for at, peer in enumerate(others)
    ]
    for copy in small_3:
        copy.start()

    for at, peer in enumerate(others):
        block = all_proj.at[own, peer]
        remote(block, block, swap_send.at[at], swap_recv.at[peer], {"expert": peer}).wait_recv()
    proj_gx = ports.copy(all_proj.at[own], all_proj.at[own], beside)
    proj_gy = ports.copy(all_proj.at[own], all_proj.at[own], across)
    proj_gx.start()
    proj_gy.start()
    far = 3 - group
    scatter.step(1) if chain.n > 1 else None
    out_copy.hand_on()
    SquareSum.arrive(wide_sent)
    close(wide_hbm, wide_a, wide_b, wide_second_a, wide_second_b, sum_1)

    def proj_half(q, side):
        return all_proj.at[q, pl.ds(side * half, half)]

    proj_gx.wait_recv()
    proj_gy.wait_recv()
    proj_fa = ports.copy(proj_half(from_x, 0), proj_half(from_x, 0), across)
    proj_fb = ports.copy(proj_half(from_y, 1), proj_half(from_y, 1), beside)
    proj_fa.start()
    proj_fb.start()
    query_width = columns - head_size

    def spread(q):
        block = pl.ds(pl.multiple_of(q * rows, rows), rows)
        for peer in range(peers):
            query_grad_ref[block, peer * query_width : (peer + 1) * query_width] = all_proj[q, peer, :, :query_width]
            shared = key_grad_ref if peer % 2 == 0 else value_grad_ref
            at = peer // 2 * head_size
            shared[block, at : at + head_size] = all_proj[q, peer, :, query_width:]

    spread(own)
    spread(from_x)
    spread(from_y)
    for at, peer in enumerate(others):
        block = small_sum.at[peer]
        remote(block, block, send_3.at[at], recv_3.at[peer], {"expert": peer}).wait_recv()
    for peer in range(peers):
        small_out_ref[:, peer * piece : (peer + 1) * piece] = small_sum[peer]
    scatter.total(total_mixture)
    output_ref[...] = (resid_ref[...] + total_mixture[...]).astype(low)
    out_copy.finish()
    proj_fa.wait_recv()
    proj_fb.wait_recv()
    spread(far)
    ports.finish()
    scatter.finish()
    for copy in small_1 + small_2 + small_3 + swaps:
        copy.wait_send()


def run_weights(
    grad_projection, out_own, attn_gain, ffn_gain, query_gain, key_gain, router, resid, first_gated, second_gated,
    down_weight, second_wide, first_wide, peers, kv_heads,
):
    width, columns = grad_projection.shape
    head_size = query_gain.shape[1]
    length = resid.shape[0]
    n = peers // 2
    shard_rows = width // peers
    rows, half = shard_rows // 4, peers // 2
    small_rows = 8 + router.shape[0]
    piece = (small_rows, width // peers)
    hidden = down_weight.shape[1]
    dma = pltpu.SemaphoreType.DMA
    kv_width = kv_heads * head_size
    query_width = columns - head_size

    _, wide_second = wide_shapes(second_wide[0])
    wide_half = (2, *wide_second[0].shape)

    def low_buffer(*shape):
        return pltpu.VMEM(shape, low)

    return pl.pallas_call(
        weights_kernel,
        out_shape=[
            jax.ShapeDtypeStruct((shard_rows, peers * query_width), low),
            jax.ShapeDtypeStruct((shard_rows, kv_width), low),
            jax.ShapeDtypeStruct((shard_rows, kv_width), low),
            jax.ShapeDtypeStruct((4 * out_own.shape[0], width), low),
            jax.ShapeDtypeStruct((small_rows, width), high),
            jax.ShapeDtypeStruct((length, width), low),
            *wide_second,
            *[jax.ShapeDtypeStruct(second_wide[0].shape[1:], low)] * 2,
        ],
        in_specs=[VMEM] * 6 + [ANY] * 13,
        out_specs=[VMEM] * 6 + [ANY] * 4,
        scratch_shapes=[
            low_buffer(peers, shard_rows, columns),
            pltpu.VMEM(resid.shape, high),
            low_buffer(2, n, 2 * length, hidden),
            low_buffer(*down_weight.shape),
            low_buffer(n, 2 * length, width),
            dma((5,)),
            low_buffer(4, peers, rows, columns),
            low_buffer(2, half, rows, columns),
            low_buffer(2, half, rows, columns),
            low_buffer(half, rows, columns),
            low_buffer(half, rows, columns),
            low_buffer(half, rows, columns),
            low_buffer(half, rows, columns),
            low_buffer(peers, rows, columns),
            pltpu.VMEM((small_rows, width), high),
            pltpu.VMEM((peers, *piece), high),
            pltpu.VMEM((4, *piece), high),
            pltpu.VMEM((peers, *piece), high),
            pltpu.VMEM((length, width), high),
            dma((16,)), dma((16,)),
            dma((peers - 1,)), dma((peers,)),
            dma((peers - 1,)), dma((peers,)),
            dma((3,)), dma((4,)),
            dma((peers - 1,)), dma((peers,)),
            low_buffer(*wide_half), low_buffer(*wide_half), dma((4,)),
            low_buffer(3, *wide_second[0].shape), dma((4,)),
            *Scatter.buffers(n, length, width),
        ],
        compiler_params=communicating(6),
        cost_estimate=pl.CostEstimate(flops=0, bytes_accessed=64 << 20, transcendentals=0),
        name="sum_weight_gradients",
    )(
        attn_gain, ffn_gain, query_gain, key_gain, router, out_own, grad_projection.reshape(peers, shard_rows, columns),
        resid, first_gated.reshape(n, 2 * length, hidden), second_gated.reshape(n, 2 * length, hidden),
        down_weight, *second_wide, *first_wide,
    )


def widen_kernel(
    gate_0, up_0, down_0, gate_1, up_1, down_1, query_in, key_in, value_in, out_in, small_ref,
    gate_ref, up_ref, down_ref, query_ref, key_ref, value_ref, out_ref,
    attn_gain_ref, ffn_gain_ref, query_gain_ref, key_gain_ref, router_ref,
):
    for expert, (gate, up, down) in enumerate(((gate_0, up_0, down_0), (gate_1, up_1, down_1))):

        @pl.when(pl.program_id(0) == expert)
        def place():
            gate_ref[0] = gate[...].astype(high)
            up_ref[0] = up[...].astype(high)
            tile = down_ref.shape[3]
            for part in range(down_ref.shape[1]):
                down_ref[0, part] = down[:, part * tile : (part + 1) * tile].astype(high)

    for source, target in ((query_in, query_ref), (key_in, key_ref), (value_in, value_ref), (out_in, out_ref)):
        target[...] = source[...].astype(high)

    @pl.when((pl.program_id(0) == 0) & (pl.program_id(1) == 0))
    def small():
        attn_gain_ref[...] = small_ref[0]
        ffn_gain_ref[...] = small_ref[1]
        query_gain_ref[...] = small_ref[2, : query_gain_ref.shape[0]]
        key_gain_ref[...] = small_ref[3, : key_gain_ref.shape[0]]
        router_ref[...] = small_ref[8:]


def run_widen(grads, weight_grads, small, head_size, hidden_units, model_width, groups):
    piece, tile = hidden_units // groups, model_width // groups
    operands, specs = [], []
    block = piece // groups

    def of_expert(expert):
        return lambda x, j: jnp.where(x == expert, j, 0 if expert else groups - 1)

    for expert, rows in enumerate(grads):
        turn = of_expert(expert)
        operands += [rows] * 3
        specs += [
            pl.BlockSpec((block, model_width), lambda x, j, turn=turn, at=at: (at * groups + turn(x, j), 0))
            for at in range(3)
        ]
    steps = 2 * groups
    small_shapes = [
        (model_width,), (model_width,), (head_size,), (head_size,), (small.shape[0] - 8, model_width),
    ]

    def rows_of(array):
        return pl.BlockSpec((array.shape[0] // steps, array.shape[1]), lambda x, j: (x * groups + j, 0))

    return pl.pallas_call(
        widen_kernel,
        grid=(2, groups),
        out_shape=[
            jax.ShapeDtypeStruct((2, piece, model_width), high),
            jax.ShapeDtypeStruct((2, piece, model_width), high),
            jax.ShapeDtypeStruct((2, groups, piece, tile), high),
            *[jax.ShapeDtypeStruct(array.shape, high) for array in weight_grads],
            *[jax.ShapeDtypeStruct(shape, high) for shape in small_shapes],
        ],
        in_specs=specs + [rows_of(array) for array in weight_grads] + [pl.BlockSpec(small.shape, lambda x, j: (0, 0))],
        out_specs=[
            pl.BlockSpec((1, block, model_width), lambda x, j: (x, j, 0)),
            pl.BlockSpec((1, block, model_width), lambda x, j: (x, j, 0)),
            pl.BlockSpec((1, groups, block, tile), lambda x, j: (x, 0, j, 0)),
            *[rows_of(array) for array in weight_grads],
            *[pl.BlockSpec(shape, lambda x, j, rank=len(shape): (0,) * rank) for shape in small_shapes],
        ],
        compiler_params=pltpu.CompilerParams(vmem_limit_bytes=60 << 20),
        name="widen",
    )(*operands, *weight_grads, small)


def gather_tokens(rows):
    return lax.all_gather(rows, "expert", axis=0, tiled=True)


def scatter_sum(partial):
    return lax.psum_scatter(partial, "expert", scatter_dimension=0, tiled=True)


def projection_gradients(grad_projection, peers, kv_heads, head_size):
    width, columns = grad_projection.shape
    shard_rows = width // peers
    local_width = columns - head_size
    sharers = peers // kv_heads
    grad_projection = grad_projection.reshape(peers, shard_rows, columns)
    grad_projection = lax.psum_scatter(grad_projection, "dp", scatter_dimension=1, tiled=True)
    grad_projection = lax.all_to_all(
        grad_projection, "expert", split_axis=0, concat_axis=0, tiled=True
    )
    grad_projection = lax.all_gather(grad_projection, "dp", axis=1, tiled=True)
    grad_query_w = (
        grad_projection[:, :, :local_width].transpose(1, 0, 2).reshape(shard_rows, peers * local_width)
    ).astype(high)
    shared = grad_projection[:, :, local_width:].reshape(kv_heads, sharers, shard_rows, head_size)
    kv_width = kv_heads * head_size
    grad_key_w = shared[:, 0].transpose(1, 0, 2).reshape(shard_rows, kv_width).astype(high)
    grad_value_w = shared[:, 1].transpose(1, 0, 2).reshape(shard_rows, kv_width).astype(high)
    return grad_query_w, grad_key_w, grad_value_w


def out_gradient(grad_out):
    summed = lax.psum_scatter(grad_out, "dp", scatter_dimension=0, tiled=True)
    return lax.all_gather(summed, "dp", axis=0, tiled=True).astype(high)


def constant_tables(length, head_size):
    half = head_size // 2
    freqs = np.float32(rope_base) ** (-np.arange(half, dtype=np.float32) * np.float32(2.0 / head_size))
    angles = np.arange(length, dtype=np.float32)[:, None] * freqs[None, :]
    cosines, sines = np.cos(angles), np.sin(angles)
    return (
        jnp.asarray(np.concatenate([cosines, cosines], 1), high),
        jnp.asarray(np.concatenate([-sines, sines], 1), high),
    )


def fits_kernels(peers, groups, sharers, experts, full_length, width):
    return groups == 4 and peers == 8 and sharers == 2 and experts == 2 * peers and full_length * width <= 1 << 21


def fused_layer(
    tokens, segments, routes, cotangent, norm_gain_attn, query_weight, key_matrix, value_matrix, query_gain,
    key_gain, out_weight, norm_gain_ffn, router_weight, gate_weight, up_weight, down_weight, heads,
):
    length, model_width = tokens.shape
    head_size = query_gain.shape[0]
    peers = lax.axis_size("expert")
    groups = lax.axis_size("dp")
    local_experts, _, hidden_units = gate_weight.shape
    experts = local_experts * peers
    full_length = length * peers
    kv_heads = peers // 2
    local_width = heads * head_size
    gain_attn_row = norm_gain_attn.reshape(1, model_width)
    gain_ffn_row = norm_gain_ffn.reshape(1, model_width)

    hidden, all_named, near, seg_col, projection, raw = run_gather(
        tokens, gain_attn_row, routes.T, segments, cotangent, query_weight, key_matrix, value_matrix, peers, groups
    )
    cosines, sines = constant_tables(full_length, head_size)
    seg_row = segments
    query_gain_row = query_gain.reshape(1, head_size)
    key_gain_row = key_gain.reshape(1, head_size)
    router = router_weight.T
    (
        key_low, value_low, own_gates, resid, ffn_local, gates, mixed, query_low, inverse, rows_all, cotangents,
        first_gated, parts, first_grads,
    ) = run_first(
        raw, query_gain_row, key_gain_row, cosines, sines, seg_col, seg_row, out_weight, tokens, gain_ffn_row,
        all_named, router, cotangent, near, gate_weight, up_weight, down_weight, peers, groups,
    )
    sums, second_gated, second_grads, *first_step = run_second(
        gates, rows_all, cotangents, gate_weight, up_weight, down_weight, parts, first_grads, peers, groups
    )
    (
        input_grad, grad_projection, out_own, gain_attn_part, gain_ffn_part, query_gain_part, key_gain_part,
        grad_router, first_end, second_step,
    ) = run_input(
        sums, own_gates, ffn_local, resid, cotangent, gain_ffn_row, router, out_weight, raw, query_low, key_low,
        value_low, inverse, mixed, query_gain_row, key_gain_row, cosines, sines, seg_col, seg_row, projection,
        hidden, tokens, gain_attn_row, (first_grads, *first_step), second_grads, experts, peers,
    )
    *weight_grads, small, output, _, _, first_sum, second_sum = run_weights(
        grad_projection, out_own, gain_attn_part, gain_ffn_part, query_gain_part, key_gain_part, grad_router,
        resid, first_gated, second_gated, down_weight, (second_grads, *second_step),
        (first_grads, *first_step, *first_end), peers, kv_heads,
    )
    grads = (first_sum, second_sum)
    gate_w, up_w, down_w, query_w, key_w, value_w, out_w, *sums = run_widen(
        grads, weight_grads, small, head_size, hidden_units, model_width, groups
    )
    gain_attn_grad, gain_ffn_grad, query_gain_grad, key_gain_grad, router_grad = sums
    return (
        output,
        input_grad,
        gain_attn_grad,
        query_w,
        key_w,
        value_w,
        query_gain_grad,
        key_gain_grad,
        out_w,
        gain_ffn_grad,
        router_grad.T,
        gate_w.transpose(0, 2, 1),
        up_w.transpose(0, 2, 1),
        down_w.reshape(local_experts, hidden_units, model_width // groups),
    )


def on_device(
    tokens,
    segments,
    routes,
    cotangent,
    norm_gain_attn,
    query_weight,
    key_matrix,
    value_matrix,
    query_gain,
    key_gain,
    out_weight,
    norm_gain_ffn,
    router_weight,
    gate_weight,
    up_weight,
    down_weight,
):
    length, model_width = tokens.shape
    head_size = query_gain.shape[0]
    peers = lax.axis_size("expert")
    groups = lax.axis_size("dp")
    me = lax.axis_index("expert")
    group = lax.axis_index("dp")
    shard_rows, query_width = query_weight.shape
    kv_width = key_matrix.shape[1]
    kv_heads = kv_width // head_size
    heads = query_width // head_size // peers
    sharers = peers // kv_heads
    local_width = heads * head_size
    local_experts = gate_weight.shape[0]
    experts = local_experts * peers
    full_length = length * peers
    piece = shard_rows // groups

    if fits_kernels(peers, groups, sharers, experts, full_length, model_width):
        return fused_layer(
            tokens, segments, routes, cotangent, norm_gain_attn, query_weight, key_matrix, value_matrix,
            query_gain, key_gain, out_weight, norm_gain_ffn, router_weight, gate_weight, up_weight, down_weight, heads,
        )

    def own_rows(matrix):
        return lax.dynamic_slice_in_dim(matrix, group * piece, piece, 0)

    def columns(matrix, width, copies):
        split = own_rows(matrix).reshape(piece, -1, width).transpose(1, 0, 2)
        return jnp.repeat(split, copies, axis=0)

    outgoing = jnp.concatenate(
        [
            columns(query_weight, local_width, 1),
            columns(key_matrix, head_size, sharers),
            columns(value_matrix, head_size, sharers),
        ],
        axis=2,
    )
    arrived = lax.all_to_all(outgoing, "expert", split_axis=0, concat_axis=0, tiled=True)
    projection = lax.all_gather(arrived, "dp", axis=1, tiled=True).reshape(model_width, -1)

    inputs = tokens.astype(high)
    hidden_local = norm_rows(inputs, norm_gain_attn).astype(low)
    hidden = gather_tokens(hidden_local)
    raw = dot(hidden, projection)
    cosines, sines = rotary_tables(full_length, head_size)
    seg_col = jnp.broadcast_to(segments.reshape(full_length, 1), (full_length, head_size))
    seg_row = jnp.broadcast_to(segments.reshape(1, full_length), (8, full_length))
    query_gain_row = query_gain.reshape(1, head_size)
    key_gain_row = key_gain.reshape(1, head_size)
    mixed, query_low, key_low, value_low, inverse = run_attention_forward(
        raw, heads, head_size, query_gain_row, key_gain_row, cosines, sines, seg_col, seg_row
    )
    attn = scatter_sum(dot(mixed, out_weight).astype(low))
    resid = inputs + attn.astype(high)
    ffn_local = norm_rows(resid, norm_gain_ffn).astype(low)
    ffn_rows = gather_tokens(ffn_local)
    cotangents = gather_tokens(cotangent)
    all_routes = gather_tokens(routes)

    def gates_of(rows, route_rows):
        logits = dot(rows, router_weight)
        named = jnp.any(
            route_rows[:, :, None] == jnp.arange(experts, dtype=jnp.int32)[None, None, :], axis=1
        )
        top = jnp.max(jnp.where(named, logits, -jnp.inf), axis=-1, keepdims=True)
        terms = jnp.where(named, jnp.exp(jnp.where(named, logits - top, 0.0)), 0.0)
        return terms / jnp.sum(terms, axis=-1, keepdims=True)

    gates_all = gates_of(ffn_rows, all_routes)
    own_gates = lax.dynamic_slice_in_dim(gates_all, me * local_experts, local_experts, 1)
    mixture = 0.0
    grad_rows = 0.0
    gate_grads, grad_gate_w, grad_up_w, grad_down_w = [], [], [], []
    for expert in range(local_experts):
        gate_col = own_gates[:, expert : expert + 1]
        gate_pre = dot(ffn_rows, gate_weight[expert])
        up_pre = dot(ffn_rows, up_weight[expert])
        share = jax.nn.sigmoid(gate_pre)
        silu = gate_pre * share
        act = silu * up_pre
        gated_act = (act * gate_col).astype(low)
        mixture = mixture + dot(gated_act, down_weight[expert])
        plain = dot_last(cotangents, down_weight[expert])
        gate_grads.append(jnp.sum(act * plain, axis=-1, keepdims=True))
        grad_act = plain * gate_col
        grad_gate_pre = (grad_act * up_pre * (share * (1.0 + gate_pre * (1.0 - share)))).astype(low)
        grad_up_pre = (grad_act * silu).astype(low)
        grad_rows = (
            grad_rows
            + dot_last(grad_gate_pre, gate_weight[expert])
            + dot_last(grad_up_pre, up_weight[expert])
        )
        hidden_units = gated_act.shape[1]
        grad_gate_w.append(dot_first(grad_gate_pre, ffn_rows).astype(low).reshape(groups, -1, model_width))
        grad_up_w.append(dot_first(grad_up_pre, ffn_rows).astype(low).reshape(groups, -1, model_width))
        cut_width = model_width // groups
        grad_down_w.append(
            jnp.stack([
                dot_first(gated_act, cotangents[:, part * cut_width : (part + 1) * cut_width]).astype(low)
                for part in range(groups)
            ])
        )

    gate_grad = jnp.concatenate(gate_grads, axis=1)
    lane_pad = 128 - 2 * experts % 128
    placed = jnp.zeros((full_length, experts), high)
    placed = lax.dynamic_update_slice_in_dim(placed, gate_grad, me * local_experts, 1)
    upper = placed.astype(low)
    lower = (placed - upper.astype(high)).astype(low)
    sent = jnp.concatenate(
        [grad_rows.astype(low), upper, lower, jnp.zeros((full_length, lane_pad), low)], axis=1
    )
    summed_rows = scatter_sum(sent)
    output = (resid + scatter_sum(mixture.astype(low)).astype(high)).astype(low)
    grad_gates = summed_rows[:, model_width : model_width + experts].astype(high) + summed_rows[
        :, model_width + experts : model_width + 2 * experts
    ].astype(high)
    gates = gates_of(ffn_local, routes)
    grad_logits = (
        gates * (grad_gates - jnp.sum(gates * grad_gates, axis=-1, keepdims=True))
    ).astype(low)
    grad_router = dot_first(ffn_local, grad_logits)
    grad_hidden_ffn = summed_rows[:, :model_width].astype(high) + dot_last(grad_logits, router_weight)
    grad_resid_norm, gain_rows_ffn = norm_back(resid, norm_gain_ffn, grad_hidden_ffn)
    grad_resid = cotangent.astype(high) + grad_resid_norm
    grad_attn = gather_tokens(grad_resid.astype(low))
    grad_mixed = dot_last(grad_attn, out_weight).astype(low)
    grad_out = dot_first(mixed, grad_attn)
    grad_query_low, grad_key_part, grad_value_part, query_gain_part = run_attention_backward(
        raw, query_low, key_low, value_low, inverse, mixed, grad_mixed, heads, head_size,
        query_gain_row, cosines, sines, seg_col, seg_row,
    )
    both = jnp.concatenate([grad_key_part, grad_value_part], axis=1)
    step = 1
    while step < sharers:
        swap = [(peer, peer ^ step) for peer in range(peers)]
        both = both + lax.ppermute(both.astype(low), "expert", swap).astype(high)
        step *= 2
    grad_key_rot, grad_value = both[:, :head_size], both[:, head_size:].astype(low)
    place = me % sharers
    half = head_size // 2
    swapped = jnp.concatenate([grad_key_rot[:, half:], grad_key_rot[:, :half]], axis=1)
    key_raw = raw[:, local_width : local_width + head_size]
    grad_key, key_gain_rows = norm_back(key_raw, key_gain, grad_key_rot * cosines - swapped * sines)
    grad_shared = jnp.where(
        place == 0, grad_key.astype(low), jnp.where(place == 1, grad_value, jnp.zeros_like(grad_value))
    )
    own_columns = jnp.concatenate([grad_query_low, grad_shared], axis=1)
    shared_weight = jnp.where(
        place == 0,
        projection[:, local_width : local_width + head_size],
        projection[:, local_width + head_size :],
    )
    own_weight = jnp.concatenate([projection[:, :local_width], shared_weight], axis=1)
    grad_hidden_attn = scatter_sum(dot_last(own_columns, own_weight).astype(low)).astype(high)
    grad_inputs_norm, gain_rows_attn = norm_back(inputs, norm_gain_attn, grad_hidden_attn)
    input_grad = grad_resid + grad_inputs_norm

    grad_query_w, grad_key_w, grad_value_w = projection_gradients(
        dot_first(hidden, own_columns).astype(low), peers, kv_heads, head_size
    )
    grad_out_w = out_gradient(grad_out.astype(low))

    wide = jnp.concatenate(grad_gate_w + grad_up_w, axis=1)
    wide = lax.psum_scatter(wide, "dp", scatter_dimension=0, tiled=True)
    wide = wide.reshape(2, local_experts, hidden_units // groups, model_width).transpose(0, 1, 3, 2)
    wide = wide.astype(high)
    down = jnp.concatenate(grad_down_w, axis=1)
    down = lax.psum_scatter(down, "dp", scatter_dimension=0, tiled=True)
    down = down.reshape(local_experts, hidden_units, cut_width).astype(high)
    expert_sums = (wide[0], wide[1], down)
    key_gain_grad = jnp.where(place == 0, jnp.sum(key_gain_rows, axis=0), 0.0)
    small = jnp.concatenate(
        [
            jnp.sum(gain_rows_attn, axis=0),
            jnp.sum(gain_rows_ffn, axis=0),
            query_gain_part[0],
            key_gain_grad,
            grad_router.reshape(-1),
        ]
    )
    small = lax.psum(small, ("dp", "expert"))
    cut = 2 * model_width
    return (
        output,
        input_grad,
        small[:model_width],
        grad_query_w,
        grad_key_w,
        grad_value_w,
        small[cut : cut + head_size],
        small[cut + head_size : cut + 2 * head_size],
        grad_out_w,
        small[model_width:cut],
        small[cut + 2 * head_size :].reshape(model_width, experts),
        *expert_sums,
    )


def solution(mesh):
    rows = P(("dp", "expert"), None)
    split = P("expert", None)
    cube = P("expert", None, None)
    cut = P("expert", None, "dp")
    return jax.shard_map(
        on_device,
        mesh=mesh,
        in_specs=(
            rows, P("dp", None), rows, rows, P(), split, split, split, P(), P(), split, P(), P(),
            cube, cube, cube,
        ),
        out_specs=(
            rows, rows, P(), split, split, split, P(), P(), split, P(), P(), cut, cut, cut,
        ),
        check_vma=False,
    )
```

```python
import functools

import jax
import jax.numpy as jnp
import numpy as np
from jax import lax
from jax.experimental import pallas as pl
from jax.experimental.pallas import tpu as pltpu
from jax.sharding import PartitionSpec as P

eps_norm = 1e-06
rope_base = 1000000.0
log2e = 1.4426950408889634
low = jnp.bfloat16
high = jnp.float32


def norm_rows(values, gain):
    factor = lax.rsqrt(jnp.mean(values * values, axis=-1, keepdims=True) + eps_norm)
    return values * factor * gain


def norm_back(values, gain, grad):
    factor = lax.rsqrt(jnp.mean(values * values, axis=-1, keepdims=True) + eps_norm)
    scaled = gain * grad
    inner = jnp.mean(values * scaled, axis=-1, keepdims=True)
    grad_values = factor * scaled - values * (factor * factor * factor * inner)
    return grad_values, grad * values * factor


def dot(left, right):
    return jnp.dot(left, right, preferred_element_type=high)


def dot_first(left, right):
    return lax.dot_general(left, right, (((0,), (0,)), ((), ())), preferred_element_type=high)


def dot_last(left, right):
    return lax.dot_general(left, right, (((1,), (1,)), ((), ())), preferred_element_type=high)


def rotary_tables(length, head_size):
    half = head_size // 2
    freqs = rope_base ** (-jnp.arange(half, dtype=high) * 2.0 / head_size)
    angles = jnp.arange(length, dtype=high)[:, None] * freqs[None, :]
    cosines, sines = jnp.cos(angles), jnp.sin(angles)
    return jnp.concatenate([cosines, cosines], 1), jnp.concatenate([-sines, sines], 1)


def rotate(values, cosines, sines):
    return values * cosines + pltpu.roll(values, values.shape[-1] // 2, 1) * sines


def unrotate(values, cosines, sines):
    return values * cosines - pltpu.roll(values, values.shape[-1] // 2, 1) * sines


def key_spans(length):
    block = min(256, length)
    longest = length // 2
    spans = []
    for begin in range(0, length, block):
        first = max(0, begin - longest + 1) // block * block
        spans.append((begin, block, first, begin + block - first))
    return spans


def tile_mask(seg_col, seg_row, begin, rows, first, keys):
    query_at = begin + lax.broadcasted_iota(jnp.int32, (rows, keys), 0)
    key_at = first + lax.broadcasted_iota(jnp.int32, (rows, keys), 1)
    return (query_at >= key_at) & (seg_col[begin : begin + rows, :1] == seg_row[:1, first : first + keys])


def attention_forward(
    query_ref, key_ref, value_ref, query_gain_ref, key_gain_ref, cos_ref, sin_ref, col_ref, row_ref,
    mixed_ref, query_low_ref, key_low_ref, value_low_ref, inverse_ref, value_wide,
):
    head_size = query_ref.shape[1]

    @pl.when(pl.program_id(0) == 0)
    def first_head():
        rotated = rotate(norm_rows(key_ref[...], key_gain_ref[...]), cos_ref[...], sin_ref[...])
        key_low_ref[...] = rotated.astype(low)
        value_low_ref[...] = value_ref[...].astype(low)
        value_wide[:, :head_size] = value_ref[...].astype(low)
        value_wide[:, head_size:] = jnp.ones_like(value_low_ref)

    rotated = rotate(norm_rows(query_ref[...], query_gain_ref[...]), cos_ref[...], sin_ref[...])
    query_low_ref[...] = (rotated * (head_size**-0.5 * log2e)).astype(low)
    for begin, rows, first, keys in key_spans(query_ref.shape[0]):
        scores = dot_last(query_low_ref[pl.ds(begin, rows)], key_low_ref[pl.ds(first, keys)])
        allowed = tile_mask(col_ref, row_ref, begin, rows, first, keys)
        terms = jnp.where(allowed, jnp.exp2(scores), 0.0).astype(low)
        sums = dot(terms, value_wide[pl.ds(first, keys)])
        inverse = 1.0 / sums[:, head_size:]
        mixed_ref[pl.ds(begin, rows)] = (sums[:, :head_size] * inverse).astype(low)
        inverse_ref[pl.ds(begin, rows)] = inverse


def attention_backward(
    query_ref, query_low_ref, key_low_ref, value_low_ref, inverse_ref, mixed_ref, grad_mixed_ref,
    query_gain_ref, cos_ref, sin_ref, col_ref, row_ref,
    grad_query_ref, grad_key_ref, grad_value_ref, grad_gain_ref,
):
    length, head_size = query_ref.shape

    @pl.when(pl.program_id(0) == 0)
    def first_head():
        grad_key_ref[...] = jnp.zeros_like(grad_key_ref)
        grad_value_ref[...] = jnp.zeros_like(grad_value_ref)
        grad_gain_ref[...] = jnp.zeros_like(grad_gain_ref)

    for begin, rows, first, keys in key_spans(length):
        block = pl.ds(begin, rows)
        query_low = query_low_ref[block]
        key_low = key_low_ref[pl.ds(first, keys)]
        scaled = grad_mixed_ref[block].astype(high) * inverse_ref[block]
        row_term = jnp.sum(scaled * mixed_ref[block].astype(high), axis=-1, keepdims=True)
        scaled = scaled.astype(low)
        scores = dot_last(query_low, key_low)
        allowed = tile_mask(col_ref, row_ref, begin, rows, first, keys)
        terms = jnp.where(allowed, jnp.exp2(scores), 0.0)
        grad_probs = dot_last(scaled, value_low_ref[pl.ds(first, keys)])
        grad_scores = (terms * (grad_probs - row_term)).astype(low)
        grad_value_ref[pl.ds(first, keys)] += dot_first(terms.astype(low), scaled)
        grad_key_ref[pl.ds(first, keys)] += dot_first(grad_scores, query_low) * (1.0 / log2e)
        grad_rotated = dot(grad_scores, key_low) * head_size**-0.5
        grad_normed = unrotate(grad_rotated, cos_ref[block], sin_ref[block])
        grad_raw, gain_rows = norm_back(query_ref[block], query_gain_ref[...], grad_normed)
        grad_query_ref[block] = grad_raw.astype(low)
        grad_gain_ref[...] += jnp.broadcast_to(
            jnp.sum(gain_rows, axis=0, keepdims=True), grad_gain_ref.shape
        )


def whole(shape):
    return pl.BlockSpec(shape, lambda head: (0,) * len(shape))


def run_attention_forward(raw, heads, head_size, query_gain, key_gain, cosines, sines, seg_col, seg_row):
    length = raw.shape[0]
    per_head = pl.BlockSpec((length, head_size), lambda head: (0, head))
    one = (length, head_size)
    wide = jax.ShapeDtypeStruct((length, heads * head_size), low)
    narrow = jax.ShapeDtypeStruct(one, low)
    return pl.pallas_call(
        attention_forward,
        grid=(heads,),
        in_specs=[
            per_head,
            pl.BlockSpec(one, lambda head: (0, heads)),
            pl.BlockSpec(one, lambda head: (0, heads + 1)),
            whole((1, head_size)),
            whole((1, head_size)),
            whole(one),
            whole(one),
            whole(one),
            whole((8, length)),
        ],
        out_specs=[per_head, per_head, whole(one), whole(one), per_head],
        out_shape=[wide, wide, narrow, narrow, jax.ShapeDtypeStruct((length, heads * head_size), high)],
        scratch_shapes=[pltpu.VMEM((length, 2 * head_size), low)],
        compiler_params=pltpu.CompilerParams(vmem_limit_bytes=50 << 20),
        cost_estimate=pl.CostEstimate(
            flops=3 * heads * length * length * head_size, bytes_accessed=8 * length * heads * head_size,
            transcendentals=heads * length * length // 2,
        ),
    )(raw, raw, raw, query_gain, key_gain, cosines, sines, seg_col, seg_row)


def run_attention_backward(
    raw, query_low, key_low, value_low, inverse, mixed, grad_mixed, heads, head_size, query_gain,
    cosines, sines, seg_col, seg_row,
):
    length = raw.shape[0]
    per_head = pl.BlockSpec((length, head_size), lambda head: (0, head))
    one = (length, head_size)
    return pl.pallas_call(
        attention_backward,
        grid=(heads,),
        in_specs=[
            per_head, per_head, whole(one), whole(one), per_head, per_head, per_head,
            whole((1, head_size)), whole(one), whole(one), whole(one), whole((8, length)),
        ],
        out_specs=[per_head, whole(one), whole(one), whole((8, head_size))],
        out_shape=[
            jax.ShapeDtypeStruct((length, heads * head_size), low),
            jax.ShapeDtypeStruct(one, high),
            jax.ShapeDtypeStruct(one, high),
            jax.ShapeDtypeStruct((8, head_size), high),
        ],
        compiler_params=pltpu.CompilerParams(vmem_limit_bytes=50 << 20),
        cost_estimate=pl.CostEstimate(
            flops=6 * heads * length * length * head_size, bytes_accessed=16 * length * heads * head_size,
            transcendentals=heads * length * length // 2,
        ),
    )(
        raw, query_low, key_low, value_low, inverse, mixed, grad_mixed, query_gain, cosines, sines,
        seg_col, seg_row,
    )


MESH = pl.DeviceIdType.MESH
VMEM = pl.BlockSpec(memory_space=pltpu.VMEM)
ANY = pl.BlockSpec(memory_space=pl.ANY)


def wait_all(copies):
    for copy in copies:
        copy.wait()


class Chain:
    def __init__(self):
        self.n = lax.axis_size("expert") // 2
        me = lax.axis_index("expert")
        self.z, self.c = me // 2, me % 2
        self.sibling, self.up, self.down = me + 1 - 2 * self.c, me + 2, me - 2
        self.has_up, self.has_down = self.z < self.n - 1, self.z > 0

    def greet(self, others=()):
        barrier = pltpu.get_barrier_semaphore()

        def signal(peer):
            pl.semaphore_signal(barrier, inc=1, device_id={"expert": peer}, device_id_type=MESH)

        signal(self.sibling)
        pl.when(self.has_up)(lambda: signal(self.up))
        pl.when(self.has_down)(lambda: signal(self.down))
        for device in others:
            pl.semaphore_signal(barrier, inc=1, device_id=device, device_id_type=MESH)
        peers = 1 + len(others) + self.has_up.astype(jnp.int32) + self.has_down.astype(jnp.int32)
        pl.semaphore_wait(barrier, peers)

    def nearest(self, step):
        turn = jnp.int32(0)
        for z in range(self.n):
            order = sorted(range(self.n), key=lambda other: (abs(other - z), other))
            for at, chip in enumerate(order):
                turn = jnp.where((self.z == z) & (step == at), chip, turn)
        return turn


class Gather:
    def __init__(self, chain, own, block, send, recv, local):
        self.chain, self.own, self.block = chain, own, block
        self.send, self.recv, self.local = send, recv, local

    @staticmethod
    def semaphores(n):
        return [
            pltpu.SemaphoreType.DMA((3, n)),
            pltpu.SemaphoreType.DMA((2 * n,)),
            pltpu.SemaphoreType.DMA(()),
        ]

    def copy(self, source, z, way, peer):
        c = self.chain.c
        return pltpu.make_async_remote_copy(
            src_ref=source,
            dst_ref=self.block(z, c),
            send_sem=self.send.at[way, z],
            recv_sem=self.recv.at[2 * z + c],
            device_id={"expert": peer},
            device_id_type=MESH,
        )

    def wait_block(self, z, c):
        block = self.block(z, c)
        pltpu.make_async_remote_copy(
            src_ref=block,
            dst_ref=block,
            send_sem=self.send.at[0, z],
            recv_sem=self.recv.at[2 * z + c],
            device_id={"expert": self.chain.sibling},
            device_id_type=MESH,
        ).wait_recv()

    def keep(self):
        return pltpu.make_async_copy(self.own, self.block(self.chain.z, self.chain.c), self.local)

    def begin(self):
        ch = self.chain
        pl.when(ch.has_up)(lambda: self.copy(self.own, ch.z, 0, ch.up).start())
        pl.when(ch.has_down)(lambda: self.copy(self.own, ch.z, 1, ch.down).start())
        self.copy(self.own, ch.z, 2, ch.sibling).start()
        self.keep().start()

    def service(self, step):
        ch = self.chain

        def from_below():
            z = ch.z - step
            self.wait_block(z, ch.c)
            pl.when(ch.has_up)(lambda: self.copy(self.block(z, ch.c), z, 0, ch.up).start())
            self.copy(self.block(z, ch.c), z, 2, ch.sibling).start()

        def from_above():
            z = ch.z + step
            self.wait_block(z, ch.c)
            pl.when(ch.has_down)(lambda: self.copy(self.block(z, ch.c), z, 1, ch.down).start())
            self.copy(self.block(z, ch.c), z, 2, ch.sibling).start()

        pl.when(ch.z - step >= 0)(from_below)
        pl.when(ch.z + step < ch.n)(from_above)

    def wait_sibling(self, z):
        self.wait_block(z, 1 - self.chain.c)

    def finish(self):
        ch = self.chain
        for z in range(ch.n):
            at = jnp.int32(z)
            block = self.block(at, ch.c)
            pl.when(ch.has_up & (ch.z >= z))(lambda: self.copy(block, at, 0, ch.up).wait_send())
            pl.when(ch.has_down & (ch.z <= z))(lambda: self.copy(block, at, 1, ch.down).wait_send())
            self.copy(block, at, 2, ch.sibling).wait_send()


class NearGather(Gather):
    def __init__(self, chain, own, near, block, send, recv, local):
        super().__init__(chain, own, block, send, recv, local)
        self.near = near

    @staticmethod
    def semaphores(n):
        return Gather.semaphores(n)[:2] + [pltpu.SemaphoreType.DMA((4,))]

    def place(self, at):
        ch = self.chain
        source = self.own if at == 3 else self.near.at[at]
        z, c = ((ch.z - 1, ch.c), (ch.z + 1, ch.c), (ch.z, 1 - ch.c), (ch.z, ch.c))[at]
        return pltpu.make_async_copy(source, self.block(z, c), self.local.at[at])

    def begin(self):
        ch = self.chain

        def below():
            pl.when(ch.has_up)(lambda: self.copy(self.near.at[0], ch.z - 1, 0, ch.up).start())
            self.copy(self.near.at[0], ch.z - 1, 2, ch.sibling).start()
            self.place(0).start()

        def above():
            pl.when(ch.has_down)(lambda: self.copy(self.near.at[1], ch.z + 1, 1, ch.down).start())
            self.copy(self.near.at[1], ch.z + 1, 2, ch.sibling).start()
            self.place(1).start()

        pl.when(ch.has_down)(below)
        pl.when(ch.has_up)(above)
        self.place(2).start()
        self.place(3).start()

    def wait_placed(self):
        pl.when(self.chain.has_down)(lambda: self.place(0).wait())
        pl.when(self.chain.has_up)(lambda: self.place(1).wait())
        self.place(2).wait()
        self.place(3).wait()

    def finish(self):
        ch = self.chain
        for z in range(ch.n):
            at = jnp.int32(z)
            block = self.block(at, ch.c)
            pl.when(ch.has_up & (ch.z > z))(lambda: self.copy(block, at, 0, ch.up).wait_send())
            pl.when(ch.has_down & (ch.z < z))(lambda: self.copy(block, at, 1, ch.down).wait_send())
            pl.when(ch.z != z)(lambda: self.copy(block, at, 2, ch.sibling).wait_send())


class Scatter:
    def __init__(self, chain, half, pair, flow, pair_send, pair_recv, flow_send, flow_recv):
        self.chain, self.half, self.pair, self.flow = chain, half, pair, flow
        self.pair_send, self.pair_recv = pair_send, pair_recv
        self.flow_send, self.flow_recv = flow_send, flow_recv

    @staticmethod
    def buffers(n, rows, width):
        return [
            pltpu.VMEM((n, rows, width), low),
            pltpu.VMEM((n + 1, rows, width), low),
            pltpu.SemaphoreType.DMA((n,)),
            pltpu.SemaphoreType.DMA((n,)),
            pltpu.SemaphoreType.DMA((n,)),
            pltpu.SemaphoreType.DMA((n + 1,)),
        ]

    def pair_copy(self, z):
        ch = self.chain
        return pltpu.make_async_remote_copy(
            src_ref=self.half(z, 1 - ch.c),
            dst_ref=self.pair.at[z],
            send_sem=self.pair_send.at[z],
            recv_sem=self.pair_recv.at[z],
            device_id={"expert": ch.sibling},
            device_id_type=MESH,
        )

    def flow_copy(self, z, slot, peer):
        return pltpu.make_async_remote_copy(
            src_ref=self.pair.at[z],
            dst_ref=self.flow.at[slot],
            send_sem=self.flow_send.at[z],
            recv_sem=self.flow_recv.at[slot],
            device_id={"expert": peer},
            device_id_type=MESH,
        )

    def wait_flow(self, slot):
        block = self.flow.at[slot]
        pltpu.make_async_remote_copy(
            src_ref=block,
            dst_ref=block,
            send_sem=self.flow_send.at[0],
            recv_sem=self.flow_recv.at[slot],
            device_id={"expert": self.chain.sibling},
            device_id_type=MESH,
        ).wait_recv()

    def start_pair(self, z):
        self.pair_copy(z).start()

    def add_pair(self, z, relayed):
        self.pair_copy(z).wait_recv()
        half = self.half(z, self.chain.c)

        def alone():
            self.pair[z] = (half[...].astype(high) + self.pair[z].astype(high)).astype(low)

        def with_flow():
            self.wait_flow(z)
            total = half[...].astype(high) + self.pair[z].astype(high) + self.flow[z].astype(high)
            self.pair[z] = total.astype(low)

        pl.when(relayed)(with_flow)
        pl.when(jnp.logical_not(relayed))(alone)

    def step(self, distance):
        ch = self.chain

        def upward():
            z = ch.z + distance
            self.add_pair(z, ch.has_down)
            self.flow_copy(z, z, ch.up).start()

        def downward():
            z = ch.z - distance
            self.add_pair(z, ch.has_up)
            self.flow_copy(z, jnp.where(distance == 1, ch.n, z), ch.down).start()

        pl.when(ch.z + distance < ch.n)(upward)
        pl.when(ch.z - distance >= 0)(downward)

    def total(self, result):
        ch = self.chain
        self.pair_copy(ch.z).wait_recv()
        result[...] = self.half(ch.z, ch.c)[...].astype(high) + self.pair[ch.z].astype(high)

        def add(slot):
            self.wait_flow(slot)
            result[...] += self.flow[slot].astype(high)

        pl.when(ch.has_down)(lambda: add(ch.z))
        pl.when(ch.has_up)(lambda: add(ch.n))

    def finish(self):
        ch = self.chain
        for z in range(ch.n):
            at = jnp.int32(z)
            self.pair_copy(at).wait_send()
            pl.when(ch.z != z)(lambda: self.flow_copy(at, at, ch.sibling).wait_send())


class Ports:
    def __init__(self, send, recv):
        self.send, self.recv, self.used, self.started = send, recv, 0, []

    def copy(self, source, target, device):
        at = self.used
        self.used += 1
        copy = pltpu.make_async_remote_copy(
            src_ref=source,
            dst_ref=target,
            send_sem=self.send.at[at],
            recv_sem=self.recv.at[at],
            device_id=device,
            device_id_type=MESH,
        )
        self.started.append(copy)
        return copy

    def finish(self):
        for copy in self.started:
            copy.wait_send()


def square():
    group = lax.axis_index("dp")
    y, x = group // 2, group % 2
    from_x, from_y = 2 * y + 1 - x, 2 * (1 - y) + x
    return group, y, x, from_x, from_y


class SquareSum:
    def __init__(self, source, result, first_a, first_b, second_a, second_b, send_a, send_b, ports):
        self.source, self.result = source, result
        self.own, self.y, self.x, self.from_x, self.from_y = square()
        self.first_a, self.first_b, self.second_a, self.second_b = first_a, first_b, second_a, second_b
        self.send_a, self.send_b = send_a, send_b
        self.rows, self.middle = source.shape[0] // 4, source.shape[1] // 2
        beside, across = {"dp": self.from_x}, {"dp": self.from_y}
        self.first = []
        for k in range(2):
            self.first.append(ports.copy(self.part(source, 0, 2 * k + 1 - self.x), first_a.at[k], beside))
            self.first.append(ports.copy(self.part(source, 1, 2 * (1 - self.y) + k), first_b.at[k], across))
        self.second = [ports.copy(send_a, second_a, across), ports.copy(send_b, second_b, beside)]

    @staticmethod
    def buffers(rows, columns):
        quarter = (rows // 4, columns // 2)
        return [pltpu.VMEM((2, *quarter), low)] * 2 + [pltpu.VMEM(quarter, low)] * 4

    def part(self, ref, side, quarter):
        rows = pl.ds(pl.multiple_of(quarter * self.rows, self.rows), self.rows)
        return ref.at[rows, pl.ds(side * self.middle, self.middle)]

    @staticmethod
    def start(copies):
        for copy in copies:
            copy.start()

    @staticmethod
    def arrive(copies):
        for copy in copies:
            copy.wait_recv()

    def begin(self):
        self.start(self.first)

    def exchange(self):
        self.arrive(self.first)
        along_y = self.part(self.source, 0, self.from_y)[...].astype(high)
        self.send_a[...] = (along_y + self.first_a[1 - self.y].astype(high)).astype(low)
        along_x = self.part(self.source, 1, self.from_x)[...].astype(high)
        self.send_b[...] = (along_x + self.first_b[1 - self.x].astype(high)).astype(low)
        self.start(self.second)

    def settle(self):
        self.arrive(self.second)
        for side, first, second in (
            (0, self.first_a[self.y], self.second_a), (1, self.first_b[self.x], self.second_b)
        ):
            total = self.part(self.source, side, self.own)[...].astype(high) + first.astype(high)
            columns = pl.ds(side * self.middle, self.middle)
            self.result[:, columns] = (total + second[...].astype(high)).astype(low)


class WideSum:
    def __init__(self, grads):
        self.grads = grads
        self.own, self.y, self.x, self.from_x, self.from_y = square()
        self.middle = grads.shape[2] // 2
        self.beside, self.across = {"dp": self.from_x}, {"dp": self.from_y}

    def part(self, side, quarter):
        return self.grads.at[quarter, :, pl.ds(side * self.middle, self.middle)]

    def first(self, first_a, first_b, ports):
        copies = []
        for k in range(2):
            copies.append(ports.copy(self.part(0, 2 * k + 1 - self.x), first_a.at[k], self.beside))
            copies.append(ports.copy(self.part(1, 2 * (1 - self.y) + k), first_b.at[k], self.across))
        return copies

    def load(self, first_a, first_b, left, right, sems):
        pairs = (
            (self.part(0, self.from_y), left.at[0]), (first_a.at[1 - self.y], left.at[1]),
            (self.part(1, self.from_x), right.at[0]), (first_b.at[1 - self.x], right.at[1]),
        )
        return [pltpu.make_async_copy(source, target, sems.at[at]) for at, (source, target) in enumerate(pairs)]

    def second(self, left, right, second_a, second_b, ports):
        for both in (left, right):
            both[0] = (both[0].astype(high) + both[1].astype(high)).astype(low)
        return [
            ports.copy(left.at[0], second_a, self.across),
            ports.copy(right.at[0], second_b, self.beside),
        ]


def wide_shapes(grads):
    _, rows, columns = grads.shape
    first = jax.ShapeDtypeStruct((2, rows, columns // 2), low)
    second = jax.ShapeDtypeStruct((rows, columns // 2), low)
    return [first, first], [second, second]


class SquareCopy:
    def __init__(self, mine, result, ports):
        own, _, _, from_x, from_y = square()
        rows, middle = mine.shape[0], mine.shape[1] // 2
        beside, across = {"dp": from_x}, {"dp": from_y}

        def quarter(at):
            return pl.ds(pl.multiple_of(at * rows, rows), rows)

        target = result.at[quarter(own)]
        self.mine, self.target = mine, target
        self.near = [ports.copy(mine, target, beside), ports.copy(mine, target, across)]
        left = result.at[quarter(from_x), pl.ds(0, middle)]
        right = result.at[quarter(from_y), pl.ds(middle, middle)]
        self.far = [ports.copy(left, left, across), ports.copy(right, right, beside)]

    def begin(self):
        SquareSum.start(self.near)
        self.target[...] = self.mine[...]

    def hand_on(self):
        SquareSum.arrive(self.near)
        SquareSum.start(self.far)

    def finish(self):
        SquareSum.arrive(self.far)


def row_block(ref, rows):
    return lambda z, c: ref.at[pl.ds(pl.multiple_of((2 * z + c) * rows, rows), rows)]


def chip_block(ref, rows):
    return lambda z, c: ref.at[z, pl.ds(pl.multiple_of(c * rows, rows), rows)]


def communicating(collective_id, mebibytes=60):
    return pltpu.CompilerParams(
        collective_id=collective_id, has_side_effects=True, vmem_limit_bytes=mebibytes << 20
    )


def gather_kernel(
    tokens_ref, gain_ref, routes_ref, segments_ref, cot_ref, query_hbm, key_hbm, value_hbm,
    hidden_hbm, all_named_ref, near_ref, col_ref, projection_hbm, raw_hbm,
    named_ref, own, stage, hidden_ref, projection_ref, raw_ref, query_ref, key_ref, value_ref,
    send_a, recv_a, local_a, send_b, recv_b, local_b, name_send, name_recv,
    swap_send, swap_recv, x_send, x_recv, y_send, y_recv, far_send, far_recv, out_sems, load_sems,
    near_send, near_recv,
):
    chain = Chain()
    n = chain.n
    peers = 2 * n
    me = lax.axis_index("expert")
    group, _, _, from_x, from_y = square()
    far = 3 - group
    beside, across = {"dp": from_x}, {"dp": from_y}
    sources = [(2 * chain.nearest(step) + core, core, step) for step in range(n) for core in range(2)]
    others = [chain.sibling] + [source for source, _, step in sources if step > 0]
    barrier = pltpu.get_barrier_semaphore()
    for device in [{"expert": peer} for peer in others] + [beside, across]:
        pl.semaphore_signal(barrier, inc=1, device_id=device, device_id_type=MESH)
    rows = stage.shape[1]
    quarter = pl.ds(pl.multiple_of(group * rows, rows), rows)
    loads = [
        pltpu.make_async_copy(source.at[quarter], target, load_sems.at[at])
        for at, (source, target) in enumerate(
            ((query_hbm, query_ref), (key_hbm, key_ref), (value_hbm, value_ref))
        )
    ]
    for load in loads:
        load.start()
    query_width = query_ref.shape[1] // peers
    head_size = key_ref.shape[1] // n
    own[...] = norm_rows(tokens_ref[...].astype(high), gain_ref[...]).astype(low)
    lanes = lax.broadcasted_iota(jnp.int32, named_ref.shape, 1)
    named = jnp.zeros(named_ref.shape, high)
    routes = routes_ref[...].astype(high).T.astype(jnp.int32)
    for at in range(routes.shape[1]):
        named = jnp.where(routes[:, at : at + 1] == lanes, 1.0, named)
    named_ref[...] = named.astype(low)
    for load in loads:
        load.wait()
    for peer in range(peers):
        shared = pl.ds(peer // 2 * head_size, head_size)
        stage[peer, :, :query_width] = query_ref[:, pl.ds(peer * query_width, query_width)]
        stage[peer, :, query_width : query_width + head_size] = key_ref[:, shared]
        stage[peer, :, query_width + head_size :] = value_ref[:, shared]
    pl.semaphore_wait(barrier, peers + 1)

    def remote(source, target, send, recv, device):
        return pltpu.make_async_remote_copy(
            src_ref=source, dst_ref=target, send_sem=send, recv_sem=recv, device_id=device, device_id_type=MESH
        )

    def block(source, place):
        return projection_ref.at[source, place]

    swaps = [
        remote(stage.at[peer], block(me, group), swap_send.at[at], swap_recv.at[me], {"expert": peer})
        for at, peer in enumerate(others)
    ]
    for copy in swaps:
        copy.start()
    length = own.shape[0]
    piece = length // 2

    def half_block(half):
        def block_of(z, c):
            return hidden_ref.at[pl.ds(pl.multiple_of((2 * z + c) * length + half * piece, piece), piece)]

        return block_of

    wide = [
        Gather(chain, own.at[pl.ds(half * piece, piece)], half_block(half), *sems)
        for half, sems in enumerate(((send_a, recv_a, local_a), (send_b, recv_b, local_b)))
    ]
    for gather in wide:
        gather.begin()
    names = [
        remote(named_ref, all_named_ref.at[me], name_send.at[at], name_recv.at[me], {"expert": peer})
        for at, peer in enumerate(others)
    ]
    for copy in names:
        copy.start()
    all_named_ref[me] = named_ref[...]
    row = jnp.broadcast_to(segments_ref[...].astype(high), (col_ref.shape[1], col_ref.shape[0]))
    col_ref[...] = row.T.astype(jnp.int32)
    projection_ref[me, group] = stage[me]

    def to_x(at, source, place):
        part = block(source, place)
        return remote(part, part, x_send.at[at], x_recv.at[source], beside)

    def to_y(at, source, place):
        part = block(source, place)
        return remote(part, part, y_send.at[at], y_recv.at[source], across)

    def to_far(at, core, source, place):
        part = block(source, place)
        return remote(part, part, far_send.at[at], far_recv.at[source], across if core == 0 else beside)

    def wait_swap(source):
        part = block(source, group)
        remote(part, part, swap_send.at[0], swap_recv.at[source], {"expert": chain.sibling}).wait_recv()

    for at, (source, core, step) in enumerate(sources):
        if step == 0:
            pl.when(chain.c != core)(lambda: wait_swap(source))
        else:
            wait_swap(source)
        to_x(at, source, group).start()
        to_y(at, source, group).start()
    for gather in wide:
        gather.service(1)
    for at, (source, core, _) in enumerate(sources):
        to_x(at, source, from_x).wait_recv()
        to_y(at, source, from_y).wait_recv()
        to_far(at, core, source, from_x if core == 0 else from_y).start()
    for step in range(2, n):
        for gather in wide:
            gather.service(step)

    def near(slot, peer):
        return remote(cot_ref, near_ref.at[slot], near_send.at[slot], near_recv.at[slot], {"expert": peer})

    pl.when(chain.has_up)(lambda: near(0, chain.up).start())
    pl.when(chain.has_down)(lambda: near(1, chain.down).start())
    near(2, chain.sibling).start()
    for gather in wide:
        for z in range(n):
            gather.wait_sibling(jnp.int32(z))
        gather.keep().wait()
    hidden_out = pltpu.make_async_copy(hidden_ref, hidden_hbm, out_sems.at[0])
    hidden_out.start()
    for at, (source, core, _) in enumerate(sources):
        to_far(at, core, source, far).wait_recv()
    projection_out = pltpu.make_async_copy(projection_ref, projection_hbm, out_sems.at[1])
    projection_out.start()
    pair_rows = 2 * own.shape[0]
    shard_rows = 4 * rows

    def raw_out(step):
        tokens = pl.ds(pl.multiple_of(step * pair_rows, pair_rows), pair_rows)
        return pltpu.make_async_copy(raw_ref.at[tokens], raw_hbm.at[tokens], out_sems.at[2 + step])

    @pl.loop(0, n)
    def each(step):
        tokens = pl.ds(pl.multiple_of(step * pair_rows, pair_rows), pair_rows)
        total = jnp.zeros((pair_rows, raw_ref.shape[1]), high)
        for source in range(peers):
            weight = projection_ref[source].reshape(shard_rows, raw_ref.shape[1])
            total = total + dot(hidden_ref[tokens, source * shard_rows : (source + 1) * shard_rows], weight)
        raw_ref[tokens] = total
        raw_out(step).start()

    for gather in wide:
        gather.finish()
    for at, peer in enumerate(others):
        part = all_named_ref.at[peer]
        remote(part, part, name_send.at[at], name_recv.at[peer], {"expert": peer}).wait_recv()
        names[at].wait_send()
    for at, (source, core, _) in enumerate(sources):
        to_x(at, source, group).wait_send()
        to_y(at, source, group).wait_send()
        to_far(at, core, source, from_x if core == 0 else from_y).wait_send()
    for copy in swaps:
        copy.wait_send()
    pl.when(chain.has_up)(lambda: near(0, chain.up).wait_send())
    pl.when(chain.has_down)(lambda: near(1, chain.down).wait_send())
    near(2, chain.sibling).wait_send()
    pl.when(chain.has_down)(lambda: near(0, chain.sibling).wait_recv())
    pl.when(chain.has_up)(lambda: near(1, chain.sibling).wait_recv())
    near(2, chain.sibling).wait_recv()
    hidden_out.wait()
    projection_out.wait()
    for step in range(n):
        raw_out(step).wait()


def run_gather(tokens, gain, routes, segments, cotangent, query_weight, key_matrix, value_matrix, peers, groups):
    length, width = tokens.shape
    n = peers // 2
    shard_rows, query_columns = query_weight.shape
    columns = query_columns // peers + 2 * key_matrix.shape[1] // n
    rows = shard_rows // groups
    dma = pltpu.SemaphoreType.DMA
    hidden, all_named, near, seg_col, projection, raw = pl.pallas_call(
        gather_kernel,
        out_shape=[
            jax.ShapeDtypeStruct((length * peers, width), low),
            jax.ShapeDtypeStruct((peers, length, 128), low),
            jax.ShapeDtypeStruct((3, length, width), low),
            jax.ShapeDtypeStruct((length * peers, 128), jnp.int32),
            jax.ShapeDtypeStruct((peers, groups, rows, columns), low),
            jax.ShapeDtypeStruct((length * peers, columns), high),
        ],
        in_specs=[VMEM] * 4 + [ANY] * 4,
        out_specs=[ANY, VMEM, ANY, VMEM, ANY, ANY],
        scratch_shapes=[
            pltpu.VMEM((length, 128), low),
            pltpu.VMEM((length, width), low),
            pltpu.VMEM((peers, rows, columns), low),
            pltpu.VMEM((length * peers, width), low),
            pltpu.VMEM((peers, groups, rows, columns), low),
            pltpu.VMEM((length * peers, columns), high),
            pltpu.VMEM((rows, query_columns), low),
            pltpu.VMEM((rows, key_matrix.shape[1]), low),
            pltpu.VMEM((rows, key_matrix.shape[1]), low),
            *Gather.semaphores(n),
            *Gather.semaphores(n),
            dma((peers - 1,)), dma((peers,)),
            dma((peers - 1,)), dma((peers,)),
            dma((peers,)), dma((peers,)), dma((peers,)), dma((peers,)), dma((peers,)), dma((peers,)),
            dma((2 + n,)),
            dma((3,)), dma((3,)), dma((3,)),
        ],
        compiler_params=communicating(1),
        cost_estimate=pl.CostEstimate(flops=0, bytes_accessed=64 << 20, transcendentals=0),
        name="gather_hidden",
    )(tokens, gain, routes, segments, cotangent, query_weight, key_matrix, value_matrix)
    return hidden, all_named, near, seg_col, projection.reshape(width, columns), raw


def attention_heads(
    raw_ref, query_gain_ref, key_gain_ref, cos_ref, sin_ref, col_ref, row_ref,
    mixed_ref, query_low_ref, key_low_ref, value_low_ref, inverse_ref, value_wide,
):
    head_size = cos_ref.shape[1]
    heads = mixed_ref.shape[1] // head_size
    key_raw = raw_ref[:, heads * head_size : (heads + 1) * head_size]
    key_low_ref[...] = rotate(norm_rows(key_raw, key_gain_ref[...]), cos_ref[...], sin_ref[...]).astype(low)
    value_low_ref[...] = raw_ref[:, (heads + 1) * head_size :].astype(low)
    value_wide[:, :head_size] = value_low_ref[...]
    value_wide[:, head_size:] = jnp.ones_like(value_low_ref)

    @pl.loop(0, heads)
    def each(head):
        columns = pl.ds(pl.multiple_of(head * head_size, head_size), head_size)
        rotated = rotate(norm_rows(raw_ref[:, columns], query_gain_ref[...]), cos_ref[...], sin_ref[...])
        query_low_ref[:, columns] = (rotated * (head_size**-0.5 * log2e)).astype(low)
        for begin, rows, first, keys in key_spans(raw_ref.shape[0]):
            block = pl.ds(begin, rows)
            scores = dot_last(query_low_ref[block, columns], key_low_ref[pl.ds(first, keys)])
            allowed = tile_mask(col_ref, row_ref, begin, rows, first, keys)
            terms = jnp.where(allowed, jnp.exp2(scores), 0.0).astype(low)
            sums = dot(terms, value_wide[pl.ds(first, keys)])
            inverse = 1.0 / sums[:, head_size:]
            mixed_ref[block, columns] = (sums[:, :head_size] * inverse).astype(low)
            inverse_ref[block, columns] = inverse


class Split:
    both = slice(None)

    @staticmethod
    def take(ref, z, half, columns=slice(None)):
        block = ref[pl.ds(2 * z, 2), half, :, columns]
        return block.reshape(-1, block.shape[-1])

    @staticmethod
    def put(ref, z, half, value, columns=slice(None)):
        halves = (2, 2) if half is Split.both else (2,)
        ref[pl.ds(2 * z, 2), half, :, columns] = value.reshape(*halves, ref.shape[2], value.shape[1])

    @staticmethod
    def every(ref, columns=slice(None)):
        block = ref[:, :, :, columns]
        return block.reshape(block.shape[0] * block.shape[1] * block.shape[2], block.shape[3])


def expert_block(rows_all, plain_of, gate_w, up_w, gate_col, gated, grad_gate, grad_up, z, half):
    hidden = gate_w.shape[1]
    chunk = hidden // 3 if hidden % 384 == 0 else hidden
    gate_grad = jnp.zeros_like(gate_col)
    for begin in range(0, hidden, chunk):
        units = pl.ds(begin, chunk)
        gate_pre = dot(Split.take(rows_all, z, half), gate_w[:, units])
        up_pre = dot(Split.take(rows_all, z, half), up_w[:, units])
        plain = plain_of(units)
        share = 1.0 / (1.0 + jnp.exp(-gate_pre))
        silu = gate_pre * share
        act = silu * up_pre
        gate_grad = gate_grad + jnp.sum(act * plain, axis=-1, keepdims=True)
        Split.put(gated, z, half, (act * gate_col).astype(low), units)
        grad_act = plain * gate_col
        slope = share + silu * (1.0 - share)
        Split.put(grad_gate, z, half, (grad_act * up_pre * slope).astype(low), units)
        Split.put(grad_up, z, half, (grad_act * silu).astype(low), units)
    return gate_grad


def gate_columns(lanes, expert, gate_grad):
    sent = jnp.where(lanes == expert, gate_grad, 0.0)
    upper = sent.astype(low).astype(high)
    lower = (sent - upper).astype(low).astype(high)
    return upper + pltpu.roll(lower, 64, 1)


class Tiles:
    def __init__(self, grads, stage, sems, gated, grad_gate, grad_up, rows_all, cots):
        self.grads, self.stage, self.sems = grads, stage, sems
        self.sources = ((grad_gate, rows_all), (grad_up, rows_all), (gated, cots))
        self.groups = sems.shape[1]
        self.hidden = gated.shape[3]
        self.piece = self.hidden // self.groups
        self.tile = stage.shape[2]

    def copies(self, kind, at, slot):
        piece = self.piece
        made = []
        for part in range(self.groups):
            if kind < 2:
                columns = pl.ds(pl.multiple_of(at * self.tile, self.tile), self.tile)
                target = self.grads.at[part, pl.ds(kind * piece, piece), columns]
            else:
                columns = pl.ds(part * self.tile, self.tile)
                target = self.grads.at[at, pl.ds(2 * piece, piece), columns]
            source = self.stage.at[slot, pl.ds(part * piece, piece)]
            made.append(pltpu.make_async_copy(source, target, self.sems.at[slot, part]))
        return made

    def run(self, kind):
        left, right = self.sources[kind]

        @pl.loop(0, self.groups)
        def each(at):
            slot = at % 2
            if kind == 0:
                pl.when(at >= 2)(lambda: wait_all(self.copies(kind, at, slot)))
            else:
                wait_all(self.copies(kind, at, slot))
            span = pl.ds(pl.multiple_of(at * self.tile, self.tile), self.tile)
            self.stage[slot] = dot_first(Split.every(left), Split.every(right, span)).astype(low)
            for copy in self.copies(kind, at, slot):
                copy.start()

    def finish(self):
        for slot in range(2):
            wait_all(self.copies(0, jnp.int32(slot), slot))


def first_kernel(
    query_gain_ref, key_gain_ref, row_ref, tokens_ref, gain_ref, named_ref, router_in, cot_ref, near_ref,
    raw_hbm, cos_hbm, sin_hbm, col_hbm, weight_hbm, gate_hbm, up_hbm, down_hbm,
    key_low_ref, value_low_ref, own_gates_ref, resid_hbm, ffn_hbm, gates_hbm,
    mixed_hbm, query_low_hbm, inverse_hbm, rows_hbm, cots_hbm, gated_hbm, parts_hbm, grads_hbm,
    resid_ref, ffn_ref, gates_ref,
    raw_ref, cos_ref, sin_ref, col_ref, weight_ref, mixed_ref, query_low_ref, inverse_ref, value_wide, router_ref, plain, attn_parts, rows_all, cots, gate_w, up_w, down_w, gated, grad_gate, grad_up,
    part_stage, tile_stage, load_sems, rows_sems, part_sems, tile_sems, cot_send, cot_recv, cot_local, *transfers,
):
    chain = Chain()
    n = chain.n
    _, _, rows, width = rows_all.shape
    block_rows = 2 * rows
    loads = [
        pltpu.make_async_copy(source, target, load_sems.at[at])
        for at, (source, target) in enumerate(
            (
                (raw_hbm, raw_ref), (cos_hbm, cos_ref), (sin_hbm, sin_ref), (col_hbm, col_ref),
                (weight_hbm, weight_ref), (down_hbm.at[0], down_w), (gate_hbm.at[0], gate_w),
                (up_hbm.at[0], up_w),
            )
        )
    ]
    for load in loads:
        load.start()
    chain.greet()
    cot_gather = NearGather(
        chain, cot_ref, near_ref, lambda z, c: cots.at[2 * z + c], cot_send, cot_recv, cot_local
    )
    cot_gather.begin()
    wait_all(loads[:4])
    router_ref[...] = jnp.zeros_like(router_ref)
    router_ref[: router_in.shape[0]] = router_in[...]
    attention_heads(
        raw_ref, query_gain_ref, key_gain_ref, cos_ref, sin_ref, col_ref, row_ref,
        mixed_ref, query_low_ref, key_low_ref, value_low_ref, inverse_ref, value_wide,
    )
    attention_copies = [
        pltpu.make_async_copy(source, target, rows_sems.at[2 + at])
        for at, (source, target) in enumerate(
            ((mixed_ref, mixed_hbm), (query_low_ref, query_low_hbm), (inverse_ref, inverse_hbm))
        )
    ]
    for copy in attention_copies:
        copy.start()
    loads[4].wait()
    scatters, gathers = [], []
    for half in range(2):
        pair, flow, *rest = transfers[9 * half : 9 * half + 9]
        scatters.append(
            Scatter(chain, lambda z, c, half=half: attn_parts.at[z, c, half], pair, flow, *rest[:4])
        )
        gathers.append(
            Gather(chain, ffn_ref.at[half], lambda z, c, half=half: rows_all.at[2 * z + c, half], *rest[4:])
        )

    def plain_rows(step):
        z = chain.nearest(step)
        pl.when(step == 0)(cot_gather.wait_placed)
        pl.when(step > 0)(lambda: cot_gather.wait_sibling(z))
        cot_rows = cots[pl.ds(2 * z, 2)].reshape(4 * rows, width)
        hidden = plain.shape[3]
        plain[pl.ds(2 * z, 2)] = dot_last(cot_rows, down_w[...]).reshape(2, 2, rows, hidden)

    @pl.loop(0, n)
    def project(step):
        z = chain.nearest(n - 1 - step)
        tokens = pl.ds(pl.multiple_of(z * 4 * rows, 4 * rows), 4 * rows)
        attn_parts[z] = dot(mixed_ref[tokens], weight_ref[...]).astype(low).reshape(2, 2, rows, width)
        for scatter in scatters:
            scatter.start_pair(z)
        pl.when(step < n - 1)(lambda: scatters[0].step(n - 1 - step))
        pl.when(step == 0)(lambda: loads[5].wait())
        pl.when(step == 1)(lambda: cot_gather.service(2))
        pl.when(step < n - 1)(lambda: plain_rows(step))

    def own_rows(half):
        span = pl.ds(half * rows, rows)
        scatters[half].total(resid_ref.at[span])
        resid_ref[span] += tokens_ref[span].astype(high)
        ffn_ref[half] = norm_rows(resid_ref[span], gain_ref[...]).astype(low)
        gathers[half].begin()

    scatters[1].step(n - 1)
    own_rows(0)
    scatters[1].step(n - 2)
    cot_gather.service(3)
    plain_rows(jnp.int32(3))
    lanes = lax.broadcasted_iota(jnp.int32, (block_rows, 128), 1)
    expert = lax.axis_index("expert") * gate_hbm.shape[0]
    tile = tile_stage.shape[2]
    wait_all(loads[6:])

    def part_copy(z, half, slot):
        return pltpu.make_async_copy(part_stage.at[slot], parts_hbm.at[pl.ds(2 * z, 2), half], part_sems.at[slot])

    @pl.loop(0, 2 * n)
    def each(turn):
        pl.when((turn >= 1) & (turn < n - 1))(lambda: gathers[0].service(turn))
        pl.when((turn >= 1) & (turn < n - 2))(lambda: scatters[1].step(n - 2 - turn))

        @pl.when(turn == n - 1)
        def middle():
            own_rows(1)
            gathers[0].service(n - 1)

        pl.when((turn >= n) & (turn < 2 * n - 1))(lambda: gathers[1].service(turn - n + 1))
        half, step = turn // n, turn % n
        z = chain.nearest(step)

        def arrived(gather):
            pl.when(step == 0)(lambda: gather.keep().wait())
            gather.wait_sibling(z)

        pl.when(half == 0)(lambda: arrived(gathers[0]))
        pl.when(half == 1)(lambda: arrived(gathers[1]))
        logits = dot_last(Split.take(rows_all, z, half), router_ref[...])
        named = Split.take(named_ref, z, half).astype(high) > 0.5
        top = jnp.max(jnp.where(named, logits, -1e30), axis=-1, keepdims=True)
        terms = jnp.where(named, jnp.exp(jnp.where(named, logits - top, 0.0)), 0.0)
        gates = terms / jnp.sum(terms, axis=-1, keepdims=True)
        Split.put(gates_ref, z, half, gates)

        @pl.when(step == 0)
        def own_gates():
            own_gates_ref[half] = jnp.where(chain.c == 0, gates[:rows], gates[rows:])

        gate_col = jnp.sum(jnp.where(lanes == expert, gates, 0.0), axis=-1, keepdims=True)
        gate_grad = expert_block(
            rows_all, lambda units: Split.take(plain, z, half, units), gate_w, up_w, gate_col, gated, grad_gate,
            grad_up, z, half,
        )
        slot = turn % 2

        pl.when(turn >= 2)(lambda: part_copy(z, half, slot).wait())

        @pl.loop(0, width // tile)
        def columns(at):
            span = pl.ds(pl.multiple_of(at * tile, tile), tile)
            grad_rows = dot_last(Split.take(grad_gate, z, half), gate_w[span, :])
            grad_rows = grad_rows + dot_last(Split.take(grad_up, z, half), up_w[span, :])
            part_stage[slot, :, :, span] = grad_rows.astype(low).reshape(2, rows, tile)

        sent = gate_columns(lanes, expert, gate_grad).astype(low)
        part_stage[slot, :, :, width:] = sent.reshape(2, rows, 128)
        part_copy(z, half, slot).start()

    whole_copies = [
        pltpu.make_async_copy(rows_all, rows_hbm, rows_sems.at[0]),
        pltpu.make_async_copy(cots, cots_hbm, rows_sems.at[1]),
        pltpu.make_async_copy(gated, gated_hbm, rows_sems.at[5]),
        pltpu.make_async_copy(resid_ref, resid_hbm, rows_sems.at[6]),
        pltpu.make_async_copy(ffn_ref, ffn_hbm, rows_sems.at[7]),
        pltpu.make_async_copy(gates_ref, gates_hbm, rows_sems.at[8]),
    ]
    for copy in whole_copies:
        copy.start()
    tiles = Tiles(grads_hbm, tile_stage, tile_sems, gated, grad_gate, grad_up, rows_all, cots)
    for kind in range(3):
        tiles.run(kind)
    for half in range(2):
        gathers[half].finish()
        scatters[half].finish()
    tiles.finish()
    for slot in range(2):
        part_copy(jnp.int32(0), 0, slot).wait()
    wait_all(whole_copies + attention_copies)
    cot_gather.finish()


def second_kernel(
    gates_ref, rows_hbm, cot_hbm, gate_hbm, up_hbm, down_hbm, parts_in, wide_hbm,
    sum_ref, gated_hbm, grads_hbm, first_a, first_b,
    rows_all, cots, gate_w, up_w, down_w, gated, grad_gate, grad_up, parts, tile_stage, load_sems, chip_sems,
    tile_sems, out_sem, port_send, port_recv, pair, flow, *scatter_sems,
):
    chain = Chain()
    n = chain.n
    width = rows_all.shape[3]
    block_rows = parts.shape[1]
    loads = [
        pltpu.make_async_copy(source, target, load_sems.at[at])
        for at, (source, target) in enumerate(
            (
                (gate_hbm.at[1], gate_w), (up_hbm.at[1], up_w), (down_hbm.at[1], down_w), (parts_in, parts),
            )
        )
    ]

    def chip_loads(z):
        block = pl.ds(2 * z, 2)
        return [
            pltpu.make_async_copy(rows_hbm.at[block], rows_all.at[block], chip_sems.at[0, z]),
            pltpu.make_async_copy(cot_hbm.at[block], cots.at[block], chip_sems.at[1, z]),
        ]

    for load in loads[:3]:
        load.start()
    for step in range(n):
        for load in chip_loads(chain.nearest(n - 1 - step)):
            load.start()
    loads[3].start()
    wide = WideSum(wide_hbm)
    chain.greet([wide.beside, wide.across])
    ports = Ports(port_send, port_recv)
    wide_sent = wide.first(first_a, first_b, ports)
    SquareSum.start(wide_sent)
    scatter = Scatter(chain, chip_block(parts, block_rows // 2), pair, flow, *scatter_sems)
    lanes = lax.broadcasted_iota(jnp.int32, (block_rows, 128), 1)
    expert = lax.axis_index("expert") * gate_hbm.shape[0] + 1
    tile = tile_stage.shape[2]
    wait_all(loads[:3])

    @pl.loop(0, n)
    def each(step):
        z = chain.nearest(n - 1 - step)
        wait_all(chip_loads(z))
        gates = Split.take(gates_ref, z, Split.both)
        gate_col = jnp.sum(jnp.where(lanes == expert, gates, 0.0), axis=-1, keepdims=True)
        gate_grad = expert_block(
            rows_all, lambda units: dot_last(Split.take(cots, z, Split.both), down_w[units, :]), gate_w, up_w,
            gate_col, gated, grad_gate, grad_up, z, Split.both,
        )
        pl.when(step == 0)(lambda: loads[3].wait())

        @pl.loop(0, width // tile)
        def columns(at):
            span = pl.ds(pl.multiple_of(at * tile, tile), tile)
            grad_rows = dot_last(Split.take(grad_gate, z, Split.both), gate_w[span, :])
            grad_rows = grad_rows + dot_last(Split.take(grad_up, z, Split.both), up_w[span, :])
            parts[z, :, span] = (parts[z, :, span].astype(high) + grad_rows).astype(low)

        sent = parts[z, :, width:].astype(high) + gate_columns(lanes, expert, gate_grad)
        parts[z, :, width:] = sent.astype(low)
        scatter.start_pair(z)
        pl.when(step < n - 1)(lambda: scatter.step(n - 1 - step))

    gated_copy = pltpu.make_async_copy(gated, gated_hbm, out_sem)
    gated_copy.start()
    tiles = Tiles(grads_hbm, tile_stage, tile_sems, gated, grad_gate, grad_up, rows_all, cots)
    for kind in range(3):
        tiles.run(kind)
    scatter.total(sum_ref)
    scatter.finish()
    tiles.finish()
    gated_copy.wait()
    SquareSum.arrive(wide_sent)
    ports.finish()


def split_rows(array, peers):
    return array.reshape(peers, 2, array.shape[0] // (2 * peers), array.shape[1])


def expert_scratch(gate_weight, up_weight, down_weight, peers, rows, width):
    hidden = gate_weight.shape[2]
    whole = pltpu.VMEM((peers, 2, rows, width), low)
    acts = pltpu.VMEM((peers, 2, rows, hidden), low)
    return [
        whole, whole,
        pltpu.VMEM(gate_weight.shape[1:], low),
        pltpu.VMEM(up_weight.shape[1:], low),
        pltpu.VMEM(down_weight.shape[1:], low),
        acts, acts, acts,
    ]


def run_first(
    raw, query_gain, key_gain, cosines, sines, seg_col, seg_row, weight, tokens, gain, named, router, cotangent, near, gate_weight, up_weight, down_weight,
    peers, groups,
):
    length, width = tokens.shape
    n, rows = peers // 2, length // 2
    hidden = gate_weight.shape[2]
    tile, sent = width // groups, width + 128
    full, local_width, head_size = length * peers, weight.shape[0], cosines.shape[1]
    dma = pltpu.SemaphoreType.DMA

    def split(columns, dtype):
        return jax.ShapeDtypeStruct((peers, 2, rows, columns), dtype)

    return pl.pallas_call(
        first_kernel,
        out_shape=[
            jax.ShapeDtypeStruct((full, head_size), low),
            jax.ShapeDtypeStruct((full, head_size), low),
            jax.ShapeDtypeStruct((2, rows, 128), high),
            jax.ShapeDtypeStruct((length, width), high),
            jax.ShapeDtypeStruct((2, rows, width), low),
            split(128, high),
            jax.ShapeDtypeStruct((full, local_width), low),
            jax.ShapeDtypeStruct((full, local_width), low),
            jax.ShapeDtypeStruct((full, local_width), high),
            split(width, low),
            split(width, low),
            split(hidden, low),
            split(sent, low),
            jax.ShapeDtypeStruct((groups, 3 * hidden // groups, width), low),
        ],
        in_specs=[VMEM] * 7 + [ANY] * 10,
        out_specs=[VMEM] * 3 + [ANY] * 11,
        scratch_shapes=[
            pltpu.VMEM((length, width), high),
            pltpu.VMEM((2, rows, width), low),
            pltpu.VMEM((peers, 2, rows, 128), high),
            pltpu.VMEM(raw.shape, high),
            pltpu.VMEM(cosines.shape, high),
            pltpu.VMEM(sines.shape, high),
            pltpu.VMEM(seg_col.shape, jnp.int32),
            pltpu.VMEM(weight.shape, low),
            pltpu.VMEM((full, local_width), low),
            pltpu.VMEM((full, local_width), low),
            pltpu.VMEM((full, local_width), high),
            pltpu.VMEM((full, 2 * head_size), low),
            pltpu.VMEM((128, width), low),
            pltpu.VMEM((peers, 2, rows, hidden), high),
            pltpu.VMEM((n, 2, 2, rows, width), low),
            *expert_scratch(gate_weight, up_weight, down_weight, peers, rows, width),
            pltpu.VMEM((2, 2, rows, sent), low),
            pltpu.VMEM((2, hidden, tile), low),
            dma((8,)), dma((9,)), dma((2,)), dma((2, groups)),
            *NearGather.semaphores(n),
            *(Scatter.buffers(n, rows, width) + Gather.semaphores(n)) * 2,
        ],
        compiler_params=communicating(3),
        cost_estimate=pl.CostEstimate(flops=0, bytes_accessed=120 << 20, transcendentals=0),
        name="attention_and_first_expert",
    )(
        query_gain, key_gain, seg_row, tokens, gain, split_rows(named.reshape(-1, 128), peers), router,
        cotangent.reshape(2, rows, width), near.reshape(3, 2, rows, width), raw, cosines, sines, seg_col, weight,
        gate_weight, up_weight, down_weight,
    )


def run_second(gates, rows_all, cotangents, gate_weight, up_weight, down_weight, parts, first_grads, peers, groups):
    _, _, rows, width = rows_all.shape
    n, length = peers // 2, 2 * rows
    hidden = gate_weight.shape[2]
    tile, sent = width // groups, width + 128
    dma = pltpu.SemaphoreType.DMA
    return pl.pallas_call(
        second_kernel,
        out_shape=[
            jax.ShapeDtypeStruct((length, sent), high),
            jax.ShapeDtypeStruct((peers, 2, rows, hidden), low),
            jax.ShapeDtypeStruct((groups, 3 * hidden // groups, width), low),
            *wide_shapes(first_grads)[0],
        ],
        in_specs=[VMEM] + [ANY] * 7,
        out_specs=[VMEM, ANY, ANY, ANY, ANY],
        scratch_shapes=[
            *expert_scratch(gate_weight, up_weight, down_weight, peers, rows, width),
            pltpu.VMEM((n, 2 * length, sent), low),
            pltpu.VMEM((2, hidden, tile), low),
            dma((4,)), dma((2, n)), dma((2, groups)), dma(()), dma((4,)), dma((4,)),
            *Scatter.buffers(n, length, sent),
        ],
        compiler_params=communicating(7),
        cost_estimate=pl.CostEstimate(flops=0, bytes_accessed=120 << 20, transcendentals=0),
        name="second_expert",
    )(
        gates, rows_all, cotangents, gate_weight, up_weight, down_weight, parts.reshape(n, 2 * length, sent),
        first_grads,
    )


def attention_block_backward(
    span_of, raw_ref, query_low_ref, key_low_ref, value_low_ref, inverse_ref, mixed_ref, grad_mixed_ref,
    query_gain_ref, cos_ref, sin_ref, col_ref, row_ref, grad_query_ref, grad_key_ref, grad_value_ref, grad_gain_ref,
):
    begin, rows, first, keys = span_of
    head_size = key_low_ref.shape[1]
    heads = query_low_ref.shape[1] // head_size
    block, span = pl.ds(begin, rows), pl.ds(first, keys)

    @pl.loop(0, heads)
    def each(head):
        columns = pl.ds(pl.multiple_of(head * head_size, head_size), head_size)
        query_low = query_low_ref[block, columns]
        key_low = key_low_ref[span]
        scaled = grad_mixed_ref[block, columns].astype(high) * inverse_ref[block, columns]
        row_term = jnp.sum(scaled * mixed_ref[block, columns].astype(high), axis=-1, keepdims=True)
        scaled = scaled.astype(low)
        scores = dot_last(query_low, key_low)
        allowed = tile_mask(col_ref, row_ref, begin, rows, first, keys)
        terms = jnp.where(allowed, jnp.exp2(scores), 0.0)
        grad_probs = dot_last(scaled, value_low_ref[span])
        grad_scores = (terms * (grad_probs - row_term)).astype(low)
        grad_value_ref[span] += dot_first(terms.astype(low), scaled)
        grad_key_ref[span] += dot_first(grad_scores, query_low) * (1.0 / log2e)
        grad_rotated = dot(grad_scores, key_low) * head_size**-0.5
        grad_normed = unrotate(grad_rotated, cos_ref[block], sin_ref[block])
        grad_raw, gain_rows = norm_back(raw_ref[block, columns], query_gain_ref[...], grad_normed)
        grad_query_ref[block, columns] = grad_raw.astype(low)
        grad_gain_ref[...] += jnp.broadcast_to(jnp.sum(gain_rows, axis=0, keepdims=True), grad_gain_ref.shape)


def input_kernel(
    sums_ref, own_gates_ref, ffn_ref, resid_ref, cot_ref, gain_ffn_ref, router_in, weight_ref,
    query_gain_ref, key_gain_ref, row_ref, tokens_ref, gain_ref,
    raw_hbm, query_low_hbm, key_low_hbm, value_low_hbm, inverse_hbm, mixed_hbm, cos_hbm, sin_hbm, col_hbm,
    projection_hbm, hidden_hbm, wide_0, wide_0a, wide_0b, wide_1,
    input_grad_ref, out_own_ref, gain_grad_ref, ffn_gain_grad_ref, query_gain_grad_ref, key_gain_grad_ref,
    router_grad_ref, projection_grad_hbm, second_a, second_b, first_a, first_b,
    raw_ref, query_low_ref, key_low_ref, value_low_ref, inverse_ref, mixed_ref, cos_ref, sin_ref, col_ref,
    projection_ref, hidden_ref,
    router_ref, own, attn_ref, grad_mixed, grad_resid, own_pair, their_pair, key_part, value_part, columns,
    parts, projection_grad, out_grad, load_sems, store_sem, swap_send, swap_recv, port_send, port_recv,
    wide_left, wide_right, wide_sems,
    send_a, recv_a, local_a, send_b, recv_b, local_b, pair, flow, *rest,
):
    chain = Chain()
    n = chain.n
    scatter_sems, square_buffers = rest[:4], rest[4:]
    full, head_size = key_part.shape
    _, _, rows, width = attn_ref.shape
    query_width = query_low_ref.shape[1]
    sources = (
        raw_hbm.at[:, pl.ds(0, query_width + head_size)], query_low_hbm, key_low_hbm, value_low_hbm, inverse_hbm, mixed_hbm, cos_hbm, sin_hbm, col_hbm,
        projection_hbm, hidden_hbm,
    )
    targets = (
        raw_ref, query_low_ref, key_low_ref, value_low_ref, inverse_ref, mixed_ref, cos_ref, sin_ref, col_ref,
        projection_ref, hidden_ref,
    )
    loads = [
        pltpu.make_async_copy(source, target, load_sems.at[at])
        for at, (source, target) in enumerate(zip(sources, targets))
    ]
    wide = WideSum(wide_0)
    wide_loads = wide.load(wide_0a, wide_0b, wide_left, wide_right, wide_sems)
    for load in wide_loads + loads:
        load.start()
    chain.greet([wide.beside, wide.across])
    ports = Ports(port_send, port_recv)
    wide_first = WideSum(wide_1).first(first_a, first_b, ports)
    SquareSum.start(wide_first)
    router_ref[...] = jnp.zeros_like(router_ref)
    router_ref[: router_in.shape[0]] = router_in[...]
    sent = sums_ref[:, width:]
    left = lax.broadcasted_iota(jnp.int32, sent.shape, 1) < 64
    grad_gates = jnp.where(left, sent + pltpu.roll(sent, 64, 1), 0.0)
    gates = own_gates_ref[...]
    inner = jnp.sum(gates * grad_gates, axis=-1, keepdims=True)
    grad_logits = (gates * (grad_gates - inner)).astype(low)
    grad_hidden = sums_ref[:, :width] + dot(grad_logits, router_ref[...])
    grad_rows, gain_rows = norm_back(resid_ref[...], gain_ffn_ref[...], grad_hidden)
    grad_resid[...] = cot_ref[...].astype(high) + grad_rows
    own[...] = grad_resid[...].astype(low).reshape(2, rows, width)
    gathers = [
        Gather(chain, own.at[half], lambda z, c, half=half: attn_ref.at[2 * z + c, half], *sems)
        for half, sems in enumerate(((send_a, recv_a, local_a), (send_b, recv_b, local_b)))
    ]
    for gather in gathers:
        gather.begin()
    wait_all(wide_loads)
    wide_second = wide.second(wide_left, wide_right, second_a, second_b, ports)
    router_grad_ref[...] = dot_first(grad_logits, ffn_ref[...])[: router_grad_ref.shape[0]]
    ffn_gain_grad_ref[...] = jnp.broadcast_to(
        jnp.sum(gain_rows, axis=0, keepdims=True), ffn_gain_grad_ref.shape
    )
    key_part[...] = jnp.zeros_like(key_part)
    value_part[...] = jnp.zeros_like(value_part)
    query_gain_grad_ref[...] = jnp.zeros_like(query_gain_grad_ref)
    wait_all(loads[:9])
    spans = key_spans(full)

    @pl.loop(0, n)
    def blocks(step):
        z = chain.nearest(step)
        for gather in gathers:
            pl.when(step > 0)(lambda: gather.service(step))
        for gather in gathers:
            pl.when(step == 0)(lambda: gather.keep().wait())
            gather.wait_sibling(z)
        tokens = pl.ds(pl.multiple_of(z * 4 * rows, 4 * rows), 4 * rows)
        grad_mixed[tokens] = dot_last(Split.take(attn_ref, z, Split.both), weight_ref[...]).astype(low)
        for at, span_of in enumerate(spans):

            @pl.when(z == at)
            def backward():
                attention_block_backward(
                    span_of, raw_ref, query_low_ref, key_low_ref, value_low_ref, inverse_ref, mixed_ref, grad_mixed,
                    query_gain_ref, cos_ref, sin_ref, col_ref, row_ref, columns, key_part, value_part,
                    query_gain_grad_ref,
                )

    own_pair[:, :head_size] = key_part[...].astype(low)
    own_pair[:, head_size:] = value_part[...].astype(low)
    swap = pltpu.make_async_remote_copy(
        src_ref=own_pair,
        dst_ref=their_pair,
        send_sem=swap_send,
        recv_sem=swap_recv,
        device_id={"expert": chain.sibling},
        device_id_type=MESH,
    )
    swap.start()
    first = chain.c == 0
    wait_all(loads[9:])
    shared = pl.ds(query_width, head_size)
    projection_ref[:, shared] = jnp.where(
        first, projection_ref[:, shared], projection_ref[:, query_width + head_size :]
    )
    own_width = query_width + head_size
    swap.wait_recv()
    grad_key = key_part[...] + their_pair[:, :head_size].astype(high)
    grad_value = value_part[...] + their_pair[:, head_size:].astype(high)
    key_raw = raw_ref[:, query_width:]
    grad_key, gain_rows = norm_back(
        key_raw, key_gain_ref[...], unrotate(grad_key, cos_ref[...], sin_ref[...])
    )
    columns[:, query_width:] = jnp.where(first, grad_key, grad_value).astype(low)
    key_gain = jnp.where(first, jnp.sum(gain_rows, axis=0, keepdims=True), 0.0)
    key_gain_grad_ref[...] = jnp.broadcast_to(key_gain, key_gain_grad_ref.shape)
    pair_rows = parts.shape[1]
    scatter = Scatter(chain, chip_block(parts, pair_rows // 2), pair, flow, *scatter_sems)
    out_total = SquareSum(out_grad, out_own_ref, *square_buffers, ports)
    projection_tile = projection_grad.shape[0] // n
    out_tile = width // n

    @pl.loop(0, n)
    def each(step):
        z = chain.nearest(n - 1 - step)
        tokens = pl.ds(pl.multiple_of(z * pair_rows, pair_rows), pair_rows)
        parts[z] = dot_last(columns[tokens], projection_ref[:, :own_width]).astype(low)
        scatter.start_pair(z)
        pl.when(step < n - 1)(lambda: scatter.step(n - 1 - step))

        @pl.when(step == 0)
        def out_gradient():
            @pl.loop(0, n)
            def tiles(at):
                span = pl.ds(pl.multiple_of(at * out_tile, out_tile), out_tile)
                out_grad[:, span] = dot_first(mixed_ref[...], Split.every(attn_ref, span)).astype(low)

            out_total.begin()
            SquareSum.start(wide_second)

        span = pl.ds(pl.multiple_of(step * projection_tile, projection_tile), projection_tile)
        projection_grad[span] = dot_first(hidden_ref[:, span], columns[...]).astype(low)

    projection_store = pltpu.make_async_copy(projection_grad, projection_grad_hbm, store_sem)
    projection_store.start()
    out_total.exchange()
    scatter.total(input_grad_ref)
    grad_rows, gain_rows = norm_back(tokens_ref[...].astype(high), gain_ref[...], input_grad_ref[...])
    input_grad_ref[...] = grad_resid[...] + grad_rows
    gain_grad_ref[...] = jnp.broadcast_to(jnp.sum(gain_rows, axis=0, keepdims=True), gain_grad_ref.shape)
    out_total.settle()
    SquareSum.arrive(wide_first + wide_second)
    swap.wait_send()
    for gather in gathers:
        gather.finish()
    scatter.finish()
    ports.finish()
    projection_store.wait()


def run_input(
    sums, own_gates, ffn, resid, cotangent, gain_ffn, router, out_weight, raw, query_low, key_low, value_low,
    inverse, mixed, query_gain, key_gain, cosines, sines, seg_col, seg_row, projection, hidden, tokens, gain,
    first_wide, second_grads, experts, peers,
):
    length, width = tokens.shape
    n, rows = peers // 2, length // 2
    full, head_size = key_low.shape
    query_width = query_low.shape[1]
    loaded = [
        raw, query_low, key_low, value_low, inverse, mixed, cosines, sines, seg_col, projection, hidden,
    ]
    dma = pltpu.SemaphoreType.DMA
    wide_first, wide_second = wide_shapes(second_grads)
    half = (2, *wide_second[0].shape)
    (
        input_grad, out_own, gain_grad, ffn_gain_grad, query_gain_grad, key_gain_grad, router_grad, projection_grad,
        *wide,
    ) = (
        pl.pallas_call(
            input_kernel,
            out_shape=[
                jax.ShapeDtypeStruct((length, width), high),
                jax.ShapeDtypeStruct((query_width // 4, width), low),
                jax.ShapeDtypeStruct((8, width), high),
                jax.ShapeDtypeStruct((8, width), high),
                jax.ShapeDtypeStruct((8, head_size), high),
                jax.ShapeDtypeStruct((8, head_size), high),
                jax.ShapeDtypeStruct((experts, width), high),
                jax.ShapeDtypeStruct((width, query_width + head_size), low),
                *wide_second,
                *wide_first,
            ],
            in_specs=[VMEM] * 13 + [ANY] * (len(loaded) + 4),
            out_specs=[VMEM] * 7 + [ANY] * 5,
            scratch_shapes=[
                pltpu.VMEM((full, query_width + head_size), high),
                *[pltpu.VMEM(array.shape, array.dtype) for array in loaded[1:]],
                pltpu.VMEM((128, width), low),
                pltpu.VMEM((2, rows, width), low),
                pltpu.VMEM((peers, 2, rows, width), low),
                pltpu.VMEM((full, query_width), low),
                pltpu.VMEM((length, width), high),
                pltpu.VMEM((full, 2 * head_size), low),
                pltpu.VMEM((full, 2 * head_size), low),
                pltpu.VMEM((full, head_size), high),
                pltpu.VMEM((full, head_size), high),
                pltpu.VMEM((full, query_width + head_size), low),
                pltpu.VMEM((n, 2 * length, width), low),
                pltpu.VMEM((width, query_width + head_size), low),
                pltpu.VMEM((query_width, width), low),
                dma((len(loaded),)), dma(()), dma(()), dma(()), dma((12,)), dma((12,)),
                pltpu.VMEM(half, low), pltpu.VMEM(half, low), dma((4,)),
                *Gather.semaphores(n) * 2,
                *Scatter.buffers(n, length, width),
                *SquareSum.buffers(query_width, width),
            ],
            compiler_params=communicating(5, 62),
            cost_estimate=pl.CostEstimate(flops=0, bytes_accessed=64 << 20, transcendentals=0),
            name="attention_backward_and_input",
        )(
            sums, own_gates.reshape(length, 128), ffn.reshape(length, width), resid, cotangent, gain_ffn, router,
            out_weight, query_gain, key_gain, seg_row, tokens, gain, *loaded, *first_wide, second_grads,
        )
    )
    return (
        input_grad, projection_grad, out_own, gain_grad, ffn_gain_grad, query_gain_grad, key_gain_grad, router_grad,
        wide[:2], wide[2:],
    )
def weights_kernel(
    attn_gain_ref, ffn_gain_ref, query_gain_ref, key_gain_ref, router_ref, out_own_ref, proj_hbm, resid_hbm,
    gated_0, gated_1, down_hbm, wide_hbm, wide_a, wide_b, done_hbm, done_a, done_b, done_second_a, done_second_b,
    query_grad_ref, key_grad_ref, value_grad_ref, out_grad_ref, small_out_ref, output_ref, wide_second_a, wide_second_b, sum_0, sum_1,
    proj_ref, resid_ref, gated, down_w, mixture, load_sems, all_proj, first_a, first_b, second_a, second_b,
    send_a, send_b, quarter, small, got, part, small_sum, total_mixture,
    port_send, port_recv, swap_send, swap_recv, send_1, recv_1, send_2, recv_2, send_3, recv_3,
    wide_left, wide_right, wide_sems, last, last_sems, pair, flow, *scatter_sems,
):
    peers = lax.axis_size("expert")
    me = lax.axis_index("expert")
    group, y, x, from_x, from_y = square()
    beside, across = {"dp": from_x}, {"dp": from_y}
    chain = Chain()
    scatter = Scatter(chain, chip_block(mixture, resid_ref.shape[0]), pair, flow, *scatter_sems)
    loads = [
        pltpu.make_async_copy(source, target, load_sems.at[at])
        for at, (source, target) in enumerate(
            (
                (proj_hbm, proj_ref), (gated_0, gated.at[0]), (gated_1, gated.at[1]),
                (down_hbm, down_w), (resid_hbm, resid_ref),
            )
        )
    ]
    wide = WideSum(wide_hbm)
    wide_loads = wide.load(wide_a, wide_b, wide_left, wide_right, wide_sems)
    for load in wide_loads + loads:
        load.start()
    width = resid_ref.shape[1]
    head_size = query_gain_ref.shape[1]
    piece = width // peers

    def small_piece(ref, peer):
        return ref.at[:, pl.ds(pl.multiple_of(peer * piece, piece), piece)]

    barrier = pltpu.get_barrier_semaphore()
    others = [(me + shift) % peers for shift in range(1, peers)]
    groups = [(group + shift) % 4 for shift in range(1, 4)]
    for peer in others:
        pl.semaphore_signal(barrier, inc=1, device_id={"expert": peer}, device_id_type=MESH)
    for other in groups:
        pl.semaphore_signal(barrier, inc=1, device_id={"dp": other}, device_id_type=MESH)
    pl.semaphore_wait(barrier, peers + 2)

    shard_rows, columns = proj_ref.shape[1:]
    rows, half = shard_rows // 4, peers // 2
    ports = Ports(port_send, port_recv)

    def proj_part(side, q, ref=proj_ref):
        return ref.at[pl.ds(side * half, half), pl.ds(pl.multiple_of(q * rows, rows), rows)]

    def remote(source, target, send, recv, device):
        return pltpu.make_async_remote_copy(
            src_ref=source, dst_ref=target, send_sem=send, recv_sem=recv, device_id=device, device_id_type=MESH
        )

    def close(grads, first_a, first_b, second_a, second_b, total):
        middle = width // 2
        for side, first, second in ((0, first_a.at[y], second_a), (1, first_b.at[x], second_b)):
            columns = pl.ds(side * middle, middle)
            pieces = [
                pltpu.make_async_copy(source, last.at[at], last_sems.at[at])
                for at, source in enumerate((grads.at[group, :, columns], first, second))
            ]
            for copy in pieces:
                copy.start()
            wait_all(pieces)
            last[0] = (last[0].astype(high) + last[1].astype(high) + last[2].astype(high)).astype(low)
            store = pltpu.make_async_copy(last.at[0], total.at[:, columns], last_sems.at[3])
            store.start()
            store.wait()

    along_x = [2 * other + 1 - x for other in range(2)]
    along_y = [2 * (1 - y) + other for other in range(2)]
    proj_1a = [ports.copy(proj_part(0, along_x[k], proj_hbm), first_a.at[k], beside) for k in range(2)]
    proj_1b = [ports.copy(proj_part(1, along_y[k], proj_hbm), first_b.at[k], across) for k in range(2)]
    for copy in proj_1a + proj_1b:
        copy.start()
    out_copy = SquareCopy(out_own_ref, out_grad_ref, ports)
    out_copy.begin()

    small[...] = jnp.zeros_like(small)
    small[0:1] = attn_gain_ref[0:1]
    small[1:2] = ffn_gain_ref[0:1]
    small[2:3, :head_size] = query_gain_ref[0:1]
    small[3:4, :head_size] = key_gain_ref[0:1]
    small[8:] = router_ref[...]
    small_1 = [
        remote(small_piece(small, peer), got.at[me], send_1.at[at], recv_1.at[me], {"expert": peer})
        for at, peer in enumerate(others)
    ]
    for copy in small_1:
        copy.start()
    got[me] = small_piece(small, me)[...]
    wait_all(loads)

    def mixture_rows(step):
        z = chain.nearest(chain.n - 1 - step)

        @pl.loop(0, 4)
        def columns(at):
            span = pl.ds(pl.multiple_of(at * (width // 4), width // 4), width // 4)
            mixture[z, :, span] = (dot(gated[0, z], down_w[0, :, span]) + dot(gated[1, z], down_w[1, :, span])).astype(low)

        scatter.start_pair(z)

    @pl.loop(0, chain.n)
    def each_chip(step):
        mixture_rows(step)


    own = group
    for_y, for_x = 2 * (1 - y) + x, 2 * y + 1 - x
    scatter.step(3) if chain.n > 3 else None
    for copy in proj_1a + proj_1b:
        copy.wait_recv()
    send_a[...] = (proj_part(0, for_y)[...].astype(high) + first_a[1 - y].astype(high)).astype(low)
    send_b[...] = (proj_part(1, for_x)[...].astype(high) + first_b[1 - x].astype(high)).astype(low)
    proj_2a = ports.copy(send_a, second_a, across)
    proj_2b = ports.copy(send_b, second_b, beside)
    proj_2a.start()
    proj_2b.start()
    wait_all(wide_loads)
    wide_sent = wide.second(wide_left, wide_right, wide_second_a, wide_second_b, ports)
    SquareSum.start(wide_sent)
    close(done_hbm, done_a, done_b, done_second_a, done_second_b, sum_0)
    scatter.step(2) if chain.n > 2 else None

    for at, peer in enumerate(others):
        remote(got.at[peer], got.at[peer], send_1.at[at], recv_1.at[peer], {"expert": peer}).wait_recv()
    total = got[0]
    for at in range(1, peers):
        total = total + got[at]
    part[group] = total
    small_2 = [
        remote(part.at[group], part.at[group], send_2.at[at], recv_2.at[group], {"dp": other})
        for at, other in enumerate(groups)
    ]
    for copy in small_2:
        copy.start()

    proj_2a.wait_recv()
    proj_2b.wait_recv()
    for side, first, second, at in ((0, first_a, second_a, y), (1, first_b, second_b, x)):
        quarter[pl.ds(side * half, half)] = (
            proj_part(side, own)[...].astype(high) + first[at].astype(high) + second[...].astype(high)
        ).astype(low)
    swaps = [
        remote(quarter.at[peer], all_proj.at[own, me], swap_send.at[at], swap_recv.at[me], {"expert": peer})
        for at, peer in enumerate(others)
    ]
    for copy in swaps:
        copy.start()
    all_proj[own, me] = quarter[me]

    for at, other in enumerate(groups):
        remote(part.at[other], part.at[other], send_2.at[at], recv_2.at[other], {"dp": other}).wait_recv()
    total = part[0]
    for at in range(1, 4):
        total = total + part[at]
    small_sum[me] = total
    small_3 = [
        remote(small_sum.at[me], small_sum.at[me], send_3.at[at], recv_3.at[me], {"expert": peer})
        for at, peer in enumerate(others)
    ]
    for copy in small_3:
        copy.start()

    for at, peer in enumerate(others):
        block = all_proj.at[own, peer]
        remote(block, block, swap_send.at[at], swap_recv.at[peer], {"expert": peer}).wait_recv()
    proj_gx = ports.copy(all_proj.at[own], all_proj.at[own], beside)
    proj_gy = ports.copy(all_proj.at[own], all_proj.at[own], across)
    proj_gx.start()
    proj_gy.start()
    far = 3 - group
    scatter.step(1) if chain.n > 1 else None
    out_copy.hand_on()
    SquareSum.arrive(wide_sent)
    close(wide_hbm, wide_a, wide_b, wide_second_a, wide_second_b, sum_1)

    def proj_half(q, side):
        return all_proj.at[q, pl.ds(side * half, half)]

    proj_gx.wait_recv()
    proj_gy.wait_recv()
    proj_fa = ports.copy(proj_half(from_x, 0), proj_half(from_x, 0), across)
    proj_fb = ports.copy(proj_half(from_y, 1), proj_half(from_y, 1), beside)
    proj_fa.start()
    proj_fb.start()
    query_width = columns - head_size

    def spread(q):
        block = pl.ds(pl.multiple_of(q * rows, rows), rows)
        for peer in range(peers):
            query_grad_ref[block, peer * query_width : (peer + 1) * query_width] = all_proj[q, peer, :, :query_width]
            shared = key_grad_ref if peer % 2 == 0 else value_grad_ref
            at = peer // 2 * head_size
            shared[block, at : at + head_size] = all_proj[q, peer, :, query_width:]

    spread(own)
    spread(from_x)
    spread(from_y)
    for at, peer in enumerate(others):
        block = small_sum.at[peer]
        remote(block, block, send_3.at[at], recv_3.at[peer], {"expert": peer}).wait_recv()
    for peer in range(peers):
        small_out_ref[:, peer * piece : (peer + 1) * piece] = small_sum[peer]
    scatter.total(total_mixture)
    output_ref[...] = (resid_ref[...] + total_mixture[...]).astype(low)
    out_copy.finish()
    proj_fa.wait_recv()
    proj_fb.wait_recv()
    spread(far)
    ports.finish()
    scatter.finish()
    for copy in small_1 + small_2 + small_3 + swaps:
        copy.wait_send()


def run_weights(
    grad_projection, out_own, attn_gain, ffn_gain, query_gain, key_gain, router, resid, first_gated, second_gated,
    down_weight, second_wide, first_wide, peers, kv_heads,
):
    width, columns = grad_projection.shape
    head_size = query_gain.shape[1]
    length = resid.shape[0]
    n = peers // 2
    shard_rows = width // peers
    rows, half = shard_rows // 4, peers // 2
    small_rows = 8 + router.shape[0]
    piece = (small_rows, width // peers)
    hidden = down_weight.shape[1]
    dma = pltpu.SemaphoreType.DMA
    kv_width = kv_heads * head_size
    query_width = columns - head_size

    _, wide_second = wide_shapes(second_wide[0])
    wide_half = (2, *wide_second[0].shape)

    def low_buffer(*shape):
        return pltpu.VMEM(shape, low)

    return pl.pallas_call(
        weights_kernel,
        out_shape=[
            jax.ShapeDtypeStruct((shard_rows, peers * query_width), low),
            jax.ShapeDtypeStruct((shard_rows, kv_width), low),
            jax.ShapeDtypeStruct((shard_rows, kv_width), low),
            jax.ShapeDtypeStruct((4 * out_own.shape[0], width), low),
            jax.ShapeDtypeStruct((small_rows, width), high),
            jax.ShapeDtypeStruct((length, width), low),
            *wide_second,
            *[jax.ShapeDtypeStruct(second_wide[0].shape[1:], low)] * 2,
        ],
        in_specs=[VMEM] * 6 + [ANY] * 13,
        out_specs=[VMEM] * 6 + [ANY] * 4,
        scratch_shapes=[
            low_buffer(peers, shard_rows, columns),
            pltpu.VMEM(resid.shape, high),
            low_buffer(2, n, 2 * length, hidden),
            low_buffer(*down_weight.shape),
            low_buffer(n, 2 * length, width),
            dma((5,)),
            low_buffer(4, peers, rows, columns),
            low_buffer(2, half, rows, columns),
            low_buffer(2, half, rows, columns),
            low_buffer(half, rows, columns),
            low_buffer(half, rows, columns),
            low_buffer(half, rows, columns),
            low_buffer(half, rows, columns),
            low_buffer(peers, rows, columns),
            pltpu.VMEM((small_rows, width), high),
            pltpu.VMEM((peers, *piece), high),
            pltpu.VMEM((4, *piece), high),
            pltpu.VMEM((peers, *piece), high),
            pltpu.VMEM((length, width), high),
            dma((16,)), dma((16,)),
            dma((peers - 1,)), dma((peers,)),
            dma((peers - 1,)), dma((peers,)),
            dma((3,)), dma((4,)),
            dma((peers - 1,)), dma((peers,)),
            low_buffer(*wide_half), low_buffer(*wide_half), dma((4,)),
            low_buffer(3, *wide_second[0].shape), dma((4,)),
            *Scatter.buffers(n, length, width),
        ],
        compiler_params=communicating(6),
        cost_estimate=pl.CostEstimate(flops=0, bytes_accessed=64 << 20, transcendentals=0),
        name="sum_weight_gradients",
    )(
        attn_gain, ffn_gain, query_gain, key_gain, router, out_own, grad_projection.reshape(peers, shard_rows, columns),
        resid, first_gated.reshape(n, 2 * length, hidden), second_gated.reshape(n, 2 * length, hidden),
        down_weight, *second_wide, *first_wide,
    )


def widen_kernel(
    gate_0, up_0, down_0, gate_1, up_1, down_1, query_in, key_in, value_in, out_in, small_ref,
    gate_ref, up_ref, down_ref, query_ref, key_ref, value_ref, out_ref,
    attn_gain_ref, ffn_gain_ref, query_gain_ref, key_gain_ref, router_ref,
):
    for expert, (gate, up, down) in enumerate(((gate_0, up_0, down_0), (gate_1, up_1, down_1))):

        @pl.when(pl.program_id(0) == expert)
        def place():
            gate_ref[0] = gate[...].astype(high)
            up_ref[0] = up[...].astype(high)
            tile = down_ref.shape[3]
            for part in range(down_ref.shape[1]):
                down_ref[0, part] = down[:, part * tile : (part + 1) * tile].astype(high)

    for source, target in ((query_in, query_ref), (key_in, key_ref), (value_in, value_ref), (out_in, out_ref)):
        target[...] = source[...].astype(high)

    @pl.when((pl.program_id(0) == 0) & (pl.program_id(1) == 0))
    def small():
        attn_gain_ref[...] = small_ref[0]
        ffn_gain_ref[...] = small_ref[1]
        query_gain_ref[...] = small_ref[2, : query_gain_ref.shape[0]]
        key_gain_ref[...] = small_ref[3, : key_gain_ref.shape[0]]
        router_ref[...] = small_ref[8:]


def run_widen(grads, weight_grads, small, head_size, hidden_units, model_width, groups):
    piece, tile = hidden_units // groups, model_width // groups
    operands, specs = [], []
    block = piece // groups

    def of_expert(expert):
        return lambda x, j: jnp.where(x == expert, j, 0 if expert else groups - 1)

    for expert, rows in enumerate(grads):
        turn = of_expert(expert)
        operands += [rows] * 3
        specs += [
            pl.BlockSpec((block, model_width), lambda x, j, turn=turn, at=at: (at * groups + turn(x, j), 0))
            for at in range(3)
        ]
    steps = 2 * groups
    small_shapes = [
        (model_width,), (model_width,), (head_size,), (head_size,), (small.shape[0] - 8, model_width),
    ]

    def rows_of(array):
        return pl.BlockSpec((array.shape[0] // steps, array.shape[1]), lambda x, j: (x * groups + j, 0))

    return pl.pallas_call(
        widen_kernel,
        grid=(2, groups),
        out_shape=[
            jax.ShapeDtypeStruct((2, piece, model_width), high),
            jax.ShapeDtypeStruct((2, piece, model_width), high),
            jax.ShapeDtypeStruct((2, groups, piece, tile), high),
            *[jax.ShapeDtypeStruct(array.shape, high) for array in weight_grads],
            *[jax.ShapeDtypeStruct(shape, high) for shape in small_shapes],
        ],
        in_specs=specs + [rows_of(array) for array in weight_grads] + [pl.BlockSpec(small.shape, lambda x, j: (0, 0))],
        out_specs=[
            pl.BlockSpec((1, block, model_width), lambda x, j: (x, j, 0)),
            pl.BlockSpec((1, block, model_width), lambda x, j: (x, j, 0)),
            pl.BlockSpec((1, groups, block, tile), lambda x, j: (x, 0, j, 0)),
            *[rows_of(array) for array in weight_grads],
            *[pl.BlockSpec(shape, lambda x, j, rank=len(shape): (0,) * rank) for shape in small_shapes],
        ],
        compiler_params=pltpu.CompilerParams(vmem_limit_bytes=60 << 20),
        name="widen",
    )(*operands, *weight_grads, small)


def gather_tokens(rows):
    return lax.all_gather(rows, "expert", axis=0, tiled=True)


def scatter_sum(partial):
    return lax.psum_scatter(partial, "expert", scatter_dimension=0, tiled=True)


def projection_gradients(grad_projection, peers, kv_heads, head_size):
    width, columns = grad_projection.shape
    shard_rows = width // peers
    local_width = columns - head_size
    sharers = peers // kv_heads
    grad_projection = grad_projection.reshape(peers, shard_rows, columns)
    grad_projection = lax.psum_scatter(grad_projection, "dp", scatter_dimension=1, tiled=True)
    grad_projection = lax.all_to_all(
        grad_projection, "expert", split_axis=0, concat_axis=0, tiled=True
    )
    grad_projection = lax.all_gather(grad_projection, "dp", axis=1, tiled=True)
    grad_query_w = (
        grad_projection[:, :, :local_width].transpose(1, 0, 2).reshape(shard_rows, peers * local_width)
    ).astype(high)
    shared = grad_projection[:, :, local_width:].reshape(kv_heads, sharers, shard_rows, head_size)
    kv_width = kv_heads * head_size
    grad_key_w = shared[:, 0].transpose(1, 0, 2).reshape(shard_rows, kv_width).astype(high)
    grad_value_w = shared[:, 1].transpose(1, 0, 2).reshape(shard_rows, kv_width).astype(high)
    return grad_query_w, grad_key_w, grad_value_w


def out_gradient(grad_out):
    summed = lax.psum_scatter(grad_out, "dp", scatter_dimension=0, tiled=True)
    return lax.all_gather(summed, "dp", axis=0, tiled=True).astype(high)


def constant_tables(length, head_size):
    half = head_size // 2
    freqs = np.float32(rope_base) ** (-np.arange(half, dtype=np.float32) * np.float32(2.0 / head_size))
    angles = np.arange(length, dtype=np.float32)[:, None] * freqs[None, :]
    cosines, sines = np.cos(angles), np.sin(angles)
    return (
        jnp.asarray(np.concatenate([cosines, cosines], 1), high),
        jnp.asarray(np.concatenate([-sines, sines], 1), high),
    )


def fits_kernels(peers, groups, sharers, experts, full_length, width):
    return groups == 4 and peers == 8 and sharers == 2 and experts == 2 * peers and full_length * width <= 1 << 21


def fused_layer(
    tokens, segments, routes, cotangent, norm_gain_attn, query_weight, key_matrix, value_matrix, query_gain,
    key_gain, out_weight, norm_gain_ffn, router_weight, gate_weight, up_weight, down_weight, heads,
):
    length, model_width = tokens.shape
    head_size = query_gain.shape[0]
    peers = lax.axis_size("expert")
    groups = lax.axis_size("dp")
    local_experts, _, hidden_units = gate_weight.shape
    experts = local_experts * peers
    full_length = length * peers
    kv_heads = peers // 2
    local_width = heads * head_size
    gain_attn_row = norm_gain_attn.reshape(1, model_width)
    gain_ffn_row = norm_gain_ffn.reshape(1, model_width)

    hidden, all_named, near, seg_col, projection, raw = run_gather(
        tokens, gain_attn_row, routes.T, segments, cotangent, query_weight, key_matrix, value_matrix, peers, groups
    )
    cosines, sines = constant_tables(full_length, head_size)
    seg_row = segments
    query_gain_row = query_gain.reshape(1, head_size)
    key_gain_row = key_gain.reshape(1, head_size)
    router = router_weight.T
    (
        key_low, value_low, own_gates, resid, ffn_local, gates, mixed, query_low, inverse, rows_all, cotangents,
        first_gated, parts, first_grads,
    ) = run_first(
        raw, query_gain_row, key_gain_row, cosines, sines, seg_col, seg_row, out_weight, tokens, gain_ffn_row,
        all_named, router, cotangent, near, gate_weight, up_weight, down_weight, peers, groups,
    )
    sums, second_gated, second_grads, *first_step = run_second(
        gates, rows_all, cotangents, gate_weight, up_weight, down_weight, parts, first_grads, peers, groups
    )
    (
        input_grad, grad_projection, out_own, gain_attn_part, gain_ffn_part, query_gain_part, key_gain_part,
        grad_router, first_end, second_step,
    ) = run_input(
        sums, own_gates, ffn_local, resid, cotangent, gain_ffn_row, router, out_weight, raw, query_low, key_low,
        value_low, inverse, mixed, query_gain_row, key_gain_row, cosines, sines, seg_col, seg_row, projection,
        hidden, tokens, gain_attn_row, (first_grads, *first_step), second_grads, experts, peers,
    )
    *weight_grads, small, output, _, _, first_sum, second_sum = run_weights(
        grad_projection, out_own, gain_attn_part, gain_ffn_part, query_gain_part, key_gain_part, grad_router,
        resid, first_gated, second_gated, down_weight, (second_grads, *second_step),
        (first_grads, *first_step, *first_end), peers, kv_heads,
    )
    grads = (first_sum, second_sum)
    gate_w, up_w, down_w, query_w, key_w, value_w, out_w, *sums = run_widen(
        grads, weight_grads, small, head_size, hidden_units, model_width, groups
    )
    gain_attn_grad, gain_ffn_grad, query_gain_grad, key_gain_grad, router_grad = sums
    return (
        output,
        input_grad,
        gain_attn_grad,
        query_w,
        key_w,
        value_w,
        query_gain_grad,
        key_gain_grad,
        out_w,
        gain_ffn_grad,
        router_grad.T,
        gate_w.transpose(0, 2, 1),
        up_w.transpose(0, 2, 1),
        down_w.reshape(local_experts, hidden_units, model_width // groups),
    )


def on_device(
    tokens,
    segments,
    routes,
    cotangent,
    norm_gain_attn,
    query_weight,
    key_matrix,
    value_matrix,
    query_gain,
    key_gain,
    out_weight,
    norm_gain_ffn,
    router_weight,
    gate_weight,
    up_weight,
    down_weight,
):
    length, model_width = tokens.shape
    head_size = query_gain.shape[0]
    peers = lax.axis_size("expert")
    groups = lax.axis_size("dp")
    me = lax.axis_index("expert")
    group = lax.axis_index("dp")
    shard_rows, query_width = query_weight.shape
    kv_width = key_matrix.shape[1]
    kv_heads = kv_width // head_size
    heads = query_width // head_size // peers
    sharers = peers // kv_heads
    local_width = heads * head_size
    local_experts = gate_weight.shape[0]
    experts = local_experts * peers
    full_length = length * peers
    piece = shard_rows // groups

    if fits_kernels(peers, groups, sharers, experts, full_length, model_width):
        return fused_layer(
            tokens, segments, routes, cotangent, norm_gain_attn, query_weight, key_matrix, value_matrix,
            query_gain, key_gain, out_weight, norm_gain_ffn, router_weight, gate_weight, up_weight, down_weight, heads,
        )

    def own_rows(matrix):
        return lax.dynamic_slice_in_dim(matrix, group * piece, piece, 0)

    def columns(matrix, width, copies):
        split = own_rows(matrix).reshape(piece, -1, width).transpose(1, 0, 2)
        return jnp.repeat(split, copies, axis=0)

    outgoing = jnp.concatenate(
        [
            columns(query_weight, local_width, 1),
            columns(key_matrix, head_size, sharers),
            columns(value_matrix, head_size, sharers),
        ],
        axis=2,
    )
    arrived = lax.all_to_all(outgoing, "expert", split_axis=0, concat_axis=0, tiled=True)
    projection = lax.all_gather(arrived, "dp", axis=1, tiled=True).reshape(model_width, -1)

    inputs = tokens.astype(high)
    hidden_local = norm_rows(inputs, norm_gain_attn).astype(low)
    hidden = gather_tokens(hidden_local)
    raw = dot(hidden, projection)
    cosines, sines = rotary_tables(full_length, head_size)
    seg_col = jnp.broadcast_to(segments.reshape(full_length, 1), (full_length, head_size))
    seg_row = jnp.broadcast_to(segments.reshape(1, full_length), (8, full_length))
    query_gain_row = query_gain.reshape(1, head_size)
    key_gain_row = key_gain.reshape(1, head_size)
    mixed, query_low, key_low, value_low, inverse = run_attention_forward(
        raw, heads, head_size, query_gain_row, key_gain_row, cosines, sines, seg_col, seg_row
    )
    attn = scatter_sum(dot(mixed, out_weight).astype(low))
    resid = inputs + attn.astype(high)
    ffn_local = norm_rows(resid, norm_gain_ffn).astype(low)
    ffn_rows = gather_tokens(ffn_local)
    cotangents = gather_tokens(cotangent)
    all_routes = gather_tokens(routes)

    def gates_of(rows, route_rows):
        logits = dot(rows, router_weight)
        named = jnp.any(
            route_rows[:, :, None] == jnp.arange(experts, dtype=jnp.int32)[None, None, :], axis=1
        )
        top = jnp.max(jnp.where(named, logits, -jnp.inf), axis=-1, keepdims=True)
        terms = jnp.where(named, jnp.exp(jnp.where(named, logits - top, 0.0)), 0.0)
        return terms / jnp.sum(terms, axis=-1, keepdims=True)

    gates_all = gates_of(ffn_rows, all_routes)
    own_gates = lax.dynamic_slice_in_dim(gates_all, me * local_experts, local_experts, 1)
    mixture = 0.0
    grad_rows = 0.0
    gate_grads, grad_gate_w, grad_up_w, grad_down_w = [], [], [], []
    for expert in range(local_experts):
        gate_col = own_gates[:, expert : expert + 1]
        gate_pre = dot(ffn_rows, gate_weight[expert])
        up_pre = dot(ffn_rows, up_weight[expert])
        share = jax.nn.sigmoid(gate_pre)
        silu = gate_pre * share
        act = silu * up_pre
        gated_act = (act * gate_col).astype(low)
        mixture = mixture + dot(gated_act, down_weight[expert])
        plain = dot_last(cotangents, down_weight[expert])
        gate_grads.append(jnp.sum(act * plain, axis=-1, keepdims=True))
        grad_act = plain * gate_col
        grad_gate_pre = (grad_act * up_pre * (share * (1.0 + gate_pre * (1.0 - share)))).astype(low)
        grad_up_pre = (grad_act * silu).astype(low)
        grad_rows = (
            grad_rows
            + dot_last(grad_gate_pre, gate_weight[expert])
            + dot_last(grad_up_pre, up_weight[expert])
        )
        hidden_units = gated_act.shape[1]
        grad_gate_w.append(dot_first(grad_gate_pre, ffn_rows).astype(low).reshape(groups, -1, model_width))
        grad_up_w.append(dot_first(grad_up_pre, ffn_rows).astype(low).reshape(groups, -1, model_width))
        cut_width = model_width // groups
        grad_down_w.append(
            jnp.stack([
                dot_first(gated_act, cotangents[:, part * cut_width : (part + 1) * cut_width]).astype(low)
                for part in range(groups)
            ])
        )

    gate_grad = jnp.concatenate(gate_grads, axis=1)
    lane_pad = 128 - 2 * experts % 128
    placed = jnp.zeros((full_length, experts), high)
    placed = lax.dynamic_update_slice_in_dim(placed, gate_grad, me * local_experts, 1)
    upper = placed.astype(low)
    lower = (placed - upper.astype(high)).astype(low)
    sent = jnp.concatenate(
        [grad_rows.astype(low), upper, lower, jnp.zeros((full_length, lane_pad), low)], axis=1
    )
    summed_rows = scatter_sum(sent)
    output = (resid + scatter_sum(mixture.astype(low)).astype(high)).astype(low)
    grad_gates = summed_rows[:, model_width : model_width + experts].astype(high) + summed_rows[
        :, model_width + experts : model_width + 2 * experts
    ].astype(high)
    gates = gates_of(ffn_local, routes)
    grad_logits = (
        gates * (grad_gates - jnp.sum(gates * grad_gates, axis=-1, keepdims=True))
    ).astype(low)
    grad_router = dot_first(ffn_local, grad_logits)
    grad_hidden_ffn = summed_rows[:, :model_width].astype(high) + dot_last(grad_logits, router_weight)
    grad_resid_norm, gain_rows_ffn = norm_back(resid, norm_gain_ffn, grad_hidden_ffn)
    grad_resid = cotangent.astype(high) + grad_resid_norm
    grad_attn = gather_tokens(grad_resid.astype(low))
    grad_mixed = dot_last(grad_attn, out_weight).astype(low)
    grad_out = dot_first(mixed, grad_attn)
    grad_query_low, grad_key_part, grad_value_part, query_gain_part = run_attention_backward(
        raw, query_low, key_low, value_low, inverse, mixed, grad_mixed, heads, head_size,
        query_gain_row, cosines, sines, seg_col, seg_row,
    )
    both = jnp.concatenate([grad_key_part, grad_value_part], axis=1)
    step = 1
    while step < sharers:
        swap = [(peer, peer ^ step) for peer in range(peers)]
        both = both + lax.ppermute(both.astype(low), "expert", swap).astype(high)
        step *= 2
    grad_key_rot, grad_value = both[:, :head_size], both[:, head_size:].astype(low)
    place = me % sharers
    half = head_size // 2
    swapped = jnp.concatenate([grad_key_rot[:, half:], grad_key_rot[:, :half]], axis=1)
    key_raw = raw[:, local_width : local_width + head_size]
    grad_key, key_gain_rows = norm_back(key_raw, key_gain, grad_key_rot * cosines - swapped * sines)
    grad_shared = jnp.where(
        place == 0, grad_key.astype(low), jnp.where(place == 1, grad_value, jnp.zeros_like(grad_value))
    )
    own_columns = jnp.concatenate([grad_query_low, grad_shared], axis=1)
    shared_weight = jnp.where(
        place == 0,
        projection[:, local_width : local_width + head_size],
        projection[:, local_width + head_size :],
    )
    own_weight = jnp.concatenate([projection[:, :local_width], shared_weight], axis=1)
    grad_hidden_attn = scatter_sum(dot_last(own_columns, own_weight).astype(low)).astype(high)
    grad_inputs_norm, gain_rows_attn = norm_back(inputs, norm_gain_attn, grad_hidden_attn)
    input_grad = grad_resid + grad_inputs_norm

    grad_query_w, grad_key_w, grad_value_w = projection_gradients(
        dot_first(hidden, own_columns).astype(low), peers, kv_heads, head_size
    )
    grad_out_w = out_gradient(grad_out.astype(low))

    wide = jnp.concatenate(grad_gate_w + grad_up_w, axis=1)
    wide = lax.psum_scatter(wide, "dp", scatter_dimension=0, tiled=True)
    wide = wide.reshape(2, local_experts, hidden_units // groups, model_width).transpose(0, 1, 3, 2)
    wide = wide.astype(high)
    down = jnp.concatenate(grad_down_w, axis=1)
    down = lax.psum_scatter(down, "dp", scatter_dimension=0, tiled=True)
    down = down.reshape(local_experts, hidden_units, cut_width).astype(high)
    expert_sums = (wide[0], wide[1], down)
    key_gain_grad = jnp.where(place == 0, jnp.sum(key_gain_rows, axis=0), 0.0)
    small = jnp.concatenate(
        [
            jnp.sum(gain_rows_attn, axis=0),
            jnp.sum(gain_rows_ffn, axis=0),
            query_gain_part[0],
            key_gain_grad,
            grad_router.reshape(-1),
        ]
    )
    small = lax.psum(small, ("dp", "expert"))
    cut = 2 * model_width
    return (
        output,
        input_grad,
        small[:model_width],
        grad_query_w,
        grad_key_w,
        grad_value_w,
        small[cut : cut + head_size],
        small[cut + head_size : cut + 2 * head_size],
        grad_out_w,
        small[model_width:cut],
        small[cut + 2 * head_size :].reshape(model_width, experts),
        *expert_sums,
    )


def solution(mesh):
    rows = P(("dp", "expert"), None)
    split = P("expert", None)
    cube = P("expert", None, None)
    cut = P("expert", None, "dp")
    return jax.shard_map(
        on_device,
        mesh=mesh,
        in_specs=(
            rows, P("dp", None), rows, rows, P(), split, split, split, P(), P(), split, P(), P(),
            cube, cube, cube,
        ),
        out_specs=(
            rows, rows, P(), split, split, split, P(), P(), split, P(), P(), cut, cut, cut,
        ),
        check_vma=False,
    )
```
